32 devices in a mesh: section: 2 (over core), dp: 4 (over y, x), tensor: 4 (over z).
Axes of the slice: x: 2, y: 2, z: 4, core: 2. Of those that a mesh axis runs over, the one named last changes fastest.
Arguments:
- boundary_in: float32 [2, 16, 577, 1024], P('section', 'dp', None, 'tensor'), may hold values from -6 to 6
- counts: int32 [4, 2], P('dp'), may hold values from 1 to 2, as said below
- qkv_weight: bfloat16 [2, 1024, 3, 1024], P('section', 'dp', None, 'tensor'), may hold values from -0.1875 to 0.1875
- proj_weight: bfloat16 [2, 1024, 1024], P('section', 'tensor', 'dp'), may hold values from -1 to 1
- fc1_weight: bfloat16 [2, 1024, 4096], P('section', 'dp', 'tensor'), may hold values from -0.1875 to 0.1875
- fc2_weight: bfloat16 [2, 4096, 1024], P('section', 'tensor', 'dp'), may hold values from -0.09375 to 0.09375
- vectors: bfloat16 [2, 8, 4, 256], P('section', None, 'tensor', 'dp')
- fc1_bias: bfloat16 [2, 4, 1024], P('section', 'tensor', 'dp'), may hold values from -3 to 3
Outputs:
- boundary_out: float32 [2, 16, 577, 1024], P('section', 'dp', None, 'tensor')
- grad_qkv: float32 [2, 1024, 3, 1024], P('section', 'dp', None, 'tensor')
- grad_proj: float32 [2, 1024, 1024], P('section', 'tensor', 'dp')
- grad_fc1: float32 [2, 1024, 4096], P('section', 'dp', 'tensor')
- grad_fc2: float32 [2, 4096, 1024], P('section', 'tensor', 'dp')
- grad_vectors: float32 [2, 8, 4, 256], P('section', None, 'tensor', 'dp')
- grad_fc1_bias: float32 [2, 4, 1024], P('section', 'tensor', 'dp')
The draws below stay inside these ranges and needn't reach their ends.
Inputs may be any that keep to these rules, and one draw needn't show every extreme that they name: The first counts[s, m] slots of micro-batch m of data shard s are live; some count equals 2 and some count equals 1.
All inputs are finite; a program needn't handle non-finite values.
Results may differ from the reference program's by a relative error of at most 0.013.
Values may be sent and summed in bfloat16 or wider, within the bound.
No kernel may reach another device: no remote copies, remote signals or barrier semaphores. Data moves between devices by JAX's collectives and lax.ppermute only.
A program may use at most 256 MiB of HBM per device.

```python
import jax
import jax.numpy as jnp
from jax import lax

D = 1024
HEADS = 16
HD = 64
FF = 4096
L = 577
MB = 2
CAP = 2
SLOTS = 16
N_TENSOR = 4


def draw_counts(key, part):
    key = jax.random.fold_in(key, 11)
    cells = SLOTS // CAP
    keyring = jax.random.split(key, 3)
    values = jax.random.randint(keyring[0], (cells,), 1, CAP + 1)
    upper = jax.random.randint(keyring[1], (), 0, cells)
    lower = (upper + 1 + jax.random.randint(keyring[2], (), 0, cells - 1)) % cells
    values = values.at[upper].set(CAP).at[lower].set(1)
    return values.reshape(cells // MB, MB).astype(jnp.int32)


def draw_vectors(key, part):
    key = jax.random.fold_in(key, 23)
    first_key, second_key = jax.random.split(key)
    gains = jax.random.uniform(first_key, (2, 8, D), jnp.float32, 0.5, 1.5)
    shifts = 0.4 * jax.random.normal(second_key, (2, 8, D), jnp.float32)
    row_index = jnp.arange(8)[None, :, None]
    is_gain = (row_index == 0) | (row_index == 5)
    values = jnp.where(is_gain, gains, shifts)
    return values.reshape(2, 8, N_TENSOR, D // N_TENSOR).astype(jnp.bfloat16)


def level_of(key, shape, cuts, smallest, largest):
    loudness = 1.0
    for axis_at, parts in cuts:
        draws = jax.random.uniform(jax.random.fold_in(jax.random.fold_in(key, 6), axis_at), (parts,), jnp.float32, smallest / len(cuts), largest / len(cuts))
        loudness = loudness * jnp.repeat(jnp.exp(draws), shape[axis_at] // parts).reshape((-1,) + (1,) * (len(shape) - 1 - axis_at))
    return loudness


def centred(key, shape, scale, most, pieces=(), kind=jnp.bfloat16):
    result = jax.random.normal(key, shape, jnp.float32) * scale
    if len(pieces) > 0:
        result = level_of(key, shape, pieces, -0.22, 0.18) * result
    return jnp.clip(result, min=-most, max=most).astype(kind)


def setup_inputs(seed: int = 0) -> dict:
    seeds = jax.random.split(jax.random.key(seed), 9)
    boundary_in = centred(seeds[0], (2, SLOTS, L, D), 1.0, 6.0, ((0, 2), (1, 4), (3, 4)), jnp.float32)
    counts = draw_counts(jax.random.fold_in(seeds[8], 71), 0)
    qkv_weight = centred(seeds[2], (2, D, 3, D), D ** -0.5, 0.1875, ((0, 2), (1, 4), (3, 4)))
    proj_weight = centred(seeds[3], (2, D, D), (D // 32) ** -0.5, 1.0, ((0, 2), (1, 4), (2, 4)))
    fc1_weight = centred(seeds[4], (2, D, FF), D ** -0.5, 0.1875, ((0, 2), (1, 4), (2, 4)))
    fc2_weight = centred(seeds[5], (2, FF, D), FF ** -0.5, 0.09375, ((0, 2), (1, 4), (2, 4)))
    vectors = draw_vectors(jax.random.fold_in(seeds[8], 71), 0)
    fc1_bias = centred(seeds[7], (2, N_TENSOR, FF // N_TENSOR), 0.5, 3.0, ((0, 2), (1, 4), (2, 4)))
    return dict(boundary_in=boundary_in, counts=counts, qkv_weight=qkv_weight, proj_weight=proj_weight, fc1_weight=fc1_weight, fc2_weight=fc2_weight, vectors=vectors, fc1_bias=fc1_bias)


EPS = 1e-06

@jax.custom_vjp
def low(v):
    return lax.optimization_barrier(v.astype(jnp.bfloat16)).astype(jnp.float32)

@jax.custom_vjp
def low_back(v):
    return v

def low_keep(v):
    return (low(v), None)

def low_pass(kept, grad):
    return (grad,)

def back_keep(v):
    return (v, None)

def back_low(kept, grad):
    return (low(grad),)
low.defvjp(low_keep, low_pass)
low_back.defvjp(back_keep, back_low)

def matmul(form, left, right):
    return jnp.einsum(form, left, right, precision=lax.Precision.HIGHEST)

def normalize(value, gain, shift):
    center = lax.optimization_barrier(jnp.mean(value, -1, keepdims=True))
    spread = lax.optimization_barrier(jnp.mean(value * value, -1, keepdims=True)) - center * center
    return (value - center) * lax.rsqrt(spread + EPS) * gain + shift

def encoder_layer(params, value):
    qkv_matrix, out_matrix, up_matrix, down_matrix, vector_rows, up_bias = params
    images, tokens, width = value.shape
    split = (images, tokens, HEADS, HD)
    normed = low(normalize(value, vector_rows[0], vector_rows[1]))
    queries = low(low_back(matmul('btd,de->bte', normed, qkv_matrix[:, 0])) + vector_rows[2])
    keyset = low(low_back(matmul('btd,de->bte', normed, qkv_matrix[:, 1])))
    valueset = low(low_back(matmul('btd,de->bte', normed, qkv_matrix[:, 2])) + vector_rows[3])
    scores = low_back(matmul('bqhd,bkhd->bhqk', queries.reshape(split), keyset.reshape(split)) * HD ** (-0.5))
    weights = low(jax.nn.softmax(scores, axis=-1))
    mixed = low(low_back(matmul('bhqk,bkhd->bqhd', weights, valueset.reshape(split)))).reshape(images, tokens, width)
    middle = value + low_back(matmul('bte,ed->btd', mixed, out_matrix)) + vector_rows[4]
    normed_two = low(normalize(middle, vector_rows[5], vector_rows[6]))
    hidden = low(jax.nn.gelu(low_back(matmul('btd,df->btf', normed_two, up_matrix)) + up_bias, approximate=False))
    return middle + low_back(matmul('btf,fd->btd', hidden, down_matrix)) + vector_rows[7]

def whole_block(params, images, live_mask):
    first_layer = tuple((item[0] for item in params))
    second_layer = tuple((item[1] for item in params))
    sent = low(low_back(encoder_layer(first_layer, images)))
    return encoder_layer(second_layer, sent) * live_mask

def reference(boundary_in, counts, qkv_weight, proj_weight, fc1_weight, fc2_weight, vectors, fc1_bias):
    params = (qkv_weight.astype(jnp.float32), proj_weight.astype(jnp.float32), fc1_weight.astype(jnp.float32), fc2_weight.astype(jnp.float32), vectors.astype(jnp.float32).reshape(2, 8, D), fc1_bias.astype(jnp.float32).reshape(2, FF))
    groups = SLOTS // CAP
    images = boundary_in[0].reshape(groups, CAP, L, D)
    cotangent = boundary_in[1].reshape(groups, CAP, L, D)
    live_all = (jnp.arange(CAP)[None, :] < counts.reshape(groups, 1)).astype(jnp.float32)[:, :, None, None]

    def one_group(totals, item):
        group_in, group_cot, group_live = item
        output, pull = jax.vjp(lambda p, x: whole_block(p, x, group_live), params, group_in)
        grad_params, grad_in = pull(group_cot)
        totals = jax.tree.map(lambda a, b: a + b, totals, grad_params)
        return (totals, (grad_in, output))
    start = jax.tree.map(lambda a: jnp.zeros(a.shape, jnp.float32), params)
    totals, (grad_in, output) = lax.scan(one_group, start, (images, cotangent, live_all))
    boundary_out = jnp.stack([grad_in.reshape(SLOTS, L, D), output.reshape(SLOTS, L, D)])
    return (boundary_out, totals[0], totals[1], totals[2], totals[3], totals[4].reshape(2, 8, N_TENSOR, D // N_TENSOR), totals[5].reshape(2, N_TENSOR, FF // N_TENSOR))
```

```python
import jax
import jax.numpy as jnp
from jax import lax
from jax.sharding import PartitionSpec as P

HD = 64
EPS = 1e-06
ALL = ("dp", "tensor")


def swap(value):
    return lax.ppermute(value, "section", [(0, 1), (1, 0)])


def pair_sum(partial):
    low = partial.astype(jnp.bfloat16)
    return low.astype(jnp.float32) + swap(low).astype(jnp.float32)


def both_layers(shard, axis, is_first):
    half = shard.shape[axis] // 2
    low = lax.slice_in_dim(shard, 0, half, axis=axis)
    high = lax.slice_in_dim(shard, half, 2 * half, axis=axis)
    kept = jnp.where(is_first, low, high)
    received = swap(jnp.where(is_first, high, low))
    return (jnp.where(is_first, kept, received), jnp.where(is_first, received, kept))


def own_layer(first, second, axis, is_first):
    kept = jnp.where(is_first, first, second)
    received = swap(jnp.where(is_first, second, first))
    low = jnp.where(is_first, kept, received)
    high = jnp.where(is_first, received, kept)
    return jnp.concatenate([low, high], axis)


def gather(shard):
    n_dp, n_tensor = lax.axis_size("dp"), lax.axis_size("tensor")
    whole = lax.all_gather(shard, ALL, axis=0, tiled=False)
    return whole.reshape((n_dp, n_tensor) + shard.shape)


def scatter(pieces):
    low = pieces.astype(jnp.bfloat16)
    flat = low.reshape((-1,) + low.shape[2:])
    return lax.psum_scatter(flat, ALL, scatter_dimension=0, tiled=False).astype(jnp.float32)


def mm(form, left, right):
    return jnp.einsum(form, left, right, preferred_element_type=jnp.float32)


def layer_norm(value, gain, shift):
    center = jnp.mean(value, -1, keepdims=True)
    spread = jnp.mean(value * value, -1, keepdims=True) - center * center
    factor = lax.rsqrt(spread + EPS)
    centred = (value - center) * factor
    return ((centred * gain + shift).astype(jnp.bfloat16), centred, factor)


def norm_backward(grad_normed, centred, factor, gain):
    scaled = grad_normed * gain
    return factor * (
        scaled
        - jnp.mean(scaled, -1, keepdims=True)
        - centred * jnp.mean(scaled * centred, -1, keepdims=True)
    )


def gelu_parts(value):
    cdf = 0.5 * (1.0 + lax.erf(value * 0.7071067811865476))
    density = jnp.exp(-0.5 * value * value) * 0.3989422804014327
    return (cdf, density)


def forward_layer(weights, value):
    w_qkv, w_out, w_up, w_down, rows, q_bias, v_bias, up_bias = weights
    tokens = value.shape[0]
    heads = w_out.shape[0] // HD
    split = (tokens, heads, HD)
    normed, centred, factor = layer_norm(value, rows[0], rows[1])
    projected = mm("td,dce->tce", normed, w_qkv)
    queries = (projected[:, 0] + q_bias).astype(jnp.bfloat16)
    keyset = projected[:, 1].astype(jnp.bfloat16)
    valueset = (projected[:, 2] + v_bias).astype(jnp.bfloat16)
    scores = mm("qhd,khd->hqk", queries.reshape(split), keyset.reshape(split)) * HD ** (-0.5)
    highest = jnp.max(scores, -1, keepdims=True)
    exponent = jnp.exp(scores - highest)
    denominator = jnp.sum(exponent, -1, keepdims=True)
    soft = (exponent / denominator).astype(jnp.bfloat16)
    log_total = highest + jnp.log(denominator)
    mixed = mm("hqk,khd->qhd", soft, valueset.reshape(split)).astype(jnp.bfloat16)
    mixed = mixed.reshape(tokens, heads * HD)
    middle = value + pair_sum(mm("te,ed->td", mixed, w_out)) + rows[4]
    normed_two, centred_two, factor_two = layer_norm(middle, rows[5], rows[6])
    before = mm("td,df->tf", normed_two, w_up) + up_bias
    hidden = (before * gelu_parts(before)[0]).astype(jnp.bfloat16)
    output = middle + pair_sum(mm("tf,fd->td", hidden, w_down)) + rows[7]
    kept = (normed, centred, factor, queries, keyset, valueset, log_total, mixed)
    return (output, kept + (normed_two, centred_two, factor_two, before, hidden))


def backward_layer(weights, kept, grad_out):
    w_qkv, w_out, w_up, w_down, rows, q_bias, v_bias, up_bias = weights
    normed, centred, factor, queries, keyset, valueset, log_total, mixed = kept[:8]
    normed_two, centred_two, factor_two, before, hidden = kept[8:]
    tokens = grad_out.shape[0]
    heads = w_out.shape[0] // HD
    split = (tokens, heads, HD)
    scale = HD ** (-0.5)
    grad_branch = grad_out.astype(jnp.bfloat16)
    grad_down = mm("tf,td->fd", hidden, grad_branch)
    cdf, density = gelu_parts(before)
    grad_before = mm("td,fd->tf", grad_branch, w_down) * (cdf + before * density)
    grad_up_bias = jnp.sum(grad_before, 0)
    before_low = grad_before.astype(jnp.bfloat16)
    grad_up = mm("td,tf->df", normed_two, before_low)
    grad_normed_two = pair_sum(mm("tf,df->td", before_low, w_up))
    grad_middle = grad_out + norm_backward(grad_normed_two, centred_two, factor_two, rows[5])
    grad_attended = grad_middle.astype(jnp.bfloat16)
    grad_outproj = mm("te,td->ed", mixed, grad_attended)
    grad_mixed = mm("td,ed->te", grad_attended, w_out).astype(jnp.bfloat16).reshape(split)
    query_heads, key_heads = queries.reshape(split), keyset.reshape(split)
    soft = jnp.exp(mm("qhd,khd->hqk", query_heads, key_heads) * scale - log_total)
    soft_low = soft.astype(jnp.bfloat16)
    grad_values = mm("hqk,qhd->khd", soft_low, grad_mixed)
    grad_soft = mm("qhd,khd->hqk", grad_mixed, valueset.reshape(split))
    row_inner = jnp.sum(grad_soft * soft, -1, keepdims=True)
    grad_scores = (soft * (grad_soft - row_inner)).astype(jnp.bfloat16)
    grad_queries = mm("hqk,khd->qhd", grad_scores, key_heads) * scale
    grad_keys = mm("hqk,qhd->khd", grad_scores, query_heads) * scale
    grad_stack = jnp.stack([grad_queries, grad_keys, grad_values], 1)
    grad_stack = grad_stack.reshape(tokens, 3, heads * HD)
    grad_query_bias = jnp.sum(grad_stack[:, 0], 0)
    grad_value_bias = jnp.sum(grad_stack[:, 2], 0)
    stack_low = grad_stack.astype(jnp.bfloat16)
    grad_qkv = mm("td,tce->dce", normed, stack_low)
    grad_normed = pair_sum(mm("tce,dce->td", stack_low, w_qkv))
    grad_value = grad_middle + norm_backward(grad_normed, centred, factor, rows[0])
    full_rows = jnp.stack(
        [
            jnp.sum(grad_normed * centred, 0),
            jnp.sum(grad_normed, 0),
            jnp.sum(grad_middle, 0),
            jnp.sum(grad_normed_two * centred_two, 0),
            jnp.sum(grad_normed_two, 0),
            jnp.sum(grad_out, 0),
        ]
    )
    small = (full_rows, grad_query_bias, grad_value_bias, grad_up_bias)
    return (grad_value, (grad_qkv, grad_outproj, grad_up, grad_down), small)


def half_cols(core, whole, n_tensor):
    cut = whole.reshape(whole.shape[:-1] + (n_tensor, 2, -1))
    cut = jnp.where(core == 0, cut[..., 0, :], cut[..., 1, :])
    return cut.reshape(whole.shape[:-1] + (-1,))


def spread_cols(core, half, n_tensor):
    cut = half.reshape(half.shape[:-1] + (n_tensor, 1, -1))
    none = jnp.zeros_like(cut)
    both = jnp.concatenate(
        [jnp.where(core == 0, cut, none), jnp.where(core == 0, none, cut)], -2
    )
    return both.reshape(half.shape[:-1] + (-1,))


def body(boundary_in, counts, qkv_weight, proj_weight, fc1_weight, fc2_weight, vectors, fc1_bias):
    core = lax.axis_index("section")
    is_first = core == 0
    place = lax.axis_index("tensor")
    n_dp, n_tensor = lax.axis_size("dp"), lax.axis_size("tensor")
    slots_per_batch = boundary_in.shape[1] // counts.shape[1]
    live = (place % slots_per_batch < counts[0, place // slots_per_batch]).astype(jnp.float32)

    small_shard = jnp.concatenate([vectors.reshape(-1), fc1_bias.reshape(-1)])
    small_other = swap(small_shard)
    small_both = jnp.stack(
        [
            jnp.where(is_first, small_shard, small_other),
            jnp.where(is_first, small_other, small_shard),
        ]
    )
    small = gather(small_both).astype(jnp.float32)
    mine = lax.all_to_all(
        boundary_in[0].astype(jnp.bfloat16), "tensor", split_axis=0, concat_axis=2, tiled=True
    )[0]
    theirs = swap(mine)
    value = jnp.where(is_first, mine, theirs).astype(jnp.float32)
    cotangent = jnp.where(is_first, theirs, mine).astype(jnp.float32) * live

    shards = [
        both_layers(qkv_weight[0], 2, is_first),
        both_layers(proj_weight[0], 0, is_first),
        both_layers(fc1_weight[0], 1, is_first),
        both_layers(fc2_weight[0], 0, is_first),
    ]
    layers = []
    n_vec = vectors.size
    for layer in range(2):
        w_qkv = gather(shards[0][layer]).transpose(0, 2, 3, 1, 4)
        w_qkv = w_qkv.reshape(n_dp * w_qkv.shape[1], 3, -1)
        w_out = gather(shards[1][layer]).transpose(1, 2, 0, 3)
        w_out = w_out.reshape(n_tensor * w_out.shape[1], -1)
        w_up = gather(shards[2][layer]).transpose(0, 2, 1, 3)
        w_up = w_up.reshape(n_dp * w_up.shape[1], -1)
        w_down = gather(shards[3][layer]).transpose(1, 2, 0, 3)
        w_down = w_down.reshape(n_tensor * w_down.shape[1], -1)
        rows = small[:, :, layer, :n_vec].reshape(n_dp, n_tensor, 8, -1)
        rows = rows.transpose(2, 1, 0, 3).reshape(8, -1)
        bias = small[:, :, layer, n_vec:].transpose(1, 0, 2).reshape(-1)
        q_bias = half_cols(core, rows[2], n_tensor)
        v_bias = half_cols(core, rows[3], n_tensor)
        up_bias = half_cols(core, bias, n_tensor)
        layers.append((w_qkv, w_out, w_up, w_down, rows, q_bias, v_bias, up_bias))

    output, kept_first = forward_layer(layers[0], value)
    sent = output.astype(jnp.bfloat16).astype(jnp.float32)
    output, kept_second = forward_layer(layers[1], sent)
    output = output * live

    grads = [None, None]
    smalls = [None, None]
    grad, big, little = backward_layer(layers[1], kept_second, cotangent)
    grads[1], smalls[1] = big, little
    grad = grad.astype(jnp.bfloat16).astype(jnp.float32)
    grad, big, little = backward_layer(layers[0], kept_first, grad)
    grads[0], smalls[0] = big, little

    ends = jnp.where(is_first, grad, output).astype(jnp.bfloat16)
    ends = lax.all_to_all(ends[None], "tensor", split_axis=2, concat_axis=0, tiled=True)
    boundary_out = ends.astype(jnp.float32)[None]

    settled = [None, None]
    for layer in (1, 0):
        g_qkv, g_out, g_up, g_down = grads[layer]
        width = g_qkv.shape[0] // n_dp
        g_qkv = g_qkv.reshape(n_dp, width, 3, n_tensor, -1).transpose(0, 3, 1, 2, 4)
        g_out = g_out.reshape(n_tensor, -1, n_dp, width).transpose(2, 0, 1, 3)
        g_up = g_up.reshape(n_dp, width, n_tensor, -1).transpose(0, 2, 1, 3)
        g_down = g_down.reshape(n_tensor, -1, n_dp, width).transpose(2, 0, 1, 3)
        settled[layer] = tuple(scatter(g) for g in (g_down, g_up, g_out, g_qkv))
    axes = (0, 1, 0, 2)
    whole = [
        own_layer(settled[0][i], settled[1][i], axes[i], is_first)[None] for i in range(4)
    ]
    grad_down, grad_up, grad_out, grad_qkv = whole

    packed = []
    for layer in range(2):
        full_rows, q_row, v_row, up_row = smalls[layer]
        full_rows = jnp.where(core == layer, full_rows, 0.0)
        q_row = spread_cols(core, q_row, n_tensor)
        v_row = spread_cols(core, v_row, n_tensor)
        up_row = spread_cols(core, up_row, n_tensor)
        rows = jnp.stack(
            [full_rows[0], full_rows[1], q_row, v_row, full_rows[2], full_rows[3], full_rows[4], full_rows[5]]
        )
        rows = rows.reshape(8, n_tensor, n_dp, -1).transpose(2, 1, 0, 3).reshape(n_dp, n_tensor, -1)
        up_row = up_row.reshape(n_tensor, n_dp, -1).transpose(1, 0, 2)
        packed.append(jnp.concatenate([rows, up_row], -1))
    ours = jnp.where(is_first, packed[0], packed[1])
    other = swap(jnp.where(is_first, packed[1], packed[0]))
    small_grad = scatter(ours + other)
    grad_vectors = small_grad[:n_vec].reshape(vectors.shape)
    grad_bias = small_grad[n_vec:].reshape(fc1_bias.shape)
    return (boundary_out, grad_qkv, grad_out, grad_up, grad_down, grad_vectors, grad_bias)


def solution(mesh):
    in_specs = (
        P("section", "dp", None, "tensor"),
        P("dp", None),
        P("section", "dp", None, "tensor"),
        P("section", "tensor", "dp"),
        P("section", "dp", "tensor"),
        P("section", "tensor", "dp"),
        P("section", None, "tensor", "dp"),
        P("section", "tensor", "dp"),
    )
    out_specs = (
        P("section", "dp", None, "tensor"),
        P("section", "dp", None, "tensor"),
        P("section", "tensor", "dp"),
        P("section", "dp", "tensor"),
        P("section", "tensor", "dp"),
        P("section", None, "tensor", "dp"),
        P("section", "tensor", "dp"),
    )
    return jax.shard_map(body, mesh=mesh, in_specs=in_specs, out_specs=out_specs, check_vma=False)
```

```python
import jax
import jax.numpy as jnp
from jax import lax
from jax.sharding import PartitionSpec as P

HD = 64
EPS = 1e-06


def swap(value):
    return lax.ppermute(value, "section", [(0, 1), (1, 0)])


def pair_sum(partial):
    low = partial.astype(jnp.bfloat16)
    return low.astype(jnp.float32) + swap(low).astype(jnp.float32)


def swap_x(value):
    n = lax.axis_size("dp")
    return lax.ppermute(value, "dp", [(i, i ^ 1) for i in range(n)])


def swap_y(value):
    n = lax.axis_size("dp")
    return lax.ppermute(value, "dp", [(i, i ^ 2) for i in range(n)])


def gather_chunk(first, second):
    n_dp = lax.axis_size("dp")
    cut = first.shape[0]
    column = lax.all_gather(jnp.concatenate([first, second], 0), "tensor", axis=1, tiled=True)
    first, second = column[:cut], column[cut:]
    if n_dp != 4:
        return (
            far_gather(first, True),
            far_gather(second, False),
        )
    first = jnp.concatenate([first, swap_y(first)], 0)
    second = jnp.concatenate([second, swap_x(second)], 0)
    first = jnp.concatenate([first, swap_x(first)], 0)
    second = jnp.concatenate([second, swap_y(second)], 0)
    return (first, second)


def far_gather(block, is_first):
    return lax.all_gather(block, "dp", axis=0, tiled=True)


def add_low(left, right):
    return (left.astype(jnp.float32) + right.astype(jnp.float32)).astype(jnp.bfloat16)


def scatter_chunk(first, second):
    n_dp = lax.axis_size("dp")
    if n_dp != 4:
        first = lax.psum_scatter(first, "dp", scatter_dimension=0, tiled=True)
        second = lax.psum_scatter(second, "dp", scatter_dimension=0, tiled=True)
    else:
        for flip in range(2):
            half, rest = first.shape[0] // 2, second.shape[0] // 2
            got_first = (swap_y if flip else swap_x)(first[half:])
            got_second = (swap_x if flip else swap_y)(second[rest:])
            first = add_low(first[:half], got_first)
            second = add_low(second[:rest], got_second)
    column = jnp.concatenate([first, second], 0)
    return lax.psum_scatter(column, "tensor", scatter_dimension=1, tiled=True)


def flip_axis(value, axis, bit):
    return jnp.where(bit == 1, jnp.flip(value, axis), value)


def relative(value, spot):
    n_dp = lax.axis_size("dp")
    lead = value.shape[:-1]
    k = len(lead)
    if n_dp != 4:
        cut = value.reshape(lead + (n_dp, 2, -1))
        return jnp.swapaxes(cut, k, k + 1).reshape(value.shape)
    cut = value.reshape(lead + (2, 2, 2, -1))
    cut = flip_axis(flip_axis(cut, k, spot // 2), k + 1, spot % 2)
    first = jnp.swapaxes(cut[..., 0, :], k, k + 1)
    second = cut[..., 1, :]
    return jnp.concatenate([first.reshape(lead + (-1,)), second.reshape(lead + (-1,))], -1)


def absolute(value, spot):
    n_dp = lax.axis_size("dp")
    lead = value.shape[:-1]
    k = len(lead)
    if n_dp != 4:
        cut = value.reshape(lead + (2, n_dp, -1))
        return jnp.swapaxes(cut, k, k + 1).reshape(value.shape)
    cut = value.reshape(lead + (2, 2, 2, -1))
    first = jnp.swapaxes(cut[..., 0, :, :, :], k, k + 1)
    second = cut[..., 1, :, :, :]
    cut = jnp.stack([first, second], k + 2)
    cut = flip_axis(flip_axis(cut, k, spot // 2), k + 1, spot % 2)
    return cut.reshape(value.shape)


def by_chip(blocks, spot):
    n_dp = lax.axis_size("dp")
    if n_dp != 4:
        return blocks
    cut = blocks.reshape((2, 2) + blocks.shape[1:])
    cut = jnp.swapaxes(cut, 0, 1)
    cut = flip_axis(flip_axis(cut, 0, spot // 2), 1, spot % 2)
    return cut.reshape(blocks.shape)


def by_arrival(blocks, spot):
    n_dp = lax.axis_size("dp")
    if n_dp != 4:
        return blocks
    cut = blocks.reshape((2, 2) + blocks.shape[1:])
    cut = flip_axis(flip_axis(cut, 0, spot // 2), 1, spot % 2)
    return jnp.swapaxes(cut, 0, 1).reshape(blocks.shape)


def mm(form, left, right):
    return jnp.einsum(form, left, right, preferred_element_type=jnp.float32)


def layer_norm(value, gain, shift):
    center = jnp.mean(value, -1, keepdims=True)
    spread = jnp.mean(value * value, -1, keepdims=True) - center * center
    factor = lax.rsqrt(spread + EPS)
    centred = (value - center) * factor
    return ((centred * gain + shift).astype(jnp.bfloat16), centred, factor)


def norm_backward(grad_normed, centred, factor, gain):
    scaled = grad_normed * gain
    return factor * (
        scaled
        - jnp.mean(scaled, -1, keepdims=True)
        - centred * jnp.mean(scaled * centred, -1, keepdims=True)
    )


def gelu_parts(value):
    cdf = 0.5 * (1.0 + lax.erf(value * 0.7071067811865476))
    density = jnp.exp(-0.5 * value * value) * 0.3989422804014327
    return (cdf, density)


def forward_layer(weights, value):
    w_qkv, w_out, w_up, w_down, rows, q_bias, v_bias, up_bias = weights
    tokens = value.shape[0]
    heads = w_out.shape[1] // HD
    split = (tokens, heads, HD)
    normed, centred, factor = layer_norm(value, rows[0], rows[1])
    projected = mm("td,dgce->tgce", normed, w_qkv)
    queries = (projected[:, :, 0].reshape(tokens, -1) + q_bias).astype(jnp.bfloat16)
    keyset = projected[:, :, 1].reshape(tokens, -1).astype(jnp.bfloat16)
    valueset = (projected[:, :, 2].reshape(tokens, -1) + v_bias).astype(jnp.bfloat16)
    scores = mm("qhd,khd->hqk", queries.reshape(split), keyset.reshape(split)) * HD ** (-0.5)
    highest = jnp.max(scores, -1, keepdims=True)
    exponent = jnp.exp(scores - highest)
    denominator = jnp.sum(exponent, -1, keepdims=True)
    soft = (exponent / denominator).astype(jnp.bfloat16)
    log_total = highest + jnp.log(denominator)
    mixed = mm("hqk,khd->qhd", soft, valueset.reshape(split)).astype(jnp.bfloat16)
    mixed = mixed.reshape(tokens, heads * HD)
    middle = value + pair_sum(mm("te,de->td", mixed, w_out)) + rows[4]
    normed_two, centred_two, factor_two = layer_norm(middle, rows[5], rows[6])
    before = mm("td,df->tf", normed_two, w_up) + up_bias
    hidden = (before * gelu_parts(before)[0]).astype(jnp.bfloat16)
    output = middle + pair_sum(mm("tf,df->td", hidden, w_down)) + rows[7]
    kept = (normed, centred, factor, queries, keyset, valueset, log_total, mixed)
    return (output, kept + (normed_two, centred_two, factor_two, before, hidden))


def backward_layer(weights, kept, grad_out):
    w_qkv, w_out, w_up, w_down, rows, q_bias, v_bias, up_bias = weights
    normed, centred, factor, queries, keyset, valueset, log_total, mixed = kept[:8]
    normed_two, centred_two, factor_two, before, hidden = kept[8:]
    tokens = grad_out.shape[0]
    heads = w_out.shape[1] // HD
    split = (tokens, heads, HD)
    scale = HD ** (-0.5)
    grad_branch = grad_out.astype(jnp.bfloat16)
    grad_down = mm("td,tf->df", grad_branch, hidden).astype(jnp.bfloat16)
    grad_down, grad_branch = lax.optimization_barrier((grad_down, grad_branch))
    cdf, density = gelu_parts(before)
    grad_before = mm("td,df->tf", grad_branch, w_down) * (cdf + before * density)
    grad_up_bias = jnp.sum(grad_before, 0)
    before_low = grad_before.astype(jnp.bfloat16)
    grad_up = mm("td,tf->df", normed_two, before_low).astype(jnp.bfloat16)
    grad_up, before_low = lax.optimization_barrier((grad_up, before_low))
    grad_normed_two = pair_sum(mm("tf,df->td", before_low, w_up))
    grad_middle = grad_out + norm_backward(grad_normed_two, centred_two, factor_two, rows[5])
    grad_attended = grad_middle.astype(jnp.bfloat16)
    grad_outproj = mm("td,te->de", grad_attended, mixed).astype(jnp.bfloat16)
    grad_mixed = mm("td,de->te", grad_attended, w_out).astype(jnp.bfloat16).reshape(split)
    query_heads, key_heads = queries.reshape(split), keyset.reshape(split)
    soft = jnp.exp(mm("qhd,khd->hqk", query_heads, key_heads) * scale - log_total)
    soft_low = soft.astype(jnp.bfloat16)
    grad_values = mm("hqk,qhd->khd", soft_low, grad_mixed)
    grad_soft = mm("qhd,khd->hqk", grad_mixed, valueset.reshape(split))
    row_inner = jnp.sum(grad_soft * soft, -1, keepdims=True)
    grad_scores = (soft * (grad_soft - row_inner)).astype(jnp.bfloat16)
    grad_queries = mm("hqk,khd->qhd", grad_scores, key_heads) * scale
    grad_keys = mm("hqk,qhd->khd", grad_scores, query_heads) * scale
    groups = w_qkv.shape[1]
    grad_query_bias = jnp.sum(grad_queries, 0).reshape(-1)
    grad_value_bias = jnp.sum(grad_values, 0).reshape(-1)
    parts = [grad_queries, grad_keys, grad_values]
    parts = [part.astype(jnp.bfloat16).reshape(tokens, groups, -1) for part in parts]
    stack_low = jnp.stack(parts, 2)
    grad_qkv = mm("td,tgce->dgce", normed, stack_low).astype(jnp.bfloat16)
    grad_qkv, stack_low = lax.optimization_barrier((grad_qkv, stack_low))
    grad_normed = pair_sum(mm("tgce,dgce->td", stack_low, w_qkv))
    grad_value = grad_middle + norm_backward(grad_normed, centred, factor, rows[0])
    full_rows = jnp.stack(
        [
            jnp.sum(grad_normed * centred, 0),
            jnp.sum(grad_normed, 0),
            jnp.sum(grad_middle, 0),
            jnp.sum(grad_normed_two * centred_two, 0),
            jnp.sum(grad_normed_two, 0),
            jnp.sum(grad_out, 0),
        ]
    )
    small = (full_rows, grad_query_bias, grad_value_bias, grad_up_bias)
    return (grad_value, (grad_qkv, grad_outproj, grad_up, grad_down), small)


def half_cols(core, whole, n_tensor):
    cut = whole.reshape(whole.shape[:-1] + (n_tensor, 2, -1))
    cut = jnp.where(core == 0, cut[..., 0, :], cut[..., 1, :])
    return cut.reshape(whole.shape[:-1] + (-1,))


def spread_cols(core, half, n_tensor):
    cut = half.reshape(half.shape[:-1] + (n_tensor, 1, -1))
    none = jnp.zeros_like(cut)
    both = jnp.concatenate(
        [jnp.where(core == 0, cut, none), jnp.where(core == 0, none, cut)], -2
    )
    return both.reshape(half.shape[:-1] + (-1,))


def body(boundary_in, counts, qkv_weight, proj_weight, fc1_weight, fc2_weight, vectors, fc1_bias):
    core = lax.axis_index("section")
    is_first = core == 0
    place = lax.axis_index("tensor")
    spot = lax.axis_index("dp")
    n_dp, n_tensor = lax.axis_size("dp"), lax.axis_size("tensor")
    slots_per_batch = boundary_in.shape[1] // counts.shape[1]
    live = (place % slots_per_batch < counts[0, place // slots_per_batch]).astype(jnp.float32)
    depth = qkv_weight.shape[1]
    mid = depth // 2
    n_vec = vectors.size

    packs = []
    for part in range(2):
        cuts = [
            jnp.split(qkv_weight[0], 2, 2)[part].reshape(depth, -1),
            jnp.split(proj_weight[0], 2, 0)[part].T,
            jnp.split(fc1_weight[0], 2, 1)[part],
            jnp.split(fc2_weight[0], 2, 0)[part].T,
        ]
        packs.append(jnp.concatenate(cuts, 1))
    kept = jnp.where(is_first, packs[0], packs[1])
    received = swap(jnp.where(is_first, packs[1], packs[0]))
    shards = (jnp.where(is_first, kept, received), jnp.where(is_first, received, kept))
    small_shard = jnp.concatenate([vectors.reshape(-1), fc1_bias.reshape(-1)])
    small_other = swap(small_shard)
    small = jnp.concatenate(
        [
            jnp.where(is_first, small_shard, small_other),
            jnp.where(is_first, small_other, small_shard),
        ]
    )
    wide = shards[0].shape[1] // 3
    extra = 16
    small = jnp.concatenate([small, jnp.zeros((extra * wide - small.size,), small.dtype)])
    small = small.reshape(extra, wide)

    mine = lax.all_to_all(
        boundary_in[0].astype(jnp.bfloat16), "tensor", split_axis=0, concat_axis=2, tiled=True
    )[0]
    theirs = swap(mine)
    value = relative(jnp.where(is_first, mine, theirs), spot).astype(jnp.float32)
    cotangent = relative(jnp.where(is_first, theirs, mine), spot).astype(jnp.float32) * live

    chunks = []
    for layer in range(2):
        for number in range(3):
            cols = shards[layer][:, number * wide : (number + 1) * wide]
            first, second = cols[:mid], cols[mid:]
            if layer == 0 and number == 0:
                first = jnp.concatenate([first, small], 0)
            chunks.append(gather_chunk(first, second))
    first, second = chunks[0]
    first = first.reshape(n_dp, mid + extra, -1)
    small = by_chip(first[:, mid:], spot).astype(jnp.float32)
    chunks[0] = (first[:, :mid].reshape(n_dp * mid, -1), second)
    small = small.reshape(n_dp, extra, n_tensor, wide).transpose(0, 2, 1, 3)
    small = small.reshape(n_dp, n_tensor, -1)

    layers = []
    for layer in range(2):
        joined = [jnp.concatenate(chunk, 0) for chunk in chunks[3 * layer : 3 * layer + 3]]
        quad = joined[0].reshape(joined[0].shape[0], n_tensor, 4, -1)
        w_qkv = quad[:, :, :3]
        w_out = quad[:, :, 3].reshape(quad.shape[0], -1)
        one = small[:, :, layer * small_shard.size : (layer + 1) * small_shard.size]
        rows = one[:, :, :n_vec].reshape(n_dp, n_tensor, 8, -1)
        rows = rows.transpose(2, 1, 0, 3).reshape(8, -1)
        bias = one[:, :, n_vec:].transpose(1, 0, 2).reshape(-1)
        q_bias = half_cols(core, rows[2], n_tensor)
        v_bias = half_cols(core, rows[3], n_tensor)
        up_bias = half_cols(core, bias, n_tensor)
        rows = relative(rows, spot)
        layers.append((w_qkv, w_out, joined[1], joined[2], rows, q_bias, v_bias, up_bias))

    output, kept_first = forward_layer(layers[0], value)
    sent = output.astype(jnp.bfloat16).astype(jnp.float32)
    output, kept_second = forward_layer(layers[1], sent)
    output = output * live

    settled = [None, None]
    smalls = [None, None]
    grad = cotangent
    for layer in (1, 0):
        keeps = (kept_first, kept_second)[layer]
        grad, big, smalls[layer] = backward_layer(layers[layer], keeps, grad)
        if layer == 1:
            grad = grad.astype(jnp.bfloat16).astype(jnp.float32)
        g_qkv, g_out, g_up, g_down = big
        quad = jnp.concatenate([g_qkv, g_out.reshape(g_qkv.shape[:2] + (1, -1))], 2)
        quad = quad.reshape(quad.shape[0], -1)
        half = quad.shape[0] // 2
        done = [scatter_chunk(g[:half], g[half:]) for g in (g_down, g_up)]
        if layer == 1:
            done.append(scatter_chunk(quad[:half], quad[half:]))
        settled[layer] = done

    ends = absolute(jnp.where(is_first, grad, output).astype(jnp.bfloat16), spot)
    ends = lax.all_to_all(ends[None], "tensor", split_axis=2, concat_axis=0, tiled=True)
    boundary_out = ends.astype(jnp.float32)[None]

    packed = []
    for layer in range(2):
        full_rows, q_row, v_row, up_row = smalls[layer]
        full_rows = absolute(jnp.where(core == layer, full_rows, 0.0), spot)
        q_row = spread_cols(core, q_row, n_tensor)
        v_row = spread_cols(core, v_row, n_tensor)
        up_row = spread_cols(core, up_row, n_tensor)
        rows = jnp.stack(
            [full_rows[0], full_rows[1], q_row, v_row, full_rows[2], full_rows[3], full_rows[4], full_rows[5]]
        )
        rows = rows.reshape(8, n_tensor, n_dp, -1).transpose(2, 1, 0, 3).reshape(n_dp, n_tensor, -1)
        up_row = up_row.reshape(n_tensor, n_dp, -1).transpose(1, 0, 2)
        packed.append(jnp.concatenate([rows, up_row], -1))
    ours = jnp.where(is_first, packed[0], packed[1])
    other = swap(jnp.where(is_first, packed[1], packed[0]))
    little = (ours + other).astype(jnp.bfloat16)
    pad = jnp.zeros((n_dp, n_tensor, extra * wide - little.shape[-1]), little.dtype)
    little = jnp.concatenate([little, pad], -1).reshape(n_dp, n_tensor, extra, wide)
    little = by_arrival(little.transpose(0, 2, 1, 3).reshape(n_dp, extra, -1), spot)
    first = jnp.concatenate([quad[:half].reshape(n_dp, mid, -1), little], 1)
    last = scatter_chunk(first.reshape(n_dp * (mid + extra), -1), quad[half:])
    little = last[mid : mid + extra].reshape(-1).astype(jnp.float32)
    settled[0].append(jnp.concatenate([last[:mid], last[mid + extra :]], 0))
    grad_vectors = little[:n_vec].reshape(vectors.shape)
    grad_bias = little[n_vec : n_vec + fc1_bias.size].reshape(fc1_bias.shape)

    lows, highs = [], []
    for number in range(3):
        kept = jnp.where(is_first, settled[0][number], settled[1][number])
        received = swap(jnp.where(is_first, settled[1][number], settled[0][number]))
        lows.append(jnp.where(is_first, kept, received).astype(jnp.float32))
        highs.append(jnp.where(is_first, received, kept).astype(jnp.float32))
    grad_down = jnp.concatenate([lows[0].T, highs[0].T], 0)[None]
    grad_up = jnp.concatenate([lows[1], highs[1]], 1)[None]
    low, high = [part[2].reshape(depth, 4, -1) for part in (lows, highs)]
    grad_qkv = jnp.concatenate([low[:, :3], high[:, :3]], 2)[None]
    grad_out = jnp.concatenate([low[:, 3].T, high[:, 3].T], 0)[None]
    return (boundary_out, grad_qkv, grad_out, grad_up, grad_down, grad_vectors, grad_bias)


def solution(mesh):
    in_specs = (
        P("section", "dp", None, "tensor"),
        P("dp", None),
        P("section", "dp", None, "tensor"),
        P("section", "tensor", "dp"),
        P("section", "dp", "tensor"),
        P("section", "tensor", "dp"),
        P("section", None, "tensor", "dp"),
        P("section", "tensor", "dp"),
    )
    out_specs = (
        P("section", "dp", None, "tensor"),
        P("section", "dp", None, "tensor"),
        P("section", "tensor", "dp"),
        P("section", "dp", "tensor"),
        P("section", "tensor", "dp"),
        P("section", None, "tensor", "dp"),
        P("section", "tensor", "dp"),
    )
    return jax.shard_map(body, mesh=mesh, in_specs=in_specs, out_specs=out_specs, check_vma=False)
```

```python
import jax
import jax.numpy as jnp
from jax import lax
from jax.experimental import pallas as pl
from jax.sharding import PartitionSpec as P

HD = 64
EPS = 1e-06


def swap(value):
    return lax.ppermute(value, "section", [(0, 1), (1, 0)])


def pair_sum(partial):
    low = partial.astype(jnp.bfloat16)
    return low.astype(jnp.float32) + swap(low).astype(jnp.float32)


def swap_x(value):
    n = lax.axis_size("dp")
    return lax.ppermute(value, "dp", [(i, i ^ 1) for i in range(n)])


def swap_y(value):
    n = lax.axis_size("dp")
    return lax.ppermute(value, "dp", [(i, i ^ 2) for i in range(n)])


def tie(values, others):
    count = len(values)

    def kernel(*refs):
        pass

    anywhere = pl.BlockSpec(memory_space=pl.ANY)
    done = pl.pallas_call(
        kernel,
        out_shape=[jax.ShapeDtypeStruct(v.shape, v.dtype) for v in values],
        in_specs=[anywhere] * (count + len(others)),
        out_specs=[anywhere] * count,
        input_output_aliases={i: i for i in range(count)},
    )(*values, *others)
    return list(done)


def gather_column(shard):
    return lax.all_gather(shard, "tensor", axis=1, tiled=True)


def exchange_one(first, second):
    if lax.axis_size("dp") != 4:
        return [lax.all_gather(v, "dp", axis=0, tiled=True) for v in (first, second)]
    return [swap_y(first), swap_x(second)]


def exchange_two(first, second, near_first, near_second):
    if lax.axis_size("dp") != 4:
        return []
    return [swap_x(first), swap_x(near_first), swap_y(second), swap_y(near_second)]


def arrived(first, second, near, far):
    if lax.axis_size("dp") != 4:
        return ([near[0]], [near[1]])
    return ([first, near[0], far[0], far[1]], [second, near[1], far[2], far[3]])


def row_cuts(depth):
    half = depth // 2
    if lax.axis_size("dp") != 4:
        return [(0, half), (half, depth), None, None]
    part = half // 2
    return [(part, half), (half + part, depth), (0, part), (half, half + part)]


def add(left, right):
    return left.astype(jnp.float32) + right.astype(jnp.float32)


def scatter_one(send_first, send_second):
    if lax.axis_size("dp") != 4:
        return [
            lax.psum_scatter(v, "dp", scatter_dimension=0, tiled=True)
            for v in (send_first, send_second)
        ]
    return [swap_x(send_first), swap_y(send_second)]


def scatter_two(keep_first, keep_second, got):
    if lax.axis_size("dp") != 4:
        return (got, [])
    stay, come = [], []
    for keep, new, far in zip((keep_first, keep_second), got, (swap_y, swap_x)):
        half = keep.shape[0] // 2
        come.append(far(add(keep[half:], new[half:]).astype(jnp.bfloat16)))
        stay.append(add(keep[:half], new[:half]).astype(jnp.bfloat16))
    return (stay, come)


def scatter_column(stay, come):
    if come:
        stay = [add(s, c).astype(jnp.bfloat16) for s, c in zip(stay, come)]
    return lax.psum_scatter(
        jnp.concatenate(stay, 0), "tensor", scatter_dimension=1, tiled=True
    )


def flip_axis(value, axis, bit):
    return jnp.where(bit == 1, jnp.flip(value, axis), value)


def relative(value, spot):
    n_dp = lax.axis_size("dp")
    lead = value.shape[:-1]
    k = len(lead)
    if n_dp != 4:
        cut = value.reshape(lead + (n_dp, 2, -1))
        return jnp.swapaxes(cut, k, k + 1).reshape(value.shape)
    cut = value.reshape(lead + (2, 2, 2, -1))
    cut = flip_axis(flip_axis(cut, k, spot // 2), k + 1, spot % 2)
    first = jnp.swapaxes(cut[..., 0, :], k, k + 1)
    second = cut[..., 1, :]
    return jnp.concatenate([first.reshape(lead + (-1,)), second.reshape(lead + (-1,))], -1)


def absolute(value, spot):
    n_dp = lax.axis_size("dp")
    lead = value.shape[:-1]
    k = len(lead)
    if n_dp != 4:
        cut = value.reshape(lead + (2, n_dp, -1))
        return jnp.swapaxes(cut, k, k + 1).reshape(value.shape)
    cut = value.reshape(lead + (2, 2, 2, -1))
    first = jnp.swapaxes(cut[..., 0, :, :, :], k, k + 1)
    second = cut[..., 1, :, :, :]
    cut = jnp.stack([first, second], k + 2)
    cut = flip_axis(flip_axis(cut, k, spot // 2), k + 1, spot % 2)
    return cut.reshape(value.shape)


def by_chip(blocks, spot):
    n_dp = lax.axis_size("dp")
    if n_dp != 4:
        return blocks
    cut = blocks.reshape((2, 2) + blocks.shape[1:])
    cut = jnp.swapaxes(cut, 0, 1)
    cut = flip_axis(flip_axis(cut, 0, spot // 2), 1, spot % 2)
    return cut.reshape(blocks.shape)


def by_arrival(blocks, spot):
    n_dp = lax.axis_size("dp")
    if n_dp != 4:
        return blocks
    cut = blocks.reshape((2, 2) + blocks.shape[1:])
    cut = flip_axis(flip_axis(cut, 0, spot // 2), 1, spot % 2)
    return jnp.swapaxes(cut, 0, 1).reshape(blocks.shape)


def mm(form, left, right):
    return jnp.einsum(form, left, right, preferred_element_type=jnp.float32)


def layer_norm(value, gain, shift):
    center = jnp.mean(value, -1, keepdims=True)
    spread = jnp.mean(value * value, -1, keepdims=True) - center * center
    factor = lax.rsqrt(spread + EPS)
    centred = (value - center) * factor
    return ((centred * gain + shift).astype(jnp.bfloat16), centred, factor)


def norm_backward(grad_normed, centred, factor, gain):
    scaled = grad_normed * gain
    return factor * (
        scaled
        - jnp.mean(scaled, -1, keepdims=True)
        - centred * jnp.mean(scaled * centred, -1, keepdims=True)
    )


def gelu_parts(value):
    cdf = 0.5 * (1.0 + lax.erf(value * 0.7071067811865476))
    density = jnp.exp(-0.5 * value * value) * 0.3989422804014327
    return (cdf, density)


def forward_attention(w_qkv, w_out, rows, q_bias, v_bias, value):
    tokens = value.shape[0]
    heads = w_out.shape[1] // HD
    split = (tokens, heads, HD)
    normed, centred, factor = layer_norm(value, rows[0], rows[1])
    projected = mm("td,dgce->tgce", normed, w_qkv)
    queries = (projected[:, :, 0].reshape(tokens, -1) + q_bias).astype(jnp.bfloat16)
    keyset = projected[:, :, 1].reshape(tokens, -1).astype(jnp.bfloat16)
    valueset = (projected[:, :, 2].reshape(tokens, -1) + v_bias).astype(jnp.bfloat16)
    scores = mm("qhd,khd->hqk", queries.reshape(split), keyset.reshape(split)) * HD ** (-0.5)
    highest = jnp.max(scores, -1, keepdims=True)
    exponent = jnp.exp(scores - highest)
    denominator = jnp.sum(exponent, -1, keepdims=True)
    soft = (exponent / denominator).astype(jnp.bfloat16)
    log_total = highest + jnp.log(denominator)
    mixed = mm("hqk,khd->qhd", soft, valueset.reshape(split)).astype(jnp.bfloat16)
    mixed = mixed.reshape(tokens, heads * HD)
    middle = value + pair_sum(mm("te,de->td", mixed, w_out)) + rows[4]
    normed_two, centred_two, factor_two = layer_norm(middle, rows[5], rows[6])
    kept = (normed, centred, factor, queries, keyset, valueset, log_total, mixed)
    return (middle, kept + (normed_two, centred_two, factor_two))


def forward_up(w_up, up_bias, normed_two):
    before = mm("td,df->tf", normed_two, w_up) + up_bias
    hidden = (before * gelu_parts(before)[0]).astype(jnp.bfloat16)
    return (before, hidden)


def forward_down(w_down, rows, middle, hidden):
    return middle + pair_sum(mm("tf,df->td", hidden, w_down)) + rows[7]


def weight_grad(form, left, right, axis=1):
    cuts = row_cuts(left.shape[axis])
    return [
        None
        if cut is None
        else mm(form, lax.slice_in_dim(left, cut[0], cut[1], axis=axis), right).astype(jnp.bfloat16)
        for cut in cuts
    ]


def backward_down(w_down, kept, before, hidden, grad_out):
    grad_branch = grad_out.astype(jnp.bfloat16)
    grad_down = weight_grad("td,tf->df", grad_branch, hidden)
    cdf, density = gelu_parts(before)
    grad_before = mm("td,df->tf", grad_branch, w_down) * (cdf + before * density)
    return (grad_down, grad_before.astype(jnp.bfloat16), jnp.sum(grad_before, 0))


def backward_up(w_up, rows, kept, before_low, grad_out):
    normed_two, centred_two, factor_two = kept[8:]
    grad_up = weight_grad("td,tf->df", normed_two, before_low)
    grad_normed_two = pair_sum(mm("tf,df->td", before_low, w_up))
    grad_middle = grad_out + norm_backward(grad_normed_two, centred_two, factor_two, rows[5])
    sums = [
        jnp.sum(grad_middle, 0),
        jnp.sum(grad_normed_two * centred_two, 0),
        jnp.sum(grad_normed_two, 0),
        jnp.sum(grad_out, 0),
    ]
    return (grad_up, grad_middle, sums)


def backward_attention(w_qkv, w_out, rows, kept, grad_middle):
    normed, centred, factor, queries, keyset, valueset, log_total, mixed = kept[:8]
    tokens = grad_middle.shape[0]
    heads = w_out.shape[1] // HD
    split = (tokens, heads, HD)
    scale = HD ** (-0.5)
    groups = w_qkv.shape[1]
    grad_attended = grad_middle.astype(jnp.bfloat16)
    grad_mixed = mm("td,de->te", grad_attended, w_out).astype(jnp.bfloat16).reshape(split)
    query_heads, key_heads = queries.reshape(split), keyset.reshape(split)
    soft = jnp.exp(mm("qhd,khd->hqk", query_heads, key_heads) * scale - log_total)
    soft_low = soft.astype(jnp.bfloat16)
    grad_values = mm("hqk,qhd->khd", soft_low, grad_mixed)
    grad_soft = mm("qhd,khd->hqk", grad_mixed, valueset.reshape(split))
    row_inner = jnp.sum(grad_soft * soft, -1, keepdims=True)
    grad_scores = (soft * (grad_soft - row_inner)).astype(jnp.bfloat16)
    grad_queries = mm("hqk,khd->qhd", grad_scores, key_heads) * scale
    grad_keys = mm("hqk,qhd->khd", grad_scores, query_heads) * scale
    parts = [grad_queries, grad_keys, grad_values]
    parts = [part.astype(jnp.bfloat16).reshape(tokens, groups, -1) for part in parts]
    stack_low = jnp.stack(parts, 2)
    grad_normed = pair_sum(mm("tgce,dgce->td", stack_low, w_qkv))
    grad_value = grad_middle + norm_backward(grad_normed, centred, factor, rows[0])
    grad_qkv = weight_grad("td,tgce->dgce", normed, stack_low)
    grad_out = weight_grad("td,te->de", grad_attended, mixed)
    quads = []
    for left, right in zip(grad_qkv, grad_out):
        if left is None:
            quads.append(None)
            continue
        right = right.reshape(left.shape[:2] + (1, -1))
        quads.append(jnp.concatenate([left, right], 2).reshape(left.shape[0], -1))
    sums = [
        jnp.sum(grad_normed * centred, 0),
        jnp.sum(grad_normed, 0),
        jnp.sum(grad_queries, 0).reshape(-1),
        jnp.sum(grad_values, 0).reshape(-1),
    ]
    return (quads, grad_value, sums)


def half_cols(core, whole, n_tensor):
    cut = whole.reshape(whole.shape[:-1] + (n_tensor, 2, -1))
    cut = jnp.where(core == 0, cut[..., 0, :], cut[..., 1, :])
    return cut.reshape(whole.shape[:-1] + (-1,))


def spread_cols(core, half, n_tensor):
    cut = half.reshape(half.shape[:-1] + (n_tensor, 1, -1))
    none = jnp.zeros_like(cut)
    both = jnp.concatenate(
        [jnp.where(core == 0, cut, none), jnp.where(core == 0, none, cut)], -2
    )
    return both.reshape(half.shape[:-1] + (-1,))


def body(boundary_in, counts, qkv_weight, proj_weight, fc1_weight, fc2_weight, vectors, fc1_bias):
    core = lax.axis_index("section")
    is_first = core == 0
    place = lax.axis_index("tensor")
    spot = lax.axis_index("dp")
    n_dp, n_tensor = lax.axis_size("dp"), lax.axis_size("tensor")
    slots_per_batch = boundary_in.shape[1] // counts.shape[1]
    live = (place % slots_per_batch < counts[0, place // slots_per_batch]).astype(jnp.float32)
    depth = qkv_weight.shape[1]
    mid = depth // 2
    n_vec = vectors.size

    small_size = n_vec + fc1_bias.size
    packs = []
    for part in range(2):
        cuts = [
            jnp.split(qkv_weight[0], 2, 2)[part].reshape(depth, -1),
            jnp.split(proj_weight[0], 2, 0)[part].T,
            jnp.split(fc1_weight[0], 2, 1)[part],
            jnp.split(fc2_weight[0], 2, 0)[part].T,
        ]
        packs.append(jnp.concatenate(cuts, 1))
    wide = packs[0].shape[1] // 3
    extra = 16
    small = jnp.concatenate([vectors.reshape(-1), fc1_bias.reshape(-1)])
    small = jnp.pad(small, (0, extra * wide - small_size)).reshape(extra, wide)
    small = jnp.pad(small, ((0, 0), (0, 2 * wide)))
    kept = jnp.concatenate([jnp.where(is_first, packs[0], packs[1]), small], 0)
    received = swap(
        jnp.concatenate([jnp.where(is_first, packs[1], packs[0]), small], 0)
    )
    shards = (jnp.where(is_first, kept, received), jnp.where(is_first, received, kept))
    columns = []
    for layer in range(2):
        for number in range(3):
            cols = shards[layer][:, number * wide : (number + 1) * wide]
            if number == 0:
                cols = jnp.concatenate([cols[:mid], cols[depth:], cols[mid:depth]], 0)
            else:
                cols = cols[:depth]
            columns.append(cols)

    tokens = boundary_in.shape[2]
    pad = -tokens % 16
    reach = (tokens + pad) // 2
    ends_in = jnp.pad(boundary_in[0].astype(jnp.bfloat16), ((0, 0), (0, pad), (0, 0)))
    ends_low, ends_high = ends_in[:, :reach], ends_in[:, reach:]
    ends_got = swap(jnp.where(is_first, ends_high, ends_low))
    half_in = jnp.where(is_first, ends_low, ends_got)
    half_cot = jnp.where(is_first, ends_got, ends_high)

    def whole_image(half):
        half = lax.all_to_all(half, "tensor", split_axis=0, concat_axis=2, tiled=True)[0]
        other = swap(half)
        both = [jnp.where(is_first, half, other), jnp.where(is_first, other, half)]
        return relative(jnp.concatenate(both, 0)[:tokens], spot)

    def image_rows(image):
        image = absolute(image.astype(jnp.bfloat16), spot)
        image = jnp.pad(image, ((0, pad), (0, 0)))
        half = jnp.where(is_first, image[:reach], image[reach:])
        half = lax.all_to_all(half[None], "tensor", split_axis=2, concat_axis=0, tiled=True)
        return half

    def small_of(piece):
        extras = jnp.concatenate(piece, 0)
        one = by_chip(extras.reshape(n_dp, extra, -1), spot).astype(jnp.float32)
        one = one.reshape(n_dp, extra, n_tensor, wide).transpose(0, 2, 1, 3)
        one = one.reshape(n_dp, n_tensor, -1)
        rows = one[:, :, :n_vec].reshape(n_dp, n_tensor, 8, -1)
        rows = rows.transpose(2, 1, 0, 3).reshape(8, -1)
        bias = one[:, :, n_vec:small_size].transpose(1, 0, 2).reshape(-1)
        q_bias = half_cols(core, rows[2], n_tensor)
        v_bias = half_cols(core, rows[3], n_tensor)
        up_bias = half_cols(core, bias, n_tensor)
        return (relative(rows, spot), q_bias, v_bias, up_bias)

    value = whole_image(half_in).astype(jnp.float32)

    number = len(columns)
    cut = [mid + extra if k % 3 == 0 else mid for k in range(number)]
    halves, near, far = [None] * number, [None] * number, [None] * number
    pieces = [None] * number
    params = [dict(), dict()]
    state = value
    output = None
    for r in range(number + 4):
        tied = []
        if r < number:
            whole = gather_column(columns[r])
            tied.append(whole)
        if 0 <= r - 1 < number:
            near[r - 1] = exchange_one(*halves[r - 1])
            tied += near[r - 1]
        if 0 <= r - 2 < number:
            far[r - 2] = exchange_two(*halves[r - 2], *near[r - 2])
            tied += far[r - 2]
        k = r - 3
        if 0 <= k < number:
            layer, kind = k // 3, k % 3
            one = params[layer]
            first, second = arrived(*halves[k], near[k], far[k])
            if kind == 0:
                blocks = [p.reshape((-1, mid + extra) + p.shape[1:]) for p in first]
                one["small"] = small_of([p[:, mid:].reshape(-1, p.shape[-1]) for p in blocks])
                first = [p[:, :mid].reshape(-1, p.shape[-1]) for p in blocks]
            matrix = jnp.concatenate(first + second, 0)
            if kind == 0:
                quad = matrix.reshape(matrix.shape[0], n_tensor, 4, -1)
                one["qkv"] = quad[:, :, :3]
                one["out"] = quad[:, :, 3].reshape(quad.shape[0], -1)
                rows, q_bias, v_bias, up_bias = one["small"]
                state, one["kept"] = forward_attention(
                    one["qkv"], one["out"], rows, q_bias, v_bias, state
                )
            elif kind == 1:
                one["up"] = matrix
                one["before"], one["hidden"] = forward_up(
                    matrix, one["small"][3], one["kept"][8]
                )
            else:
                one["down"] = matrix
                state = forward_down(matrix, one["small"][0], state, one["hidden"])
                if layer == 0:
                    state = state.astype(jnp.bfloat16).astype(jnp.float32)
        if r < number + 2:
            extras = [state] if r >= 3 else []
            if r >= 3 and (r - 3) % 3 == 1:
                extras.append(params[(r - 3) // 3]["hidden"])
            if r == 5:
                extras.append(half_cot)
            if r + 1 < number:
                extras.append(columns[r + 1])
            done = tie(tied + extras, [])
            if r + 1 < number:
                columns[r + 1] = done.pop()
            if r == 5:
                half_cot = done.pop()
            if r >= 3 and (r - 3) % 3 == 1:
                params[(r - 3) // 3]["hidden"] = done.pop()
            if r >= 3:
                state = done.pop()
            at = 0
            if r < number:
                halves[r] = (done[0][: cut[r]], done[0][cut[r] :])
                at = 1
            if 0 <= r - 1 < number:
                near[r - 1] = done[at : at + 2]
                at += 2
            if 0 <= r - 2 < number:
                far[r - 2] = done[at:]
        if r == 5:
            cotangent = whole_image(half_cot).astype(jnp.float32) * live
    output = state * live
    out_rows = image_rows(output)

    grads, got, moved, settled = [None] * number, [None] * number, [None] * number, [None] * number
    sums = [dict(), dict()]
    grad = cotangent
    for r in range(number):
        layer, kind = (number - 1 - r) // 3, (number - 1 - r) % 3
        one, total = params[layer], sums[layer]
        rows = one["small"][0]
        tied = []
        if r >= 1:
            got[r - 1] = scatter_one(*grads[r - 1][:2])
            tied += got[r - 1]
        if r >= 2:
            moved[r - 2] = scatter_two(*grads[r - 2][2:], got[r - 2])
            tied += moved[r - 2][0] + moved[r - 2][1]
        if r >= 3:
            settled[r - 3] = scatter_column(*moved[r - 3])
            tied.append(settled[r - 3])
        if kind == 2:
            grads[r], low, total["up_bias"] = backward_down(
                one["down"], one["kept"], one["before"], one["hidden"], grad
            )
            carry = low
        elif kind == 1:
            grads[r], middle, total["two"] = backward_up(
                one["up"], rows, one["kept"], low, grad
            )
            carry = middle
        else:
            grads[r], grad, total["one"] = backward_attention(
                one["qkv"], one["out"], rows, one["kept"], middle
            )
            if layer == 1:
                grad = grad.astype(jnp.bfloat16).astype(jnp.float32)
            carry = grad
        if r < number - 1:
            new = [g for g in grads[r] if g is not None]
            done = tie([carry] + new + tied, [])
            if kind == 2:
                low = done[0]
            elif kind == 1:
                middle = done[0]
            else:
                grad = done[0]
            grads[r] = (done[1 : 1 + len(new)] + [None, None])[:4]
            done = done[1 + len(new) :]
            if r >= 1:
                got[r - 1], done = done[:2], done[2:]
            if r >= 2:
                count = len(moved[r - 2][1])
                moved[r - 2] = (done[:2], done[2 : 2 + count])
                done = done[2 + count :]
            if r >= 3:
                settled[r - 3] = done[0]

    grad_rows = image_rows(grad)
    packed = []
    for layer in range(2):
        total = sums[layer]
        full = [total["one"][0], total["one"][1]] + total["two"]
        full = absolute(jnp.where(core == layer, jnp.stack(full), 0.0), spot)
        q_row = spread_cols(core, total["one"][2], n_tensor)
        v_row = spread_cols(core, total["one"][3], n_tensor)
        up_row = spread_cols(core, total["up_bias"], n_tensor)
        rows = jnp.concatenate([full[:2], q_row[None], v_row[None], full[2:]], 0)
        rows = rows.reshape(8, n_tensor, n_dp, -1).transpose(2, 1, 0, 3).reshape(n_dp, n_tensor, -1)
        up_row = up_row.reshape(n_tensor, n_dp, -1).transpose(1, 0, 2)
        packed.append(jnp.concatenate([rows, up_row], -1))
    ours = jnp.where(is_first, packed[0], packed[1])
    other = swap(jnp.where(is_first, packed[1], packed[0]))
    little = (ours + other).astype(jnp.bfloat16).reshape(n_dp * n_tensor, -1)
    little = lax.psum_scatter(little, ("dp", "tensor"), scatter_dimension=0, tiled=True)[0]
    little = little.astype(jnp.float32)

    last = number - 1
    got[last] = scatter_one(*grads[last][:2])
    for k in range(number):
        if moved[k] is None:
            moved[k] = scatter_two(*grads[k][2:], got[k])
    for k in range(number):
        if settled[k] is None:
            settled[k] = scatter_column(*moved[k])
    grad_vectors = little[:n_vec].reshape(vectors.shape)
    grad_bias = little[n_vec:small_size].reshape(fc1_bias.shape)

    own = jnp.where(is_first, grad_rows, out_rows)
    other = swap(jnp.where(is_first, out_rows, grad_rows))
    ends = [jnp.where(is_first, own, other), jnp.where(is_first, other, own)]
    boundary_out = jnp.concatenate(ends, 1)[:, :tokens].astype(jnp.float32)[None]
    lows, highs = [], []
    for kind in range(3):
        first, second = settled[last - kind], settled[last - kind - 3]
        kept = jnp.where(is_first, first, second)
        received = swap(jnp.where(is_first, second, first))
        lows.append(jnp.where(is_first, kept, received).astype(jnp.float32))
        highs.append(jnp.where(is_first, received, kept).astype(jnp.float32))
    low, high = [part[0].reshape(depth, 4, -1) for part in (lows, highs)]
    grad_qkv = jnp.concatenate([low[:, :3], high[:, :3]], 2)[None]
    grad_proj = jnp.concatenate([low[:, 3].T, high[:, 3].T], 0)[None]
    grad_up = jnp.concatenate([lows[1], highs[1]], 1)[None]
    grad_down = jnp.concatenate([lows[2].T, highs[2].T], 0)[None]
    return (boundary_out, grad_qkv, grad_proj, grad_up, grad_down, grad_vectors, grad_bias)


def solution(mesh):
    in_specs = (
        P("section", "dp", None, "tensor"),
        P("dp", None),
        P("section", "dp", None, "tensor"),
        P("section", "tensor", "dp"),
        P("section", "dp", "tensor"),
        P("section", "tensor", "dp"),
        P("section", None, "tensor", "dp"),
        P("section", "tensor", "dp"),
    )
    out_specs = (
        P("section", "dp", None, "tensor"),
        P("section", "dp", None, "tensor"),
        P("section", "tensor", "dp"),
        P("section", "dp", "tensor"),
        P("section", "tensor", "dp"),
        P("section", None, "tensor", "dp"),
        P("section", "tensor", "dp"),
    )
    return jax.shard_map(body, mesh=mesh, in_specs=in_specs, out_specs=out_specs, check_vma=False)
```

```python
import jax
import jax.numpy as jnp
from jax import lax
from jax.experimental import pallas as pl
from jax.experimental.pallas import tpu as pltpu
from jax.sharding import PartitionSpec as P

HD = 64
EPS = 1e-06


def swap(value):
    return lax.ppermute(value, "section", [(0, 1), (1, 0)])


def pair_sum(partial):
    low = partial.astype(jnp.bfloat16)
    return low.astype(jnp.float32) + swap(low).astype(jnp.float32)


def swap_x(value):
    n = lax.axis_size("dp")
    return lax.ppermute(value, "dp", [(i, i ^ 1) for i in range(n)])


def swap_y(value):
    n = lax.axis_size("dp")
    return lax.ppermute(value, "dp", [(i, i ^ 2) for i in range(n)])


def tie(values, others):
    count = len(values)

    def kernel(*refs):
        pass

    anywhere = pl.BlockSpec(memory_space=pl.ANY)
    done = pl.pallas_call(
        kernel,
        out_shape=[jax.ShapeDtypeStruct(v.shape, v.dtype) for v in values],
        in_specs=[anywhere] * (count + len(others)),
        out_specs=[anywhere] * count,
        input_output_aliases={i: i for i in range(count)},
    )(*values, *others)
    return list(done)


def gather_column(shard):
    return lax.all_gather(shard, "tensor", axis=1, tiled=True)


def exchange_one(first, second):
    if lax.axis_size("dp") != 4:
        return [lax.all_gather(v, "dp", axis=0, tiled=True) for v in (first, second)]
    return [swap_y(first), swap_x(second)]


def exchange_two(first, second, near_first, near_second):
    if lax.axis_size("dp") != 4:
        return []
    return [swap_x(first), swap_x(near_first), swap_y(second), swap_y(near_second)]


def arrived(first, second, near, far):
    if lax.axis_size("dp") != 4:
        return ([near[0]], [near[1]])
    return ([first, near[0], far[0], far[1]], [second, near[1], far[2], far[3]])


def row_cuts(depth):
    half = depth // 2
    if lax.axis_size("dp") != 4:
        return [(0, half), (half, depth), None, None]
    part = half // 2
    return [(part, half), (half + part, depth), (0, part), (half, half + part)]


def add(left, right):
    return left.astype(jnp.float32) + right.astype(jnp.float32)


def scatter_one(send_first, send_second):
    if lax.axis_size("dp") != 4:
        return [
            lax.psum_scatter(v, "dp", scatter_dimension=0, tiled=True)
            for v in (send_first, send_second)
        ]
    return [swap_x(send_first), swap_y(send_second)]


def scatter_two(keep_first, keep_second, got):
    if lax.axis_size("dp") != 4:
        return (got, [])
    stay, come = [], []
    for keep, new, far in zip((keep_first, keep_second), got, (swap_y, swap_x)):
        half = keep.shape[0] // 2
        come.append(far(add(keep[half:], new[half:]).astype(jnp.bfloat16)))
        stay.append(add(keep[:half], new[:half]).astype(jnp.bfloat16))
    return (stay, come)


def scatter_column(stay, come):
    if come:
        stay = [add(s, c).astype(jnp.bfloat16) for s, c in zip(stay, come)]
    return lax.psum_scatter(
        jnp.concatenate(stay, 0), "tensor", scatter_dimension=1, tiled=True
    )


def flip_axis(value, axis, bit):
    return jnp.where(bit == 1, jnp.flip(value, axis), value)


def relative(value, spot):
    n_dp = lax.axis_size("dp")
    lead = value.shape[:-1]
    k = len(lead)
    if n_dp != 4:
        cut = value.reshape(lead + (n_dp, 2, -1))
        return jnp.swapaxes(cut, k, k + 1).reshape(value.shape)
    cut = value.reshape(lead + (2, 2, 2, -1))
    cut = flip_axis(flip_axis(cut, k, spot // 2), k + 1, spot % 2)
    first = jnp.swapaxes(cut[..., 0, :], k, k + 1)
    second = cut[..., 1, :]
    return jnp.concatenate([first.reshape(lead + (-1,)), second.reshape(lead + (-1,))], -1)


def absolute(value, spot):
    n_dp = lax.axis_size("dp")
    lead = value.shape[:-1]
    k = len(lead)
    if n_dp != 4:
        cut = value.reshape(lead + (2, n_dp, -1))
        return jnp.swapaxes(cut, k, k + 1).reshape(value.shape)
    cut = value.reshape(lead + (2, 2, 2, -1))
    first = jnp.swapaxes(cut[..., 0, :, :, :], k, k + 1)
    second = cut[..., 1, :, :, :]
    cut = jnp.stack([first, second], k + 2)
    cut = flip_axis(flip_axis(cut, k, spot // 2), k + 1, spot % 2)
    return cut.reshape(value.shape)


def by_chip(blocks, spot):
    n_dp = lax.axis_size("dp")
    if n_dp != 4:
        return blocks
    cut = blocks.reshape((2, 2) + blocks.shape[1:])
    cut = jnp.swapaxes(cut, 0, 1)
    cut = flip_axis(flip_axis(cut, 0, spot // 2), 1, spot % 2)
    return cut.reshape(blocks.shape)


def by_arrival(blocks, spot):
    n_dp = lax.axis_size("dp")
    if n_dp != 4:
        return blocks
    cut = blocks.reshape((2, 2) + blocks.shape[1:])
    cut = flip_axis(flip_axis(cut, 0, spot // 2), 1, spot % 2)
    return jnp.swapaxes(cut, 0, 1).reshape(blocks.shape)


VMEM_BYTES = 50 * 2**20
BF = jnp.bfloat16
F32 = jnp.float32


def shape(dims, kind=jnp.bfloat16):
    return jax.ShapeDtypeStruct(dims, kind)


def run(kernel, outs, ins, flops):
    block = pl.BlockSpec(memory_space=pltpu.VMEM)
    moved = sum(v.size * v.dtype.itemsize for v in list(ins) + list(outs))
    done = pl.pallas_call(
        kernel,
        out_shape=list(outs),
        in_specs=[block] * len(ins),
        out_specs=[block] * len(outs),
        cost_estimate=pl.CostEstimate(flops=flops, bytes_accessed=moved, transcendentals=0),
        compiler_params=pltpu.CompilerParams(vmem_limit_bytes=VMEM_BYTES),
    )(*ins)
    return list(done)


def nn(left, right):
    return lax.dot_general(left, right, (((1,), (0,)), ((), ())), preferred_element_type=F32)


def nt(left, right):
    return lax.dot_general(left, right, (((1,), (1,)), ((), ())), preferred_element_type=F32)


def tn(left, right):
    return lax.dot_general(left, right, (((0,), (0,)), ((), ())), preferred_element_type=F32)


def stack_rows(pieces, counts, cols):
    return jnp.concatenate([p[:n, cols] for p, n in zip(pieces, counts)], 0)


def center_scale(value):
    center = jnp.mean(value, -1, keepdims=True)
    spread = jnp.mean(value * value, -1, keepdims=True) - center * center
    factor = lax.rsqrt(spread + EPS)
    return ((value - center) * factor, factor)


def norm_backward(grad_normed, centred, factor, gain):
    scaled = grad_normed * gain
    return factor * (
        scaled
        - jnp.mean(scaled, -1, keepdims=True)
        - centred * jnp.mean(scaled * centred, -1, keepdims=True)
    )


def column_sum(value):
    return jnp.sum(value, 0, keepdims=True)


def attention_forward(tokens, terms, bias_row, low, weights, rows, q_bias, v_bias):
    pieces, counts = weights
    size, depth = terms[0].shape
    wide = pieces[0].shape[1]
    groups = wide // 512
    half = groups * 128
    n_terms, n_pieces = len(terms), len(pieces)

    def kernel(*refs):
        term_refs, refs = refs[:n_terms], refs[n_terms:]
        bias_ref, rows_ref, qb_ref, vb_ref = refs[:4]
        piece_refs, refs = refs[4 : 4 + n_pieces], refs[4 + n_pieces :]
        u_ref, n_ref, q_ref, k_ref, v_ref, p_ref, o_ref, part_ref = refs
        value = term_refs[0][...].astype(F32)
        for ref in term_refs[1:]:
            value = value + ref[...].astype(F32)
        if n_terms > 1:
            value = value + bias_ref[...]
        if low:
            value = value.astype(BF).astype(F32)
        u_ref[...] = value
        centred, factor = center_scale(value)
        n_ref[...] = (centred * rows_ref[0:1] + rows_ref[1:2]).astype(BF)
        lane = lax.broadcasted_iota(jnp.int32, (size, 128), 1)
        key_lane = lax.broadcasted_iota(jnp.int32, (size, size), 1)
        normed = n_ref[...]
        for g in range(groups):
            at = slice(g * 128, (g + 1) * 128)
            matrix = stack_rows(piece_refs, counts, slice(g * 512, g * 512 + 384))
            projected = nn(normed, matrix)
            q = (projected[:, :128] + qb_ref[:, at]).astype(BF)
            k = projected[:, 128:256].astype(BF)
            v = (projected[:, 256:384] + vb_ref[:, at]).astype(BF)
            q_ref[:, at] = q
            k_ref[:, at] = k
            v_ref[:, at] = v
            mixed = None
            for h in range(2):
                mine = (lane // HD) == h
                scores = nt(jnp.where(mine, q, jnp.zeros_like(q)), k) * HD ** (-0.5)
                scores = jnp.where(key_lane < tokens, scores, -1e30)
                highest = jnp.max(scores, -1, keepdims=True)
                exponent = jnp.exp(scores - highest)
                inverse = 1.0 / jnp.sum(exponent, -1, keepdims=True)
                soft = (exponent * inverse).astype(BF)
                p_ref[2 * g + h] = soft
                out = nn(soft, v)
                mixed = out if h == 0 else jnp.where(mine, out, mixed)
            o_ref[:, at] = mixed.astype(BF)
        matrix = jnp.concatenate(
            [stack_rows(piece_refs, counts, slice(g * 512 + 384, g * 512 + 512)) for g in range(groups)], 1
        )
        part_ref[...] = nt(o_ref[...], matrix).astype(BF)

    outs = [shape((size, depth), F32), shape((size, depth))] + [shape((size, half))] * 3
    outs += [shape((2 * groups, size, size)), shape((size, half)), shape((size, depth))]
    flops = 2 * size * depth * wide + 8 * size * size * half
    return run(kernel, outs, [*terms, bias_row, rows, q_bias, v_bias, *pieces], flops)


def up_forward(terms, weights, rows, up_bias):
    pieces, counts = weights
    size, depth = terms[0].shape
    wide = pieces[0].shape[1]

    def kernel(*refs):
        u_ref, own_ref, far_ref, rows_ref, bias_ref = refs[:5]
        piece_refs = refs[5 : 5 + len(pieces)]
        mid_ref, n_ref, slope_ref, hidden_ref = refs[5 + len(pieces) :]
        value = u_ref[...] + own_ref[...].astype(F32) + far_ref[...].astype(F32) + rows_ref[4:5]
        mid_ref[...] = value
        centred, factor = center_scale(value)
        n_ref[...] = (centred * rows_ref[5:6] + rows_ref[6:7]).astype(BF)
        step = 512
        for at in range(0, wide, step):
            cols = slice(at, at + step)
            before = nn(n_ref[...], stack_rows(piece_refs, counts, cols)) + bias_ref[:, cols]
            cdf = 0.5 * (1.0 + lax.erf(before * 0.7071067811865476))
            density = jnp.exp(-0.5 * before * before) * 0.3989422804014327
            hidden_ref[:, cols] = (before * cdf).astype(BF)
            slope_ref[:, cols] = (cdf + before * density).astype(BF)

    outs = [shape((size, depth), F32), shape((size, depth)), shape((size, wide)), shape((size, wide))]
    return run(kernel, outs, [*terms, rows, up_bias, *pieces], 2 * size * depth * wide)


def contract_wide(left, weights):
    pieces, counts = weights
    size, wide = left.shape
    depth = sum(counts)

    def kernel(*refs):
        left_ref, piece_refs, out_ref = refs[0], refs[1:-1], refs[-1]
        matrix = stack_rows(piece_refs, counts, slice(0, wide))
        out_ref[...] = nt(left_ref[...], matrix).astype(BF)

    return run(kernel, [shape((size, depth))], [left, *pieces], 2 * size * depth * wide)[0]


def weight_outs(depth, wide):
    cuts = [c for c in row_cuts(depth) if c is not None]
    return cuts, [shape((c[1] - c[0], wide)) for c in cuts]


def fill(grads):
    return (list(grads) + [None, None])[:4]


def down_backward(grad_out, hidden, slope, weights):
    pieces, counts = weights
    size, depth = grad_out.shape
    wide = hidden.shape[1]
    cuts, grad_outs = weight_outs(depth, wide)

    def kernel(*refs):
        g_ref, hidden_ref, slope_ref = refs[:3]
        piece_refs, refs = refs[3 : 3 + len(pieces)], refs[3 + len(pieces) :]
        low_ref, sum_ref, bias_ref = refs[:3]
        sum_ref[...] = column_sum(g_ref[...])
        branch = g_ref[...].astype(BF)
        for cut, ref in zip(cuts, refs[3:]):
            ref[...] = tn(branch[:, cut[0] : cut[1]], hidden_ref[...]).astype(BF)
        step = 512
        for at in range(0, wide, step):
            cols = slice(at, at + step)
            back = nn(branch, stack_rows(piece_refs, counts, cols)) * slope_ref[:, cols].astype(F32)
            bias_ref[:, cols] = column_sum(back)
            low_ref[:, cols] = back.astype(BF)

    outs = [shape((size, wide)), shape((1, depth), F32), shape((1, wide), F32)] + grad_outs
    done = run(kernel, outs, [grad_out, hidden, slope, *pieces], 4 * size * depth * wide)
    return done[0], done[1], done[2], fill(done[3:])


def up_grad(normed, low):
    size, depth = normed.shape
    wide = low.shape[1]
    cuts, outs = weight_outs(depth, wide)

    def kernel(n_ref, low_ref, *refs):
        for cut, ref in zip(cuts, refs):
            ref[...] = tn(n_ref[:, cut[0] : cut[1]], low_ref[...]).astype(BF)

    return fill(run(kernel, outs, [normed, low], 2 * size * depth * wide))


def attention_backward(grad_out, own, far, middle, rows, saved, weights):
    pieces, counts = weights
    size, depth = grad_out.shape
    wide = pieces[0].shape[1]
    groups = wide // 512
    half = groups * 128
    scale = HD ** (-0.5)

    def kernel(*refs):
        g_ref, own_ref, far_ref, mid_ref, rows_ref, q_ref, k_ref, v_ref, p_ref, o_ref = refs[:10]
        piece_refs, refs = refs[10 : 10 + len(pieces)], refs[10 + len(pieces) :]
        dmid_ref, dz_ref, dq_ref, dk_ref, dv_ref, part_ref, sum_ref, qs_ref, vs_ref = refs
        grad_normed = own_ref[...].astype(F32) + far_ref[...].astype(F32)
        centred, factor = center_scale(mid_ref[...])
        sum_ref[1:2] = column_sum(grad_normed * centred)
        sum_ref[2:3] = column_sum(grad_normed)
        dmid = g_ref[...] + norm_backward(grad_normed, centred, factor, rows_ref[5:6])
        dmid_ref[...] = dmid
        sum_ref[0:1] = column_sum(dmid)
        dz_ref[...] = dmid.astype(BF)
        lane = lax.broadcasted_iota(jnp.int32, (size, 128), 1)
        for g in range(groups):
            at = slice(g * 128, (g + 1) * 128)
            matrix = stack_rows(piece_refs, counts, slice(g * 512 + 384, g * 512 + 512))
            grad_mixed = nn(dz_ref[...], matrix).astype(BF)
            q, k, v = q_ref[:, at], k_ref[:, at], v_ref[:, at]
            inner = grad_mixed.astype(F32) * o_ref[:, at].astype(F32)
            dq, dk, dv = None, None, None
            for h in range(2):
                mine = (lane // HD) == h
                soft = p_ref[2 * g + h]
                none = jnp.zeros_like(q)
                do = jnp.where(mine, grad_mixed, none)
                total = jnp.sum(jnp.where(mine, inner, 0.0), -1, keepdims=True)
                grad_soft = nt(do, v)
                grad_scores = (soft.astype(F32) * (grad_soft - total)).astype(BF)
                new_q = nn(grad_scores, k)
                new_k = tn(jnp.where(mine, q, none), grad_scores)
                new_v = tn(do, soft)
                dq = new_q if h == 0 else jnp.where(mine, new_q, dq)
                dk = new_k if h == 0 else dk + new_k
                dv = new_v if h == 0 else dv + new_v
            dq, dk, dv = dq * scale, dk.T * scale, dv.T
            qs_ref[:, at] = column_sum(dq)
            vs_ref[:, at] = column_sum(dv)
            dq_ref[:, at] = dq.astype(BF)
            dk_ref[:, at] = dk.astype(BF)
            dv_ref[:, at] = dv.astype(BF)
        total = None
        for g in range(groups):
            at = slice(g * 128, (g + 1) * 128)
            left = jnp.concatenate([dq_ref[:, at], dk_ref[:, at], dv_ref[:, at]], 1)
            new = nt(left, stack_rows(piece_refs, counts, slice(g * 512, g * 512 + 384)))
            total = new if g == 0 else total + new
        part_ref[...] = total.astype(BF)

    outs = [shape((size, depth), F32), shape((size, depth))] + [shape((size, half))] * 3
    outs += [shape((size, depth)), shape((3, depth), F32)] + [shape((1, half), F32)] * 2
    flops = 2 * size * depth * wide + 16 * size * size * half
    return run(kernel, outs, [grad_out, own, far, middle, rows, *saved, *pieces], flops)


def attention_grad(normed, dz, dq, dk, dv, mixed):
    size, depth = normed.shape
    groups = dq.shape[1] // 128
    cuts, outs = weight_outs(depth, groups * 512)

    def kernel(n_ref, dz_ref, dq_ref, dk_ref, dv_ref, o_ref, *refs):
        for cut, ref in zip(cuts, refs):
            rows = slice(cut[0], cut[1])
            for g in range(groups):
                at = slice(g * 128, (g + 1) * 128)
                right = jnp.concatenate([dq_ref[:, at], dk_ref[:, at], dv_ref[:, at]], 1)
                ref[:, g * 512 : g * 512 + 384] = tn(n_ref[:, rows], right).astype(BF)
                ref[:, g * 512 + 384 : g * 512 + 512] = tn(dz_ref[:, rows], o_ref[:, at]).astype(BF)

    flops = 2 * size * depth * groups * 512
    return fill(run(kernel, outs, [normed, dz, dq, dk, dv, mixed], flops))


def value_backward(dmid, own, far, value, rows, low):
    size, depth = dmid.shape

    def kernel(dmid_ref, own_ref, far_ref, u_ref, rows_ref, out_ref, sum_ref):
        grad_normed = own_ref[...].astype(F32) + far_ref[...].astype(F32)
        centred, factor = center_scale(u_ref[...])
        sum_ref[0:1] = column_sum(grad_normed * centred)
        sum_ref[1:2] = column_sum(grad_normed)
        out = dmid_ref[...] + norm_backward(grad_normed, centred, factor, rows_ref[0:1])
        if low:
            out = out.astype(BF).astype(F32)
        out_ref[...] = out

    outs = [shape((size, depth), F32), shape((2, depth), F32)]
    return run(kernel, outs, [dmid, own, far, value, rows], 20 * size * depth)


def half_cols(core, whole, n_tensor):
    cut = whole.reshape(whole.shape[:-1] + (n_tensor, 2, -1))
    cut = jnp.where(core == 0, cut[..., 0, :], cut[..., 1, :])
    return cut.reshape(whole.shape[:-1] + (-1,))


def spread_cols(core, half, n_tensor):
    cut = half.reshape(half.shape[:-1] + (n_tensor, 1, -1))
    none = jnp.zeros_like(cut)
    both = jnp.concatenate(
        [jnp.where(core == 0, cut, none), jnp.where(core == 0, none, cut)], -2
    )
    return both.reshape(half.shape[:-1] + (-1,))


def body(boundary_in, counts, qkv_weight, proj_weight, fc1_weight, fc2_weight, vectors, fc1_bias):
    core = lax.axis_index("section")
    is_first = core == 0
    place = lax.axis_index("tensor")
    spot = lax.axis_index("dp")
    n_dp, n_tensor = lax.axis_size("dp"), lax.axis_size("tensor")
    slots_per_batch = boundary_in.shape[1] // counts.shape[1]
    live = (place % slots_per_batch < counts[0, place // slots_per_batch]).astype(jnp.float32)
    depth = qkv_weight.shape[1]
    mid = depth // 2
    n_vec = vectors.size

    small_size = n_vec + fc1_bias.size
    packs = []
    for part in range(2):
        cuts = [
            jnp.split(qkv_weight[0], 2, 2)[part].reshape(depth, -1),
            jnp.split(proj_weight[0], 2, 0)[part].T,
            jnp.split(fc1_weight[0], 2, 1)[part],
            jnp.split(fc2_weight[0], 2, 0)[part].T,
        ]
        packs.append(jnp.concatenate(cuts, 1))
    wide = packs[0].shape[1] // 3
    extra = 16
    small = jnp.concatenate([vectors.reshape(-1), fc1_bias.reshape(-1)])
    small = jnp.pad(small, (0, extra * wide - small_size)).reshape(extra, wide)
    small = jnp.pad(small, ((0, 0), (0, 2 * wide)))
    kept = jnp.concatenate([jnp.where(is_first, packs[0], packs[1]), small], 0)
    received = swap(
        jnp.concatenate([jnp.where(is_first, packs[1], packs[0]), small], 0)
    )
    shards = (jnp.where(is_first, kept, received), jnp.where(is_first, received, kept))
    columns = []
    for layer in range(2):
        for number in range(3):
            cols = shards[layer][:, number * wide : (number + 1) * wide]
            if number == 0:
                cols = jnp.concatenate([cols[:mid], cols[depth:], cols[mid:depth]], 0)
            else:
                cols = cols[:depth]
            columns.append(cols)

    tokens = boundary_in.shape[2]
    pad = -tokens % 16
    reach = (tokens + pad) // 2
    ends_in = jnp.pad(boundary_in[0].astype(jnp.bfloat16), ((0, 0), (0, pad), (0, 0)))
    ends_low, ends_high = ends_in[:, :reach], ends_in[:, reach:]
    ends_got = swap(jnp.where(is_first, ends_high, ends_low))
    half_in = jnp.where(is_first, ends_low, ends_got)
    half_cot = jnp.where(is_first, ends_got, ends_high)

    def whole_image(half):
        half = lax.all_to_all(half, "tensor", split_axis=0, concat_axis=2, tiled=True)[0]
        other = swap(half)
        both = [jnp.where(is_first, half, other), jnp.where(is_first, other, half)]
        return relative(jnp.concatenate(both, 0), spot)

    def image_rows(image):
        image = absolute(image.astype(jnp.bfloat16), spot)
        half = jnp.where(is_first, image[:reach], image[reach:])
        half = lax.all_to_all(half[None], "tensor", split_axis=2, concat_axis=0, tiled=True)
        return half

    def small_of(piece):
        extras = jnp.concatenate(piece, 0)
        one = by_chip(extras.reshape(n_dp, extra, -1), spot).astype(jnp.float32)
        one = one.reshape(n_dp, extra, n_tensor, wide).transpose(0, 2, 1, 3)
        one = one.reshape(n_dp, n_tensor, -1)
        rows = one[:, :, :n_vec].reshape(n_dp, n_tensor, 8, -1)
        rows = rows.transpose(2, 1, 0, 3).reshape(8, -1)
        bias = one[:, :, n_vec:small_size].transpose(1, 0, 2).reshape(-1)
        q_bias = half_cols(core, rows[2], n_tensor)
        v_bias = half_cols(core, rows[3], n_tensor)
        up_bias = half_cols(core, bias, n_tensor)
        return (relative(rows, spot), q_bias[None], v_bias[None], up_bias[None])

    value = whole_image(half_in).astype(jnp.float32)

    number = len(columns)
    cut = [mid + extra if k % 3 == 0 else mid for k in range(number)]
    halves, near, far = [None] * number, [None] * number, [None] * number
    params = [dict(), dict()]
    output = None
    for r in range(number + 3):
        tied = []
        if r < number:
            whole = gather_column(columns[r])
            tied.append(whole)
        if 0 <= r - 1 < number:
            near[r - 1] = exchange_one(*halves[r - 1])
            tied += near[r - 1]
        if 0 <= r - 2 < number:
            far[r - 2] = exchange_two(*halves[r - 2], *near[r - 2])
            tied += far[r - 2]
        k = r - 3
        ready = None
        if 0 <= k < number:
            layer, kind = k // 3, k % 3
            one = params[layer]
            first, second = arrived(*halves[k], near[k], far[k])
            if kind == 0:
                blocks = [p.reshape((-1, mid + extra) + p.shape[1:]) for p in first]
                one["small"] = small_of([p[:, mid:].reshape(-1, p.shape[-1]) for p in blocks])
                if n_dp != 4:
                    first = [p[:, :mid].reshape(-1, p.shape[-1]) for p in blocks]
            pieces = first + second
            counts = [mid if n_dp == 4 else p.shape[0] for p in pieces]
            weights = (pieces, counts)
            rows, q_bias, v_bias, up_bias = one["small"]
            if kind == 0:
                one["qkvo"] = weights
                terms = [value] if layer == 0 else [state, *pair]
                bias_row = (rows if layer == 0 else params[0]["small"][0])[7:8]
                done = attention_forward(
                    tokens, terms, bias_row, layer == 1, weights, rows, q_bias, v_bias
                )
                one["u"], one["n1"], one["saved"], part = done[0], done[1], done[2:7], done[7]
                pair = [part, swap(part)]
                ready = pair
            elif kind == 1:
                one["up"] = weights
                one["mid"], one["n2"], one["slope"], one["hidden"] = up_forward(
                    [one["u"], *pair], weights, rows, up_bias
                )
                ready = [one["hidden"]]
            else:
                one["down"] = weights
                part = contract_wide(one["hidden"], weights)
                state = one["mid"]
                pair = [part, swap(part)]
                ready = pair
        if r < number + 2:
            extras = list(ready) if ready else []
            count = len(extras)
            if r == 5:
                extras.append(half_cot)
            if r + 1 < number:
                extras.append(columns[r + 1])
            done = tie(tied + extras, [])
            if r + 1 < number:
                columns[r + 1] = done.pop()
            if r == 5:
                half_cot = done.pop()
            if count == 2:
                pair = done[-2:]
            elif count == 1:
                one["hidden"] = done[-1]
            at = 0
            if r < number:
                halves[r] = (done[0][: cut[r]], done[0][cut[r] :])
                at = 1
            if 0 <= r - 1 < number:
                near[r - 1] = done[at : at + 2]
                at += 2
            if 0 <= r - 2 < number:
                far[r - 2] = done[at : at + len(far[r - 2])]
        if r == 5:
            cotangent = whole_image(half_cot).astype(jnp.float32) * live
    last_rows = params[1]["small"][0]
    output = state + pair[0].astype(jnp.float32) + pair[1].astype(jnp.float32) + last_rows[7:8]
    out_rows = image_rows(output * live)

    grads, got, moved, settled = [None] * number, [None] * number, [None] * number, [None] * number
    sums = [dict(), dict()]
    grad = cotangent
    for r in range(number):
        layer, kind = (number - 1 - r) // 3, (number - 1 - r) % 3
        one, total = params[layer], sums[layer]
        rows = one["small"][0]
        tied = []
        if r >= 1:
            got[r - 1] = scatter_one(*grads[r - 1][:2])
            tied += got[r - 1]
        if r >= 2:
            moved[r - 2] = scatter_two(*grads[r - 2][2:], got[r - 2])
            tied += moved[r - 2][0] + moved[r - 2][1]
        if r >= 3:
            settled[r - 3] = scatter_column(*moved[r - 3])
            tied.append(settled[r - 3])
        if kind == 2:
            low, total["out"], total["up_bias"], grads[r] = down_backward(
                grad, one["hidden"], one["slope"], one["down"]
            )
            carry = low
        elif kind == 1:
            part = contract_wide(low, one["up"])
            grads[r] = up_grad(one["n2"], low)
            pair = [part, swap(part)]
            done = attention_backward(
                grad, *pair, one["mid"], rows, one["saved"], one["qkvo"]
            )
            dmid, dz, dq, dk, dv, part, total["mid"], total["q"], total["v"] = done
            carry = part
        else:
            pair = [part, swap(part)]
            grads[r] = attention_grad(one["n1"], dz, dq, dk, dv, one["saved"][4])
            grad, total["one"] = value_backward(dmid, *pair, one["u"], rows, layer == 1)
            carry = grad
        if r < number - 1:
            new = [g for g in grads[r] if g is not None]
            done = tie([carry] + new + tied, [])
            if kind == 2:
                low = done[0]
            elif kind == 1:
                part = done[0]
            else:
                grad = done[0]
            grads[r] = fill(done[1 : 1 + len(new)])
            done = done[1 + len(new) :]
            if r >= 1:
                got[r - 1], done = done[:2], done[2:]
            if r >= 2:
                count = len(moved[r - 2][1])
                moved[r - 2] = (done[:2], done[2 : 2 + count])
                done = done[2 + count :]
            if r >= 3:
                settled[r - 3] = done[0]

    grad_rows = image_rows(grad)
    packed = []
    for layer in range(2):
        total = sums[layer]
        full = jnp.concatenate([total["one"], total["mid"], total["out"]], 0)
        full = absolute(jnp.where(core == layer, full, 0.0), spot)
        q_row = spread_cols(core, total["q"][0], n_tensor)
        v_row = spread_cols(core, total["v"][0], n_tensor)
        up_row = spread_cols(core, total["up_bias"][0], n_tensor)
        rows = jnp.concatenate([full[:2], q_row[None], v_row[None], full[2:]], 0)
        rows = rows.reshape(8, n_tensor, n_dp, -1).transpose(2, 1, 0, 3).reshape(n_dp, n_tensor, -1)
        up_row = up_row.reshape(n_tensor, n_dp, -1).transpose(1, 0, 2)
        packed.append(jnp.concatenate([rows, up_row], -1))
    ours = jnp.where(is_first, packed[0], packed[1])
    other = swap(jnp.where(is_first, packed[1], packed[0]))
    little = (ours + other).astype(jnp.bfloat16)
    room = jnp.zeros((n_dp, n_tensor, extra * wide - small_size), little.dtype)
    little = jnp.concatenate([little, room], -1).reshape(n_dp, n_tensor, extra, wide)
    little = by_arrival(little.transpose(0, 2, 1, 3).reshape(n_dp, extra, -1), spot)
    if n_dp != 4:
        little = lax.psum_scatter(little, "dp", scatter_dimension=0, tiled=True)[0]
    else:
        little = add(little[:2], swap_x(little[2:])).astype(jnp.bfloat16)
        little = add(little[0], swap_y(little[1])).astype(jnp.bfloat16)

    last = number - 1
    got[last] = scatter_one(*grads[last][:2])
    for k in range(number):
        if moved[k] is None:
            moved[k] = scatter_two(*grads[k][2:], got[k])
    for k in range(number):
        if settled[k] is None:
            stay, come = moved[k]
            if k == last:
                stay = [add(s, c).astype(jnp.bfloat16) for s, c in zip(stay, come)] if come else stay
                stay, come = [*stay, little], []
            settled[k] = scatter_column(stay, come)
    little = settled[last][depth:].reshape(-1).astype(jnp.float32)
    settled[last] = settled[last][:depth]
    grad_vectors = little[:n_vec].reshape(vectors.shape)
    grad_bias = little[n_vec:small_size].reshape(fc1_bias.shape)

    own = jnp.where(is_first, grad_rows, out_rows)
    other = swap(jnp.where(is_first, out_rows, grad_rows))
    ends = [jnp.where(is_first, own, other), jnp.where(is_first, other, own)]
    boundary_out = jnp.concatenate(ends, 1)[:, :tokens].astype(jnp.float32)[None]
    lows, highs = [], []
    for kind in range(3):
        first, second = settled[last - kind], settled[last - kind - 3]
        kept = jnp.where(is_first, first, second)
        received = swap(jnp.where(is_first, second, first))
        lows.append(jnp.where(is_first, kept, received).astype(jnp.float32))
        highs.append(jnp.where(is_first, received, kept).astype(jnp.float32))
    low, high = [part[0].reshape(depth, 4, -1) for part in (lows, highs)]
    grad_qkv = jnp.concatenate([low[:, :3], high[:, :3]], 2)[None]
    grad_proj = jnp.concatenate([low[:, 3].T, high[:, 3].T], 0)[None]
    grad_up = jnp.concatenate([lows[1], highs[1]], 1)[None]
    grad_down = jnp.concatenate([lows[2].T, highs[2].T], 0)[None]
    return (boundary_out, grad_qkv, grad_proj, grad_up, grad_down, grad_vectors, grad_bias)


def solution(mesh):
    in_specs = (
        P("section", "dp", None, "tensor"),
        P("dp", None),
        P("section", "dp", None, "tensor"),
        P("section", "tensor", "dp"),
        P("section", "dp", "tensor"),
        P("section", "tensor", "dp"),
        P("section", None, "tensor", "dp"),
        P("section", "tensor", "dp"),
    )
    out_specs = (
        P("section", "dp", None, "tensor"),
        P("section", "dp", None, "tensor"),
        P("section", "tensor", "dp"),
        P("section", "dp", "tensor"),
        P("section", "tensor", "dp"),
        P("section", None, "tensor", "dp"),
        P("section", "tensor", "dp"),
    )
    return jax.shard_map(body, mesh=mesh, in_specs=in_specs, out_specs=out_specs, check_vma=False)
```

```python
import jax
import jax.numpy as jnp
from jax import lax
from jax.experimental import pallas as pl
from jax.experimental.pallas import tpu as pltpu
from jax.sharding import PartitionSpec as P

HD = 64
EPS = 1e-06


def swap(value):
    return lax.ppermute(value, "section", [(0, 1), (1, 0)])


def pair_sum(partial):
    low = partial.astype(jnp.bfloat16)
    return low.astype(jnp.float32) + swap(low).astype(jnp.float32)


def swap_x(value):
    n = lax.axis_size("dp")
    return lax.ppermute(value, "dp", [(i, i ^ 1) for i in range(n)])


def swap_y(value):
    n = lax.axis_size("dp")
    return lax.ppermute(value, "dp", [(i, i ^ 2) for i in range(n)])


def tie(values, others):
    count = len(values)

    def kernel(*refs):
        pass

    anywhere = pl.BlockSpec(memory_space=pl.ANY)
    done = pl.pallas_call(
        kernel,
        out_shape=[jax.ShapeDtypeStruct(v.shape, v.dtype) for v in values],
        in_specs=[anywhere] * (count + len(others)),
        out_specs=[anywhere] * count,
        input_output_aliases={i: i for i in range(count)},
    )(*values, *others)
    return list(done)


def gather_column(shard):
    return lax.all_gather(shard, "tensor", axis=1, tiled=True)


def exchange_one(first, second):
    if lax.axis_size("dp") != 4:
        return [lax.all_gather(v, "dp", axis=0, tiled=True) for v in (first, second)]
    return [swap_y(first), swap_x(second)]


def exchange_two(first, second, near_first, near_second):
    if lax.axis_size("dp") != 4:
        return []
    return [swap_x(first), swap_x(near_first), swap_y(second), swap_y(near_second)]


def arrived(first, second, near, far):
    if lax.axis_size("dp") != 4:
        return ([near[0]], [near[1]])
    return ([first, near[0], far[0], far[1]], [second, near[1], far[2], far[3]])


def row_cuts(depth):
    half = depth // 2
    if lax.axis_size("dp") != 4:
        return [(0, half), (half, depth), None, None]
    part = half // 2
    return [(part, half), (half + part, depth), (0, part), (half, half + part)]


def add(left, right):
    return left.astype(jnp.float32) + right.astype(jnp.float32)


def scatter_one(send_first, send_second):
    if lax.axis_size("dp") != 4:
        return [
            lax.psum_scatter(v, "dp", scatter_dimension=0, tiled=True)
            for v in (send_first, send_second)
        ]
    return [swap_x(send_first), swap_y(send_second)]


def scatter_two(keep_first, keep_second, got):
    if lax.axis_size("dp") != 4:
        return (got, [])
    stay, come = [], []
    for keep, new, far in zip((keep_first, keep_second), got, (swap_y, swap_x)):
        half = keep.shape[0] // 2
        come.append(far(add(keep[half:], new[half:]).astype(jnp.bfloat16)))
        stay.append(add(keep[:half], new[:half]).astype(jnp.bfloat16))
    return (stay, come)


def scatter_column(stay, come):
    if come:
        stay = [add(s, c).astype(jnp.bfloat16) for s, c in zip(stay, come)]
    return lax.psum_scatter(
        jnp.concatenate(stay, 0), "tensor", scatter_dimension=1, tiled=True
    )


def flip_axis(value, axis, bit):
    return jnp.where(bit == 1, jnp.flip(value, axis), value)


def relative(value, spot):
    n_dp = lax.axis_size("dp")
    lead = value.shape[:-1]
    k = len(lead)
    if n_dp != 4:
        cut = value.reshape(lead + (n_dp, 2, -1))
        return jnp.swapaxes(cut, k, k + 1).reshape(value.shape)
    cut = value.reshape(lead + (2, 2, 2, -1))
    cut = flip_axis(flip_axis(cut, k, spot // 2), k + 1, spot % 2)
    first = jnp.swapaxes(cut[..., 0, :], k, k + 1)
    second = cut[..., 1, :]
    return jnp.concatenate([first.reshape(lead + (-1,)), second.reshape(lead + (-1,))], -1)


def absolute(value, spot):
    n_dp = lax.axis_size("dp")
    lead = value.shape[:-1]
    k = len(lead)
    if n_dp != 4:
        cut = value.reshape(lead + (2, n_dp, -1))
        return jnp.swapaxes(cut, k, k + 1).reshape(value.shape)
    cut = value.reshape(lead + (2, 2, 2, -1))
    first = jnp.swapaxes(cut[..., 0, :, :, :], k, k + 1)
    second = cut[..., 1, :, :, :]
    cut = jnp.stack([first, second], k + 2)
    cut = flip_axis(flip_axis(cut, k, spot // 2), k + 1, spot % 2)
    return cut.reshape(value.shape)


def by_chip(blocks, spot):
    n_dp = lax.axis_size("dp")
    if n_dp != 4:
        return blocks
    cut = blocks.reshape((2, 2) + blocks.shape[1:])
    cut = jnp.swapaxes(cut, 0, 1)
    cut = flip_axis(flip_axis(cut, 0, spot // 2), 1, spot % 2)
    return cut.reshape(blocks.shape)


def by_arrival(blocks, spot):
    n_dp = lax.axis_size("dp")
    if n_dp != 4:
        return blocks
    cut = blocks.reshape((2, 2) + blocks.shape[1:])
    cut = flip_axis(flip_axis(cut, 0, spot // 2), 1, spot % 2)
    return jnp.swapaxes(cut, 0, 1).reshape(blocks.shape)


VMEM_BYTES = 50 * 2**20
BF = jnp.bfloat16
F32 = jnp.float32


def shape(dims, kind=jnp.bfloat16):
    return jax.ShapeDtypeStruct(dims, kind)


def run(kernel, outs, ins):
    block = pl.BlockSpec(memory_space=pltpu.VMEM)
    done = pl.pallas_call(
        kernel,
        out_shape=list(outs),
        in_specs=[block] * len(ins),
        out_specs=[block] * len(outs),
        cost_estimate=pl.CostEstimate(flops=1, bytes_accessed=1, transcendentals=0),
        compiler_params=pltpu.CompilerParams(vmem_limit_bytes=VMEM_BYTES),
    )(*ins)
    return list(done)


def nn(left, right):
    return lax.dot_general(left, right, (((1,), (0,)), ((), ())), preferred_element_type=F32)


def nt(left, right):
    return lax.dot_general(left, right, (((1,), (1,)), ((), ())), preferred_element_type=F32)


def tn(left, right):
    return lax.dot_general(left, right, (((0,), (0,)), ((), ())), preferred_element_type=F32)


def stack_rows(pieces, counts, cols):
    return jnp.concatenate([p[:n, cols] for p, n in zip(pieces, counts)], 0)


def center_scale(value):
    center = jnp.mean(value, -1, keepdims=True)
    spread = jnp.mean(value * value, -1, keepdims=True) - center * center
    factor = lax.rsqrt(spread + EPS)
    return ((value - center) * factor, factor)


def norm_backward(grad_normed, centred, factor, gain):
    scaled = grad_normed * gain
    return factor * (
        scaled
        - jnp.mean(scaled, -1, keepdims=True)
        - centred * jnp.mean(scaled * centred, -1, keepdims=True)
    )


def column_sum(value):
    return jnp.sum(value, 0, keepdims=True)


def attention_forward(tokens, terms, bias_row, low, weights, rows, q_bias, v_bias):
    pieces, counts = weights
    size, depth = terms[0].shape
    wide = pieces[0].shape[1]
    groups = wide // 512
    half = groups * 128
    n_terms, n_pieces = len(terms), len(pieces)

    def kernel(*refs):
        term_refs, refs = refs[:n_terms], refs[n_terms:]
        bias_ref, rows_ref, qb_ref, vb_ref = refs[:4]
        piece_refs, refs = refs[4 : 4 + n_pieces], refs[4 + n_pieces :]
        u_ref, n_ref, q_ref, k_ref, v_ref, p_ref, o_ref, part_ref = refs
        value = term_refs[0][...].astype(F32)
        for ref in term_refs[1:]:
            value = value + ref[...].astype(F32)
        if n_terms > 1:
            value = value + bias_ref[...]
        if low:
            value = value.astype(BF).astype(F32)
        u_ref[...] = value
        centred, factor = center_scale(value)
        n_ref[...] = (centred * rows_ref[0:1] + rows_ref[1:2]).astype(BF)
        lane = lax.broadcasted_iota(jnp.int32, (size, 128), 1)
        key_lane = lax.broadcasted_iota(jnp.int32, (size, size), 1)
        normed = n_ref[...]
        for g in range(groups):
            at = slice(g * 128, (g + 1) * 128)
            matrix = stack_rows(piece_refs, counts, slice(g * 512, g * 512 + 384))
            projected = nn(normed, matrix)
            q = (projected[:, :128] + qb_ref[:, at]).astype(BF)
            k = projected[:, 128:256].astype(BF)
            v = (projected[:, 256:384] + vb_ref[:, at]).astype(BF)
            q_ref[:, at] = q
            k_ref[:, at] = k
            v_ref[:, at] = v
            mixed = None
            for h in range(2):
                mine = (lane // HD) == h
                scores = nt(jnp.where(mine, q, jnp.zeros_like(q)), k) * HD ** (-0.5)
                scores = jnp.where(key_lane < tokens, scores, -1e30)
                highest = jnp.max(scores, -1, keepdims=True)
                exponent = jnp.exp(scores - highest)
                inverse = 1.0 / jnp.sum(exponent, -1, keepdims=True)
                soft = (exponent * inverse).astype(BF)
                p_ref[2 * g + h] = soft
                out = nn(soft, v)
                mixed = out if h == 0 else jnp.where(mine, out, mixed)
            o_ref[:, at] = mixed.astype(BF)
        matrix = jnp.concatenate(
            [stack_rows(piece_refs, counts, slice(g * 512 + 384, g * 512 + 512)) for g in range(groups)], 1
        )
        part_ref[...] = nt(o_ref[...], matrix).astype(BF)

    outs = [shape((size, depth), F32), shape((size, depth))] + [shape((size, half))] * 3
    outs += [shape((2 * groups, size, size)), shape((size, half)), shape((size, depth))]
    return run(kernel, outs, [*terms, bias_row, rows, q_bias, v_bias, *pieces])


def up_forward(terms, weights, rows, up_bias):
    pieces, counts = weights
    size, depth = terms[0].shape
    wide = pieces[0].shape[1]

    def kernel(*refs):
        u_ref, own_ref, far_ref, rows_ref, bias_ref = refs[:5]
        piece_refs = refs[5 : 5 + len(pieces)]
        mid_ref, n_ref, slope_ref, hidden_ref = refs[5 + len(pieces) :]
        value = u_ref[...] + own_ref[...].astype(F32) + far_ref[...].astype(F32) + rows_ref[4:5]
        mid_ref[...] = value
        centred, factor = center_scale(value)
        n_ref[...] = (centred * rows_ref[5:6] + rows_ref[6:7]).astype(BF)
        step = 512
        for at in range(0, wide, step):
            cols = slice(at, at + step)
            before = nn(n_ref[...], stack_rows(piece_refs, counts, cols)) + bias_ref[:, cols]
            cdf = 0.5 * (1.0 + lax.erf(before * 0.7071067811865476))
            density = jnp.exp(-0.5 * before * before) * 0.3989422804014327
            hidden_ref[:, cols] = (before * cdf).astype(BF)
            slope_ref[:, cols] = (cdf + before * density).astype(BF)

    outs = [shape((size, depth), F32), shape((size, depth)), shape((size, wide)), shape((size, wide))]
    return run(kernel, outs, [*terms, rows, up_bias, *pieces])


def contract_wide(left, weights):
    pieces, counts = weights
    size, wide = left.shape
    depth = sum(counts)

    def kernel(*refs):
        left_ref, piece_refs, out_ref = refs[0], refs[1:-1], refs[-1]
        matrix = stack_rows(piece_refs, counts, slice(0, wide))
        out_ref[...] = nt(left_ref[...], matrix).astype(BF)

    return run(kernel, [shape((size, depth))], [left, *pieces])[0]


def weight_outs(depth, wide):
    cuts = [c for c in row_cuts(depth) if c is not None]
    return cuts, [shape((c[1] - c[0], wide)) for c in cuts]


def fill(grads):
    return (list(grads) + [None, None])[:4]


def down_backward(grad_out, hidden, slope, weights):
    pieces, counts = weights
    size, depth = grad_out.shape
    wide = hidden.shape[1]
    cuts, grad_outs = weight_outs(depth, wide)

    def kernel(*refs):
        g_ref, hidden_ref, slope_ref = refs[:3]
        piece_refs, refs = refs[3 : 3 + len(pieces)], refs[3 + len(pieces) :]
        low_ref, sum_ref, bias_ref = refs[:3]
        sum_ref[...] = column_sum(g_ref[...])
        branch = g_ref[...].astype(BF)
        for cut, ref in zip(cuts, refs[3:]):
            ref[...] = tn(branch[:, cut[0] : cut[1]], hidden_ref[...]).astype(BF)
        step = 512
        for at in range(0, wide, step):
            cols = slice(at, at + step)
            back = nn(branch, stack_rows(piece_refs, counts, cols)) * slope_ref[:, cols].astype(F32)
            bias_ref[:, cols] = column_sum(back)
            low_ref[:, cols] = back.astype(BF)

    outs = [shape((size, wide)), shape((1, depth), F32), shape((1, wide), F32)] + grad_outs
    done = run(kernel, outs, [grad_out, hidden, slope, *pieces])
    return done[0], done[1], done[2], fill(done[3:])


def up_grad(normed, low):
    size, depth = normed.shape
    wide = low.shape[1]
    cuts, outs = weight_outs(depth, wide)

    def kernel(n_ref, low_ref, *refs):
        for cut, ref in zip(cuts, refs):
            ref[...] = tn(n_ref[:, cut[0] : cut[1]], low_ref[...]).astype(BF)

    return fill(run(kernel, outs, [normed, low]))


def attention_backward(grad_out, own, far, middle, rows, saved, weights):
    pieces, counts = weights
    size, depth = grad_out.shape
    wide = pieces[0].shape[1]
    groups = wide // 512
    half = groups * 128
    scale = HD ** (-0.5)

    def kernel(*refs):
        g_ref, own_ref, far_ref, mid_ref, rows_ref, q_ref, k_ref, v_ref, p_ref, o_ref = refs[:10]
        piece_refs, refs = refs[10 : 10 + len(pieces)], refs[10 + len(pieces) :]
        dmid_ref, dz_ref, dq_ref, dk_ref, dv_ref, part_ref, sum_ref, qs_ref, vs_ref = refs
        grad_normed = own_ref[...].astype(F32) + far_ref[...].astype(F32)
        centred, factor = center_scale(mid_ref[...])
        sum_ref[1:2] = column_sum(grad_normed * centred)
        sum_ref[2:3] = column_sum(grad_normed)
        dmid = g_ref[...] + norm_backward(grad_normed, centred, factor, rows_ref[5:6])
        dmid_ref[...] = dmid
        sum_ref[0:1] = column_sum(dmid)
        dz_ref[...] = dmid.astype(BF)
        lane = lax.broadcasted_iota(jnp.int32, (size, 128), 1)
        for g in range(groups):
            at = slice(g * 128, (g + 1) * 128)
            matrix = stack_rows(piece_refs, counts, slice(g * 512 + 384, g * 512 + 512))
            grad_mixed = nn(dz_ref[...], matrix).astype(BF)
            q, k, v = q_ref[:, at], k_ref[:, at], v_ref[:, at]
            inner = grad_mixed.astype(F32) * o_ref[:, at].astype(F32)
            dq, dk, dv = None, None, None
            for h in range(2):
                mine = (lane // HD) == h
                soft = p_ref[2 * g + h]
                none = jnp.zeros_like(q)
                do = jnp.where(mine, grad_mixed, none)
                total = jnp.sum(jnp.where(mine, inner, 0.0), -1, keepdims=True)
                grad_soft = nt(do, v)
                grad_scores = (soft.astype(F32) * (grad_soft - total)).astype(BF)
                new_q = nn(grad_scores, k)
                new_k = tn(jnp.where(mine, q, none), grad_scores)
                new_v = tn(do, soft)
                dq = new_q if h == 0 else jnp.where(mine, new_q, dq)
                dk = new_k if h == 0 else dk + new_k
                dv = new_v if h == 0 else dv + new_v
            dq, dk, dv = dq * scale, dk.T * scale, dv.T
            qs_ref[:, at] = column_sum(dq)
            vs_ref[:, at] = column_sum(dv)
            dq_ref[:, at] = dq.astype(BF)
            dk_ref[:, at] = dk.astype(BF)
            dv_ref[:, at] = dv.astype(BF)
        total = None
        for g in range(groups):
            at = slice(g * 128, (g + 1) * 128)
            left = jnp.concatenate([dq_ref[:, at], dk_ref[:, at], dv_ref[:, at]], 1)
            new = nt(left, stack_rows(piece_refs, counts, slice(g * 512, g * 512 + 384)))
            total = new if g == 0 else total + new
        part_ref[...] = total.astype(BF)

    outs = [shape((size, depth), F32), shape((size, depth))] + [shape((size, half))] * 3
    outs += [shape((size, depth)), shape((3, depth), F32)] + [shape((1, half), F32)] * 2
    return run(kernel, outs, [grad_out, own, far, middle, rows, *saved, *pieces])


def attention_grad(normed, dz, dq, dk, dv, mixed):
    size, depth = normed.shape
    groups = dq.shape[1] // 128
    cuts, outs = weight_outs(depth, groups * 512)

    def kernel(n_ref, dz_ref, dq_ref, dk_ref, dv_ref, o_ref, *refs):
        for cut, ref in zip(cuts, refs):
            rows = slice(cut[0], cut[1])
            for g in range(groups):
                at = slice(g * 128, (g + 1) * 128)
                right = jnp.concatenate([dq_ref[:, at], dk_ref[:, at], dv_ref[:, at]], 1)
                ref[:, g * 512 : g * 512 + 384] = tn(n_ref[:, rows], right).astype(BF)
                ref[:, g * 512 + 384 : g * 512 + 512] = tn(dz_ref[:, rows], o_ref[:, at]).astype(BF)

    return fill(run(kernel, outs, [normed, dz, dq, dk, dv, mixed]))


def value_backward(dmid, own, far, value, rows, low):
    size, depth = dmid.shape

    def kernel(dmid_ref, own_ref, far_ref, u_ref, rows_ref, out_ref, sum_ref):
        grad_normed = own_ref[...].astype(F32) + far_ref[...].astype(F32)
        centred, factor = center_scale(u_ref[...])
        sum_ref[0:1] = column_sum(grad_normed * centred)
        sum_ref[1:2] = column_sum(grad_normed)
        out = dmid_ref[...] + norm_backward(grad_normed, centred, factor, rows_ref[0:1])
        if low:
            out = out.astype(BF).astype(F32)
        out_ref[...] = out

    outs = [shape((size, depth), F32), shape((2, depth), F32)]
    return run(kernel, outs, [dmid, own, far, value, rows])


def block_lanes(spot, chunk):
    ry, rx = chunk // 2 ^ spot // 2, chunk % 2 ^ spot % 2
    return [(rx * 2 + ry) * 128, 512 + (ry * 2 + rx) * 128]


def place_in(lanes, blocks):
    size, width = blocks[0].shape
    half = width // 2

    def kernel(lanes_ref, *refs):
        out_ref = refs[-1]
        for d, ref in enumerate(refs[:-1]):
            for h in range(2):
                at = pl.multiple_of(lanes_ref[2 * d + h], 128)
                out_ref[:, pl.ds(at, half)] = ref[:, h * half : (h + 1) * half]

    block = pl.BlockSpec(memory_space=pltpu.VMEM)
    return pl.pallas_call(
        kernel,
        out_shape=shape((size, width * len(blocks))),
        in_specs=[pl.BlockSpec(memory_space=pltpu.SMEM)] + [block] * len(blocks),
        out_specs=block,
        compiler_params=pltpu.CompilerParams(vmem_limit_bytes=VMEM_BYTES),
    )(lanes, *blocks)


def place_out(numbers, scale, terms, bias_row, count):
    size, depth = terms[0].shape
    width = depth // count
    half = width // 2

    def kernel(numbers_ref, scale_ref, *refs):
        term_refs, bias_ref, out_ref = refs[: len(terms)], refs[-2], refs[-1]
        start = pl.multiple_of(numbers_ref[2 * count], 8)
        rows = pl.ds(start, size // 2)
        for d in range(count):
            for h in range(2):
                lanes = pl.ds(pl.multiple_of(numbers_ref[2 * d + h], 128), half)
                value = term_refs[0][rows, lanes]
                for ref in term_refs[1:]:
                    value = value + ref[rows, lanes]
                value = (value + bias_ref[:, lanes]) * scale_ref[0]
                out_ref[d, :, h * half : (h + 1) * half] = value.astype(BF)

    block = pl.BlockSpec(memory_space=pltpu.VMEM)
    scalar = pl.BlockSpec(memory_space=pltpu.SMEM)
    return pl.pallas_call(
        kernel,
        out_shape=shape((count, size // 2, width)),
        in_specs=[scalar, scalar] + [block] * (len(terms) + 1),
        out_specs=block,
        compiler_params=pltpu.CompilerParams(vmem_limit_bytes=VMEM_BYTES),
    )(numbers, scale, *terms, bias_row)


def shifts(blocks):
    n = lax.axis_size("tensor")
    out = [blocks[0]]
    for d in range(1, n):
        out.append(lax.ppermute(blocks[d], "tensor", [(i, (i + d) % n) for i in range(n)]))
    return out


def half_cols(core, whole, n_tensor):
    cut = whole.reshape(whole.shape[:-1] + (n_tensor, 2, -1))
    cut = jnp.where(core == 0, cut[..., 0, :], cut[..., 1, :])
    return cut.reshape(whole.shape[:-1] + (-1,))


def spread_cols(core, half, n_tensor):
    cut = half.reshape(half.shape[:-1] + (n_tensor, 1, -1))
    none = jnp.zeros_like(cut)
    both = jnp.concatenate(
        [jnp.where(core == 0, cut, none), jnp.where(core == 0, none, cut)], -2
    )
    return both.reshape(half.shape[:-1] + (-1,))


def body(boundary_in, counts, qkv_weight, proj_weight, fc1_weight, fc2_weight, vectors, fc1_bias):
    core = lax.axis_index("section")
    is_first = core == 0
    place = lax.axis_index("tensor")
    spot = lax.axis_index("dp")
    n_dp, n_tensor = lax.axis_size("dp"), lax.axis_size("tensor")
    slots_per_batch = boundary_in.shape[1] // counts.shape[1]
    live = (place % slots_per_batch < counts[0, place // slots_per_batch]).astype(jnp.float32)
    depth = qkv_weight.shape[1]
    mid = depth // 2
    n_vec = vectors.size

    small_size = n_vec + fc1_bias.size
    packs = []
    for part in range(2):
        cuts = [
            jnp.split(qkv_weight[0], 2, 2)[part].reshape(depth, -1),
            jnp.split(proj_weight[0], 2, 0)[part].T,
            jnp.split(fc1_weight[0], 2, 1)[part],
            jnp.split(fc2_weight[0], 2, 0)[part].T,
        ]
        packs.append(jnp.concatenate(cuts, 1))
    wide = packs[0].shape[1] // 3
    extra = 16
    small = jnp.concatenate([vectors.reshape(-1), fc1_bias.reshape(-1)])
    small = jnp.pad(small, (0, extra * wide - small_size)).reshape(extra, wide)
    small = jnp.pad(small, ((0, 0), (0, 2 * wide)))
    kept = jnp.concatenate([jnp.where(is_first, packs[0], packs[1]), small], 0)
    received = swap(
        jnp.concatenate([jnp.where(is_first, packs[1], packs[0]), small], 0)
    )
    shards = (jnp.where(is_first, kept, received), jnp.where(is_first, received, kept))
    columns = []
    for layer in range(2):
        for number in range(3):
            cols = shards[layer][:, number * wide : (number + 1) * wide]
            if number == 0:
                cols = jnp.concatenate([cols[:mid], cols[depth:], cols[mid:depth]], 0)
            else:
                cols = cols[:depth]
            columns.append(cols)

    tokens = boundary_in.shape[2]
    pad = -tokens % 16
    reach = (tokens + pad) // 2
    ends_in = jnp.pad(boundary_in[0].astype(jnp.bfloat16), ((0, 0), (0, pad), (0, 0)))
    ends_low, ends_high = ends_in[:, :reach], ends_in[:, reach:]
    ends_got = swap(jnp.where(is_first, ends_high, ends_low))
    half_in = jnp.where(is_first, ends_low, ends_got)
    half_cot = jnp.where(is_first, ends_got, ends_high)

    below = [(place - d) % n_tensor for d in range(n_tensor)]
    above = [(place + d) % n_tensor for d in range(n_tensor)]

    def to_send(half):
        return [lax.dynamic_index_in_dim(half, j, 0, False) for j in above]

    def image_half(blocks):
        if n_dp == 4:
            lanes = [lane for t in below for lane in block_lanes(spot, t)]
            return place_in(jnp.stack(lanes).astype(jnp.int32), blocks)
        blocks = jnp.stack(blocks)
        blocks = [lax.dynamic_index_in_dim(blocks, (place - i) % n_tensor, 0, False) for i in range(n_tensor)]
        return relative(jnp.concatenate(blocks, 1), spot)

    def whole_image(half):
        other = swap(half)
        both = [jnp.where(is_first, half, other), jnp.where(is_first, other, half)]
        return jnp.concatenate(both, 0)

    def image_rows(scale, terms, bias_row):
        if n_dp == 4:
            numbers = [lane for t in above for lane in block_lanes(spot, t)]
            numbers.append(jnp.where(is_first, 0, reach))
            numbers = jnp.stack(numbers).astype(jnp.int32)
            blocks = place_out(numbers, scale.reshape(1), terms, bias_row, n_tensor)
            return [blocks[d] for d in range(n_tensor)]
        image = absolute((sum(terms[1:], terms[0]) + bias_row) * scale, spot).astype(jnp.bfloat16)
        half = jnp.where(is_first, image[:reach], image[reach:])
        half = half.reshape(reach, n_tensor, -1).transpose(1, 0, 2)
        return to_send(half)

    def by_image(blocks):
        blocks = jnp.stack(blocks)
        blocks = [lax.dynamic_index_in_dim(blocks, (place - i) % n_tensor, 0, False) for i in range(n_tensor)]
        return jnp.stack(blocks)

    def small_of(piece):
        extras = jnp.concatenate(piece, 0)
        one = by_chip(extras.reshape(n_dp, extra, -1), spot).astype(jnp.float32)
        one = one.reshape(n_dp, extra, n_tensor, wide).transpose(0, 2, 1, 3)
        one = one.reshape(n_dp, n_tensor, -1)
        rows = one[:, :, :n_vec].reshape(n_dp, n_tensor, 8, -1)
        rows = rows.transpose(2, 1, 0, 3).reshape(8, -1)
        bias = one[:, :, n_vec:small_size].transpose(1, 0, 2).reshape(-1)
        q_bias = half_cols(core, rows[2], n_tensor)
        v_bias = half_cols(core, rows[3], n_tensor)
        up_bias = half_cols(core, bias, n_tensor)
        return (relative(rows, spot), q_bias[None], v_bias[None], up_bias[None])

    number = len(columns)
    cut = [mid + extra if k % 3 == 0 else mid for k in range(number)]
    halves, near, far = [None] * number, [None] * number, [None] * number
    params = [dict(), dict()]
    blocks_in, blocks_cot = to_send(half_in), to_send(half_cot)
    pair, state = None, None
    for r in range(number + 2):
        tied = []
        if r < number:
            tied.append(gather_column(columns[r]))
        if 0 <= r - 1 < number:
            near[r - 1] = exchange_one(*halves[r - 1])
            far[r - 1] = exchange_two(*halves[r - 1], *near[r - 1])
            tied += near[r - 1] + far[r - 1]
        if r == 1:
            blocks_in = shifts(blocks_in)
        if r == number:
            blocks_cot = shifts(blocks_cot)
        ready = []
        k = r - 2
        if k >= 0:
            layer, kind = k // 3, k % 3
            one = params[layer]
            first, second = arrived(*halves[k], near[k], far[k])
            if kind == 0:
                blocks = [p.reshape((-1, mid + extra) + p.shape[1:]) for p in first]
                one["small"] = small_of([p[:, mid:].reshape(-1, p.shape[-1]) for p in blocks])
                if n_dp != 4:
                    first = [p[:, :mid].reshape(-1, p.shape[-1]) for p in blocks]
            pieces = first + second
            counts = [mid if n_dp == 4 else p.shape[0] for p in pieces]
            weights = (pieces, counts)
            rows, q_bias, v_bias, up_bias = one["small"]
            if pair is not None:
                pair = [pair[0], swap(pair[0])]
            if kind == 0:
                one["qkvo"] = weights
                if layer == 0:
                    terms = [whole_image(image_half(blocks_in)).astype(jnp.float32)]
                else:
                    terms = [state, *pair]
                bias_row = params[0]["small"][0][7:8]
                done = attention_forward(
                    tokens, terms, bias_row, layer == 1, weights, rows, q_bias, v_bias
                )
                one["u"], one["n1"], one["saved"], part = done[0], done[1], done[2:7], done[7]
                pair, ready = [part], [part]
            elif kind == 1:
                one["up"] = weights
                one["mid"], one["n2"], one["slope"], one["hidden"] = up_forward(
                    [one["u"], *pair], weights, rows, up_bias
                )
                pair, ready = None, [one["hidden"]]
            else:
                one["down"] = weights
                state = one["mid"]
                part = contract_wide(one["hidden"], weights)
                pair, ready = [part], [part]
        if r <= number:
            count = len(ready)
            extras = list(ready)
            if r <= 1:
                extras += blocks_in
            if r == number - 1:
                extras += blocks_cot
            if r + 1 < number:
                extras.append(columns[r + 1])
            done = tie(tied + extras, [])
            if r + 1 < number:
                columns[r + 1] = done.pop()
            if r <= 1:
                done, blocks_in = done[:-n_tensor], done[-n_tensor:]
            if r == number - 1:
                done, blocks_cot = done[:-n_tensor], done[-n_tensor:]
            if count and kind == 1:
                one["hidden"] = done[-1]
            elif count:
                pair = [done[-1]]
            at = 0
            if r < number:
                halves[r] = (done[0][: cut[r]], done[0][cut[r] :])
                at = 1
            if 0 <= r - 1 < number:
                near[r - 1] = done[at : at + 2]
                far[r - 1] = done[at + 2 : at + 2 + len(far[r - 1])]
    cotangent = whole_image(image_half(blocks_cot)).astype(jnp.float32) * live
    pair = [pair[0], swap(pair[0])]
    last_rows = params[1]["small"][0]
    out_blocks = image_rows(live, [state, *pair], last_rows[7:8])

    grads, got, moved, settled = [None] * number, [None] * number, [None] * number, [None] * number
    made = [0, 1, 3, 4, 5, 7]
    sums = [dict(), dict()]
    grad = cotangent
    for r in range(8):
        layer, stage = 1 - r // 4, r % 4
        one, total = params[layer], sums[layer]
        rows = one["small"][0]
        tied, slots = [], []
        for c in range(number):
            if r == made[c] + 1:
                got[c] = scatter_one(*grads[c][:2])
                slots.append((got, c, len(got[c])))
                tied += got[c]
            elif r == made[c] + 2:
                stay, come = scatter_two(*grads[c][2:], got[c])
                moved[c] = [*stay, *come]
                slots.append((moved, c, len(moved[c])))
                tied += moved[c]
            elif r == made[c] + 3:
                settled[c] = scatter_column(moved[c][:2], moved[c][2:])
                slots.append((settled, c, 0))
                tied.append(settled[c])
        new = None
        if stage == 0:
            low, total["out"], total["up_bias"], new = down_backward(
                grad, one["hidden"], one["slope"], one["down"]
            )
            carry = [low]
        elif stage == 1:
            part = contract_wide(low, one["up"])
            new = up_grad(one["n2"], low)
            carry = [part]
        elif stage == 2:
            done = attention_backward(
                grad, part, swap(part), one["mid"], rows, one["saved"], one["qkvo"]
            )
            dmid, dz, dq, dk, dv, part, total["mid"], total["q"], total["v"] = done
            carry = [part, dz]
        else:
            far_part = swap(part)
            new = attention_grad(one["n1"], dz, dq, dk, dv, one["saved"][4])
            grad, total["one"] = value_backward(dmid, part, far_part, one["u"], rows, layer == 1)
            carry = [grad]
        if new is not None:
            c = made.index(r)
            grads[c] = new
            fresh = [g for g in new if g is not None]
        else:
            fresh = []
        if r == 1:
            out_blocks = shifts(out_blocks)
            carry += out_blocks
        if r < 7:
            done = tie(carry + fresh + tied, [])
            if stage == 0:
                low = done[0]
            elif stage == 1:
                part = done[0]
            elif stage == 2:
                part, dz = done[:2]
            else:
                grad = done[0]
            if r == 1:
                out_blocks = done[1 : 1 + n_tensor]
            done = done[len(carry) :]
            if fresh:
                grads[c] = fill(done[: len(fresh)])
                done = done[len(fresh) :]
            for store, at, count in slots:
                store[at] = done[:count] if count else done[0]
                done = done[max(count, 1) :]

    one_scale = jnp.ones((), jnp.float32)
    grad_blocks = shifts(image_rows(one_scale, [grad], jnp.zeros((1, grad.shape[1]), jnp.float32)))
    grad_rows, out_rows = by_image(grad_blocks), by_image(out_blocks)
    packed = []
    for layer in range(2):
        total = sums[layer]
        full = jnp.concatenate([total["one"], total["mid"], total["out"]], 0)
        full = absolute(jnp.where(core == layer, full, 0.0), spot)
        q_row = spread_cols(core, total["q"][0], n_tensor)
        v_row = spread_cols(core, total["v"][0], n_tensor)
        up_row = spread_cols(core, total["up_bias"][0], n_tensor)
        rows = jnp.concatenate([full[:2], q_row[None], v_row[None], full[2:]], 0)
        rows = rows.reshape(8, n_tensor, n_dp, -1).transpose(2, 1, 0, 3).reshape(n_dp, n_tensor, -1)
        up_row = up_row.reshape(n_tensor, n_dp, -1).transpose(1, 0, 2)
        packed.append(jnp.concatenate([rows, up_row], -1))
    ours = jnp.where(is_first, packed[0], packed[1])
    other = swap(jnp.where(is_first, packed[1], packed[0]))
    little = (ours + other).astype(jnp.bfloat16)
    room = jnp.zeros((n_dp, n_tensor, extra * wide - small_size), little.dtype)
    little = jnp.concatenate([little, room], -1).reshape(n_dp, n_tensor, extra, wide)
    little = by_arrival(little.transpose(0, 2, 1, 3).reshape(n_dp, extra, -1), spot)
    if n_dp != 4:
        little = lax.psum_scatter(little, "dp", scatter_dimension=0, tiled=True)[0]
    else:
        little = add(little[:2], swap_x(little[2:])).astype(jnp.bfloat16)
        little = add(little[0], swap_y(little[1])).astype(jnp.bfloat16)

    last = number - 1
    got[last] = scatter_one(*grads[last][:2])
    settled[last - 1] = scatter_column(moved[last - 1][:2], moved[last - 1][2:])
    stay, come = scatter_two(*grads[last][2:], got[last])
    if come:
        stay = [add(s, c).astype(jnp.bfloat16) for s, c in zip(stay, come)]
    settled[last] = scatter_column([*stay, little], [])
    little = settled[last][depth:].reshape(-1).astype(jnp.float32)
    settled[last] = settled[last][:depth]
    grad_vectors = little[:n_vec].reshape(vectors.shape)
    grad_bias = little[n_vec:small_size].reshape(fc1_bias.shape)

    own = jnp.where(is_first, grad_rows, out_rows)
    other = swap(jnp.where(is_first, out_rows, grad_rows))
    ends = [jnp.where(is_first, own, other), jnp.where(is_first, other, own)]
    boundary_out = jnp.concatenate(ends, 1)[:, :tokens].astype(jnp.float32)[None]
    lows, highs = [], []
    for kind in range(3):
        first, second = settled[last - kind], settled[last - kind - 3]
        kept = jnp.where(is_first, first, second)
        received = swap(jnp.where(is_first, second, first))
        lows.append(jnp.where(is_first, kept, received).astype(jnp.float32))
        highs.append(jnp.where(is_first, received, kept).astype(jnp.float32))
    low, high = [part[0].reshape(depth, 4, -1) for part in (lows, highs)]
    grad_qkv = jnp.concatenate([low[:, :3], high[:, :3]], 2)[None]
    grad_proj = jnp.concatenate([low[:, 3].T, high[:, 3].T], 0)[None]
    grad_up = jnp.concatenate([lows[1], highs[1]], 1)[None]
    grad_down = jnp.concatenate([lows[2].T, highs[2].T], 0)[None]
    return (boundary_out, grad_qkv, grad_proj, grad_up, grad_down, grad_vectors, grad_bias)


def solution(mesh):
    in_specs = (
        P("section", "dp", None, "tensor"),
        P("dp", None),
        P("section", "dp", None, "tensor"),
        P("section", "tensor", "dp"),
        P("section", "dp", "tensor"),
        P("section", "tensor", "dp"),
        P("section", None, "tensor", "dp"),
        P("section", "tensor", "dp"),
    )
    out_specs = (
        P("section", "dp", None, "tensor"),
        P("section", "dp", None, "tensor"),
        P("section", "tensor", "dp"),
        P("section", "dp", "tensor"),
        P("section", "tensor", "dp"),
        P("section", None, "tensor", "dp"),
        P("section", "tensor", "dp"),
    )
    return jax.shard_map(body, mesh=mesh, in_specs=in_specs, out_specs=out_specs, check_vma=False)
```

```python
import jax
import jax.numpy as jnp
from jax import lax
from jax.experimental import pallas as pl
from jax.experimental.pallas import tpu as pltpu
from jax.sharding import PartitionSpec as P

HD = 64
EPS = 1e-06


def swap(value):
    return lax.ppermute(value, "section", [(0, 1), (1, 0)])


def pair_sum(partial):
    low = partial.astype(jnp.bfloat16)
    return low.astype(jnp.float32) + swap(low).astype(jnp.float32)


def swap_x(value):
    n = lax.axis_size("dp")
    return lax.ppermute(value, "dp", [(i, i ^ 1) for i in range(n)])


def swap_y(value):
    n = lax.axis_size("dp")
    return lax.ppermute(value, "dp", [(i, i ^ 2) for i in range(n)])


def tie(values, others):
    count = len(values)

    def kernel(*refs):
        pass

    anywhere = pl.BlockSpec(memory_space=pl.ANY)
    done = pl.pallas_call(
        kernel,
        out_shape=[jax.ShapeDtypeStruct(v.shape, v.dtype) for v in values],
        in_specs=[anywhere] * (count + len(others)),
        out_specs=[anywhere] * count,
        input_output_aliases={i: i for i in range(count)},
    )(*values, *others)
    return list(done)


def gather_column(shard):
    return lax.all_gather(shard, "tensor", axis=1, tiled=True)


def exchange_one(first, second):
    if lax.axis_size("dp") != 4:
        return [lax.all_gather(v, "dp", axis=0, tiled=True) for v in (first, second)]
    return [swap_y(first), swap_x(second)]


def exchange_two(first, second, near_first, near_second):
    if lax.axis_size("dp") != 4:
        return []
    return [swap_x(first), swap_x(near_first), swap_y(second), swap_y(near_second)]


def arrived(first, second, near, far):
    if lax.axis_size("dp") != 4:
        return ([near[0]], [near[1]])
    return ([first, near[0], far[0], far[1]], [second, near[1], far[2], far[3]])


def row_cuts(depth):
    half = depth // 2
    if lax.axis_size("dp") != 4:
        return [(0, half), (half, depth), None, None]
    part = half // 2
    return [(part, half), (half + part, depth), (0, part), (half, half + part)]


def add(left, right):
    return left.astype(jnp.float32) + right.astype(jnp.float32)


def scatter_one(send_first, send_second):
    if lax.axis_size("dp") != 4:
        return [
            lax.psum_scatter(v, "dp", scatter_dimension=0, tiled=True)
            for v in (send_first, send_second)
        ]
    return [swap_x(send_first), swap_y(send_second)]


def scatter_two(keep_first, keep_second, got):
    if lax.axis_size("dp") != 4:
        return (got, [])
    stay, come = [], []
    for keep, new, far in zip((keep_first, keep_second), got, (swap_y, swap_x)):
        half = keep.shape[0] // 2
        come.append(far(add(keep[half:], new[half:]).astype(jnp.bfloat16)))
        stay.append(add(keep[:half], new[:half]).astype(jnp.bfloat16))
    return (stay, come)


def scatter_column(stay, come):
    if come:
        stay = [add(s, c).astype(jnp.bfloat16) for s, c in zip(stay, come)]
    return lax.psum_scatter(
        jnp.concatenate(stay, 0), "tensor", scatter_dimension=1, tiled=True
    )


def flip_axis(value, axis, bit):
    return jnp.where(bit == 1, jnp.flip(value, axis), value)


def relative(value, spot):
    n_dp = lax.axis_size("dp")
    lead = value.shape[:-1]
    k = len(lead)
    if n_dp != 4:
        cut = value.reshape(lead + (n_dp, 2, -1))
        return jnp.swapaxes(cut, k, k + 1).reshape(value.shape)
    cut = value.reshape(lead + (2, 2, 2, -1))
    cut = flip_axis(flip_axis(cut, k, spot // 2), k + 1, spot % 2)
    first = jnp.swapaxes(cut[..., 0, :], k, k + 1)
    second = cut[..., 1, :]
    return jnp.concatenate([first.reshape(lead + (-1,)), second.reshape(lead + (-1,))], -1)


def absolute(value, spot):
    n_dp = lax.axis_size("dp")
    lead = value.shape[:-1]
    k = len(lead)
    if n_dp != 4:
        cut = value.reshape(lead + (2, n_dp, -1))
        return jnp.swapaxes(cut, k, k + 1).reshape(value.shape)
    cut = value.reshape(lead + (2, 2, 2, -1))
    first = jnp.swapaxes(cut[..., 0, :, :, :], k, k + 1)
    second = cut[..., 1, :, :, :]
    cut = jnp.stack([first, second], k + 2)
    cut = flip_axis(flip_axis(cut, k, spot // 2), k + 1, spot % 2)
    return cut.reshape(value.shape)


def by_chip(blocks, spot):
    n_dp = lax.axis_size("dp")
    if n_dp != 4:
        return blocks
    cut = blocks.reshape((2, 2) + blocks.shape[1:])
    cut = jnp.swapaxes(cut, 0, 1)
    cut = flip_axis(flip_axis(cut, 0, spot // 2), 1, spot % 2)
    return cut.reshape(blocks.shape)


def by_arrival(blocks, spot):
    n_dp = lax.axis_size("dp")
    if n_dp != 4:
        return blocks
    cut = blocks.reshape((2, 2) + blocks.shape[1:])
    cut = flip_axis(flip_axis(cut, 0, spot // 2), 1, spot % 2)
    return jnp.swapaxes(cut, 0, 1).reshape(blocks.shape)


VMEM_BYTES = 50 * 2**20
BF = jnp.bfloat16
F32 = jnp.float32


def shape(dims, kind=jnp.bfloat16):
    return jax.ShapeDtypeStruct(dims, kind)


def run(kernel, outs, ins):
    block = pl.BlockSpec(memory_space=pltpu.VMEM)
    done = pl.pallas_call(
        kernel,
        out_shape=list(outs),
        in_specs=[block] * len(ins),
        out_specs=[block] * len(outs),
        cost_estimate=pl.CostEstimate(flops=1, bytes_accessed=1, transcendentals=0),
        compiler_params=pltpu.CompilerParams(vmem_limit_bytes=VMEM_BYTES),
    )(*ins)
    return list(done)


def nn(left, right):
    return lax.dot_general(left, right, (((1,), (0,)), ((), ())), preferred_element_type=F32)


def nt(left, right):
    return lax.dot_general(left, right, (((1,), (1,)), ((), ())), preferred_element_type=F32)


def tn(left, right):
    return lax.dot_general(left, right, (((0,), (0,)), ((), ())), preferred_element_type=F32)


def stack_rows(pieces, counts, cols):
    return jnp.concatenate([p[:n, cols] for p, n in zip(pieces, counts)], 0)


def center_scale(value):
    center = jnp.mean(value, -1, keepdims=True)
    spread = jnp.mean(value * value, -1, keepdims=True) - center * center
    factor = lax.rsqrt(spread + EPS)
    return ((value - center) * factor, factor)


def norm_backward(grad_normed, centred, factor, gain):
    scaled = grad_normed * gain
    return factor * (
        scaled
        - jnp.mean(scaled, -1, keepdims=True)
        - centred * jnp.mean(scaled * centred, -1, keepdims=True)
    )


def column_sum(value):
    return jnp.sum(value, 0, keepdims=True)


def attention_forward(tokens, terms, bias_row, low, weights, rows, q_bias, v_bias):
    pieces, counts = weights
    size, depth = terms[0].shape
    wide = pieces[0].shape[1]
    groups = wide // 512
    half = groups * 128
    n_terms, n_pieces = len(terms), len(pieces)

    def kernel(*refs):
        term_refs, refs = refs[:n_terms], refs[n_terms:]
        bias_ref, rows_ref, qb_ref, vb_ref = refs[:4]
        piece_refs, refs = refs[4 : 4 + n_pieces], refs[4 + n_pieces :]
        u_ref, n_ref, q_ref, k_ref, v_ref, p_ref, o_ref, part_ref = refs
        value = term_refs[0][...].astype(F32)
        for ref in term_refs[1:]:
            value = value + ref[...].astype(F32)
        if n_terms > 1:
            value = value + bias_ref[...]
        if low:
            value = value.astype(BF).astype(F32)
        u_ref[...] = value
        centred, factor = center_scale(value)
        n_ref[...] = (centred * rows_ref[0:1] + rows_ref[1:2]).astype(BF)
        lane = lax.broadcasted_iota(jnp.int32, (size, 128), 1)
        key_lane = lax.broadcasted_iota(jnp.int32, (size, size), 1)
        normed = n_ref[...]
        for g in range(groups):
            at = slice(g * 128, (g + 1) * 128)
            matrix = stack_rows(piece_refs, counts, slice(g * 512, g * 512 + 384))
            projected = nn(normed, matrix)
            q = (projected[:, :128] + qb_ref[:, at]).astype(BF)
            k = projected[:, 128:256].astype(BF)
            v = (projected[:, 256:384] + vb_ref[:, at]).astype(BF)
            q_ref[:, at] = q
            k_ref[:, at] = k
            v_ref[:, at] = v
            mixed = None
            for h in range(2):
                mine = (lane // HD) == h
                scores = nt(jnp.where(mine, q, jnp.zeros_like(q)), k) * HD ** (-0.5)
                scores = jnp.where(key_lane < tokens, scores, -1e30)
                highest = jnp.max(scores, -1, keepdims=True)
                exponent = jnp.exp(scores - highest)
                inverse = 1.0 / jnp.sum(exponent, -1, keepdims=True)
                soft = (exponent * inverse).astype(BF)
                p_ref[2 * g + h] = soft
                out = nn(soft, v)
                mixed = out if h == 0 else jnp.where(mine, out, mixed)
            o_ref[:, at] = mixed.astype(BF)
        matrix = jnp.concatenate(
            [stack_rows(piece_refs, counts, slice(g * 512 + 384, g * 512 + 512)) for g in range(groups)], 1
        )
        part_ref[...] = nt(o_ref[...], matrix).astype(BF)

    outs = [shape((size, depth), F32), shape((size, depth))] + [shape((size, half))] * 3
    outs += [shape((2 * groups, size, size)), shape((size, half)), shape((size, depth))]
    return run(kernel, outs, [*terms, bias_row, rows, q_bias, v_bias, *pieces])


def up_forward(terms, weights, rows, up_bias):
    pieces, counts = weights
    size, depth = terms[0].shape
    wide = pieces[0].shape[1]

    def kernel(*refs):
        u_ref, own_ref, far_ref, rows_ref, bias_ref = refs[:5]
        piece_refs = refs[5 : 5 + len(pieces)]
        mid_ref, n_ref, slope_ref, hidden_ref = refs[5 + len(pieces) :]
        value = u_ref[...] + own_ref[...].astype(F32) + far_ref[...].astype(F32) + rows_ref[4:5]
        mid_ref[...] = value
        centred, factor = center_scale(value)
        n_ref[...] = (centred * rows_ref[5:6] + rows_ref[6:7]).astype(BF)
        step = 512
        for at in range(0, wide, step):
            cols = slice(at, at + step)
            before = nn(n_ref[...], stack_rows(piece_refs, counts, cols)) + bias_ref[:, cols]
            cdf = 0.5 * (1.0 + lax.erf(before * 0.7071067811865476))
            density = jnp.exp(-0.5 * before * before) * 0.3989422804014327
            hidden_ref[:, cols] = (before * cdf).astype(BF)
            slope_ref[:, cols] = (cdf + before * density).astype(BF)

    outs = [shape((size, depth), F32), shape((size, depth)), shape((size, wide)), shape((size, wide))]
    return run(kernel, outs, [*terms, rows, up_bias, *pieces])


def contract_wide(left, weights):
    pieces, counts = weights
    size, wide = left.shape
    depth = sum(counts)

    def kernel(*refs):
        left_ref, piece_refs, out_ref = refs[0], refs[1:-1], refs[-1]
        matrix = stack_rows(piece_refs, counts, slice(0, wide))
        out_ref[...] = nt(left_ref[...], matrix).astype(BF)

    return run(kernel, [shape((size, depth))], [left, *pieces])[0]


def weight_outs(depth, wide):
    cuts = [c for c in row_cuts(depth) if c is not None]
    return cuts, [shape((c[1] - c[0], wide)) for c in cuts]


def fill(grads):
    return (list(grads) + [None, None])[:4]


def down_backward(grad_out, hidden, slope, weights):
    pieces, counts = weights
    size, depth = grad_out.shape
    wide = hidden.shape[1]
    cuts, grad_outs = weight_outs(depth, wide)

    def kernel(*refs):
        g_ref, hidden_ref, slope_ref = refs[:3]
        piece_refs, refs = refs[3 : 3 + len(pieces)], refs[3 + len(pieces) :]
        low_ref, sum_ref, bias_ref = refs[:3]
        sum_ref[...] = column_sum(g_ref[...])
        branch = g_ref[...].astype(BF)
        for cut, ref in zip(cuts, refs[3:]):
            ref[...] = tn(branch[:, cut[0] : cut[1]], hidden_ref[...]).astype(BF)
        step = 512
        for at in range(0, wide, step):
            cols = slice(at, at + step)
            back = nn(branch, stack_rows(piece_refs, counts, cols)) * slope_ref[:, cols].astype(F32)
            bias_ref[:, cols] = column_sum(back)
            low_ref[:, cols] = back.astype(BF)

    outs = [shape((size, wide)), shape((1, depth), F32), shape((1, wide), F32)] + grad_outs
    done = run(kernel, outs, [grad_out, hidden, slope, *pieces])
    return done[0], done[1], done[2], fill(done[3:])


def up_grad(normed, low):
    size, depth = normed.shape
    wide = low.shape[1]
    cuts, outs = weight_outs(depth, wide)

    def kernel(n_ref, low_ref, *refs):
        for cut, ref in zip(cuts, refs):
            ref[...] = tn(n_ref[:, cut[0] : cut[1]], low_ref[...]).astype(BF)

    return fill(run(kernel, outs, [normed, low]))


def attention_backward(grad_out, own, far, middle, rows, saved, weights):
    pieces, counts = weights
    size, depth = grad_out.shape
    wide = pieces[0].shape[1]
    groups = wide // 512
    half = groups * 128
    scale = HD ** (-0.5)

    def kernel(*refs):
        g_ref, own_ref, far_ref, mid_ref, rows_ref, q_ref, k_ref, v_ref, p_ref, o_ref = refs[:10]
        piece_refs, refs = refs[10 : 10 + len(pieces)], refs[10 + len(pieces) :]
        dmid_ref, dz_ref, dq_ref, dk_ref, dv_ref, part_ref, sum_ref, qs_ref, vs_ref = refs
        grad_normed = own_ref[...].astype(F32) + far_ref[...].astype(F32)
        centred, factor = center_scale(mid_ref[...])
        sum_ref[1:2] = column_sum(grad_normed * centred)
        sum_ref[2:3] = column_sum(grad_normed)
        dmid = g_ref[...] + norm_backward(grad_normed, centred, factor, rows_ref[5:6])
        dmid_ref[...] = dmid
        sum_ref[0:1] = column_sum(dmid)
        dz_ref[...] = dmid.astype(BF)
        lane = lax.broadcasted_iota(jnp.int32, (size, 128), 1)
        for g in range(groups):
            at = slice(g * 128, (g + 1) * 128)
            matrix = stack_rows(piece_refs, counts, slice(g * 512 + 384, g * 512 + 512))
            grad_mixed = nn(dz_ref[...], matrix).astype(BF)
            q, k, v = q_ref[:, at], k_ref[:, at], v_ref[:, at]
            inner = grad_mixed.astype(F32) * o_ref[:, at].astype(F32)
            dq, dk, dv = None, None, None
            for h in range(2):
                mine = (lane // HD) == h
                soft = p_ref[2 * g + h]
                none = jnp.zeros_like(q)
                do = jnp.where(mine, grad_mixed, none)
                total = jnp.sum(jnp.where(mine, inner, 0.0), -1, keepdims=True)
                grad_soft = nt(do, v)
                grad_scores = (soft.astype(F32) * (grad_soft - total)).astype(BF)
                new_q = nn(grad_scores, k)
                new_k = tn(jnp.where(mine, q, none), grad_scores)
                new_v = tn(do, soft)
                dq = new_q if h == 0 else jnp.where(mine, new_q, dq)
                dk = new_k if h == 0 else dk + new_k
                dv = new_v if h == 0 else dv + new_v
            dq, dk, dv = dq * scale, dk.T * scale, dv.T
            qs_ref[:, at] = column_sum(dq)
            vs_ref[:, at] = column_sum(dv)
            dq_ref[:, at] = dq.astype(BF)
            dk_ref[:, at] = dk.astype(BF)
            dv_ref[:, at] = dv.astype(BF)
        total = None
        for g in range(groups):
            at = slice(g * 128, (g + 1) * 128)
            left = jnp.concatenate([dq_ref[:, at], dk_ref[:, at], dv_ref[:, at]], 1)
            new = nt(left, stack_rows(piece_refs, counts, slice(g * 512, g * 512 + 384)))
            total = new if g == 0 else total + new
        part_ref[...] = total.astype(BF)

    outs = [shape((size, depth), F32), shape((size, depth))] + [shape((size, half))] * 3
    outs += [shape((size, depth)), shape((3, depth), F32)] + [shape((1, half), F32)] * 2
    return run(kernel, outs, [grad_out, own, far, middle, rows, *saved, *pieces])


def attention_grad(normed, dz, dq, dk, dv, mixed):
    size, depth = normed.shape
    groups = dq.shape[1] // 128
    cuts, outs = weight_outs(depth, groups * 512)

    def kernel(n_ref, dz_ref, dq_ref, dk_ref, dv_ref, o_ref, *refs):
        for cut, ref in zip(cuts, refs):
            rows = slice(cut[0], cut[1])
            for g in range(groups):
                at = slice(g * 128, (g + 1) * 128)
                right = jnp.concatenate([dq_ref[:, at], dk_ref[:, at], dv_ref[:, at]], 1)
                ref[:, g * 512 : g * 512 + 384] = tn(n_ref[:, rows], right).astype(BF)
                ref[:, g * 512 + 384 : g * 512 + 512] = tn(dz_ref[:, rows], o_ref[:, at]).astype(BF)

    return fill(run(kernel, outs, [normed, dz, dq, dk, dv, mixed]))


def value_backward(dmid, own, far, value, rows, low):
    size, depth = dmid.shape

    def kernel(dmid_ref, own_ref, far_ref, u_ref, rows_ref, out_ref, sum_ref):
        grad_normed = own_ref[...].astype(F32) + far_ref[...].astype(F32)
        centred, factor = center_scale(u_ref[...])
        sum_ref[0:1] = column_sum(grad_normed * centred)
        sum_ref[1:2] = column_sum(grad_normed)
        out = dmid_ref[...] + norm_backward(grad_normed, centred, factor, rows_ref[0:1])
        if low:
            out = out.astype(BF).astype(F32)
        out_ref[...] = out

    outs = [shape((size, depth), F32), shape((2, depth), F32)]
    return run(kernel, outs, [dmid, own, far, value, rows])


def block_lanes(spot, chunk):
    ry, rx = chunk // 2 ^ spot // 2, chunk % 2 ^ spot % 2
    return [(rx * 2 + ry) * 128, 512 + (ry * 2 + rx) * 128]


def place_in(lanes, blocks):
    size, width = blocks[0].shape
    half = width // 2

    def kernel(lanes_ref, *refs):
        out_ref = refs[-1]
        for d, ref in enumerate(refs[:-1]):
            for h in range(2):
                at = pl.multiple_of(lanes_ref[2 * d + h], 128)
                out_ref[:, pl.ds(at, half)] = ref[:, h * half : (h + 1) * half]

    block = pl.BlockSpec(memory_space=pltpu.VMEM)
    return pl.pallas_call(
        kernel,
        out_shape=shape((size, width * len(blocks))),
        in_specs=[pl.BlockSpec(memory_space=pltpu.SMEM)] + [block] * len(blocks),
        out_specs=block,
        compiler_params=pltpu.CompilerParams(vmem_limit_bytes=VMEM_BYTES),
    )(lanes, *blocks)


def place_out(numbers, scale, terms, bias_row, count):
    size, depth = terms[0].shape
    width = depth // count
    half = width // 2

    def kernel(numbers_ref, scale_ref, *refs):
        term_refs, bias_ref, out_ref = refs[: len(terms)], refs[-2], refs[-1]
        start = pl.multiple_of(numbers_ref[2 * count], 8)
        rows = pl.ds(start, size // 2)
        for d in range(count):
            for h in range(2):
                lanes = pl.ds(pl.multiple_of(numbers_ref[2 * d + h], 128), half)
                value = term_refs[0][rows, lanes]
                for ref in term_refs[1:]:
                    value = value + ref[rows, lanes]
                value = (value + bias_ref[:, lanes]) * scale_ref[0]
                out_ref[d, :, h * half : (h + 1) * half] = value.astype(BF)

    block = pl.BlockSpec(memory_space=pltpu.VMEM)
    scalar = pl.BlockSpec(memory_space=pltpu.SMEM)
    return pl.pallas_call(
        kernel,
        out_shape=shape((count, size // 2, width)),
        in_specs=[scalar, scalar] + [block] * (len(terms) + 1),
        out_specs=block,
        compiler_params=pltpu.CompilerParams(vmem_limit_bytes=VMEM_BYTES),
    )(numbers, scale, *terms, bias_row)


def shifts(blocks):
    n = lax.axis_size("tensor")
    out = [blocks[0]]
    for d in range(1, n):
        out.append(lax.ppermute(blocks[d], "tensor", [(i, (i + d) % n) for i in range(n)]))
    return out


def half_cols(core, whole, n_tensor):
    cut = whole.reshape(whole.shape[:-1] + (n_tensor, 2, -1))
    cut = jnp.where(core == 0, cut[..., 0, :], cut[..., 1, :])
    return cut.reshape(whole.shape[:-1] + (-1,))


def spread_cols(core, half, n_tensor):
    cut = half.reshape(half.shape[:-1] + (n_tensor, 1, -1))
    none = jnp.zeros_like(cut)
    both = jnp.concatenate(
        [jnp.where(core == 0, cut, none), jnp.where(core == 0, none, cut)], -2
    )
    return both.reshape(half.shape[:-1] + (-1,))


def body(boundary_in, counts, qkv_weight, proj_weight, fc1_weight, fc2_weight, vectors, fc1_bias):
    core = lax.axis_index("section")
    is_first = core == 0
    place = lax.axis_index("tensor")
    spot = lax.axis_index("dp")
    n_dp, n_tensor = lax.axis_size("dp"), lax.axis_size("tensor")
    slots_per_batch = boundary_in.shape[1] // counts.shape[1]
    live = (place % slots_per_batch < counts[0, place // slots_per_batch]).astype(jnp.float32)
    depth = qkv_weight.shape[1]
    mid = depth // 2
    n_vec = vectors.size

    small_size = n_vec + fc1_bias.size
    packs = []
    for part in range(2):
        cuts = [
            jnp.split(qkv_weight[0], 2, 2)[part].reshape(depth, -1),
            jnp.split(proj_weight[0], 2, 0)[part].T,
            jnp.split(fc1_weight[0], 2, 1)[part],
            jnp.split(fc2_weight[0], 2, 0)[part].T,
        ]
        packs.append(jnp.concatenate(cuts, 1))
    wide = packs[0].shape[1] // 3
    extra = 16
    small = jnp.concatenate([vectors.reshape(-1), fc1_bias.reshape(-1)])
    small = jnp.pad(small, (0, extra * wide - small_size)).reshape(extra, wide)
    small = jnp.pad(small, ((0, 0), (0, 2 * wide)))
    kept = jnp.concatenate([jnp.where(is_first, packs[0], packs[1]), small], 0)
    received = swap(
        jnp.concatenate([jnp.where(is_first, packs[1], packs[0]), small], 0)
    )
    shards = (jnp.where(is_first, kept, received), jnp.where(is_first, received, kept))
    columns = []
    for layer in range(2):
        for number in range(3):
            cols = shards[layer][:, number * wide : (number + 1) * wide]
            if layer == 0 and number == 0:
                room = extra // 2
                both = [shard[depth : depth + room, :wide] for shard in shards]
                cols = jnp.concatenate([cols[:mid], *both, cols[mid:depth]], 0)
            else:
                cols = cols[:depth]
            columns.append(cols)

    tokens = boundary_in.shape[2]
    pad = -tokens % 16
    reach = (tokens + pad) // 2
    ends_in = jnp.pad(boundary_in[0].astype(jnp.bfloat16), ((0, 0), (0, pad), (0, 0)))
    ends_low, ends_high = ends_in[:, :reach], ends_in[:, reach:]
    ends_got = swap(jnp.where(is_first, ends_high, ends_low))
    half_in = jnp.where(is_first, ends_low, ends_got)
    half_cot = jnp.where(is_first, ends_got, ends_high)

    below = [(place - d) % n_tensor for d in range(n_tensor)]
    above = [(place + d) % n_tensor for d in range(n_tensor)]

    def to_send(half):
        return [lax.dynamic_index_in_dim(half, j, 0, False) for j in above]

    def image_half(blocks):
        if n_dp == 4:
            lanes = [lane for t in below for lane in block_lanes(spot, t)]
            return place_in(jnp.stack(lanes).astype(jnp.int32), blocks)
        blocks = jnp.stack(blocks)
        blocks = [lax.dynamic_index_in_dim(blocks, (place - i) % n_tensor, 0, False) for i in range(n_tensor)]
        return relative(jnp.concatenate(blocks, 1), spot)

    def whole_image(half):
        other = swap(half)
        both = [jnp.where(is_first, half, other), jnp.where(is_first, other, half)]
        return jnp.concatenate(both, 0)

    def image_rows(scale, terms, bias_row):
        if n_dp == 4:
            numbers = [lane for t in above for lane in block_lanes(spot, t)]
            numbers.append(jnp.where(is_first, 0, reach))
            numbers = jnp.stack(numbers).astype(jnp.int32)
            blocks = place_out(numbers, scale.reshape(1), terms, bias_row, n_tensor)
            return [blocks[d] for d in range(n_tensor)]
        image = absolute((sum(terms[1:], terms[0]) + bias_row) * scale, spot).astype(jnp.bfloat16)
        half = jnp.where(is_first, image[:reach], image[reach:])
        half = half.reshape(reach, n_tensor, -1).transpose(1, 0, 2)
        return to_send(half)

    def by_image(blocks):
        blocks = jnp.stack(blocks)
        blocks = [lax.dynamic_index_in_dim(blocks, (place - i) % n_tensor, 0, False) for i in range(n_tensor)]
        return jnp.stack(blocks)

    def small_of(piece):
        extras = jnp.concatenate(piece, 0)
        both = by_chip(extras.reshape(n_dp, extra, -1), spot).astype(jnp.float32)
        both = both.reshape(n_dp, 2, extra // 2, n_tensor, wide).transpose(1, 0, 3, 2, 4)
        both = both.reshape(2, n_dp, n_tensor, -1)
        rows = both[..., :n_vec].reshape(2, n_dp, n_tensor, 8, -1)
        rows = relative(rows.transpose(0, 3, 2, 1, 4).reshape(2, 8, -1), spot)
        bias = both[..., n_vec:small_size].transpose(0, 2, 1, 3).reshape(2, -1)
        plain = both[..., :n_vec].reshape(2, n_dp, n_tensor, 8, -1)[..., 2:4, :]
        plain = plain.transpose(0, 3, 2, 1, 4).reshape(2, 2, -1)
        parts = [half_cols(core, plain[:, 0], n_tensor), half_cols(core, plain[:, 1], n_tensor)]
        parts.append(half_cols(core, bias, n_tensor))
        return [(rows[i], parts[0][i : i + 1], parts[1][i : i + 1], parts[2][i : i + 1]) for i in range(2)]

    number = len(columns)
    cut = [mid + extra if k == 0 else mid for k in range(number)]
    halves, near, far = [None] * number, [None] * number, [None] * number
    params = [dict(), dict()]
    blocks_in, blocks_cot = to_send(half_in), to_send(half_cot)
    pair, state = None, None
    for r in range(number + 2):
        tied = []
        if r < number:
            tied.append(gather_column(columns[r]))
        if 0 <= r - 1 < number:
            near[r - 1] = exchange_one(*halves[r - 1])
        if r == 1:
            blocks_in = shifts(blocks_in)
        if r == number:
            blocks_cot = shifts(blocks_cot)
        ready = []
        k = r - 2
        if k >= 0:
            layer, kind = k // 3, k % 3
            one = params[layer]
            first, second = arrived(*halves[k], near[k], far[k])
            if k == 0:
                blocks = [p.reshape((-1, mid + extra) + p.shape[1:]) for p in first]
                smalls = small_of([p[:, mid:].reshape(-1, p.shape[-1]) for p in blocks])
                params[0]["small"], params[1]["small"] = smalls
                if n_dp != 4:
                    first = [p[:, :mid].reshape(-1, p.shape[-1]) for p in blocks]
            pieces = first + second
            counts = [mid if n_dp == 4 else p.shape[0] for p in pieces]
            weights = (pieces, counts)
            rows, q_bias, v_bias, up_bias = one["small"]
            if pair is not None:
                pair = [pair[0], swap(pair[0])]
            if kind == 0:
                one["qkvo"] = weights
                if layer == 0:
                    terms = [whole_image(image_half(blocks_in)).astype(jnp.float32)]
                else:
                    terms = [state, *pair]
                bias_row = params[0]["small"][0][7:8]
                done = attention_forward(
                    tokens, terms, bias_row, layer == 1, weights, rows, q_bias, v_bias
                )
                one["u"], one["n1"], one["saved"], part = done[0], done[1], done[2:7], done[7]
                pair, ready = [part], [part]
            elif kind == 1:
                one["up"] = weights
                one["mid"], one["n2"], one["slope"], one["hidden"] = up_forward(
                    [one["u"], *pair], weights, rows, up_bias
                )
                pair, ready = None, [one["hidden"]]
            else:
                one["down"] = weights
                state = one["mid"]
                part = contract_wide(one["hidden"], weights)
                pair, ready = [part], [part]
        if r <= number:
            count = len(ready)
            extras = list(ready)
            if 0 <= r - 1 < number:
                if ready:
                    done = tie(near[r - 1] + extras, [])
                    near[r - 1], extras = done[: len(near[r - 1])], done[len(near[r - 1]) :]
                far[r - 1] = exchange_two(*halves[r - 1], *near[r - 1])
                tied += near[r - 1] + far[r - 1]
            if r <= 1:
                extras += blocks_in
            if r >= number - 1:
                extras += blocks_cot
            if r + 1 < number:
                extras.append(columns[r + 1])
            done = tie(tied + extras, [])
            if r + 1 < number:
                columns[r + 1] = done.pop()
            if r <= 1:
                done, blocks_in = done[:-n_tensor], done[-n_tensor:]
            if r >= number - 1:
                done, blocks_cot = done[:-n_tensor], done[-n_tensor:]
            if count and kind == 1:
                one["hidden"] = done[-1]
            elif count:
                pair = [done[-1]]
            at = 0
            if r < number:
                halves[r] = (done[0][: cut[r]], done[0][cut[r] :])
                at = 1
            if 0 <= r - 1 < number:
                near[r - 1] = done[at : at + 2]
                far[r - 1] = done[at + 2 : at + 2 + len(far[r - 1])]
    cotangent = whole_image(image_half(blocks_cot)).astype(jnp.float32) * live
    pair = [pair[0], swap(pair[0])]
    last_rows = params[1]["small"][0]
    out_blocks = image_rows(live, [state, *pair], last_rows[7:8])

    grads, got, moved, settled = [None] * number, [None] * number, [None] * number, [None] * number
    made = [0, 1, 2, 4, 5, 6]
    sums = [dict(), dict()]
    grad = cotangent
    for r in range(8):
        layer, stage = 1 - r // 4, r % 4
        one, total = params[layer], sums[layer]
        rows = one["small"][0]
        tied, slots = [], []
        for c in range(number):
            if r == made[c] + 1:
                got[c] = scatter_one(*grads[c][:2])
                slots.append((got, c, len(got[c])))
                tied += got[c]
            elif r == made[c] + 2:
                stay, come = scatter_two(*grads[c][2:], got[c])
                moved[c] = [*stay, *come]
                slots.append((moved, c, len(moved[c])))
                tied += moved[c]
            elif r == made[c] + 3:
                settled[c] = scatter_column(moved[c][:2], moved[c][2:])
                slots.append((settled, c, 0))
                tied.append(settled[c])
        new = None
        if stage == 0:
            low, total["out"], total["up_bias"], new = down_backward(
                grad, one["hidden"], one["slope"], one["down"]
            )
            carry = [low]
        elif stage == 1:
            part = contract_wide(low, one["up"])
            new = up_grad(one["n2"], low)
            carry = [part]
        elif stage == 2:
            done = attention_backward(
                grad, part, swap(part), one["mid"], rows, one["saved"], one["qkvo"]
            )
            dmid, dz, dq, dk, dv, part, total["mid"], total["q"], total["v"] = done
            new = attention_grad(one["n1"], dz, dq, dk, dv, one["saved"][4])
            carry = [part]
        else:
            grad, total["one"] = value_backward(dmid, part, swap(part), one["u"], rows, layer == 1)
            carry = [grad]
            if r == 7:
                one_scale = jnp.ones((), jnp.float32)
                no_bias = jnp.zeros((1, grad.shape[1]), jnp.float32)
                carry = shifts(image_rows(one_scale, [grad], no_bias))
        if new is not None:
            c = made.index(r)
            grads[c] = new
            fresh = [g for g in new if g is not None]
        else:
            fresh = []
        if r == 1:
            out_blocks = shifts(out_blocks)
            carry += out_blocks
        if r < 8:
            done = tie(carry + fresh + tied, [])
            if stage == 0:
                low = done[0]
            elif stage == 1:
                part = done[0]
            elif stage == 2:
                part = done[0]
            elif r < 7:
                grad = done[0]
            else:
                grad_blocks = done[:n_tensor]
            if r == 1:
                out_blocks = done[1 : 1 + n_tensor]
            done = done[len(carry) :]
            if fresh:
                grads[c] = fill(done[: len(fresh)])
                done = done[len(fresh) :]
            for store, at, count in slots:
                store[at] = done[:count] if count else done[0]
                done = done[max(count, 1) :]

    grad_rows, out_rows = by_image(grad_blocks), by_image(out_blocks)
    packed = []
    for layer in range(2):
        total = sums[layer]
        full = jnp.concatenate([total["one"], total["mid"], total["out"]], 0)
        full = absolute(jnp.where(core == layer, full, 0.0), spot)
        q_row = spread_cols(core, total["q"][0], n_tensor)
        v_row = spread_cols(core, total["v"][0], n_tensor)
        up_row = spread_cols(core, total["up_bias"][0], n_tensor)
        rows = jnp.concatenate([full[:2], q_row[None], v_row[None], full[2:]], 0)
        rows = rows.reshape(8, n_tensor, n_dp, -1).transpose(2, 1, 0, 3).reshape(n_dp, n_tensor, -1)
        up_row = up_row.reshape(n_tensor, n_dp, -1).transpose(1, 0, 2)
        packed.append(jnp.concatenate([rows, up_row], -1))
    ours = jnp.where(is_first, packed[0], packed[1])
    other = swap(jnp.where(is_first, packed[1], packed[0]))
    little = (ours + other).astype(jnp.bfloat16)
    room = jnp.zeros((n_dp, n_tensor, extra * wide - small_size), little.dtype)
    little = jnp.concatenate([little, room], -1).reshape(n_dp, n_tensor, extra, wide)
    little = by_arrival(little.transpose(0, 2, 1, 3).reshape(n_dp, extra, -1), spot)
    if n_dp != 4:
        little = lax.psum_scatter(little, "dp", scatter_dimension=0, tiled=True)[0]
    else:
        little = add(little[:2], swap_x(little[2:])).astype(jnp.bfloat16)
        little = add(little[0], swap_y(little[1])).astype(jnp.bfloat16)

    last = number - 1
    settled[last - 1] = scatter_column(moved[last - 1][:2], moved[last - 1][2:])
    stay, come = scatter_two(*grads[last][2:], got[last])
    if come:
        stay = [add(s, c).astype(jnp.bfloat16) for s, c in zip(stay, come)]
    settled[last] = scatter_column([*stay, little], [])
    little = settled[last][depth:].reshape(-1).astype(jnp.float32)
    settled[last] = settled[last][:depth]
    grad_vectors = little[:n_vec].reshape(vectors.shape)
    grad_bias = little[n_vec:small_size].reshape(fc1_bias.shape)

    own = jnp.where(is_first, grad_rows, out_rows)
    other = swap(jnp.where(is_first, out_rows, grad_rows))
    ends = [jnp.where(is_first, own, other), jnp.where(is_first, other, own)]
    boundary_out = jnp.concatenate(ends, 1)[:, :tokens].astype(jnp.float32)[None]
    lows, highs = [], []
    for kind in range(3):
        first, second = settled[last - kind], settled[last - kind - 3]
        kept = jnp.where(is_first, first, second)
        received = swap(jnp.where(is_first, second, first))
        lows.append(jnp.where(is_first, kept, received).astype(jnp.float32))
        highs.append(jnp.where(is_first, received, kept).astype(jnp.float32))
    low, high = [part[0].reshape(depth, 4, -1) for part in (lows, highs)]
    grad_qkv = jnp.concatenate([low[:, :3], high[:, :3]], 2)[None]
    grad_proj = jnp.concatenate([low[:, 3].T, high[:, 3].T], 0)[None]
    grad_up = jnp.concatenate([lows[1], highs[1]], 1)[None]
    grad_down = jnp.concatenate([lows[2].T, highs[2].T], 0)[None]
    return (boundary_out, grad_qkv, grad_proj, grad_up, grad_down, grad_vectors, grad_bias)


def solution(mesh):
    in_specs = (
        P("section", "dp", None, "tensor"),
        P("dp", None),
        P("section", "dp", None, "tensor"),
        P("section", "tensor", "dp"),
        P("section", "dp", "tensor"),
        P("section", "tensor", "dp"),
        P("section", None, "tensor", "dp"),
        P("section", "tensor", "dp"),
    )
    out_specs = (
        P("section", "dp", None, "tensor"),
        P("section", "dp", None, "tensor"),
        P("section", "tensor", "dp"),
        P("section", "dp", "tensor"),
        P("section", "tensor", "dp"),
        P("section", None, "tensor", "dp"),
        P("section", "tensor", "dp"),
    )
    return jax.shard_map(body, mesh=mesh, in_specs=in_specs, out_specs=out_specs, check_vma=False)
```

```python
import jax
import jax.numpy as jnp
from jax import lax
from jax.experimental import pallas as pl
from jax.experimental.pallas import tpu as pltpu
from jax.sharding import PartitionSpec as P

HD = 64
EPS = 1e-06


def swap(value):
    return lax.ppermute(value, "section", [(0, 1), (1, 0)])


def pair_sum(partial):
    low = partial.astype(jnp.bfloat16)
    return low.astype(jnp.float32) + swap(low).astype(jnp.float32)


def swap_x(value):
    n = lax.axis_size("dp")
    return lax.ppermute(value, "dp", [(i, i ^ 1) for i in range(n)])


def swap_y(value):
    n = lax.axis_size("dp")
    return lax.ppermute(value, "dp", [(i, i ^ 2) for i in range(n)])


def tie(values, others):
    count = len(values)

    def kernel(*refs):
        pass

    anywhere = pl.BlockSpec(memory_space=pl.ANY)
    done = pl.pallas_call(
        kernel,
        out_shape=[jax.ShapeDtypeStruct(v.shape, v.dtype) for v in values],
        in_specs=[anywhere] * (count + len(others)),
        out_specs=[anywhere] * count,
        input_output_aliases={i: i for i in range(count)},
    )(*values, *others)
    return list(done)


def gather_column(shard):
    return lax.all_gather(shard, "tensor", axis=1, tiled=True)


def exchange_one(first, second):
    if lax.axis_size("dp") != 4:
        return [lax.all_gather(v, "dp", axis=0, tiled=True) for v in (first, second)]
    return [swap_y(first), swap_x(second)]


def exchange_two(first, second, near_first, near_second):
    if lax.axis_size("dp") != 4:
        return []
    return [swap_x(first), swap_x(near_first), swap_y(second), swap_y(near_second)]


def arrived(first, second, near, far):
    if lax.axis_size("dp") != 4:
        return ([near[0]], [near[1]])
    return ([first, near[0], far[0], far[1]], [second, near[1], far[2], far[3]])


def row_cuts(depth):
    half = depth // 2
    if lax.axis_size("dp") != 4:
        return [(0, half), (half, depth), None, None]
    part = half // 2
    return [(part, half), (half + part, depth), (0, part), (half, half + part)]


def add(left, right):
    return left.astype(jnp.float32) + right.astype(jnp.float32)


def scatter_one(send_first, send_second):
    if lax.axis_size("dp") != 4:
        return [
            lax.psum_scatter(v, "dp", scatter_dimension=0, tiled=True)
            for v in (send_first, send_second)
        ]
    return [swap_x(send_first), swap_y(send_second)]


def scatter_two(keep_first, keep_second, got):
    if lax.axis_size("dp") != 4:
        return (got, [])
    stay, come = [], []
    for keep, new, far in zip((keep_first, keep_second), got, (swap_y, swap_x)):
        half = keep.shape[0] // 2
        come.append(far(add(keep[half:], new[half:]).astype(jnp.bfloat16)))
        stay.append(add(keep[:half], new[:half]).astype(jnp.bfloat16))
    return (stay, come)


def scatter_column(stay, come):
    if come:
        stay = [add(s, c).astype(jnp.bfloat16) for s, c in zip(stay, come)]
    return lax.psum_scatter(
        jnp.concatenate(stay, 0), "tensor", scatter_dimension=1, tiled=True
    )


def flip_axis(value, axis, bit):
    return jnp.where(bit == 1, jnp.flip(value, axis), value)


def relative(value, spot):
    n_dp = lax.axis_size("dp")
    lead = value.shape[:-1]
    k = len(lead)
    if n_dp != 4:
        cut = value.reshape(lead + (n_dp, 2, -1))
        return jnp.swapaxes(cut, k, k + 1).reshape(value.shape)
    cut = value.reshape(lead + (2, 2, 2, -1))
    cut = flip_axis(flip_axis(cut, k, spot // 2), k + 1, spot % 2)
    first = jnp.swapaxes(cut[..., 0, :], k, k + 1)
    second = cut[..., 1, :]
    return jnp.concatenate([first.reshape(lead + (-1,)), second.reshape(lead + (-1,))], -1)


def absolute(value, spot):
    n_dp = lax.axis_size("dp")
    lead = value.shape[:-1]
    k = len(lead)
    if n_dp != 4:
        cut = value.reshape(lead + (2, n_dp, -1))
        return jnp.swapaxes(cut, k, k + 1).reshape(value.shape)
    cut = value.reshape(lead + (2, 2, 2, -1))
    first = jnp.swapaxes(cut[..., 0, :, :, :], k, k + 1)
    second = cut[..., 1, :, :, :]
    cut = jnp.stack([first, second], k + 2)
    cut = flip_axis(flip_axis(cut, k, spot // 2), k + 1, spot % 2)
    return cut.reshape(value.shape)


def by_chip(blocks, spot):
    n_dp = lax.axis_size("dp")
    if n_dp != 4:
        return blocks
    cut = blocks.reshape((2, 2) + blocks.shape[1:])
    cut = jnp.swapaxes(cut, 0, 1)
    cut = flip_axis(flip_axis(cut, 0, spot // 2), 1, spot % 2)
    return cut.reshape(blocks.shape)


def by_arrival(blocks, spot):
    n_dp = lax.axis_size("dp")
    if n_dp != 4:
        return blocks
    cut = blocks.reshape((2, 2) + blocks.shape[1:])
    cut = flip_axis(flip_axis(cut, 0, spot // 2), 1, spot % 2)
    return jnp.swapaxes(cut, 0, 1).reshape(blocks.shape)


VMEM_BYTES = 50 * 2**20
BF = jnp.bfloat16
F32 = jnp.float32


def shape(dims, kind=jnp.bfloat16):
    return jax.ShapeDtypeStruct(dims, kind)


def run(kernel, outs, ins):
    block = pl.BlockSpec(memory_space=pltpu.VMEM)
    done = pl.pallas_call(
        kernel,
        out_shape=list(outs),
        in_specs=[block] * len(ins),
        out_specs=[block] * len(outs),
        cost_estimate=pl.CostEstimate(flops=1, bytes_accessed=1, transcendentals=0),
        compiler_params=pltpu.CompilerParams(vmem_limit_bytes=VMEM_BYTES),
    )(*ins)
    return list(done)


def nn(left, right):
    return lax.dot_general(left, right, (((1,), (0,)), ((), ())), preferred_element_type=F32)


def nt(left, right):
    return lax.dot_general(left, right, (((1,), (1,)), ((), ())), preferred_element_type=F32)


def tn(left, right):
    return lax.dot_general(left, right, (((0,), (0,)), ((), ())), preferred_element_type=F32)


def stack_rows(pieces, counts, cols):
    return jnp.concatenate([p[:n, cols] for p, n in zip(pieces, counts)], 0)


def center_scale(value):
    center = jnp.mean(value, -1, keepdims=True)
    spread = jnp.mean(value * value, -1, keepdims=True) - center * center
    factor = lax.rsqrt(spread + EPS)
    return ((value - center) * factor, factor)


def norm_backward(grad_normed, centred, factor, gain):
    scaled = grad_normed * gain
    return factor * (
        scaled
        - jnp.mean(scaled, -1, keepdims=True)
        - centred * jnp.mean(scaled * centred, -1, keepdims=True)
    )


def column_sum(value):
    return jnp.sum(value, 0, keepdims=True)


def attention_forward(tokens, terms, bias_row, low, weights, rows, q_bias, v_bias):
    pieces, counts = weights
    size, depth = terms[0].shape
    wide = pieces[0].shape[1]
    groups = wide // 512
    half = groups * 128
    n_terms, n_pieces = len(terms), len(pieces)

    def kernel(*refs):
        term_refs, refs = refs[:n_terms], refs[n_terms:]
        bias_ref, rows_ref, qb_ref, vb_ref = refs[:4]
        piece_refs, refs = refs[4 : 4 + n_pieces], refs[4 + n_pieces :]
        u_ref, n_ref, q_ref, k_ref, v_ref, p_ref, o_ref, part_ref = refs
        value = term_refs[0][...].astype(F32)
        for ref in term_refs[1:]:
            value = value + ref[...].astype(F32)
        if n_terms > 1:
            value = value + bias_ref[...]
        if low:
            value = value.astype(BF).astype(F32)
        u_ref[...] = value
        centred, factor = center_scale(value)
        n_ref[...] = (centred * rows_ref[0:1] + rows_ref[1:2]).astype(BF)
        lane = lax.broadcasted_iota(jnp.int32, (size, 128), 1)
        key_lane = lax.broadcasted_iota(jnp.int32, (size, size), 1)
        normed = n_ref[...]
        for g in range(groups):
            at = slice(g * 128, (g + 1) * 128)
            matrix = stack_rows(piece_refs, counts, slice(g * 512, g * 512 + 384))
            projected = nn(normed, matrix)
            q = (projected[:, :128] + qb_ref[:, at]).astype(BF)
            k = projected[:, 128:256].astype(BF)
            v = (projected[:, 256:384] + vb_ref[:, at]).astype(BF)
            q_ref[:, at] = q
            k_ref[:, at] = k
            v_ref[:, at] = v
            mixed = None
            for h in range(2):
                mine = (lane // HD) == h
                scores = nt(jnp.where(mine, q, jnp.zeros_like(q)), k) * HD ** (-0.5)
                scores = jnp.where(key_lane < tokens, scores, -1e30)
                highest = jnp.max(scores, -1, keepdims=True)
                exponent = jnp.exp(scores - highest)
                inverse = 1.0 / jnp.sum(exponent, -1, keepdims=True)
                soft = (exponent * inverse).astype(BF)
                p_ref[2 * g + h] = soft
                out = nn(soft, v)
                mixed = out if h == 0 else jnp.where(mine, out, mixed)
            o_ref[:, at] = mixed.astype(BF)
        matrix = jnp.concatenate(
            [stack_rows(piece_refs, counts, slice(g * 512 + 384, g * 512 + 512)) for g in range(groups)], 1
        )
        part_ref[...] = nt(o_ref[...], matrix).astype(BF)

    outs = [shape((size, depth), F32), shape((size, depth))] + [shape((size, half))] * 3
    outs += [shape((2 * groups, size, size)), shape((size, half)), shape((size, depth))]
    return run(kernel, outs, [*terms, bias_row, rows, q_bias, v_bias, *pieces])


def up_forward(terms, weights, rows, up_bias):
    pieces, counts = weights
    size, depth = terms[0].shape
    wide = pieces[0].shape[1]

    def kernel(*refs):
        u_ref, own_ref, far_ref, rows_ref, bias_ref = refs[:5]
        piece_refs = refs[5 : 5 + len(pieces)]
        mid_ref, n_ref, slope_ref, hidden_ref = refs[5 + len(pieces) :]
        value = u_ref[...] + own_ref[...].astype(F32) + far_ref[...].astype(F32) + rows_ref[4:5]
        mid_ref[...] = value
        centred, factor = center_scale(value)
        n_ref[...] = (centred * rows_ref[5:6] + rows_ref[6:7]).astype(BF)
        step = 512
        for at in range(0, wide, step):
            cols = slice(at, at + step)
            before = nn(n_ref[...], stack_rows(piece_refs, counts, cols)) + bias_ref[:, cols]
            cdf = 0.5 * (1.0 + lax.erf(before * 0.7071067811865476))
            density = jnp.exp(-0.5 * before * before) * 0.3989422804014327
            hidden_ref[:, cols] = (before * cdf).astype(BF)
            slope_ref[:, cols] = (cdf + before * density).astype(BF)

    outs = [shape((size, depth), F32), shape((size, depth)), shape((size, wide)), shape((size, wide))]
    return run(kernel, outs, [*terms, rows, up_bias, *pieces])


def contract_wide(left, weights):
    pieces, counts = weights
    size, wide = left.shape
    depth = sum(counts)

    def kernel(*refs):
        left_ref, piece_refs, out_ref = refs[0], refs[1:-1], refs[-1]
        matrix = stack_rows(piece_refs, counts, slice(0, wide))
        out_ref[...] = nt(left_ref[...], matrix).astype(BF)

    return run(kernel, [shape((size, depth))], [left, *pieces])[0]


def weight_outs(depth, wide):
    cuts = [c for c in row_cuts(depth) if c is not None]
    return cuts, [shape((c[1] - c[0], wide)) for c in cuts]


def fill(grads):
    return (list(grads) + [None, None])[:4]


def down_backward(grad_out, hidden, slope, weights):
    pieces, counts = weights
    size, depth = grad_out.shape
    wide = hidden.shape[1]
    cuts, grad_outs = weight_outs(depth, wide)

    def kernel(*refs):
        g_ref, hidden_ref, slope_ref = refs[:3]
        piece_refs, refs = refs[3 : 3 + len(pieces)], refs[3 + len(pieces) :]
        low_ref, sum_ref, bias_ref = refs[:3]
        sum_ref[...] = column_sum(g_ref[...])
        branch = g_ref[...].astype(BF)
        for cut, ref in zip(cuts, refs[3:]):
            ref[...] = tn(branch[:, cut[0] : cut[1]], hidden_ref[...]).astype(BF)
        step = 512
        for at in range(0, wide, step):
            cols = slice(at, at + step)
            back = nn(branch, stack_rows(piece_refs, counts, cols)) * slope_ref[:, cols].astype(F32)
            bias_ref[:, cols] = column_sum(back)
            low_ref[:, cols] = back.astype(BF)

    outs = [shape((size, wide)), shape((1, depth), F32), shape((1, wide), F32)] + grad_outs
    done = run(kernel, outs, [grad_out, hidden, slope, *pieces])
    return done[0], done[1], done[2], fill(done[3:])


def up_grad(normed, low):
    size, depth = normed.shape
    wide = low.shape[1]
    cuts, outs = weight_outs(depth, wide)

    def kernel(n_ref, low_ref, *refs):
        for cut, ref in zip(cuts, refs):
            ref[...] = tn(n_ref[:, cut[0] : cut[1]], low_ref[...]).astype(BF)

    return fill(run(kernel, outs, [normed, low]))


def attention_backward(grad_out, own, far, middle, rows, saved, weights):
    pieces, counts = weights
    size, depth = grad_out.shape
    wide = pieces[0].shape[1]
    groups = wide // 512
    half = groups * 128
    scale = HD ** (-0.5)

    def kernel(*refs):
        g_ref, own_ref, far_ref, mid_ref, rows_ref, q_ref, k_ref, v_ref, p_ref, o_ref = refs[:10]
        piece_refs, refs = refs[10 : 10 + len(pieces)], refs[10 + len(pieces) :]
        dmid_ref, dz_ref, dq_ref, dk_ref, dv_ref, part_ref, sum_ref, qs_ref, vs_ref = refs
        grad_normed = own_ref[...].astype(F32) + far_ref[...].astype(F32)
        centred, factor = center_scale(mid_ref[...])
        sum_ref[1:2] = column_sum(grad_normed * centred)
        sum_ref[2:3] = column_sum(grad_normed)
        dmid = g_ref[...] + norm_backward(grad_normed, centred, factor, rows_ref[5:6])
        dmid_ref[...] = dmid
        sum_ref[0:1] = column_sum(dmid)
        dz_ref[...] = dmid.astype(BF)
        lane = lax.broadcasted_iota(jnp.int32, (size, 128), 1)
        for g in range(groups):
            at = slice(g * 128, (g + 1) * 128)
            matrix = stack_rows(piece_refs, counts, slice(g * 512 + 384, g * 512 + 512))
            grad_mixed = nn(dz_ref[...], matrix).astype(BF)
            q, k, v = q_ref[:, at], k_ref[:, at], v_ref[:, at]
            inner = grad_mixed.astype(F32) * o_ref[:, at].astype(F32)
            dq, dk, dv = None, None, None
            for h in range(2):
                mine = (lane // HD) == h
                soft = p_ref[2 * g + h]
                none = jnp.zeros_like(q)
                do = jnp.where(mine, grad_mixed, none)
                total = jnp.sum(jnp.where(mine, inner, 0.0), -1, keepdims=True)
                grad_soft = nt(do, v)
                grad_scores = (soft.astype(F32) * (grad_soft - total)).astype(BF)
                new_q = nn(grad_scores, k)
                new_k = tn(jnp.where(mine, q, none), grad_scores)
                new_v = tn(do, soft)
                dq = new_q if h == 0 else jnp.where(mine, new_q, dq)
                dk = new_k if h == 0 else dk + new_k
                dv = new_v if h == 0 else dv + new_v
            dq, dk, dv = dq * scale, dk.T * scale, dv.T
            qs_ref[:, at] = column_sum(dq)
            vs_ref[:, at] = column_sum(dv)
            dq_ref[:, at] = dq.astype(BF)
            dk_ref[:, at] = dk.astype(BF)
            dv_ref[:, at] = dv.astype(BF)
        total = None
        for g in range(groups):
            at = slice(g * 128, (g + 1) * 128)
            left = jnp.concatenate([dq_ref[:, at], dk_ref[:, at], dv_ref[:, at]], 1)
            new = nt(left, stack_rows(piece_refs, counts, slice(g * 512, g * 512 + 384)))
            total = new if g == 0 else total + new
        part_ref[...] = total.astype(BF)

    outs = [shape((size, depth), F32), shape((size, depth))] + [shape((size, half))] * 3
    outs += [shape((size, depth)), shape((3, depth), F32)] + [shape((1, half), F32)] * 2
    return run(kernel, outs, [grad_out, own, far, middle, rows, *saved, *pieces])


def attention_grad(normed, dz, dq, dk, dv, mixed):
    size, depth = normed.shape
    groups = dq.shape[1] // 128
    cuts, outs = weight_outs(depth, groups * 512)

    def kernel(n_ref, dz_ref, dq_ref, dk_ref, dv_ref, o_ref, *refs):
        for cut, ref in zip(cuts, refs):
            rows = slice(cut[0], cut[1])
            for g in range(groups):
                at = slice(g * 128, (g + 1) * 128)
                right = jnp.concatenate([dq_ref[:, at], dk_ref[:, at], dv_ref[:, at]], 1)
                ref[:, g * 512 : g * 512 + 384] = tn(n_ref[:, rows], right).astype(BF)
                ref[:, g * 512 + 384 : g * 512 + 512] = tn(dz_ref[:, rows], o_ref[:, at]).astype(BF)

    return fill(run(kernel, outs, [normed, dz, dq, dk, dv, mixed]))


def value_backward(dmid, own, far, value, rows, low):
    size, depth = dmid.shape

    def kernel(dmid_ref, own_ref, far_ref, u_ref, rows_ref, out_ref, sum_ref):
        grad_normed = own_ref[...].astype(F32) + far_ref[...].astype(F32)
        centred, factor = center_scale(u_ref[...])
        sum_ref[0:1] = column_sum(grad_normed * centred)
        sum_ref[1:2] = column_sum(grad_normed)
        out = dmid_ref[...] + norm_backward(grad_normed, centred, factor, rows_ref[0:1])
        if low:
            out = out.astype(BF).astype(F32)
        out_ref[...] = out

    outs = [shape((size, depth), F32), shape((2, depth), F32)]
    return run(kernel, outs, [dmid, own, far, value, rows])


def block_lanes(spot, chunk):
    ry, rx = chunk // 2 ^ spot // 2, chunk % 2 ^ spot % 2
    return [(rx * 2 + ry) * 128, 512 + (ry * 2 + rx) * 128]


def place_in(lanes, blocks):
    size, width = blocks[0].shape
    half = width // 2

    def kernel(lanes_ref, *refs):
        out_ref = refs[-1]
        for d, ref in enumerate(refs[:-1]):
            for h in range(2):
                at = pl.multiple_of(lanes_ref[2 * d + h], 128)
                out_ref[:, pl.ds(at, half)] = ref[:, h * half : (h + 1) * half]

    block = pl.BlockSpec(memory_space=pltpu.VMEM)
    return pl.pallas_call(
        kernel,
        out_shape=shape((size, width * len(blocks))),
        in_specs=[pl.BlockSpec(memory_space=pltpu.SMEM)] + [block] * len(blocks),
        out_specs=block,
        compiler_params=pltpu.CompilerParams(vmem_limit_bytes=VMEM_BYTES),
    )(lanes, *blocks)


def place_out(numbers, scale, terms, bias_row, count):
    size, depth = terms[0].shape
    width = depth // count
    half = width // 2

    def kernel(numbers_ref, scale_ref, *refs):
        term_refs, bias_ref, out_ref = refs[: len(terms)], refs[-2], refs[-1]
        start = pl.multiple_of(numbers_ref[2 * count], 8)
        rows = pl.ds(start, size // 2)
        for d in range(count):
            for h in range(2):
                lanes = pl.ds(pl.multiple_of(numbers_ref[2 * d + h], 128), half)
                value = term_refs[0][rows, lanes]
                for ref in term_refs[1:]:
                    value = value + ref[rows, lanes]
                value = (value + bias_ref[:, lanes]) * scale_ref[0]
                out_ref[d, :, h * half : (h + 1) * half] = value.astype(BF)

    block = pl.BlockSpec(memory_space=pltpu.VMEM)
    scalar = pl.BlockSpec(memory_space=pltpu.SMEM)
    return pl.pallas_call(
        kernel,
        out_shape=shape((count, size // 2, width)),
        in_specs=[scalar, scalar] + [block] * (len(terms) + 1),
        out_specs=block,
        compiler_params=pltpu.CompilerParams(vmem_limit_bytes=VMEM_BYTES),
    )(numbers, scale, *terms, bias_row)


def shifts(blocks):
    n = lax.axis_size("tensor")
    out = [blocks[0]]
    for d in range(1, n):
        out.append(lax.ppermute(blocks[d], "tensor", [(i, (i + d) % n) for i in range(n)]))
    return out


def half_cols(core, whole, n_tensor):
    cut = whole.reshape(whole.shape[:-1] + (n_tensor, 2, -1))
    cut = jnp.where(core == 0, cut[..., 0, :], cut[..., 1, :])
    return cut.reshape(whole.shape[:-1] + (-1,))


def spread_cols(core, half, n_tensor):
    cut = half.reshape(half.shape[:-1] + (n_tensor, 1, -1))
    none = jnp.zeros_like(cut)
    both = jnp.concatenate(
        [jnp.where(core == 0, cut, none), jnp.where(core == 0, none, cut)], -2
    )
    return both.reshape(half.shape[:-1] + (-1,))


def body(boundary_in, counts, qkv_weight, proj_weight, fc1_weight, fc2_weight, vectors, fc1_bias):
    core = lax.axis_index("section")
    is_first = core == 0
    place = lax.axis_index("tensor")
    spot = lax.axis_index("dp")
    n_dp, n_tensor = lax.axis_size("dp"), lax.axis_size("tensor")
    slots_per_batch = boundary_in.shape[1] // counts.shape[1]
    live = (place % slots_per_batch < counts[0, place // slots_per_batch]).astype(jnp.float32)
    depth = qkv_weight.shape[1]
    mid = depth // 2
    n_vec = vectors.size

    small_size = n_vec + fc1_bias.size
    packs = []
    for part in range(2):
        cuts = [
            jnp.split(qkv_weight[0], 2, 2)[part].reshape(depth, -1),
            jnp.split(proj_weight[0], 2, 0)[part].T,
            jnp.split(fc1_weight[0], 2, 1)[part],
            jnp.split(fc2_weight[0], 2, 0)[part].T,
        ]
        packs.append(jnp.concatenate(cuts, 1))
    wide = packs[0].shape[1] // 3
    extra = 16
    small = jnp.concatenate([vectors.reshape(-1), fc1_bias.reshape(-1)])
    small = jnp.pad(small, (0, extra * wide - small_size)).reshape(extra, wide)
    small = jnp.pad(small, ((0, 0), (0, 2 * wide)))
    kept = jnp.concatenate([jnp.where(is_first, packs[0], packs[1]), small], 0)
    received = swap(
        jnp.concatenate([jnp.where(is_first, packs[1], packs[0]), small], 0)
    )
    shards = (jnp.where(is_first, kept, received), jnp.where(is_first, received, kept))
    columns = []
    for layer in range(2):
        for number in range(3):
            cols = shards[layer][:, number * wide : (number + 1) * wide]
            if layer == 0 and number == 0:
                room = extra // 2
                both = [shard[depth : depth + room, :wide] for shard in shards]
                cols = jnp.concatenate([cols[:depth], *both], 0)
            else:
                cols = cols[:depth]
            columns.append(cols)

    tokens = boundary_in.shape[2]
    pad = -tokens % 16
    reach = (tokens + pad) // 2
    ends_in = jnp.pad(boundary_in[0].astype(jnp.bfloat16), ((0, 0), (0, pad), (0, 0)))
    ends_low, ends_high = ends_in[:, :reach], ends_in[:, reach:]
    ends_got = swap(jnp.where(is_first, ends_high, ends_low))
    half_in = jnp.where(is_first, ends_low, ends_got)
    half_cot = jnp.where(is_first, ends_got, ends_high)

    below = [(place - d) % n_tensor for d in range(n_tensor)]
    above = [(place + d) % n_tensor for d in range(n_tensor)]

    def to_send(half):
        return [lax.dynamic_index_in_dim(half, j, 0, False) for j in above]

    def image_half(blocks):
        if n_dp == 4:
            lanes = [lane for t in below for lane in block_lanes(spot, t)]
            return place_in(jnp.stack(lanes).astype(jnp.int32), blocks)
        blocks = jnp.stack(blocks)
        blocks = [lax.dynamic_index_in_dim(blocks, (place - i) % n_tensor, 0, False) for i in range(n_tensor)]
        return relative(jnp.concatenate(blocks, 1), spot)

    def whole_image(half):
        other = swap(half)
        both = [jnp.where(is_first, half, other), jnp.where(is_first, other, half)]
        return jnp.concatenate(both, 0)

    def image_rows(scale, terms, bias_row):
        if n_dp == 4:
            numbers = [lane for t in above for lane in block_lanes(spot, t)]
            numbers.append(jnp.where(is_first, 0, reach))
            numbers = jnp.stack(numbers).astype(jnp.int32)
            blocks = place_out(numbers, scale.reshape(1), terms, bias_row, n_tensor)
            return [blocks[d] for d in range(n_tensor)]
        image = absolute((sum(terms[1:], terms[0]) + bias_row) * scale, spot).astype(jnp.bfloat16)
        half = jnp.where(is_first, image[:reach], image[reach:])
        half = half.reshape(reach, n_tensor, -1).transpose(1, 0, 2)
        return to_send(half)

    def by_image(blocks):
        blocks = jnp.stack(blocks)
        blocks = [lax.dynamic_index_in_dim(blocks, (place - i) % n_tensor, 0, False) for i in range(n_tensor)]
        return jnp.stack(blocks)

    def small_of(extras):
        if n_dp != 4:
            extras = lax.all_gather(extras, "dp", axis=0, tiled=True)
        else:
            extras = jnp.concatenate([extras, swap_y(extras)], 0)
            extras = jnp.concatenate([extras, swap_x(extras)], 0)
        both = by_chip(extras.reshape(n_dp, extra, -1), spot).astype(jnp.float32)
        both = both.reshape(n_dp, 2, extra // 2, n_tensor, wide).transpose(1, 0, 3, 2, 4)
        both = both.reshape(2, n_dp, n_tensor, -1)
        rows = both[..., :n_vec].reshape(2, n_dp, n_tensor, 8, -1)
        rows = relative(rows.transpose(0, 3, 2, 1, 4).reshape(2, 8, -1), spot)
        bias = both[..., n_vec:small_size].transpose(0, 2, 1, 3).reshape(2, -1)
        plain = both[..., :n_vec].reshape(2, n_dp, n_tensor, 8, -1)[..., 2:4, :]
        plain = plain.transpose(0, 3, 2, 1, 4).reshape(2, 2, -1)
        parts = [half_cols(core, plain[:, 0], n_tensor), half_cols(core, plain[:, 1], n_tensor)]
        parts.append(half_cols(core, bias, n_tensor))
        return [(rows[i], parts[0][i : i + 1], parts[1][i : i + 1], parts[2][i : i + 1]) for i in range(2)]

    number = len(columns)
    halves, near, far = [None] * number, [None] * number, [None] * number
    params = [dict(), dict()]
    blocks_in, blocks_cot = to_send(half_in), to_send(half_cot)
    pair, state = None, None
    for r in range(number + 2):
        tied = []
        if r < number:
            tied.append(gather_column(columns[r]))
        if 0 <= r - 1 < number:
            near[r - 1] = exchange_one(*halves[r - 1])
        if r == 1:
            smalls = small_of(extra_rows)
            blocks_in = shifts(blocks_in)
        if r == number:
            blocks_cot = shifts(blocks_cot)
        ready = []
        k = r - 2
        if k >= 0:
            layer, kind = k // 3, k % 3
            one = params[layer]
            first, second = arrived(*halves[k], near[k], far[k])
            pieces = first + second
            counts = [p.shape[0] for p in pieces]
            weights = (pieces, counts)
            rows, q_bias, v_bias, up_bias = one["small"]
            if pair is not None:
                pair = [pair[0], swap(pair[0])]
            if kind == 0:
                one["qkvo"] = weights
                if layer == 0:
                    terms = [whole_image(image_half(blocks_in)).astype(jnp.float32)]
                else:
                    terms = [state, *pair]
                bias_row = params[0]["small"][0][7:8]
                done = attention_forward(
                    tokens, terms, bias_row, layer == 1, weights, rows, q_bias, v_bias
                )
                one["u"], one["n1"], one["saved"], part = done[0], done[1], done[2:7], done[7]
                pair, ready = [part], [part]
            elif kind == 1:
                one["up"] = weights
                one["mid"], one["n2"], one["slope"], one["hidden"] = up_forward(
                    [one["u"], *pair], weights, rows, up_bias
                )
                pair, ready = None, [one["hidden"]]
            else:
                one["down"] = weights
                state = one["mid"]
                part = contract_wide(one["hidden"], weights)
                pair, ready = [part], [part]
        if r <= number:
            count = len(ready)
            extras = list(ready)
            if 0 <= r - 1 < number:
                if ready:
                    done = tie(near[r - 1] + extras, [])
                    near[r - 1], extras = done[: len(near[r - 1])], done[len(near[r - 1]) :]
                far[r - 1] = exchange_two(*halves[r - 1], *near[r - 1])
                tied += near[r - 1] + far[r - 1]
            if r <= 1:
                extras += blocks_in
            if r == 1:
                extras += [v for layer in range(2) for v in smalls[layer]]
            if r >= number - 1:
                extras += blocks_cot
            if r + 1 < number:
                extras.append(columns[r + 1])
            done = tie(tied + extras, [])
            if r + 1 < number:
                columns[r + 1] = done.pop()
            if r == 1:
                done, smalls = done[:-8], done[-8:]
                params[0]["small"], params[1]["small"] = smalls[:4], smalls[4:]
            if r <= 1:
                done, blocks_in = done[:-n_tensor], done[-n_tensor:]
            if r >= number - 1:
                done, blocks_cot = done[:-n_tensor], done[-n_tensor:]
            if count and kind == 1:
                one["hidden"] = done[-1]
            elif count:
                pair = [done[-1]]
            at = 0
            if r < number:
                halves[r] = (done[0][:mid], done[0][mid:depth])
                if r == 0:
                    extra_rows = done[0][depth:]
                at = 1
            if 0 <= r - 1 < number:
                near[r - 1] = done[at : at + 2]
                far[r - 1] = done[at + 2 : at + 2 + len(far[r - 1])]
    cotangent = whole_image(image_half(blocks_cot)).astype(jnp.float32) * live
    pair = [pair[0], swap(pair[0])]
    last_rows = params[1]["small"][0]
    out_blocks = image_rows(live, [state, *pair], last_rows[7:8])

    sums = [dict(), dict()]

    def small_grads():
        packed = []
        for layer in range(2):
            total = sums[layer]
            full = jnp.concatenate([total["one"], total["mid"], total["out"]], 0)
            full = absolute(jnp.where(core == layer, full, 0.0), spot)
            q_row = spread_cols(core, total["q"][0], n_tensor)
            v_row = spread_cols(core, total["v"][0], n_tensor)
            up_row = spread_cols(core, total["up_bias"][0], n_tensor)
            rows = jnp.concatenate([full[:2], q_row[None], v_row[None], full[2:]], 0)
            rows = rows.reshape(8, n_tensor, n_dp, -1).transpose(2, 1, 0, 3).reshape(n_dp, n_tensor, -1)
            up_row = up_row.reshape(n_tensor, n_dp, -1).transpose(1, 0, 2)
            packed.append(jnp.concatenate([rows, up_row], -1))
        ours = jnp.where(is_first, packed[0], packed[1])
        other = swap(jnp.where(is_first, packed[1], packed[0]))
        little = (ours + other).astype(jnp.bfloat16)
        return little

    grads, got, moved, settled = [None] * number, [None] * number, [None] * number, [None] * number
    made = [0, 1, 2, 4, 5, 6]
    grad = cotangent
    for r in range(8):
        layer, stage = 1 - r // 4, r % 4
        one, total = params[layer], sums[layer]
        rows = one["small"][0]
        tied, slots = [], []
        for c in range(number):
            if r == made[c] + 1:
                got[c] = scatter_one(*grads[c][:2])
                slots.append((got, c, len(got[c])))
                tied += got[c]
            elif r == made[c] + 2:
                stay, come = scatter_two(*grads[c][2:], got[c])
                moved[c] = [*stay, *come]
                if r < 7:
                    slots.append((moved, c, len(moved[c])))
                    tied += moved[c]
            elif r == made[c] + 3:
                settled[c] = scatter_column(moved[c][:2], moved[c][2:])
                slots.append((settled, c, 0))
                tied.append(settled[c])
        new = None
        if stage == 0:
            low, total["out"], total["up_bias"], new = down_backward(
                grad, one["hidden"], one["slope"], one["down"]
            )
            carry = [low]
        elif stage == 1:
            part = contract_wide(low, one["up"])
            new = up_grad(one["n2"], low)
            carry = [part]
        elif stage == 2:
            done = attention_backward(
                grad, part, swap(part), one["mid"], rows, one["saved"], one["qkvo"]
            )
            dmid, dz, dq, dk, dv, part, total["mid"], total["q"], total["v"] = done
            new = attention_grad(one["n1"], dz, dq, dk, dv, one["saved"][4])
            carry = [part]
        else:
            grad, total["one"] = value_backward(dmid, part, swap(part), one["u"], rows, layer == 1)
            carry = [grad]
            if r == 7:
                one_scale = jnp.ones((), jnp.float32)
                no_bias = jnp.zeros((1, grad.shape[1]), jnp.float32)
                carry = [small_grads(), *shifts(image_rows(one_scale, [grad], no_bias))]
        if new is not None:
            c = made.index(r)
            grads[c] = new
            fresh = [g for g in new if g is not None]
        else:
            fresh = []
        if r == 1:
            out_blocks = shifts(out_blocks)
            carry += out_blocks
        if r < 8:
            done = tie(carry + fresh + tied, [])
            if stage == 0:
                low = done[0]
            elif stage == 1:
                part = done[0]
            elif stage == 2:
                part = done[0]
            elif r < 7:
                grad = done[0]
            else:
                little, grad_blocks = done[0], done[1 : 1 + n_tensor]
            if r == 1:
                out_blocks = done[1 : 1 + n_tensor]
            done = done[len(carry) :]
            if fresh:
                grads[c] = fill(done[: len(fresh)])
                done = done[len(fresh) :]
            for store, at, count in slots:
                store[at] = done[:count] if count else done[0]
                done = done[max(count, 1) :]

    grad_rows, out_rows = by_image(grad_blocks), by_image(out_blocks)
    room = jnp.zeros((n_dp, n_tensor, extra * wide - small_size), little.dtype)
    little = jnp.concatenate([little, room], -1).reshape(n_dp, n_tensor, extra, wide)
    little = by_arrival(little.transpose(0, 2, 1, 3).reshape(n_dp, extra, -1), spot)
    if n_dp != 4:
        little = lax.psum_scatter(little, "dp", scatter_dimension=0, tiled=True)[0]
    else:
        little = add(little[:2], swap_x(little[2:])).astype(jnp.bfloat16)
        little = add(little[0], swap_y(little[1])).astype(jnp.bfloat16)

    last = number - 1
    settled[last - 1] = scatter_column(moved[last - 1][:2], moved[last - 1][2:])
    stay, come = scatter_two(*grads[last][2:], got[last])
    if come:
        stay = [add(s, c).astype(jnp.bfloat16) for s, c in zip(stay, come)]
    settled[last] = scatter_column([*stay, little], [])
    little = settled[last][depth:].reshape(-1).astype(jnp.float32)
    settled[last] = settled[last][:depth]
    grad_vectors = little[:n_vec].reshape(vectors.shape)
    grad_bias = little[n_vec:small_size].reshape(fc1_bias.shape)

    own = jnp.where(is_first, grad_rows, out_rows)
    other = swap(jnp.where(is_first, out_rows, grad_rows))
    ends = [jnp.where(is_first, own, other), jnp.where(is_first, other, own)]
    boundary_out = jnp.concatenate(ends, 1)[:, :tokens].astype(jnp.float32)[None]
    lows, highs = [], []
    for kind in range(3):
        first, second = settled[last - kind], settled[last - kind - 3]
        kept = jnp.where(is_first, first, second)
        received = swap(jnp.where(is_first, second, first))
        lows.append(jnp.where(is_first, kept, received).astype(jnp.float32))
        highs.append(jnp.where(is_first, received, kept).astype(jnp.float32))
    low, high = [part[0].reshape(depth, 4, -1) for part in (lows, highs)]
    grad_qkv = jnp.concatenate([low[:, :3], high[:, :3]], 2)[None]
    grad_proj = jnp.concatenate([low[:, 3].T, high[:, 3].T], 0)[None]
    grad_up = jnp.concatenate([lows[1], highs[1]], 1)[None]
    grad_down = jnp.concatenate([lows[2].T, highs[2].T], 0)[None]
    return (boundary_out, grad_qkv, grad_proj, grad_up, grad_down, grad_vectors, grad_bias)


def solution(mesh):
    in_specs = (
        P("section", "dp", None, "tensor"),
        P("dp", None),
        P("section", "dp", None, "tensor"),
        P("section", "tensor", "dp"),
        P("section", "dp", "tensor"),
        P("section", "tensor", "dp"),
        P("section", None, "tensor", "dp"),
        P("section", "tensor", "dp"),
    )
    out_specs = (
        P("section", "dp", None, "tensor"),
        P("section", "dp", None, "tensor"),
        P("section", "tensor", "dp"),
        P("section", "dp", "tensor"),
        P("section", "tensor", "dp"),
        P("section", None, "tensor", "dp"),
        P("section", "tensor", "dp"),
    )
    return jax.shard_map(body, mesh=mesh, in_specs=in_specs, out_specs=out_specs, check_vma=False)
```

```python
import jax
import jax.numpy as jnp
from jax import lax
from jax.experimental import pallas as pl
from jax.experimental.pallas import tpu as pltpu
from jax.sharding import PartitionSpec as P

HD = 64
EPS = 1e-06


def swap(value):
    return lax.ppermute(value, "section", [(0, 1), (1, 0)])


def pair_sum(partial):
    low = partial.astype(jnp.bfloat16)
    return low.astype(jnp.float32) + swap(low).astype(jnp.float32)


def swap_x(value):
    n = lax.axis_size("dp")
    return lax.ppermute(value, "dp", [(i, i ^ 1) for i in range(n)])


def swap_y(value):
    n = lax.axis_size("dp")
    return lax.ppermute(value, "dp", [(i, i ^ 2) for i in range(n)])


def tie(values, others):
    count = len(values)

    def kernel(*refs):
        pass

    anywhere = pl.BlockSpec(memory_space=pl.ANY)
    done = pl.pallas_call(
        kernel,
        out_shape=[jax.ShapeDtypeStruct(v.shape, v.dtype) for v in values],
        in_specs=[anywhere] * (count + len(others)),
        out_specs=[anywhere] * count,
        input_output_aliases={i: i for i in range(count)},
    )(*values, *others)
    return list(done)


def gather_column(shard):
    return lax.all_gather(shard, "tensor", axis=1, tiled=True)


def exchange_one(first, second):
    if lax.axis_size("dp") != 4:
        return [lax.all_gather(v, "dp", axis=0, tiled=True) for v in (first, second)]
    return [swap_y(first), swap_x(second)]


def exchange_two(first, second, near_first, near_second):
    if lax.axis_size("dp") != 4:
        return []
    return [swap_x(first), swap_x(near_first), swap_y(second), swap_y(near_second)]


def arrived(first, second, near, far):
    if lax.axis_size("dp") != 4:
        return ([near[0]], [near[1]])
    return ([first, near[0], far[0], far[1]], [second, near[1], far[2], far[3]])


def row_cuts(depth):
    half = depth // 2
    if lax.axis_size("dp") != 4:
        return [(0, half), (half, depth), None, None]
    part = half // 2
    return [(part, half), (half + part, depth), (0, part), (half, half + part)]


def add(left, right):
    return left.astype(jnp.float32) + right.astype(jnp.float32)


def scatter_one(send_first, send_second):
    if lax.axis_size("dp") != 4:
        return [
            lax.psum_scatter(v, "dp", scatter_dimension=0, tiled=True)
            for v in (send_first, send_second)
        ]
    return [swap_x(send_first), swap_y(send_second)]


def scatter_two(keep_first, keep_second, got):
    if lax.axis_size("dp") != 4:
        return (got, [])
    stay, come = [], []
    for keep, new, far in zip((keep_first, keep_second), got, (swap_y, swap_x)):
        half = keep.shape[0] // 2
        come.append(far(add(keep[half:], new[half:]).astype(jnp.bfloat16)))
        stay.append(add(keep[:half], new[:half]).astype(jnp.bfloat16))
    return (stay, come)


def scatter_column(stay, come):
    if come:
        stay = [add(s, c).astype(jnp.bfloat16) for s, c in zip(stay, come)]
    return lax.psum_scatter(
        jnp.concatenate(stay, 0), "tensor", scatter_dimension=1, tiled=True
    )


def flip_axis(value, axis, bit):
    return jnp.where(bit == 1, jnp.flip(value, axis), value)


def relative(value, spot):
    n_dp = lax.axis_size("dp")
    lead = value.shape[:-1]
    k = len(lead)
    if n_dp != 4:
        cut = value.reshape(lead + (n_dp, 2, -1))
        return jnp.swapaxes(cut, k, k + 1).reshape(value.shape)
    cut = value.reshape(lead + (2, 2, 2, -1))
    cut = flip_axis(flip_axis(cut, k, spot // 2), k + 1, spot % 2)
    first = jnp.swapaxes(cut[..., 0, :], k, k + 1)
    second = cut[..., 1, :]
    return jnp.concatenate([first.reshape(lead + (-1,)), second.reshape(lead + (-1,))], -1)


def absolute(value, spot):
    n_dp = lax.axis_size("dp")
    lead = value.shape[:-1]
    k = len(lead)
    if n_dp != 4:
        cut = value.reshape(lead + (2, n_dp, -1))
        return jnp.swapaxes(cut, k, k + 1).reshape(value.shape)
    cut = value.reshape(lead + (2, 2, 2, -1))
    first = jnp.swapaxes(cut[..., 0, :, :, :], k, k + 1)
    second = cut[..., 1, :, :, :]
    cut = jnp.stack([first, second], k + 2)
    cut = flip_axis(flip_axis(cut, k, spot // 2), k + 1, spot % 2)
    return cut.reshape(value.shape)


def by_chip(blocks, spot):
    n_dp = lax.axis_size("dp")
    if n_dp != 4:
        return blocks
    cut = blocks.reshape((2, 2) + blocks.shape[1:])
    cut = jnp.swapaxes(cut, 0, 1)
    cut = flip_axis(flip_axis(cut, 0, spot // 2), 1, spot % 2)
    return cut.reshape(blocks.shape)


def by_arrival(blocks, spot):
    n_dp = lax.axis_size("dp")
    if n_dp != 4:
        return blocks
    cut = blocks.reshape((2, 2) + blocks.shape[1:])
    cut = flip_axis(flip_axis(cut, 0, spot // 2), 1, spot % 2)
    return jnp.swapaxes(cut, 0, 1).reshape(blocks.shape)


VMEM_BYTES = 50 * 2**20
BF = jnp.bfloat16
F32 = jnp.float32


def shape(dims, kind=jnp.bfloat16):
    return jax.ShapeDtypeStruct(dims, kind)


def run(kernel, outs, ins):
    block = pl.BlockSpec(memory_space=pltpu.VMEM)
    done = pl.pallas_call(
        kernel,
        out_shape=list(outs),
        in_specs=[block] * len(ins),
        out_specs=[block] * len(outs),
        cost_estimate=pl.CostEstimate(flops=1, bytes_accessed=1, transcendentals=0),
        compiler_params=pltpu.CompilerParams(vmem_limit_bytes=VMEM_BYTES),
    )(*ins)
    return list(done)


def nn(left, right):
    return lax.dot_general(left, right, (((1,), (0,)), ((), ())), preferred_element_type=F32)


def nt(left, right):
    return lax.dot_general(left, right, (((1,), (1,)), ((), ())), preferred_element_type=F32)


def tn(left, right):
    return lax.dot_general(left, right, (((0,), (0,)), ((), ())), preferred_element_type=F32)


def stack_rows(pieces, counts, cols):
    return jnp.concatenate([p[:n, cols] for p, n in zip(pieces, counts)], 0)


def center_scale(value):
    center = jnp.mean(value, -1, keepdims=True)
    spread = jnp.mean(value * value, -1, keepdims=True) - center * center
    factor = lax.rsqrt(spread + EPS)
    return ((value - center) * factor, factor)


def norm_backward(grad_normed, centred, factor, gain):
    scaled = grad_normed * gain
    return factor * (
        scaled
        - jnp.mean(scaled, -1, keepdims=True)
        - centred * jnp.mean(scaled * centred, -1, keepdims=True)
    )


def column_sum(value):
    return jnp.sum(value, 0, keepdims=True)


def attention_forward(tokens, terms, bias_row, low, weights, rows, q_bias, v_bias):
    pieces, counts = weights
    size, depth = terms[0].shape
    wide = pieces[0].shape[1]
    groups = wide // 512
    half = groups * 128
    n_terms, n_pieces = len(terms), len(pieces)

    def kernel(*refs):
        term_refs, refs = refs[:n_terms], refs[n_terms:]
        bias_ref, rows_ref, qb_ref, vb_ref = refs[:4]
        piece_refs, refs = refs[4 : 4 + n_pieces], refs[4 + n_pieces :]
        u_ref, n_ref, q_ref, k_ref, v_ref, p_ref, o_ref, part_ref = refs
        value = term_refs[0][...].astype(F32)
        for ref in term_refs[1:]:
            value = value + ref[...].astype(F32)
        if n_terms > 1:
            value = value + bias_ref[...]
        if low:
            value = value.astype(BF).astype(F32)
        u_ref[...] = value
        centred, factor = center_scale(value)
        n_ref[...] = (centred * rows_ref[0:1] + rows_ref[1:2]).astype(BF)
        lane = lax.broadcasted_iota(jnp.int32, (size, 128), 1)
        key_lane = lax.broadcasted_iota(jnp.int32, (size, size), 1)
        normed = n_ref[...]
        for g in range(groups):
            at = slice(g * 128, (g + 1) * 128)
            matrix = stack_rows(piece_refs, counts, slice(g * 512, g * 512 + 384))
            projected = nn(normed, matrix)
            q = (projected[:, :128] + qb_ref[:, at]).astype(BF)
            k = projected[:, 128:256].astype(BF)
            v = (projected[:, 256:384] + vb_ref[:, at]).astype(BF)
            q_ref[:, at] = q
            k_ref[:, at] = k
            v_ref[:, at] = v
            mixed = None
            for h in range(2):
                mine = (lane // HD) == h
                scores = nt(jnp.where(mine, q, jnp.zeros_like(q)), k) * HD ** (-0.5)
                scores = jnp.where(key_lane < tokens, scores, -1e30)
                highest = jnp.max(scores, -1, keepdims=True)
                exponent = jnp.exp(scores - highest)
                inverse = 1.0 / jnp.sum(exponent, -1, keepdims=True)
                soft = (exponent * inverse).astype(BF)
                p_ref[2 * g + h] = soft
                out = nn(soft, v)
                mixed = out if h == 0 else jnp.where(mine, out, mixed)
            o_ref[:, at] = mixed.astype(BF)
        matrix = jnp.concatenate(
            [stack_rows(piece_refs, counts, slice(g * 512 + 384, g * 512 + 512)) for g in range(groups)], 1
        )
        part_ref[...] = nt(o_ref[...], matrix).astype(BF)

    outs = [shape((size, depth), F32), shape((size, depth))] + [shape((size, half))] * 3
    outs += [shape((2 * groups, size, size)), shape((size, half)), shape((size, depth))]
    return run(kernel, outs, [*terms, bias_row, rows, q_bias, v_bias, *pieces])


def up_forward(terms, weights, rows, up_bias):
    pieces, counts = weights
    size, depth = terms[0].shape
    wide = pieces[0].shape[1]

    def kernel(*refs):
        u_ref, own_ref, far_ref, rows_ref, bias_ref = refs[:5]
        piece_refs = refs[5 : 5 + len(pieces)]
        mid_ref, n_ref, slope_ref, hidden_ref = refs[5 + len(pieces) :]
        value = u_ref[...] + own_ref[...].astype(F32) + far_ref[...].astype(F32) + rows_ref[4:5]
        mid_ref[...] = value
        centred, factor = center_scale(value)
        n_ref[...] = (centred * rows_ref[5:6] + rows_ref[6:7]).astype(BF)
        step = 512
        for at in range(0, wide, step):
            cols = slice(at, at + step)
            before = nn(n_ref[...], stack_rows(piece_refs, counts, cols)) + bias_ref[:, cols]
            cdf = 0.5 * (1.0 + lax.erf(before * 0.7071067811865476))
            density = jnp.exp(-0.5 * before * before) * 0.3989422804014327
            hidden_ref[:, cols] = (before * cdf).astype(BF)
            slope_ref[:, cols] = (cdf + before * density).astype(BF)

    outs = [shape((size, depth), F32), shape((size, depth)), shape((size, wide)), shape((size, wide))]
    return run(kernel, outs, [*terms, rows, up_bias, *pieces])


def contract_wide(left, weights):
    pieces, counts = weights
    size, wide = left.shape
    depth = sum(counts)

    def kernel(*refs):
        left_ref, piece_refs, out_ref = refs[0], refs[1:-1], refs[-1]
        matrix = stack_rows(piece_refs, counts, slice(0, wide))
        out_ref[...] = nt(left_ref[...], matrix).astype(BF)

    return run(kernel, [shape((size, depth))], [left, *pieces])[0]


def weight_outs(depth, wide):
    cuts = [c for c in row_cuts(depth) if c is not None]
    return cuts, [shape((c[1] - c[0], wide)) for c in cuts]


def fill(grads):
    return (list(grads) + [None, None])[:4]


def down_backward(grad_out, hidden, slope, weights):
    pieces, counts = weights
    size, depth = grad_out.shape
    wide = hidden.shape[1]
    cuts, grad_outs = weight_outs(depth, wide)

    def kernel(*refs):
        g_ref, hidden_ref, slope_ref = refs[:3]
        piece_refs, refs = refs[3 : 3 + len(pieces)], refs[3 + len(pieces) :]
        low_ref, sum_ref, bias_ref = refs[:3]
        sum_ref[...] = column_sum(g_ref[...])
        branch = g_ref[...].astype(BF)
        for cut, ref in zip(cuts, refs[3:]):
            ref[...] = tn(branch[:, cut[0] : cut[1]], hidden_ref[...]).astype(BF)
        step = 512
        for at in range(0, wide, step):
            cols = slice(at, at + step)
            back = nn(branch, stack_rows(piece_refs, counts, cols)) * slope_ref[:, cols].astype(F32)
            bias_ref[:, cols] = column_sum(back)
            low_ref[:, cols] = back.astype(BF)

    outs = [shape((size, wide)), shape((1, depth), F32), shape((1, wide), F32)] + grad_outs
    done = run(kernel, outs, [grad_out, hidden, slope, *pieces])
    return done[0], done[1], done[2], fill(done[3:])


def up_grad(normed, low):
    size, depth = normed.shape
    wide = low.shape[1]
    cuts, outs = weight_outs(depth, wide)

    def kernel(n_ref, low_ref, *refs):
        for cut, ref in zip(cuts, refs):
            ref[...] = tn(n_ref[:, cut[0] : cut[1]], low_ref[...]).astype(BF)

    return fill(run(kernel, outs, [normed, low]))


def attention_backward(grad_out, own, far, middle, rows, saved, weights):
    pieces, counts = weights
    size, depth = grad_out.shape
    wide = pieces[0].shape[1]
    groups = wide // 512
    half = groups * 128
    scale = HD ** (-0.5)

    def kernel(*refs):
        g_ref, own_ref, far_ref, mid_ref, rows_ref, q_ref, k_ref, v_ref, p_ref, o_ref = refs[:10]
        piece_refs, refs = refs[10 : 10 + len(pieces)], refs[10 + len(pieces) :]
        dmid_ref, dz_ref, dq_ref, dk_ref, dv_ref, part_ref, sum_ref, qs_ref, vs_ref = refs
        grad_normed = own_ref[...].astype(F32) + far_ref[...].astype(F32)
        centred, factor = center_scale(mid_ref[...])
        sum_ref[1:2] = column_sum(grad_normed * centred)
        sum_ref[2:3] = column_sum(grad_normed)
        dmid = g_ref[...] + norm_backward(grad_normed, centred, factor, rows_ref[5:6])
        dmid_ref[...] = dmid
        sum_ref[0:1] = column_sum(dmid)
        dz_ref[...] = dmid.astype(BF)
        lane = lax.broadcasted_iota(jnp.int32, (size, 128), 1)
        for g in range(groups):
            at = slice(g * 128, (g + 1) * 128)
            matrix = stack_rows(piece_refs, counts, slice(g * 512 + 384, g * 512 + 512))
            grad_mixed = nn(dz_ref[...], matrix).astype(BF)
            q, k, v = q_ref[:, at], k_ref[:, at], v_ref[:, at]
            inner = grad_mixed.astype(F32) * o_ref[:, at].astype(F32)
            dq, dk, dv = None, None, None
            for h in range(2):
                mine = (lane // HD) == h
                soft = p_ref[2 * g + h]
                none = jnp.zeros_like(q)
                do = jnp.where(mine, grad_mixed, none)
                total = jnp.sum(jnp.where(mine, inner, 0.0), -1, keepdims=True)
                grad_soft = nt(do, v)
                grad_scores = (soft.astype(F32) * (grad_soft - total)).astype(BF)
                new_q = nn(grad_scores, k)
                new_k = tn(jnp.where(mine, q, none), grad_scores)
                new_v = tn(do, soft)
                dq = new_q if h == 0 else jnp.where(mine, new_q, dq)
                dk = new_k if h == 0 else dk + new_k
                dv = new_v if h == 0 else dv + new_v
            dq, dk, dv = dq * scale, dk.T * scale, dv.T
            qs_ref[:, at] = column_sum(dq)
            vs_ref[:, at] = column_sum(dv)
            dq_ref[:, at] = dq.astype(BF)
            dk_ref[:, at] = dk.astype(BF)
            dv_ref[:, at] = dv.astype(BF)
        total = None
        for g in range(groups):
            at = slice(g * 128, (g + 1) * 128)
            left = jnp.concatenate([dq_ref[:, at], dk_ref[:, at], dv_ref[:, at]], 1)
            new = nt(left, stack_rows(piece_refs, counts, slice(g * 512, g * 512 + 384)))
            total = new if g == 0 else total + new
        part_ref[...] = total.astype(BF)

    outs = [shape((size, depth), F32), shape((size, depth))] + [shape((size, half))] * 3
    outs += [shape((size, depth)), shape((3, depth), F32)] + [shape((1, half), F32)] * 2
    return run(kernel, outs, [grad_out, own, far, middle, rows, *saved, *pieces])


def attention_grad(normed, dz, dq, dk, dv, mixed):
    size, depth = normed.shape
    groups = dq.shape[1] // 128
    cuts, outs = weight_outs(depth, groups * 512)

    def kernel(n_ref, dz_ref, dq_ref, dk_ref, dv_ref, o_ref, *refs):
        for cut, ref in zip(cuts, refs):
            rows = slice(cut[0], cut[1])
            for g in range(groups):
                at = slice(g * 128, (g + 1) * 128)
                right = jnp.concatenate([dq_ref[:, at], dk_ref[:, at], dv_ref[:, at]], 1)
                ref[:, g * 512 : g * 512 + 384] = tn(n_ref[:, rows], right).astype(BF)
                ref[:, g * 512 + 384 : g * 512 + 512] = tn(dz_ref[:, rows], o_ref[:, at]).astype(BF)

    return fill(run(kernel, outs, [normed, dz, dq, dk, dv, mixed]))


def value_backward(dmid, own, far, value, rows, low):
    size, depth = dmid.shape

    def kernel(dmid_ref, own_ref, far_ref, u_ref, rows_ref, out_ref, sum_ref):
        grad_normed = own_ref[...].astype(F32) + far_ref[...].astype(F32)
        centred, factor = center_scale(u_ref[...])
        sum_ref[0:1] = column_sum(grad_normed * centred)
        sum_ref[1:2] = column_sum(grad_normed)
        out = dmid_ref[...] + norm_backward(grad_normed, centred, factor, rows_ref[0:1])
        if low:
            out = out.astype(BF).astype(F32)
        out_ref[...] = out

    outs = [shape((size, depth), F32), shape((2, depth), F32)]
    return run(kernel, outs, [dmid, own, far, value, rows])


def block_lanes(spot, chunk):
    ry, rx = chunk // 2 ^ spot // 2, chunk % 2 ^ spot % 2
    return [(rx * 2 + ry) * 128, 512 + (ry * 2 + rx) * 128]


def place_in(lanes, blocks):
    size, width = blocks[0].shape
    half = width // 2

    def kernel(lanes_ref, *refs):
        out_ref = refs[-1]
        for d, ref in enumerate(refs[:-1]):
            for h in range(2):
                at = pl.multiple_of(lanes_ref[2 * d + h], 128)
                out_ref[:, pl.ds(at, half)] = ref[:, h * half : (h + 1) * half]

    block = pl.BlockSpec(memory_space=pltpu.VMEM)
    return pl.pallas_call(
        kernel,
        out_shape=shape((size, width * len(blocks))),
        in_specs=[pl.BlockSpec(memory_space=pltpu.SMEM)] + [block] * len(blocks),
        out_specs=block,
        compiler_params=pltpu.CompilerParams(vmem_limit_bytes=VMEM_BYTES),
    )(lanes, *blocks)


def place_out(numbers, scale, terms, bias_row, count):
    size, depth = terms[0].shape
    width = depth // count
    half = width // 2

    def kernel(numbers_ref, scale_ref, *refs):
        term_refs, bias_ref, out_ref = refs[: len(terms)], refs[-2], refs[-1]
        start = pl.multiple_of(numbers_ref[2 * count], 8)
        rows = pl.ds(start, size // 2)
        for d in range(count):
            for h in range(2):
                lanes = pl.ds(pl.multiple_of(numbers_ref[2 * d + h], 128), half)
                value = term_refs[0][rows, lanes]
                for ref in term_refs[1:]:
                    value = value + ref[rows, lanes]
                value = (value + bias_ref[:, lanes]) * scale_ref[0]
                out_ref[d, :, h * half : (h + 1) * half] = value.astype(BF)

    block = pl.BlockSpec(memory_space=pltpu.VMEM)
    scalar = pl.BlockSpec(memory_space=pltpu.SMEM)
    return pl.pallas_call(
        kernel,
        out_shape=shape((count, size // 2, width)),
        in_specs=[scalar, scalar] + [block] * (len(terms) + 1),
        out_specs=block,
        compiler_params=pltpu.CompilerParams(vmem_limit_bytes=VMEM_BYTES),
    )(numbers, scale, *terms, bias_row)


def shifts(blocks):
    n = lax.axis_size("tensor")
    out = [blocks[0]]
    for d in range(1, n):
        out.append(lax.ppermute(blocks[d], "tensor", [(i, (i + d) % n) for i in range(n)]))
    return out


def half_cols(core, whole, n_tensor):
    cut = whole.reshape(whole.shape[:-1] + (n_tensor, 2, -1))
    cut = jnp.where(core == 0, cut[..., 0, :], cut[..., 1, :])
    return cut.reshape(whole.shape[:-1] + (-1,))


def spread_cols(core, half, n_tensor):
    cut = half.reshape(half.shape[:-1] + (n_tensor, 1, -1))
    none = jnp.zeros_like(cut)
    both = jnp.concatenate(
        [jnp.where(core == 0, cut, none), jnp.where(core == 0, none, cut)], -2
    )
    return both.reshape(half.shape[:-1] + (-1,))


def body(boundary_in, counts, qkv_weight, proj_weight, fc1_weight, fc2_weight, vectors, fc1_bias):
    core = lax.axis_index("section")
    is_first = core == 0
    place = lax.axis_index("tensor")
    spot = lax.axis_index("dp")
    n_dp, n_tensor = lax.axis_size("dp"), lax.axis_size("tensor")
    slots_per_batch = boundary_in.shape[1] // counts.shape[1]
    live = (place % slots_per_batch < counts[0, place // slots_per_batch]).astype(jnp.float32)
    depth = qkv_weight.shape[1]
    mid = depth // 2
    n_vec = vectors.size

    small_size = n_vec + fc1_bias.size
    packs = []
    for part in range(2):
        cuts = [
            jnp.split(qkv_weight[0], 2, 2)[part].reshape(depth, -1),
            jnp.split(proj_weight[0], 2, 0)[part].T,
            jnp.split(fc1_weight[0], 2, 1)[part],
            jnp.split(fc2_weight[0], 2, 0)[part].T,
        ]
        packs.append(jnp.concatenate(cuts, 1))
    wide = packs[0].shape[1] // 3
    extra = 16
    small = jnp.concatenate([vectors.reshape(-1), fc1_bias.reshape(-1)])
    small = jnp.pad(small, (0, extra * wide - small_size)).reshape(extra, wide)
    small = jnp.pad(small, ((0, 0), (0, 2 * wide)))
    kept = jnp.concatenate([jnp.where(is_first, packs[0], packs[1]), small], 0)
    received = swap(
        jnp.concatenate([jnp.where(is_first, packs[1], packs[0]), small], 0)
    )
    shards = (jnp.where(is_first, kept, received), jnp.where(is_first, received, kept))
    columns = []
    for layer in range(2):
        for number in range(3):
            cols = shards[layer][:, number * wide : (number + 1) * wide]
            if layer == 0 and number == 0:
                room = extra // 2
                both = [shard[depth : depth + room, :wide] for shard in shards]
                cols = jnp.concatenate([cols[:depth], *both], 0)
            else:
                cols = cols[:depth]
            columns.append(cols)

    tokens = boundary_in.shape[2]
    pad = -tokens % 16
    reach = (tokens + pad) // 2
    ends_in = jnp.pad(boundary_in[0].astype(jnp.bfloat16), ((0, 0), (0, pad), (0, 0)))
    ends_low, ends_high = ends_in[:, :reach], ends_in[:, reach:]
    ends_got = swap(jnp.where(is_first, ends_high, ends_low))
    half_in = jnp.where(is_first, ends_low, ends_got)
    half_cot = jnp.where(is_first, ends_got, ends_high)

    below = [(place - d) % n_tensor for d in range(n_tensor)]
    above = [(place + d) % n_tensor for d in range(n_tensor)]

    def to_send(half):
        return [lax.dynamic_index_in_dim(half, j, 0, False) for j in above]

    def image_half(blocks):
        if n_dp == 4:
            lanes = [lane for t in below for lane in block_lanes(spot, t)]
            return place_in(jnp.stack(lanes).astype(jnp.int32), blocks)
        blocks = jnp.stack(blocks)
        blocks = [lax.dynamic_index_in_dim(blocks, (place - i) % n_tensor, 0, False) for i in range(n_tensor)]
        return relative(jnp.concatenate(blocks, 1), spot)

    def whole_image(half):
        other = swap(half)
        both = [jnp.where(is_first, half, other), jnp.where(is_first, other, half)]
        return jnp.concatenate(both, 0)

    def image_rows(scale, terms, bias_row):
        if n_dp == 4:
            numbers = [lane for t in above for lane in block_lanes(spot, t)]
            numbers.append(jnp.where(is_first, 0, reach))
            numbers = jnp.stack(numbers).astype(jnp.int32)
            blocks = place_out(numbers, scale.reshape(1), terms, bias_row, n_tensor)
            return [blocks[d] for d in range(n_tensor)]
        image = absolute((sum(terms[1:], terms[0]) + bias_row) * scale, spot).astype(jnp.bfloat16)
        half = jnp.where(is_first, image[:reach], image[reach:])
        half = half.reshape(reach, n_tensor, -1).transpose(1, 0, 2)
        return to_send(half)

    def by_image(blocks):
        blocks = jnp.stack(blocks)
        blocks = [lax.dynamic_index_in_dim(blocks, (place - i) % n_tensor, 0, False) for i in range(n_tensor)]
        return jnp.stack(blocks)

    def small_of(extras):
        if n_dp != 4:
            extras = lax.all_gather(extras, "dp", axis=0, tiled=True)
        else:
            extras = jnp.concatenate([extras, swap_y(extras)], 0)
            extras = jnp.concatenate([extras, swap_x(extras)], 0)
        both = by_chip(extras.reshape(n_dp, extra, -1), spot).astype(jnp.float32)
        both = both.reshape(n_dp, 2, extra // 2, n_tensor, wide).transpose(1, 0, 3, 2, 4)
        both = both.reshape(2, n_dp, n_tensor, -1)
        rows = both[..., :n_vec].reshape(2, n_dp, n_tensor, 8, -1)
        rows = relative(rows.transpose(0, 3, 2, 1, 4).reshape(2, 8, -1), spot)
        bias = both[..., n_vec:small_size].transpose(0, 2, 1, 3).reshape(2, -1)
        plain = both[..., :n_vec].reshape(2, n_dp, n_tensor, 8, -1)[..., 2:4, :]
        plain = plain.transpose(0, 3, 2, 1, 4).reshape(2, 2, -1)
        parts = [half_cols(core, plain[:, 0], n_tensor), half_cols(core, plain[:, 1], n_tensor)]
        parts.append(half_cols(core, bias, n_tensor))
        return [(rows[i], parts[0][i : i + 1], parts[1][i : i + 1], parts[2][i : i + 1]) for i in range(2)]

    number = len(columns)
    halves, near, far = [None] * number, [None] * number, [None] * number
    params = [dict(), dict()]
    blocks_in, blocks_cot = to_send(half_in), to_send(half_cot)
    pair, state = None, None

    def weights_of(k):
        first, second = arrived(*halves[k], near[k], far[k])
        return (first + second, [p.shape[0] for p in first + second])

    for r in range(number + 1):
        tied = []
        if r < number:
            tied.append(gather_column(columns[r]))
        if 0 <= r - 1 < number:
            near[r - 1] = exchange_one(*halves[r - 1])
        if r == 1:
            smalls = small_of(extra_rows)
            blocks_in = shifts(blocks_in)
        if r == number - 2:
            blocks_cot = shifts(blocks_cot)
        if r == number - 1:
            cot_half = image_half(blocks_cot)
        if r == number:
            cotangent = whole_image(cot_half).astype(jnp.float32) * live
        ready = []
        k = r - 2
        if k >= 0:
            layer, kind = k // 3, k % 3
            one = params[layer]
            weights = weights_of(k)
            rows, q_bias, v_bias, up_bias = one["small"]
            if pair is not None:
                pair = [pair[0], swap(pair[0])]
            if kind == 0:
                one["qkvo"] = weights
                if layer == 0:
                    terms = [whole_image(image_half(blocks_in)).astype(jnp.float32)]
                else:
                    terms = [state, *pair]
                bias_row = params[0]["small"][0][7:8]
                done = attention_forward(
                    tokens, terms, bias_row, layer == 1, weights, rows, q_bias, v_bias
                )
                one["u"], one["n1"], one["saved"], part = done[0], done[1], done[2:7], done[7]
                pair, ready = [part], [part]
            elif kind == 1:
                one["up"] = weights
                one["mid"], one["n2"], one["slope"], one["hidden"] = up_forward(
                    [one["u"], *pair], weights, rows, up_bias
                )
                pair, ready = None, [one["hidden"]]
            else:
                one["down"] = weights
                state = one["mid"]
                part = contract_wide(one["hidden"], weights)
                pair, ready = [part], [part]
        if r <= number:
            count = len(ready)
            extras = list(ready)
            if 0 <= r - 1 < number:
                if ready:
                    done = tie(near[r - 1] + extras, [])
                    near[r - 1], extras = done[: len(near[r - 1])], done[len(near[r - 1]) :]
                far[r - 1] = exchange_two(*halves[r - 1], *near[r - 1])
                tied += near[r - 1] + far[r - 1]
            if r <= 1:
                extras += blocks_in
            if r == 1:
                extras += [v for layer in range(2) for v in smalls[layer]]
            if r in (number - 3, number - 2):
                extras += blocks_cot
            elif r == number - 1:
                extras.append(cot_half)
            elif r == number:
                extras.append(cotangent)
            if r + 1 < number:
                extras.append(columns[r + 1])
            done = tie(tied + extras, [])
            if r + 1 < number:
                columns[r + 1] = done.pop()
            if r == 1:
                done, smalls = done[:-8], done[-8:]
                params[0]["small"], params[1]["small"] = smalls[:4], smalls[4:]
            if r <= 1:
                done, blocks_in = done[:-n_tensor], done[-n_tensor:]
            if r in (number - 3, number - 2):
                done, blocks_cot = done[:-n_tensor], done[-n_tensor:]
            elif r == number - 1:
                cot_half = done.pop()
            elif r == number:
                cotangent = done.pop()
            if count and kind == 1:
                one["hidden"] = done[-1]
            elif count:
                pair = [done[-1]]
            at = 0
            if r < number:
                halves[r] = (done[0][:mid], done[0][mid:depth])
                if r == 0:
                    extra_rows = done[0][depth:]
                at = 1
            if 0 <= r - 1 < number:
                near[r - 1] = done[at : at + 2]
                far[r - 1] = done[at + 2 : at + 2 + len(far[r - 1])]

    sums = [dict(), dict()]

    def small_grads():
        packed = []
        for layer in range(2):
            total = sums[layer]
            full = jnp.concatenate([total["one"], total["mid"], total["out"]], 0)
            full = absolute(jnp.where(core == layer, full, 0.0), spot)
            q_row = spread_cols(core, total["q"][0], n_tensor)
            v_row = spread_cols(core, total["v"][0], n_tensor)
            up_row = spread_cols(core, total["up_bias"][0], n_tensor)
            rows = jnp.concatenate([full[:2], q_row[None], v_row[None], full[2:]], 0)
            rows = rows.reshape(8, n_tensor, n_dp, -1).transpose(2, 1, 0, 3).reshape(n_dp, n_tensor, -1)
            up_row = up_row.reshape(n_tensor, n_dp, -1).transpose(1, 0, 2)
            packed.append(jnp.concatenate([rows, up_row], -1))
        ours = jnp.where(is_first, packed[0], packed[1])
        other = swap(jnp.where(is_first, packed[1], packed[0]))
        little = (ours + other).astype(jnp.bfloat16)
        return little

    grads, got, moved, settled = [None] * number, [None] * number, [None] * number, [None] * number
    made = [0, 1, 2, 4, 5, 6]
    grad = cotangent
    last_down = weights_of(number - 1)
    params[1]["down"] = last_down
    last_bias = params[1]["small"][0][7:8]
    for r in range(8):
        layer, stage = 1 - r // 4, r % 4
        one, total = params[layer], sums[layer]
        rows = one["small"][0]
        tied, slots = [], []
        for c in range(number):
            if r == made[c] + 1 and c != 2:
                got[c] = scatter_one(*grads[c][:2])
                slots.append((got, c, len(got[c])))
                tied += got[c]
            elif r == made[c] + 2:
                stay, come = scatter_two(*grads[c][2:], got[c])
                moved[c] = [*stay, *come]
                if r < 7:
                    slots.append((moved, c, len(moved[c])))
                    tied += moved[c]
            elif r == made[c] + 3:
                settled[c] = scatter_column(moved[c][:2], moved[c][2:])
                slots.append((settled, c, 0))
                tied.append(settled[c])
        new, made_now = None, None
        if stage == 0:
            low, total["out"], total["up_bias"], new = down_backward(
                grad, one["hidden"], one["slope"], one["down"]
            )
            carry = [low]
        elif stage == 1:
            part = contract_wide(low, one["up"])
            new = up_grad(one["n2"], low)
            carry = [part]
        elif stage == 2:
            done = attention_backward(
                grad, part, swap(part), one["mid"], rows, one["saved"], one["qkvo"]
            )
            dmid, dz, dq, dk, dv, part, total["mid"], total["q"], total["v"] = done
            if layer == 0:
                new = attention_grad(one["n1"], dz, dq, dk, dv, one["saved"][4])
            carry = [part]
        else:
            if layer == 1:
                made_now = attention_grad(one["n1"], dz, dq, dk, dv, one["saved"][4])
                got[2] = scatter_one(*made_now[:2])
                slots.append((got, 2, len(got[2])))
                tied += got[2]
            grad, total["one"] = value_backward(dmid, part, swap(part), one["u"], rows, layer == 1)
            carry = [grad]
            if r == 7:
                one_scale = jnp.ones((), jnp.float32)
                no_bias = jnp.zeros((1, grad.shape[1]), jnp.float32)
                carry = [small_grads()]
                grad_blocks = shifts(image_rows(one_scale, [grad], no_bias))
        if made_now is not None:
            c, grads[2] = 2, made_now
            fresh = [g for g in made_now[2:] if g is not None]
        elif new is not None:
            c = made.index(r)
            grads[c] = new
            fresh = [g for g in new if g is not None]
        else:
            fresh = []
        if r == 3:
            last_part = contract_wide(params[1]["hidden"], last_down)
            carry.append(last_part)
        elif r == 4:
            out_blocks = shifts(image_rows(
                live, [params[1]["mid"], last_part, swap(last_part)], last_bias
            ))
            carry += out_blocks
        if r < 8:
            done = tie(carry + fresh + tied, [])
            if stage == 0:
                low = done[0]
            elif stage == 1:
                part = done[0]
            elif stage == 2:
                part = done[0]
            elif r < 7:
                grad = done[0]
            else:
                little = done[0]
            if r == 3:
                last_part = done[1]
            elif r == 4:
                out_blocks = done[1 : 1 + n_tensor]
            done = done[len(carry) :]
            if made_now is not None:
                grads[c][2 : 2 + len(fresh)] = done[: len(fresh)]
                done = done[len(fresh) :]
            elif fresh:
                grads[c] = fill(done[: len(fresh)])
                done = done[len(fresh) :]
            for store, at, count in slots:
                store[at] = done[:count] if count else done[0]
                done = done[max(count, 1) :]

    room = jnp.zeros((n_dp, n_tensor, extra * wide - small_size), little.dtype)
    little = jnp.concatenate([little, room], -1).reshape(n_dp, n_tensor, extra, wide)
    little = by_arrival(little.transpose(0, 2, 1, 3).reshape(n_dp, extra, -1), spot)
    if n_dp != 4:
        little = lax.psum_scatter(little, "dp", scatter_dimension=0, tiled=True)[0]
    else:
        little = add(little[:2], swap_x(little[2:])).astype(jnp.bfloat16)
        little = add(little[0], swap_y(little[1])).astype(jnp.bfloat16)

    last = number - 1
    settled[last - 1] = scatter_column(moved[last - 1][:2], moved[last - 1][2:])
    stay, come = scatter_two(*grads[last][2:], got[last])
    done = tie([*grad_blocks, *stay, *come], [])
    grad_blocks, done = done[:n_tensor], done[n_tensor:]
    grad_rows, out_rows = by_image(grad_blocks), by_image(out_blocks)
    stay, come = done[:2], done[2:]
    if come:
        stay = [add(s, c).astype(jnp.bfloat16) for s, c in zip(stay, come)]
    settled[last] = scatter_column([*stay, little], [])
    little = settled[last][depth:].reshape(-1).astype(jnp.float32)
    settled[last] = settled[last][:depth]
    grad_vectors = little[:n_vec].reshape(vectors.shape)
    grad_bias = little[n_vec:small_size].reshape(fc1_bias.shape)

    own = jnp.where(is_first, grad_rows, out_rows)
    other = swap(jnp.where(is_first, out_rows, grad_rows))
    ends = [jnp.where(is_first, own, other), jnp.where(is_first, other, own)]
    boundary_out = jnp.concatenate(ends, 1)[:, :tokens].astype(jnp.float32)[None]
    lows, highs = [], []
    for kind in range(3):
        first, second = settled[last - kind], settled[last - kind - 3]
        kept = jnp.where(is_first, first, second)
        received = swap(jnp.where(is_first, second, first))
        lows.append(jnp.where(is_first, kept, received).astype(jnp.float32))
        highs.append(jnp.where(is_first, received, kept).astype(jnp.float32))
    low, high = [part[0].reshape(depth, 4, -1) for part in (lows, highs)]
    grad_qkv = jnp.concatenate([low[:, :3], high[:, :3]], 2)[None]
    grad_proj = jnp.concatenate([low[:, 3].T, high[:, 3].T], 0)[None]
    grad_up = jnp.concatenate([lows[1], highs[1]], 1)[None]
    grad_down = jnp.concatenate([lows[2].T, highs[2].T], 0)[None]
    return (boundary_out, grad_qkv, grad_proj, grad_up, grad_down, grad_vectors, grad_bias)


def solution(mesh):
    in_specs = (
        P("section", "dp", None, "tensor"),
        P("dp", None),
        P("section", "dp", None, "tensor"),
        P("section", "tensor", "dp"),
        P("section", "dp", "tensor"),
        P("section", "tensor", "dp"),
        P("section", None, "tensor", "dp"),
        P("section", "tensor", "dp"),
    )
    out_specs = (
        P("section", "dp", None, "tensor"),
        P("section", "dp", None, "tensor"),
        P("section", "tensor", "dp"),
        P("section", "dp", "tensor"),
        P("section", "tensor", "dp"),
        P("section", None, "tensor", "dp"),
        P("section", "tensor", "dp"),
    )
    return jax.shard_map(body, mesh=mesh, in_specs=in_specs, out_specs=out_specs, check_vma=False)
```

```python
import jax
import jax.numpy as jnp
from jax import lax
from jax.experimental import pallas as pl
from jax.experimental.pallas import tpu as pltpu
from jax.sharding import PartitionSpec as P

HD = 64
EPS = 1e-06


def swap(value):
    return lax.ppermute(value, "section", [(0, 1), (1, 0)])


def pair_sum(partial):
    low = partial.astype(jnp.bfloat16)
    return low.astype(jnp.float32) + swap(low).astype(jnp.float32)


def swap_x(value):
    n = lax.axis_size("dp")
    return lax.ppermute(value, "dp", [(i, i ^ 1) for i in range(n)])


def swap_y(value):
    n = lax.axis_size("dp")
    return lax.ppermute(value, "dp", [(i, i ^ 2) for i in range(n)])


def tie(values, others):
    count = len(values)

    def kernel(*refs):
        pass

    anywhere = pl.BlockSpec(memory_space=pl.ANY)
    done = pl.pallas_call(
        kernel,
        out_shape=[jax.ShapeDtypeStruct(v.shape, v.dtype) for v in values],
        in_specs=[anywhere] * (count + len(others)),
        out_specs=[anywhere] * count,
        input_output_aliases={i: i for i in range(count)},
    )(*values, *others)
    return list(done)


def gather_column(shard):
    return lax.all_gather(shard, "tensor", axis=1, tiled=True)


def exchange_one(first, second):
    if lax.axis_size("dp") != 4:
        return [lax.all_gather(v, "dp", axis=0, tiled=True) for v in (first, second)]
    return [swap_y(first), swap_x(second)]


def exchange_two(first, second, near_first, near_second):
    if lax.axis_size("dp") != 4:
        return []
    return [swap_x(first), swap_x(near_first), swap_y(second), swap_y(near_second)]


def arrived(first, second, near, far):
    if lax.axis_size("dp") != 4:
        return ([near[0]], [near[1]])
    return ([first, near[0], far[0], far[1]], [second, near[1], far[2], far[3]])


def row_cuts(depth):
    half = depth // 2
    if lax.axis_size("dp") != 4:
        return [(0, half), (half, depth), None, None]
    part = half // 2
    return [(part, half), (half + part, depth), (0, part), (half, half + part)]


def add(left, right):
    return left.astype(jnp.float32) + right.astype(jnp.float32)


def scatter_one(send_first, send_second):
    if lax.axis_size("dp") != 4:
        return [
            lax.psum_scatter(v, "dp", scatter_dimension=0, tiled=True)
            for v in (send_first, send_second)
        ]
    return [swap_x(send_first), swap_y(send_second)]


def scatter_two(keep_first, keep_second, got):
    if lax.axis_size("dp") != 4:
        return (got, [])
    stay, send = [], []
    for keep, new in zip((keep_first, keep_second), got):
        half = keep.shape[0] // 2
        send.append(add(keep[half:], new[half:]).astype(jnp.bfloat16))
        stay.append(add(keep[:half], new[:half]).astype(jnp.bfloat16))
    return (stay, [swap_y(send[0]), swap_x(send[1])])


def scatter_column(stay, come):
    if come:
        stay = [add(s, c).astype(jnp.bfloat16) for s, c in zip(stay, come)]
    return lax.psum_scatter(
        jnp.concatenate(stay, 0), "tensor", scatter_dimension=1, tiled=True
    )


def flip_axis(value, axis, bit):
    return jnp.where(bit == 1, jnp.flip(value, axis), value)


def relative(value, spot):
    n_dp = lax.axis_size("dp")
    lead = value.shape[:-1]
    k = len(lead)
    if n_dp != 4:
        cut = value.reshape(lead + (n_dp, 2, -1))
        return jnp.swapaxes(cut, k, k + 1).reshape(value.shape)
    cut = value.reshape(lead + (2, 2, 2, -1))
    cut = flip_axis(flip_axis(cut, k, spot // 2), k + 1, spot % 2)
    first = jnp.swapaxes(cut[..., 0, :], k, k + 1)
    second = cut[..., 1, :]
    return jnp.concatenate([first.reshape(lead + (-1,)), second.reshape(lead + (-1,))], -1)


def absolute(value, spot):
    n_dp = lax.axis_size("dp")
    lead = value.shape[:-1]
    k = len(lead)
    if n_dp != 4:
        cut = value.reshape(lead + (2, n_dp, -1))
        return jnp.swapaxes(cut, k, k + 1).reshape(value.shape)
    cut = value.reshape(lead + (2, 2, 2, -1))
    first = jnp.swapaxes(cut[..., 0, :, :, :], k, k + 1)
    second = cut[..., 1, :, :, :]
    cut = jnp.stack([first, second], k + 2)
    cut = flip_axis(flip_axis(cut, k, spot // 2), k + 1, spot % 2)
    return cut.reshape(value.shape)


def by_chip(blocks, spot):
    n_dp = lax.axis_size("dp")
    if n_dp != 4:
        return blocks
    cut = blocks.reshape((2, 2) + blocks.shape[1:])
    cut = jnp.swapaxes(cut, 0, 1)
    cut = flip_axis(flip_axis(cut, 0, spot // 2), 1, spot % 2)
    return cut.reshape(blocks.shape)


def by_arrival(blocks, spot):
    n_dp = lax.axis_size("dp")
    if n_dp != 4:
        return blocks
    cut = blocks.reshape((2, 2) + blocks.shape[1:])
    cut = flip_axis(flip_axis(cut, 0, spot // 2), 1, spot % 2)
    return jnp.swapaxes(cut, 0, 1).reshape(blocks.shape)


VMEM_BYTES = 50 * 2**20
BF = jnp.bfloat16
F32 = jnp.float32


def shape(dims, kind=jnp.bfloat16):
    return jax.ShapeDtypeStruct(dims, kind)


def run(kernel, outs, ins):
    block = pl.BlockSpec(memory_space=pltpu.VMEM)
    done = pl.pallas_call(
        kernel,
        out_shape=list(outs),
        in_specs=[block] * len(ins),
        out_specs=[block] * len(outs),
        cost_estimate=pl.CostEstimate(flops=1, bytes_accessed=1, transcendentals=0),
        compiler_params=pltpu.CompilerParams(vmem_limit_bytes=VMEM_BYTES),
    )(*ins)
    return list(done)


def nn(left, right):
    return lax.dot_general(left, right, (((1,), (0,)), ((), ())), preferred_element_type=F32)


def nt(left, right):
    return lax.dot_general(left, right, (((1,), (1,)), ((), ())), preferred_element_type=F32)


def tn(left, right):
    return lax.dot_general(left, right, (((0,), (0,)), ((), ())), preferred_element_type=F32)


def stack_rows(pieces, counts, cols):
    return jnp.concatenate([p[:n, cols] for p, n in zip(pieces, counts)], 0)


def center_scale(value):
    center = jnp.mean(value, -1, keepdims=True)
    spread = jnp.mean(value * value, -1, keepdims=True) - center * center
    factor = lax.rsqrt(spread + EPS)
    return ((value - center) * factor, factor)


def norm_backward(grad_normed, centred, factor, gain):
    scaled = grad_normed * gain
    return factor * (
        scaled
        - jnp.mean(scaled, -1, keepdims=True)
        - centred * jnp.mean(scaled * centred, -1, keepdims=True)
    )


def column_sum(value):
    return jnp.sum(value, 0, keepdims=True)


def attention_forward(tokens, terms, bias_row, low, weights, rows, q_bias, v_bias):
    pieces, counts = weights
    size, depth = terms[0].shape
    wide = pieces[0].shape[1]
    groups = wide // 512
    half = groups * 128
    n_terms, n_pieces = len(terms), len(pieces)

    def kernel(*refs):
        term_refs, refs = refs[:n_terms], refs[n_terms:]
        bias_ref, rows_ref, qb_ref, vb_ref = refs[:4]
        piece_refs, refs = refs[4 : 4 + n_pieces], refs[4 + n_pieces :]
        u_ref, n_ref, q_ref, k_ref, v_ref, p_ref, o_ref, part_ref = refs
        value = term_refs[0][...].astype(F32)
        for ref in term_refs[1:]:
            value = value + ref[...].astype(F32)
        if n_terms > 1:
            value = value + bias_ref[...]
        if low:
            value = value.astype(BF).astype(F32)
        u_ref[...] = value
        centred, factor = center_scale(value)
        n_ref[...] = (centred * rows_ref[0:1] + rows_ref[1:2]).astype(BF)
        lane = lax.broadcasted_iota(jnp.int32, (size, 128), 1)
        key_lane = lax.broadcasted_iota(jnp.int32, (size, size), 1)
        normed = n_ref[...]
        for g in range(groups):
            at = slice(g * 128, (g + 1) * 128)
            matrix = stack_rows(piece_refs, counts, slice(g * 512, g * 512 + 384))
            projected = nn(normed, matrix)
            q = (projected[:, :128] + qb_ref[:, at]).astype(BF)
            k = projected[:, 128:256].astype(BF)
            v = (projected[:, 256:384] + vb_ref[:, at]).astype(BF)
            q_ref[:, at] = q
            k_ref[:, at] = k
            v_ref[:, at] = v
            mixed = None
            for h in range(2):
                mine = (lane // HD) == h
                scores = nt(jnp.where(mine, q, jnp.zeros_like(q)), k) * HD ** (-0.5)
                scores = jnp.where(key_lane < tokens, scores, -1e30)
                highest = jnp.max(scores, -1, keepdims=True)
                exponent = jnp.exp(scores - highest)
                inverse = 1.0 / jnp.sum(exponent, -1, keepdims=True)
                soft = (exponent * inverse).astype(BF)
                p_ref[2 * g + h] = soft
                out = nn(soft, v)
                mixed = out if h == 0 else jnp.where(mine, out, mixed)
            o_ref[:, at] = mixed.astype(BF)
        matrix = jnp.concatenate(
            [stack_rows(piece_refs, counts, slice(g * 512 + 384, g * 512 + 512)) for g in range(groups)], 1
        )
        part_ref[...] = nt(o_ref[...], matrix).astype(BF)

    outs = [shape((size, depth), F32), shape((size, depth))] + [shape((size, half))] * 3
    outs += [shape((2 * groups, size, size)), shape((size, half)), shape((size, depth))]
    return run(kernel, outs, [*terms, bias_row, rows, q_bias, v_bias, *pieces])


def up_forward(terms, weights, rows, up_bias):
    pieces, counts = weights
    size, depth = terms[0].shape
    wide = pieces[0].shape[1]

    def kernel(*refs):
        u_ref, own_ref, far_ref, rows_ref, bias_ref = refs[:5]
        piece_refs = refs[5 : 5 + len(pieces)]
        mid_ref, n_ref, slope_ref, hidden_ref = refs[5 + len(pieces) :]
        value = u_ref[...] + own_ref[...].astype(F32) + far_ref[...].astype(F32) + rows_ref[4:5]
        mid_ref[...] = value
        centred, factor = center_scale(value)
        n_ref[...] = (centred * rows_ref[5:6] + rows_ref[6:7]).astype(BF)
        step = 512
        for at in range(0, wide, step):
            cols = slice(at, at + step)
            before = nn(n_ref[...], stack_rows(piece_refs, counts, cols)) + bias_ref[:, cols]
            cdf = 0.5 * (1.0 + lax.erf(before * 0.7071067811865476))
            density = jnp.exp(-0.5 * before * before) * 0.3989422804014327
            hidden_ref[:, cols] = (before * cdf).astype(BF)
            slope_ref[:, cols] = (cdf + before * density).astype(BF)

    outs = [shape((size, depth), F32), shape((size, depth)), shape((size, wide)), shape((size, wide))]
    return run(kernel, outs, [*terms, rows, up_bias, *pieces])


def contract_wide(left, weights):
    pieces, counts = weights
    size, wide = left.shape
    depth = sum(counts)

    def kernel(*refs):
        left_ref, piece_refs, out_ref = refs[0], refs[1:-1], refs[-1]
        matrix = stack_rows(piece_refs, counts, slice(0, wide))
        out_ref[...] = nt(left_ref[...], matrix).astype(BF)

    return run(kernel, [shape((size, depth))], [left, *pieces])[0]


def weight_outs(depth, wide):
    cuts = [c for c in row_cuts(depth) if c is not None]
    return cuts, [shape((c[1] - c[0], wide)) for c in cuts]


def fill(grads):
    return (list(grads) + [None, None])[:4]


def down_backward(grad_out, hidden, slope, weights):
    pieces, counts = weights
    size, depth = grad_out.shape
    wide = hidden.shape[1]
    cuts, grad_outs = weight_outs(depth, wide)

    def kernel(*refs):
        g_ref, hidden_ref, slope_ref = refs[:3]
        piece_refs, refs = refs[3 : 3 + len(pieces)], refs[3 + len(pieces) :]
        low_ref, sum_ref, bias_ref = refs[:3]
        sum_ref[...] = column_sum(g_ref[...])
        branch = g_ref[...].astype(BF)
        for cut, ref in zip(cuts, refs[3:]):
            ref[...] = tn(branch[:, cut[0] : cut[1]], hidden_ref[...]).astype(BF)
        step = 512
        for at in range(0, wide, step):
            cols = slice(at, at + step)
            back = nn(branch, stack_rows(piece_refs, counts, cols)) * slope_ref[:, cols].astype(F32)
            bias_ref[:, cols] = column_sum(back)
            low_ref[:, cols] = back.astype(BF)

    outs = [shape((size, wide)), shape((1, depth), F32), shape((1, wide), F32)] + grad_outs
    done = run(kernel, outs, [grad_out, hidden, slope, *pieces])
    return done[0], done[1], done[2], fill(done[3:])


def up_grad(normed, low):
    size, depth = normed.shape
    wide = low.shape[1]
    cuts, outs = weight_outs(depth, wide)

    def kernel(n_ref, low_ref, *refs):
        for cut, ref in zip(cuts, refs):
            ref[...] = tn(n_ref[:, cut[0] : cut[1]], low_ref[...]).astype(BF)

    return fill(run(kernel, outs, [normed, low]))


def attention_backward(grad_out, own, far, middle, rows, saved, weights):
    pieces, counts = weights
    size, depth = grad_out.shape
    wide = pieces[0].shape[1]
    groups = wide // 512
    half = groups * 128
    scale = HD ** (-0.5)

    def kernel(*refs):
        g_ref, own_ref, far_ref, mid_ref, rows_ref, q_ref, k_ref, v_ref, p_ref, o_ref = refs[:10]
        piece_refs, refs = refs[10 : 10 + len(pieces)], refs[10 + len(pieces) :]
        dmid_ref, dz_ref, dq_ref, dk_ref, dv_ref, part_ref, sum_ref, qs_ref, vs_ref = refs
        grad_normed = own_ref[...].astype(F32) + far_ref[...].astype(F32)
        centred, factor = center_scale(mid_ref[...])
        sum_ref[1:2] = column_sum(grad_normed * centred)
        sum_ref[2:3] = column_sum(grad_normed)
        dmid = g_ref[...] + norm_backward(grad_normed, centred, factor, rows_ref[5:6])
        dmid_ref[...] = dmid
        sum_ref[0:1] = column_sum(dmid)
        dz_ref[...] = dmid.astype(BF)
        lane = lax.broadcasted_iota(jnp.int32, (size, 128), 1)
        for g in range(groups):
            at = slice(g * 128, (g + 1) * 128)
            matrix = stack_rows(piece_refs, counts, slice(g * 512 + 384, g * 512 + 512))
            grad_mixed = nn(dz_ref[...], matrix).astype(BF)
            q, k, v = q_ref[:, at], k_ref[:, at], v_ref[:, at]
            inner = grad_mixed.astype(F32) * o_ref[:, at].astype(F32)
            dq, dk, dv = None, None, None
            for h in range(2):
                mine = (lane // HD) == h
                soft = p_ref[2 * g + h]
                none = jnp.zeros_like(q)
                do = jnp.where(mine, grad_mixed, none)
                total = jnp.sum(jnp.where(mine, inner, 0.0), -1, keepdims=True)
                grad_soft = nt(do, v)
                grad_scores = (soft.astype(F32) * (grad_soft - total)).astype(BF)
                new_q = nn(grad_scores, k)
                new_k = tn(jnp.where(mine, q, none), grad_scores)
                new_v = tn(do, soft)
                dq = new_q if h == 0 else jnp.where(mine, new_q, dq)
                dk = new_k if h == 0 else dk + new_k
                dv = new_v if h == 0 else dv + new_v
            dq, dk, dv = dq * scale, dk.T * scale, dv.T
            qs_ref[:, at] = column_sum(dq)
            vs_ref[:, at] = column_sum(dv)
            dq_ref[:, at] = dq.astype(BF)
            dk_ref[:, at] = dk.astype(BF)
            dv_ref[:, at] = dv.astype(BF)
        total = None
        for g in range(groups):
            at = slice(g * 128, (g + 1) * 128)
            left = jnp.concatenate([dq_ref[:, at], dk_ref[:, at], dv_ref[:, at]], 1)
            new = nt(left, stack_rows(piece_refs, counts, slice(g * 512, g * 512 + 384)))
            total = new if g == 0 else total + new
        part_ref[...] = total.astype(BF)

    outs = [shape((size, depth), F32), shape((size, depth))] + [shape((size, half))] * 3
    outs += [shape((size, depth)), shape((3, depth), F32)] + [shape((1, half), F32)] * 2
    return run(kernel, outs, [grad_out, own, far, middle, rows, *saved, *pieces])


def attention_grad(normed, dz, dq, dk, dv, mixed):
    size, depth = normed.shape
    groups = dq.shape[1] // 128
    cuts, outs = weight_outs(depth, groups * 512)

    def kernel(n_ref, dz_ref, dq_ref, dk_ref, dv_ref, o_ref, *refs):
        for cut, ref in zip(cuts, refs):
            rows = slice(cut[0], cut[1])
            for g in range(groups):
                at = slice(g * 128, (g + 1) * 128)
                right = jnp.concatenate([dq_ref[:, at], dk_ref[:, at], dv_ref[:, at]], 1)
                ref[:, g * 512 : g * 512 + 384] = tn(n_ref[:, rows], right).astype(BF)
                ref[:, g * 512 + 384 : g * 512 + 512] = tn(dz_ref[:, rows], o_ref[:, at]).astype(BF)

    return fill(run(kernel, outs, [normed, dz, dq, dk, dv, mixed]))


def value_backward(dmid, own, far, value, rows, low):
    size, depth = dmid.shape

    def kernel(dmid_ref, own_ref, far_ref, u_ref, rows_ref, out_ref, sum_ref):
        grad_normed = own_ref[...].astype(F32) + far_ref[...].astype(F32)
        centred, factor = center_scale(u_ref[...])
        sum_ref[0:1] = column_sum(grad_normed * centred)
        sum_ref[1:2] = column_sum(grad_normed)
        out = dmid_ref[...] + norm_backward(grad_normed, centred, factor, rows_ref[0:1])
        if low:
            out = out.astype(BF).astype(F32)
        out_ref[...] = out

    outs = [shape((size, depth), F32), shape((2, depth), F32)]
    return run(kernel, outs, [dmid, own, far, value, rows])


def block_lanes(spot, chunk):
    ry, rx = chunk // 2 ^ spot // 2, chunk % 2 ^ spot % 2
    return [(rx * 2 + ry) * 128, 512 + (ry * 2 + rx) * 128]


def place_in(lanes, blocks):
    size, width = blocks[0].shape
    half = width // 2

    def kernel(lanes_ref, *refs):
        out_ref = refs[-1]
        for d, ref in enumerate(refs[:-1]):
            for h in range(2):
                at = pl.multiple_of(lanes_ref[2 * d + h], 128)
                out_ref[:, pl.ds(at, half)] = ref[:, h * half : (h + 1) * half]

    block = pl.BlockSpec(memory_space=pltpu.VMEM)
    return pl.pallas_call(
        kernel,
        out_shape=shape((size, width * len(blocks))),
        in_specs=[pl.BlockSpec(memory_space=pltpu.SMEM)] + [block] * len(blocks),
        out_specs=block,
        compiler_params=pltpu.CompilerParams(vmem_limit_bytes=VMEM_BYTES),
    )(lanes, *blocks)


def place_out(numbers, scale, terms, bias_row, count):
    size, depth = terms[0].shape
    width = depth // count
    half = width // 2

    def kernel(numbers_ref, scale_ref, *refs):
        term_refs, bias_ref, out_ref = refs[: len(terms)], refs[-2], refs[-1]
        start = pl.multiple_of(numbers_ref[2 * count], 8)
        rows = pl.ds(start, size // 2)
        for d in range(count):
            for h in range(2):
                lanes = pl.ds(pl.multiple_of(numbers_ref[2 * d + h], 128), half)
                value = term_refs[0][rows, lanes]
                for ref in term_refs[1:]:
                    value = value + ref[rows, lanes]
                value = (value + bias_ref[:, lanes]) * scale_ref[0]
                out_ref[d, :, h * half : (h + 1) * half] = value.astype(BF)

    block = pl.BlockSpec(memory_space=pltpu.VMEM)
    scalar = pl.BlockSpec(memory_space=pltpu.SMEM)
    return pl.pallas_call(
        kernel,
        out_shape=shape((count, size // 2, width)),
        in_specs=[scalar, scalar] + [block] * (len(terms) + 1),
        out_specs=block,
        compiler_params=pltpu.CompilerParams(vmem_limit_bytes=VMEM_BYTES),
    )(numbers, scale, *terms, bias_row)


def shift(block, d):
    n = lax.axis_size("tensor")
    return lax.ppermute(block, "tensor", [(i, (i + d) % n) for i in range(n)])


def shifts(blocks):
    return [blocks[0]] + [shift(block, d) for d, block in enumerate(blocks) if d > 0]


def half_cols(core, whole, n_tensor):
    cut = whole.reshape(whole.shape[:-1] + (n_tensor, 2, -1))
    cut = jnp.where(core == 0, cut[..., 0, :], cut[..., 1, :])
    return cut.reshape(whole.shape[:-1] + (-1,))


def spread_cols(core, half, n_tensor):
    cut = half.reshape(half.shape[:-1] + (n_tensor, 1, -1))
    none = jnp.zeros_like(cut)
    both = jnp.concatenate(
        [jnp.where(core == 0, cut, none), jnp.where(core == 0, none, cut)], -2
    )
    return both.reshape(half.shape[:-1] + (-1,))


def body(boundary_in, counts, qkv_weight, proj_weight, fc1_weight, fc2_weight, vectors, fc1_bias):
    core = lax.axis_index("section")
    is_first = core == 0
    place = lax.axis_index("tensor")
    spot = lax.axis_index("dp")
    n_dp, n_tensor = lax.axis_size("dp"), lax.axis_size("tensor")
    slots_per_batch = boundary_in.shape[1] // counts.shape[1]
    live = (place % slots_per_batch < counts[0, place // slots_per_batch]).astype(jnp.float32)
    depth = qkv_weight.shape[1]
    mid = depth // 2
    n_vec = vectors.size

    small_size = n_vec + fc1_bias.size
    packs = []
    for part in range(2):
        cuts = [
            jnp.split(qkv_weight[0], 2, 2)[part].reshape(depth, -1),
            jnp.split(proj_weight[0], 2, 0)[part].T,
            jnp.split(fc1_weight[0], 2, 1)[part],
            jnp.split(fc2_weight[0], 2, 0)[part].T,
        ]
        packs.append(jnp.concatenate(cuts, 1))
    wide = packs[0].shape[1] // 3
    extra = 16
    small = jnp.concatenate([vectors.reshape(-1), fc1_bias.reshape(-1)])
    small = jnp.pad(small, (0, extra * wide - small_size)).reshape(extra, wide)
    small = jnp.pad(small, ((0, 0), (0, 2 * wide)))
    kept = jnp.concatenate([jnp.where(is_first, packs[0], packs[1]), small], 0)
    received = swap(
        jnp.concatenate([jnp.where(is_first, packs[1], packs[0]), small], 0)
    )
    shards = (jnp.where(is_first, kept, received), jnp.where(is_first, received, kept))
    columns = []
    for layer in range(2):
        for number in range(3):
            cols = shards[layer][:, number * wide : (number + 1) * wide]
            if layer == 0 and number == 0:
                room = extra // 2
                both = [shard[depth : depth + room, :wide] for shard in shards]
                cols = jnp.concatenate([cols[:depth], *both], 0)
            else:
                cols = cols[:depth]
            columns.append(cols)

    tokens = boundary_in.shape[2]
    pad = -tokens % 16
    reach = (tokens + pad) // 2
    ends_in = jnp.pad(boundary_in[0].astype(jnp.bfloat16), ((0, 0), (0, pad), (0, 0)))
    ends_low, ends_high = ends_in[:, :reach], ends_in[:, reach:]
    ends_got = swap(jnp.where(is_first, ends_high, ends_low))
    half_in = jnp.where(is_first, ends_low, ends_got)
    half_cot = jnp.where(is_first, ends_got, ends_high)

    below = [(place - d) % n_tensor for d in range(n_tensor)]
    above = [(place + d) % n_tensor for d in range(n_tensor)]

    def to_send(half):
        return [lax.dynamic_index_in_dim(half, j, 0, False) for j in above]

    def image_half(blocks):
        if n_dp == 4:
            lanes = [lane for t in below for lane in block_lanes(spot, t)]
            return place_in(jnp.stack(lanes).astype(jnp.int32), blocks)
        blocks = jnp.stack(blocks)
        blocks = [lax.dynamic_index_in_dim(blocks, (place - i) % n_tensor, 0, False) for i in range(n_tensor)]
        return relative(jnp.concatenate(blocks, 1), spot)

    def whole_image(half):
        other = swap(half)
        both = [jnp.where(is_first, half, other), jnp.where(is_first, other, half)]
        return jnp.concatenate(both, 0)

    def image_rows(scale, terms, bias_row):
        if n_dp == 4:
            numbers = [lane for t in above for lane in block_lanes(spot, t)]
            numbers.append(jnp.where(is_first, 0, reach))
            numbers = jnp.stack(numbers).astype(jnp.int32)
            blocks = place_out(numbers, scale.reshape(1), terms, bias_row, n_tensor)
            return [blocks[d] for d in range(n_tensor)]
        image = absolute((sum(terms[1:], terms[0]) + bias_row) * scale, spot).astype(jnp.bfloat16)
        half = jnp.where(is_first, image[:reach], image[reach:])
        half = half.reshape(reach, n_tensor, -1).transpose(1, 0, 2)
        return to_send(half)

    def by_image(blocks):
        blocks = jnp.stack(blocks)
        blocks = [lax.dynamic_index_in_dim(blocks, (place - i) % n_tensor, 0, False) for i in range(n_tensor)]
        return jnp.stack(blocks)

    def small_of(extras):
        if n_dp != 4:
            extras = lax.all_gather(extras, "dp", axis=0, tiled=True)
        else:
            over = lax.ppermute(extras, "dp", [(i, i ^ 3) for i in range(n_dp)])
            extras = jnp.concatenate([extras, swap_y(extras), swap_x(extras), over], 0)
        both = by_chip(extras.reshape(n_dp, extra, -1), spot).astype(jnp.float32)
        both = both.reshape(n_dp, 2, extra // 2, n_tensor, wide).transpose(1, 0, 3, 2, 4)
        both = both.reshape(2, n_dp, n_tensor, -1)
        rows = both[..., :n_vec].reshape(2, n_dp, n_tensor, 8, -1)
        rows = relative(rows.transpose(0, 3, 2, 1, 4).reshape(2, 8, -1), spot)
        bias = both[..., n_vec:small_size].transpose(0, 2, 1, 3).reshape(2, -1)
        plain = both[..., :n_vec].reshape(2, n_dp, n_tensor, 8, -1)[..., 2:4, :]
        plain = plain.transpose(0, 3, 2, 1, 4).reshape(2, 2, -1)
        parts = [half_cols(core, plain[:, 0], n_tensor), half_cols(core, plain[:, 1], n_tensor)]
        parts.append(half_cols(core, bias, n_tensor))
        return [(rows[i], parts[0][i : i + 1], parts[1][i : i + 1], parts[2][i : i + 1]) for i in range(2)]

    number = len(columns)
    halves, near, far = [None] * number, [None] * number, [None] * number
    params = [dict(), dict()]
    blocks_in, blocks_cot = to_send(half_in), to_send(half_cot)
    pair, state = None, None

    def weights_of(k):
        first, second = arrived(*halves[k], near[k], far[k])
        return (first + second, [p.shape[0] for p in first + second])

    for r in range(number + 1):
        tied = []
        if r < number:
            tied.append(gather_column(columns[r]))
        if 0 <= r - 1 < number:
            near[r - 1] = exchange_one(*halves[r - 1])
        if r == 1:
            smalls = small_of(extra_rows)
            blocks_in = shifts(blocks_in)
        if 2 <= r <= 1 + n_tensor - 1:
            blocks_cot[r - 1] = shift(blocks_cot[r - 1], r - 1)
        if r == number - 1:
            cot_half = image_half(blocks_cot)
        if r == number:
            cotangent = whole_image(cot_half).astype(jnp.float32) * live
        ready = []
        k = r - 2
        if k >= 0:
            layer, kind = k // 3, k % 3
            one = params[layer]
            weights = weights_of(k)
            rows, q_bias, v_bias, up_bias = one["small"]
            if pair is not None:
                pair = [pair[0], swap(pair[0])]
            if kind == 0:
                one["qkvo"] = weights
                if layer == 0:
                    terms = [whole_image(image_half(blocks_in)).astype(jnp.float32)]
                else:
                    terms = [state, *pair]
                bias_row = params[0]["small"][0][7:8]
                done = attention_forward(
                    tokens, terms, bias_row, layer == 1, weights, rows, q_bias, v_bias
                )
                one["u"], one["n1"], one["saved"], part = done[0], done[1], done[2:7], done[7]
                pair, ready = [part], [part]
            elif kind == 1:
                one["up"] = weights
                one["mid"], one["n2"], one["slope"], one["hidden"] = up_forward(
                    [one["u"], *pair], weights, rows, up_bias
                )
                pair, ready = None, [one["hidden"]]
            else:
                one["down"] = weights
                state = one["mid"]
                part = contract_wide(one["hidden"], weights)
                pair, ready = [part], [part]
        if r <= number:
            count = len(ready)
            extras = list(ready)
            if 0 <= r - 1 < number:
                if ready:
                    done = tie(near[r - 1] + extras, [])
                    near[r - 1], extras = done[: len(near[r - 1])], done[len(near[r - 1]) :]
                far[r - 1] = exchange_two(*halves[r - 1], *near[r - 1])
                tied += near[r - 1] + far[r - 1]
            if r <= 1:
                extras += blocks_in
            if r == 1:
                extras += [v for layer in range(2) for v in smalls[layer]]
            if 1 <= r <= number - 2:
                extras += blocks_cot
            elif r == number - 1:
                extras.append(cot_half)
            elif r == number:
                extras.append(cotangent)
            if r + 1 < number:
                extras.append(columns[r + 1])
            done = tie(tied + extras, [])
            if r + 1 < number:
                columns[r + 1] = done.pop()
            if 1 <= r <= number - 2:
                done, blocks_cot = done[:-n_tensor], done[-n_tensor:]
            elif r == number - 1:
                cot_half = done.pop()
            elif r == number:
                cotangent = done.pop()
            if r == 1:
                done, smalls = done[:-8], done[-8:]
                params[0]["small"], params[1]["small"] = smalls[:4], smalls[4:]
            if r <= 1:
                done, blocks_in = done[:-n_tensor], done[-n_tensor:]
            if count and kind == 1:
                one["hidden"] = done[-1]
            elif count:
                pair = [done[-1]]
            at = 0
            if r < number:
                halves[r] = (done[0][:mid], done[0][mid:depth])
                if r == 0:
                    extra_rows = done[0][depth:]
                at = 1
            if 0 <= r - 1 < number:
                near[r - 1] = done[at : at + 2]
                far[r - 1] = done[at + 2 : at + 2 + len(far[r - 1])]

    sums = [dict(), dict()]

    def small_grads():
        packed = []
        for layer in range(2):
            total = sums[layer]
            full = jnp.concatenate([total["one"], total["mid"], total["out"]], 0)
            full = absolute(jnp.where(core == layer, full, 0.0), spot)
            q_row = spread_cols(core, total["q"][0], n_tensor)
            v_row = spread_cols(core, total["v"][0], n_tensor)
            up_row = spread_cols(core, total["up_bias"][0], n_tensor)
            rows = jnp.concatenate([full[:2], q_row[None], v_row[None], full[2:]], 0)
            rows = rows.reshape(8, n_tensor, n_dp, -1).transpose(2, 1, 0, 3).reshape(n_dp, n_tensor, -1)
            up_row = up_row.reshape(n_tensor, n_dp, -1).transpose(1, 0, 2)
            packed.append(jnp.concatenate([rows, up_row], -1))
        ours = jnp.where(is_first, packed[0], packed[1])
        other = swap(jnp.where(is_first, packed[1], packed[0]))
        little = (ours + other).astype(jnp.bfloat16)
        return little

    grads, got, moved, settled = [None] * number, [None] * number, [None] * number, [None] * number
    made = [0, 1, 3, 4, 5, 6]
    grad = cotangent
    last_down = weights_of(number - 1)
    params[1]["down"] = last_down
    last_bias = params[1]["small"][0][7:8]
    for r in range(8):
        layer, stage = 1 - r // 4, r % 4
        one, total = params[layer], sums[layer]
        rows = one["small"][0]
        tied, slots = [], []
        for c in range(number):
            if r == made[c] + 1:
                got[c] = scatter_one(*grads[c][:2])
                slots.append((got, c, len(got[c])))
                tied += got[c]
            elif r == made[c] + 2:
                stay, come = scatter_two(*grads[c][2:], got[c])
                moved[c] = [*stay, *come]
                if r < 7:
                    slots.append((moved, c, len(moved[c])))
                    tied += moved[c]
            elif r == made[c] + 3:
                settled[c] = scatter_column(moved[c][:2], moved[c][2:])
                slots.append((settled, c, 0))
                tied.append(settled[c])
        new = None
        if stage == 0:
            low, total["out"], total["up_bias"], new = down_backward(
                grad, one["hidden"], one["slope"], one["down"]
            )
            carry = [low]
        elif stage == 1:
            part = contract_wide(low, one["up"])
            new = up_grad(one["n2"], low)
            carry = [part]
        elif stage == 2:
            done = attention_backward(
                grad, part, swap(part), one["mid"], rows, one["saved"], one["qkvo"]
            )
            dmid, dz, dq, dk, dv, part, total["mid"], total["q"], total["v"] = done
            if layer == 0:
                new = attention_grad(one["n1"], dz, dq, dk, dv, one["saved"][4])
            carry = [part]
        else:
            if layer == 1:
                new = attention_grad(one["n1"], dz, dq, dk, dv, one["saved"][4])
            grad, total["one"] = value_backward(dmid, part, swap(part), one["u"], rows, layer == 1)
            carry = [grad]
            if r == 7:
                one_scale = jnp.ones((), jnp.float32)
                no_bias = jnp.zeros((1, grad.shape[1]), jnp.float32)
                carry = [small_grads()]
                grad_blocks = shifts(image_rows(one_scale, [grad], no_bias))
        if new is not None:
            c = made.index(r)
            grads[c] = new
            fresh = [g for g in new if g is not None]
        else:
            fresh = []
        if r == 3:
            last_part = contract_wide(params[1]["hidden"], last_down)
            carry.append(last_part)
        elif r == 4:
            out_blocks = image_rows(
                live, [params[1]["mid"], last_part, swap(last_part)], last_bias
            )
        if 4 <= r < 4 + n_tensor - 1:
            out_blocks[r - 3] = shift(out_blocks[r - 3], r - 3)
            carry += out_blocks
        if r < 8:
            done = tie(carry + fresh + tied, [])
            if stage == 0:
                low = done[0]
            elif stage == 1:
                part = done[0]
            elif stage == 2:
                part = done[0]
            elif r < 7:
                grad = done[0]
            else:
                little = done[0]
            if r == 3:
                last_part = done[1]
            elif 4 <= r < 4 + n_tensor - 1:
                out_blocks = done[1 : 1 + n_tensor]
            done = done[len(carry) :]
            if fresh:
                grads[c] = fill(done[: len(fresh)])
                done = done[len(fresh) :]
            for store, at, count in slots:
                store[at] = done[:count] if count else done[0]
                done = done[max(count, 1) :]

    room = jnp.zeros((n_dp, n_tensor, extra * wide - small_size), little.dtype)
    little = jnp.concatenate([little, room], -1).reshape(n_dp, n_tensor, extra, wide)
    little = by_arrival(little.transpose(0, 2, 1, 3).reshape(n_dp, extra, -1), spot)
    if n_dp != 4:
        little = lax.psum_scatter(little, "dp", scatter_dimension=0, tiled=True)[0]
    else:
        little = add(little[:2], swap_x(little[2:])).astype(jnp.bfloat16)
        little = add(little[0], swap_y(little[1])).astype(jnp.bfloat16)

    last = number - 1
    settled[last - 1] = scatter_column(moved[last - 1][:2], moved[last - 1][2:])
    stay, come = scatter_two(*grads[last][2:], got[last])
    done = tie([*grad_blocks, *stay, *come], [])
    grad_blocks, done = done[:n_tensor], done[n_tensor:]
    grad_rows, out_rows = by_image(grad_blocks), by_image(out_blocks)
    stay, come = done[:2], done[2:]
    if come:
        stay = [add(s, c).astype(jnp.bfloat16) for s, c in zip(stay, come)]
    settled[last] = scatter_column([*stay, little], [])
    little = settled[last][depth:].reshape(-1).astype(jnp.float32)
    settled[last] = settled[last][:depth]
    grad_vectors = little[:n_vec].reshape(vectors.shape)
    grad_bias = little[n_vec:small_size].reshape(fc1_bias.shape)

    own = jnp.where(is_first, grad_rows, out_rows)
    other = swap(jnp.where(is_first, out_rows, grad_rows))
    ends = [jnp.where(is_first, own, other), jnp.where(is_first, other, own)]
    boundary_out = jnp.concatenate(ends, 1)[:, :tokens].astype(jnp.float32)[None]
    lows, highs = [], []
    for kind in range(3):
        first, second = settled[last - kind], settled[last - kind - 3]
        kept = jnp.where(is_first, first, second)
        received = swap(jnp.where(is_first, second, first))
        lows.append(jnp.where(is_first, kept, received).astype(jnp.float32))
        highs.append(jnp.where(is_first, received, kept).astype(jnp.float32))
    low, high = [part[0].reshape(depth, 4, -1) for part in (lows, highs)]
    grad_qkv = jnp.concatenate([low[:, :3], high[:, :3]], 2)[None]
    grad_proj = jnp.concatenate([low[:, 3].T, high[:, 3].T], 0)[None]
    grad_up = jnp.concatenate([lows[1], highs[1]], 1)[None]
    grad_down = jnp.concatenate([lows[2].T, highs[2].T], 0)[None]
    return (boundary_out, grad_qkv, grad_proj, grad_up, grad_down, grad_vectors, grad_bias)


def solution(mesh):
    in_specs = (
        P("section", "dp", None, "tensor"),
        P("dp", None),
        P("section", "dp", None, "tensor"),
        P("section", "tensor", "dp"),
        P("section", "dp", "tensor"),
        P("section", "tensor", "dp"),
        P("section", None, "tensor", "dp"),
        P("section", "tensor", "dp"),
    )
    out_specs = (
        P("section", "dp", None, "tensor"),
        P("section", "dp", None, "tensor"),
        P("section", "tensor", "dp"),
        P("section", "dp", "tensor"),
        P("section", "tensor", "dp"),
        P("section", None, "tensor", "dp"),
        P("section", "tensor", "dp"),
    )
    return jax.shard_map(body, mesh=mesh, in_specs=in_specs, out_specs=out_specs, check_vma=False)
```

```python
import jax
import jax.numpy as jnp
from jax import lax
from jax.experimental import pallas as pl
from jax.experimental.pallas import tpu as pltpu
from jax.sharding import PartitionSpec as P

HD = 64
EPS = 1e-06


def swap(value):
    return lax.ppermute(value, "section", [(0, 1), (1, 0)])


def pair_sum(partial):
    low = partial.astype(jnp.bfloat16)
    return low.astype(jnp.float32) + swap(low).astype(jnp.float32)


def swap_x(value):
    n = lax.axis_size("dp")
    return lax.ppermute(value, "dp", [(i, i ^ 1) for i in range(n)])


def swap_y(value):
    n = lax.axis_size("dp")
    return lax.ppermute(value, "dp", [(i, i ^ 2) for i in range(n)])


def tie(values, others):
    count = len(values)

    def kernel(*refs):
        pass

    anywhere = pl.BlockSpec(memory_space=pl.ANY)
    done = pl.pallas_call(
        kernel,
        out_shape=[jax.ShapeDtypeStruct(v.shape, v.dtype) for v in values],
        in_specs=[anywhere] * (count + len(others)),
        out_specs=[anywhere] * count,
        input_output_aliases={i: i for i in range(count)},
    )(*values, *others)
    return list(done)


def gather_column(shard):
    return lax.all_gather(shard, "tensor", axis=1, tiled=True)


def exchange_one(first, second):
    if lax.axis_size("dp") != 4:
        return [lax.all_gather(v, "dp", axis=0, tiled=True) for v in (first, second)]
    return [swap_y(first), swap_x(second)]


def exchange_two(first, second, near_first, near_second):
    if lax.axis_size("dp") != 4:
        return []
    return [swap_x(first), swap_x(near_first), swap_y(second), swap_y(near_second)]


def arrived(first, second, near, far):
    if lax.axis_size("dp") != 4:
        return ([near[0]], [near[1]])
    return ([first, near[0], far[0], far[1]], [second, near[1], far[2], far[3]])


def row_plan(depth):
    late = depth // 8 if lax.axis_size("dp") == 4 else 0
    return (depth - late) // 2, late


def row_cuts(features):
    n_dp = lax.axis_size("dp")
    half, late = row_plan(features // n_dp)
    if n_dp != 4:
        return [[(0, features // 2)], [(features // 2, features)], None, None]
    part = late // 2
    base = 8 * half

    def ranges(second, outer):
        out = []
        for inner in range(2):
            start = (4 * second + 2 * outer + inner) * half
            chip = 2 * inner + outer if second else 2 * outer + inner
            extra = base + chip * late + second * part
            out += [(start, start + half), (extra, extra + part)]
        return out

    return [ranges(0, 1), ranges(1, 1), ranges(0, 0), ranges(1, 0)]


def add(left, right):
    return left.astype(jnp.float32) + right.astype(jnp.float32)


def scatter_one(send_first, send_second):
    if lax.axis_size("dp") != 4:
        return [
            lax.psum_scatter(v, "dp", scatter_dimension=0, tiled=True)
            for v in (send_first, send_second)
        ]
    return [swap_x(send_first), swap_y(send_second)]


def scatter_two(keep_first, keep_second, got):
    if lax.axis_size("dp") != 4:
        return (got, [])
    stay, send = [], []
    for keep, new in zip((keep_first, keep_second), got):
        half = keep.shape[0] // 2
        send.append(add(keep[half:], new[half:]).astype(jnp.bfloat16))
        stay.append(add(keep[:half], new[:half]).astype(jnp.bfloat16))
    return (stay, [swap_y(send[0]), swap_x(send[1])])


def scatter_column(stay, come):
    if come:
        stay = [add(s, c).astype(jnp.bfloat16) for s, c in zip(stay, come)]
    return lax.psum_scatter(
        jnp.concatenate(stay, 0), "tensor", scatter_dimension=1, tiled=True
    )


def flip_axis(value, axis, bit):
    return jnp.where(bit == 1, jnp.flip(value, axis), value)


def feature_order(features, spot):
    n_dp = lax.axis_size("dp")
    depth = features // n_dp
    half, late = row_plan(depth)
    if n_dp == 4:
        chip = [[(ry ^ spot // 2) * 2 + (rx ^ spot % 2) for ry in range(2)] for rx in range(2)]
        first = [chip[rx][ry] for rx in range(2) for ry in range(2)]
        second = [chip[rx][ry] for ry in range(2) for rx in range(2)]
    else:
        first = second = range(n_dp)
    parts = [p * depth + jnp.arange(half) for p in first]
    parts += [p * depth + half + jnp.arange(half) for p in second]
    if late:
        parts += [p * depth + 2 * half + jnp.arange(late) for p in first]
    return jnp.concatenate(parts).astype(jnp.int32)


def chooser(order):
    return (jnp.arange(order.size)[:, None] == order[None, :]).astype(jnp.bfloat16)


def by_chip(blocks, spot):
    n_dp = lax.axis_size("dp")
    if n_dp != 4:
        return blocks
    cut = blocks.reshape((2, 2) + blocks.shape[1:])
    cut = jnp.swapaxes(cut, 0, 1)
    cut = flip_axis(flip_axis(cut, 0, spot // 2), 1, spot % 2)
    return cut.reshape(blocks.shape)


def by_arrival(blocks, spot):
    n_dp = lax.axis_size("dp")
    if n_dp != 4:
        return blocks
    cut = blocks.reshape((2, 2) + blocks.shape[1:])
    cut = flip_axis(flip_axis(cut, 0, spot // 2), 1, spot % 2)
    return jnp.swapaxes(cut, 0, 1).reshape(blocks.shape)


def mm(form, left, right):
    return jnp.einsum(form, left, right, preferred_element_type=jnp.float32)


VMEM_BYTES = 50 * 2**20
BF = jnp.bfloat16
F32 = jnp.float32


def shape(dims, kind=jnp.bfloat16):
    return jax.ShapeDtypeStruct(dims, kind)


def run(kernel, outs, ins):
    block = pl.BlockSpec(memory_space=pltpu.VMEM)
    done = pl.pallas_call(
        kernel,
        out_shape=list(outs),
        in_specs=[block] * len(ins),
        out_specs=[block] * len(outs),
        cost_estimate=pl.CostEstimate(flops=1, bytes_accessed=1, transcendentals=0),
        compiler_params=pltpu.CompilerParams(vmem_limit_bytes=VMEM_BYTES),
    )(*ins)
    return list(done)


def nn(left, right):
    return lax.dot_general(left, right, (((1,), (0,)), ((), ())), preferred_element_type=F32)


def nt(left, right):
    return lax.dot_general(left, right, (((1,), (1,)), ((), ())), preferred_element_type=F32)


def tn(left, right):
    return lax.dot_general(left, right, (((0,), (0,)), ((), ())), preferred_element_type=F32)


def stack_rows(pieces, counts, cols):
    return jnp.concatenate([pieces[i][a : a + n, cols] for i, a, n in counts], 0)


def write_rows(refs, cuts, cols, full):
    for ref, ranges in zip(refs, cuts):
        at = 0
        for a, b in ranges:
            ref[at : at + b - a, cols] = full[a:b].astype(BF)
            at += b - a


def center_scale(value):
    center = jnp.mean(value, -1, keepdims=True)
    spread = jnp.mean(value * value, -1, keepdims=True) - center * center
    factor = lax.rsqrt(spread + EPS)
    return ((value - center) * factor, factor)


def norm_backward(grad_normed, centred, factor, gain):
    scaled = grad_normed * gain
    return factor * (
        scaled
        - jnp.mean(scaled, -1, keepdims=True)
        - centred * jnp.mean(scaled * centred, -1, keepdims=True)
    )


def column_sum(value):
    return jnp.sum(value, 0, keepdims=True)


def attention_forward(tokens, terms, bias_row, low, weights, rows, q_bias, v_bias):
    pieces, counts = weights
    size, depth = terms[0].shape
    wide = pieces[0].shape[1]
    groups = wide // 512
    half = groups * 128
    n_terms, n_pieces = len(terms), len(pieces)

    def kernel(*refs):
        term_refs, refs = refs[:n_terms], refs[n_terms:]
        bias_ref, rows_ref, qb_ref, vb_ref = refs[:4]
        piece_refs, refs = refs[4 : 4 + n_pieces], refs[4 + n_pieces :]
        u_ref, n_ref, q_ref, k_ref, v_ref, p_ref, o_ref, part_ref = refs
        value = term_refs[0][...].astype(F32)
        for ref in term_refs[1:]:
            value = value + ref[...].astype(F32)
        if n_terms > 1:
            value = value + bias_ref[...]
        if low:
            value = value.astype(BF).astype(F32)
        u_ref[...] = value
        centred, factor = center_scale(value)
        n_ref[...] = (centred * rows_ref[0:1] + rows_ref[1:2]).astype(BF)
        lane = lax.broadcasted_iota(jnp.int32, (size, 128), 1)
        key_lane = lax.broadcasted_iota(jnp.int32, (size, size), 1)
        normed = n_ref[...]
        for g in range(groups):
            at = slice(g * 128, (g + 1) * 128)
            matrix = stack_rows(piece_refs, counts, slice(g * 512, g * 512 + 384))
            projected = nn(normed, matrix)
            q = (projected[:, :128] + qb_ref[:, at]).astype(BF)
            k = projected[:, 128:256].astype(BF)
            v = (projected[:, 256:384] + vb_ref[:, at]).astype(BF)
            q_ref[:, at] = q
            k_ref[:, at] = k
            v_ref[:, at] = v
            mixed = None
            for h in range(2):
                mine = (lane // HD) == h
                scores = nt(jnp.where(mine, q, jnp.zeros_like(q)), k) * HD ** (-0.5)
                scores = jnp.where(key_lane < tokens, scores, -1e30)
                highest = jnp.max(scores, -1, keepdims=True)
                exponent = jnp.exp(scores - highest)
                inverse = 1.0 / jnp.sum(exponent, -1, keepdims=True)
                soft = (exponent * inverse).astype(BF)
                p_ref[2 * g + h] = soft
                out = nn(soft, v)
                mixed = out if h == 0 else jnp.where(mine, out, mixed)
            o_ref[:, at] = mixed.astype(BF)
        matrix = jnp.concatenate(
            [stack_rows(piece_refs, counts, slice(g * 512 + 384, g * 512 + 512)) for g in range(groups)], 1
        )
        part_ref[...] = nt(o_ref[...], matrix).astype(BF)

    outs = [shape((size, depth), F32), shape((size, depth))] + [shape((size, half))] * 3
    outs += [shape((2 * groups, size, size)), shape((size, half)), shape((size, depth))]
    return run(kernel, outs, [*terms, bias_row, rows, q_bias, v_bias, *pieces])


def up_forward(terms, weights, rows, up_bias):
    pieces, counts = weights
    size, depth = terms[0].shape
    wide = pieces[0].shape[1]

    def kernel(*refs):
        u_ref, own_ref, far_ref, rows_ref, bias_ref = refs[:5]
        piece_refs = refs[5 : 5 + len(pieces)]
        mid_ref, n_ref, slope_ref, hidden_ref = refs[5 + len(pieces) :]
        value = u_ref[...] + own_ref[...].astype(F32) + far_ref[...].astype(F32) + rows_ref[4:5]
        mid_ref[...] = value
        centred, factor = center_scale(value)
        n_ref[...] = (centred * rows_ref[5:6] + rows_ref[6:7]).astype(BF)
        step = 512
        for at in range(0, wide, step):
            cols = slice(at, at + step)
            before = nn(n_ref[...], stack_rows(piece_refs, counts, cols)) + bias_ref[:, cols]
            cdf = 0.5 * (1.0 + lax.erf(before * 0.7071067811865476))
            density = jnp.exp(-0.5 * before * before) * 0.3989422804014327
            hidden_ref[:, cols] = (before * cdf).astype(BF)
            slope_ref[:, cols] = (cdf + before * density).astype(BF)

    outs = [shape((size, depth), F32), shape((size, depth)), shape((size, wide)), shape((size, wide))]
    return run(kernel, outs, [*terms, rows, up_bias, *pieces])


def contract_wide(left, weights):
    pieces, counts = weights
    size, wide = left.shape
    depth = sum(n for _, _, n in counts)

    def kernel(*refs):
        left_ref, piece_refs, out_ref = refs[0], refs[1:-1], refs[-1]
        matrix = stack_rows(piece_refs, counts, slice(0, wide))
        out_ref[...] = nt(left_ref[...], matrix).astype(BF)

    return run(kernel, [shape((size, depth))], [left, *pieces])[0]


def weight_outs(depth, wide):
    cuts = [c for c in row_cuts(depth) if c is not None]
    return cuts, [shape((sum(b - a for a, b in c), wide)) for c in cuts]


def fill(grads):
    return (list(grads) + [None, None])[:4]


def down_backward(grad_out, hidden, slope, weights):
    pieces, counts = weights
    size, depth = grad_out.shape
    wide = hidden.shape[1]
    cuts, grad_outs = weight_outs(depth, wide)

    def kernel(*refs):
        g_ref, hidden_ref, slope_ref = refs[:3]
        piece_refs, refs = refs[3 : 3 + len(pieces)], refs[3 + len(pieces) :]
        low_ref, sum_ref, bias_ref = refs[:3]
        sum_ref[...] = column_sum(g_ref[...])
        branch = g_ref[...].astype(BF)
        step = 512
        for at in range(0, wide, step):
            cols = slice(at, at + step)
            write_rows(refs[3:], cuts, cols, tn(branch, hidden_ref[:, cols]))
            back = nn(branch, stack_rows(piece_refs, counts, cols)) * slope_ref[:, cols].astype(F32)
            bias_ref[:, cols] = column_sum(back)
            low_ref[:, cols] = back.astype(BF)

    outs = [shape((size, wide)), shape((1, depth), F32), shape((1, wide), F32)] + grad_outs
    done = run(kernel, outs, [grad_out, hidden, slope, *pieces])
    return done[0], done[1], done[2], fill(done[3:])


def up_grad(normed, low):
    size, depth = normed.shape
    wide = low.shape[1]
    cuts, outs = weight_outs(depth, wide)

    def kernel(n_ref, low_ref, *refs):
        step = 512
        for at in range(0, wide, step):
            cols = slice(at, at + step)
            write_rows(refs, cuts, cols, tn(n_ref[...], low_ref[:, cols]))

    return fill(run(kernel, outs, [normed, low]))


def attention_backward(grad_out, own, far, middle, rows, saved, weights):
    pieces, counts = weights
    size, depth = grad_out.shape
    wide = pieces[0].shape[1]
    groups = wide // 512
    half = groups * 128
    scale = HD ** (-0.5)

    def kernel(*refs):
        g_ref, own_ref, far_ref, mid_ref, rows_ref, q_ref, k_ref, v_ref, p_ref, o_ref = refs[:10]
        piece_refs, refs = refs[10 : 10 + len(pieces)], refs[10 + len(pieces) :]
        dmid_ref, dz_ref, dq_ref, dk_ref, dv_ref, part_ref, sum_ref, qs_ref, vs_ref = refs
        grad_normed = own_ref[...].astype(F32) + far_ref[...].astype(F32)
        centred, factor = center_scale(mid_ref[...])
        sum_ref[1:2] = column_sum(grad_normed * centred)
        sum_ref[2:3] = column_sum(grad_normed)
        dmid = g_ref[...] + norm_backward(grad_normed, centred, factor, rows_ref[5:6])
        dmid_ref[...] = dmid
        sum_ref[0:1] = column_sum(dmid)
        dz_ref[...] = dmid.astype(BF)
        lane = lax.broadcasted_iota(jnp.int32, (size, 128), 1)
        for g in range(groups):
            at = slice(g * 128, (g + 1) * 128)
            matrix = stack_rows(piece_refs, counts, slice(g * 512 + 384, g * 512 + 512))
            grad_mixed = nn(dz_ref[...], matrix).astype(BF)
            q, k, v = q_ref[:, at], k_ref[:, at], v_ref[:, at]
            inner = grad_mixed.astype(F32) * o_ref[:, at].astype(F32)
            dq, dk, dv = None, None, None
            for h in range(2):
                mine = (lane // HD) == h
                soft = p_ref[2 * g + h]
                none = jnp.zeros_like(q)
                do = jnp.where(mine, grad_mixed, none)
                total = jnp.sum(jnp.where(mine, inner, 0.0), -1, keepdims=True)
                grad_soft = nt(do, v)
                grad_scores = (soft.astype(F32) * (grad_soft - total)).astype(BF)
                new_q = nn(grad_scores, k)
                new_k = tn(jnp.where(mine, q, none), grad_scores)
                new_v = tn(do, soft)
                dq = new_q if h == 0 else jnp.where(mine, new_q, dq)
                dk = new_k if h == 0 else dk + new_k
                dv = new_v if h == 0 else dv + new_v
            dq, dk, dv = dq * scale, dk.T * scale, dv.T
            qs_ref[:, at] = column_sum(dq)
            vs_ref[:, at] = column_sum(dv)
            dq_ref[:, at] = dq.astype(BF)
            dk_ref[:, at] = dk.astype(BF)
            dv_ref[:, at] = dv.astype(BF)
        total = None
        for g in range(groups):
            at = slice(g * 128, (g + 1) * 128)
            left = jnp.concatenate([dq_ref[:, at], dk_ref[:, at], dv_ref[:, at]], 1)
            new = nt(left, stack_rows(piece_refs, counts, slice(g * 512, g * 512 + 384)))
            total = new if g == 0 else total + new
        part_ref[...] = total.astype(BF)

    outs = [shape((size, depth), F32), shape((size, depth))] + [shape((size, half))] * 3
    outs += [shape((size, depth)), shape((3, depth), F32)] + [shape((1, half), F32)] * 2
    return run(kernel, outs, [grad_out, own, far, middle, rows, *saved, *pieces])


def attention_grad(normed, dz, dq, dk, dv, mixed):
    size, depth = normed.shape
    groups = dq.shape[1] // 128
    cuts, outs = weight_outs(depth, groups * 512)

    def kernel(n_ref, dz_ref, dq_ref, dk_ref, dv_ref, o_ref, *refs):
        for g in range(groups):
            at = slice(g * 128, (g + 1) * 128)
            right = jnp.concatenate([dq_ref[:, at], dk_ref[:, at], dv_ref[:, at]], 1)
            cols = slice(g * 512, g * 512 + 384)
            write_rows(refs, cuts, cols, tn(n_ref[...], right))
            cols = slice(g * 512 + 384, g * 512 + 512)
            write_rows(refs, cuts, cols, tn(dz_ref[...], o_ref[:, at]))

    return fill(run(kernel, outs, [normed, dz, dq, dk, dv, mixed]))


def value_backward(dmid, own, far, value, rows, low):
    size, depth = dmid.shape

    def kernel(dmid_ref, own_ref, far_ref, u_ref, rows_ref, out_ref, sum_ref):
        grad_normed = own_ref[...].astype(F32) + far_ref[...].astype(F32)
        centred, factor = center_scale(u_ref[...])
        sum_ref[0:1] = column_sum(grad_normed * centred)
        sum_ref[1:2] = column_sum(grad_normed)
        out = dmid_ref[...] + norm_backward(grad_normed, centred, factor, rows_ref[0:1])
        if low:
            out = out.astype(BF).astype(F32)
        out_ref[...] = out

    outs = [shape((size, depth), F32), shape((2, depth), F32)]
    return run(kernel, outs, [dmid, own, far, value, rows])


def place_in(lanes, blocks):
    size, width = blocks[0].shape
    features = width * len(blocks)

    def kernel(lanes_ref, *refs):
        value = jnp.concatenate([ref[...] for ref in refs[:-1]], 1)
        place = lax.broadcasted_iota(jnp.int32, (features, features), 0)
        pick = (place == lanes_ref[...]).astype(F32).astype(BF)
        refs[-1][...] = nn(value, pick).astype(BF)

    return run(kernel, [shape((size, features))], [lanes, *blocks])[0]


def place_out(lanes, start, scale, terms, bias_row, count):
    size, features = terms[0].shape
    width = features // count

    def kernel(start_ref, scale_ref, lanes_ref, *refs):
        term_refs, bias_ref, out_ref = refs[: len(terms)], refs[-2], refs[-1]
        rows = pl.ds(pl.multiple_of(start_ref[0], 8), size // 2)
        value = term_refs[0][rows, :]
        for ref in term_refs[1:]:
            value = value + ref[rows, :]
        value = ((value + bias_ref[...]) * scale_ref[0]).astype(BF)
        place = lax.broadcasted_iota(jnp.int32, (features, features), 0)
        pick = (place == lanes_ref[...]).astype(F32).astype(BF)
        value = nt(value, pick).astype(BF)
        for d in range(count):
            out_ref[d] = value[:, d * width : (d + 1) * width]

    block = pl.BlockSpec(memory_space=pltpu.VMEM)
    scalar = pl.BlockSpec(memory_space=pltpu.SMEM)
    return pl.pallas_call(
        kernel,
        out_shape=shape((count, size // 2, width)),
        in_specs=[scalar, scalar] + [block] * (len(terms) + 2),
        out_specs=block,
        compiler_params=pltpu.CompilerParams(vmem_limit_bytes=VMEM_BYTES),
    )(start, scale, lanes, *terms, bias_row)


def shift(block, d):
    n = lax.axis_size("tensor")
    return lax.ppermute(block, "tensor", [(i, (i + d) % n) for i in range(n)])


def shifts(blocks):
    return [blocks[0]] + [shift(block, d) for d, block in enumerate(blocks) if d > 0]


def half_cols(core, whole, n_tensor):
    cut = whole.reshape(whole.shape[:-1] + (n_tensor, 2, -1))
    cut = jnp.where(core == 0, cut[..., 0, :], cut[..., 1, :])
    return cut.reshape(whole.shape[:-1] + (-1,))


def spread_cols(core, half, n_tensor):
    cut = half.reshape(half.shape[:-1] + (n_tensor, 1, -1))
    none = jnp.zeros_like(cut)
    both = jnp.concatenate(
        [jnp.where(core == 0, cut, none), jnp.where(core == 0, none, cut)], -2
    )
    return both.reshape(half.shape[:-1] + (-1,))


def body(boundary_in, counts, qkv_weight, proj_weight, fc1_weight, fc2_weight, vectors, fc1_bias):
    core = lax.axis_index("section")
    is_first = core == 0
    place = lax.axis_index("tensor")
    spot = lax.axis_index("dp")
    n_dp, n_tensor = lax.axis_size("dp"), lax.axis_size("tensor")
    slots_per_batch = boundary_in.shape[1] // counts.shape[1]
    live = (place % slots_per_batch < counts[0, place // slots_per_batch]).astype(jnp.float32)
    depth = qkv_weight.shape[1]
    half_rows, late = row_plan(depth)
    early = 2 * half_rows
    features = n_dp * depth
    order = feature_order(features, spot)
    pick = chooser(order)
    n_vec = vectors.size

    small_size = n_vec + fc1_bias.size
    packs = []
    for part in range(2):
        cuts = [
            jnp.split(qkv_weight[0], 2, 2)[part].reshape(depth, -1),
            jnp.split(proj_weight[0], 2, 0)[part].T,
            jnp.split(fc1_weight[0], 2, 1)[part],
            jnp.split(fc2_weight[0], 2, 0)[part].T,
        ]
        packs.append(jnp.concatenate(cuts, 1))
    wide = packs[0].shape[1] // 3
    extra = 16
    small = jnp.concatenate([vectors.reshape(-1), fc1_bias.reshape(-1)])
    small = jnp.pad(small, (0, extra * wide - small_size)).reshape(extra, wide)
    small = jnp.pad(small, ((0, 0), (0, 2 * wide)))
    kept = jnp.concatenate([jnp.where(is_first, packs[0], packs[1]), small], 0)
    received = swap(
        jnp.concatenate([jnp.where(is_first, packs[1], packs[0]), small], 0)
    )
    shards = (jnp.where(is_first, kept, received), jnp.where(is_first, received, kept))
    room = extra // 2
    both = [shard[depth : depth + room, :wide] for shard in shards]
    if late:
        last = jnp.concatenate([shard[early:depth] for shard in shards], 0)
        over = lax.ppermute(last, "dp", [(i, i ^ 3) for i in range(n_dp)])
        last = jnp.stack([last, swap_y(last), swap_x(last), over])
        last = last.reshape(n_dp, 2, late, -1)
    columns, late_rows = [], []
    for layer in range(2):
        for number in range(3):
            cols = slice(number * wide, (number + 1) * wide)
            columns.append(shards[layer][:early, cols])
            if late:
                late_rows.append(last[:, layer, :, cols].reshape(n_dp * late, -1))
    columns[0] = jnp.concatenate([columns[0], *both], 0)
    late_at = [(k, early) for k in range(len(columns))]
    if late:
        for k in range(1, len(columns)):
            more = late_rows[:2] if k == 1 else [late_rows[k]]
            columns[k] = jnp.concatenate([columns[k], *more], 0)
        late_at[:2] = [(1, early), (1, early + n_dp * late)]

    tokens = boundary_in.shape[2]
    pad = -tokens % 16
    reach = (tokens + pad) // 2
    ends_in = jnp.pad(boundary_in[0].astype(jnp.bfloat16), ((0, 0), (0, pad), (0, 0)))
    ends_low, ends_high = ends_in[:, :reach], ends_in[:, reach:]
    ends_got = swap(jnp.where(is_first, ends_high, ends_low))
    half_in = jnp.where(is_first, ends_low, ends_got)
    half_cot = jnp.where(is_first, ends_got, ends_high)

    below = [(place - d) % n_tensor for d in range(n_tensor)]
    above = [(place + d) % n_tensor for d in range(n_tensor)]

    def to_send(half):
        return [lax.dynamic_index_in_dim(half, j, 0, False) for j in above]

    width = features // n_tensor
    lanes_in = ((place - order // width) % n_tensor * width + order % width)[None]
    lanes_out = ((order // width - place) % n_tensor * width + order % width)[None]

    def image_half(blocks):
        return place_in(lanes_in, blocks)

    def whole_image(half):
        other = swap(half)
        both = [jnp.where(is_first, half, other), jnp.where(is_first, other, half)]
        return jnp.concatenate(both, 0)

    def image_rows(scale, terms, bias_row):
        start = jnp.where(is_first, 0, reach).astype(jnp.int32).reshape(1)
        blocks = place_out(lanes_out, start, scale.reshape(1), terms, bias_row, n_tensor)
        return [blocks[d] for d in range(n_tensor)]

    def by_image(blocks):
        blocks = jnp.stack(blocks)
        blocks = [lax.dynamic_index_in_dim(blocks, (place - i) % n_tensor, 0, False) for i in range(n_tensor)]
        return jnp.stack(blocks)

    def small_of(extras):
        if n_dp != 4:
            extras = lax.all_gather(extras, "dp", axis=0, tiled=True)
        else:
            over = lax.ppermute(extras, "dp", [(i, i ^ 3) for i in range(n_dp)])
            extras = jnp.concatenate([extras, swap_y(extras), swap_x(extras), over], 0)
        both = by_chip(extras.reshape(n_dp, extra, -1), spot).astype(jnp.float32)
        both = both.reshape(n_dp, 2, extra // 2, n_tensor, wide).transpose(1, 0, 3, 2, 4)
        both = both.reshape(2, n_dp, n_tensor, -1)
        rows = both[..., :n_vec].reshape(2, n_dp, n_tensor, 8, -1)
        rows = rows.transpose(0, 3, 2, 1, 4).reshape(16, -1).astype(jnp.bfloat16)
        rows = mm("kd,dr->kr", rows, pick).reshape(2, 8, -1)
        bias = both[..., n_vec:small_size].transpose(0, 2, 1, 3).reshape(2, -1)
        plain = both[..., :n_vec].reshape(2, n_dp, n_tensor, 8, -1)[..., 2:4, :]
        plain = plain.transpose(0, 3, 2, 1, 4).reshape(2, 2, -1)
        parts = [half_cols(core, plain[:, 0], n_tensor), half_cols(core, plain[:, 1], n_tensor)]
        parts.append(half_cols(core, bias, n_tensor))
        return [(rows[i], parts[0][i : i + 1], parts[1][i : i + 1], parts[2][i : i + 1]) for i in range(2)]

    number = len(columns)
    halves, near, far = [None] * number, [None] * number, [None] * number
    params = [dict(), dict()]
    blocks_in, blocks_cot = to_send(half_in), to_send(half_cot)
    pair, state = None, None

    wholes = [None] * number

    def weights_of(k):
        first, second = arrived(*halves[k], near[k], far[k])
        arrays = first + second
        counts = [(i, 0, p.shape[0]) for i, p in enumerate(arrays)]
        if late:
            source, start = late_at[k]
            counts.append((len(arrays), start, n_dp * late))
            arrays = [*arrays, wholes[source]]
        return (arrays, counts)

    for r in range(number + 1):
        tied = []
        if r < number:
            tied.append(gather_column(columns[r]))
        if 0 <= r - 1 < number:
            near[r - 1] = exchange_one(*halves[r - 1])
        if r == 1:
            smalls = small_of(extra_rows)
            blocks_in = shifts(blocks_in)
        if 2 <= r <= 1 + n_tensor - 1:
            blocks_cot[r - 1] = shift(blocks_cot[r - 1], r - 1)
        if r == number - 1:
            cot_half = image_half(blocks_cot)
        if r == number:
            cotangent = whole_image(cot_half).astype(jnp.float32) * live
        ready = []
        k = r - 2
        if k >= 0:
            layer, kind = k // 3, k % 3
            one = params[layer]
            weights = weights_of(k)
            rows, q_bias, v_bias, up_bias = one["small"]
            if pair is not None:
                pair = [pair[0], swap(pair[0])]
            if kind == 0:
                one["qkvo"] = weights
                if layer == 0:
                    terms = [whole_image(image_half(blocks_in)).astype(jnp.float32)]
                else:
                    terms = [state, *pair]
                bias_row = params[0]["small"][0][7:8]
                done = attention_forward(
                    tokens, terms, bias_row, layer == 1, weights, rows, q_bias, v_bias
                )
                one["u"], one["n1"], one["saved"], part = done[0], done[1], done[2:7], done[7]
                pair, ready = [part], [part]
            elif kind == 1:
                one["up"] = weights
                one["mid"], one["n2"], one["slope"], one["hidden"] = up_forward(
                    [one["u"], *pair], weights, rows, up_bias
                )
                pair, ready = None, [one["hidden"]]
            else:
                one["down"] = weights
                state = one["mid"]
                part = contract_wide(one["hidden"], weights)
                pair, ready = [part], [part]
        if r <= number:
            count = len(ready)
            extras = list(ready)
            if 0 <= r - 1 < number:
                if ready:
                    done = tie(near[r - 1] + extras, [])
                    near[r - 1], extras = done[: len(near[r - 1])], done[len(near[r - 1]) :]
                far[r - 1] = exchange_two(*halves[r - 1], *near[r - 1])
                tied += near[r - 1] + far[r - 1]
            if r <= 1:
                extras += blocks_in
            if r == 1:
                extras += [v for layer in range(2) for v in smalls[layer]]
            if 1 <= r <= number - 2:
                extras += blocks_cot
            elif r == number - 1:
                extras.append(cot_half)
            elif r == number:
                extras.append(cotangent)
            if r + 1 < number:
                extras.append(columns[r + 1])
            done = tie(tied + extras, [])
            if r + 1 < number:
                columns[r + 1] = done.pop()
            if 1 <= r <= number - 2:
                done, blocks_cot = done[:-n_tensor], done[-n_tensor:]
            elif r == number - 1:
                cot_half = done.pop()
            elif r == number:
                cotangent = done.pop()
            if r == 1:
                done, smalls = done[:-8], done[-8:]
                params[0]["small"], params[1]["small"] = smalls[:4], smalls[4:]
            if r <= 1:
                done, blocks_in = done[:-n_tensor], done[-n_tensor:]
            if count and kind == 1:
                one["hidden"] = done[-1]
            elif count:
                pair = [done[-1]]
            at = 0
            if r < number:
                wholes[r] = done[0]
                halves[r] = (done[0][:half_rows], done[0][half_rows:early])
                if r == 0:
                    extra_rows = done[0][early:]
                at = 1
            if 0 <= r - 1 < number:
                near[r - 1] = done[at : at + 2]
                far[r - 1] = done[at + 2 : at + 2 + len(far[r - 1])]

    sums = [dict(), dict()]

    def small_grads():
        packed = []
        for layer in range(2):
            total = sums[layer]
            full = jnp.concatenate([total["one"], total["mid"], total["out"]], 0)
            full = jnp.where(core == layer, full, 0.0).astype(jnp.bfloat16)
            full = mm("kr,dr->kd", full, pick)
            q_row = spread_cols(core, total["q"][0], n_tensor)
            v_row = spread_cols(core, total["v"][0], n_tensor)
            up_row = spread_cols(core, total["up_bias"][0], n_tensor)
            rows = jnp.concatenate([full[:2], q_row[None], v_row[None], full[2:]], 0)
            rows = rows.reshape(8, n_tensor, n_dp, -1).transpose(2, 1, 0, 3).reshape(n_dp, n_tensor, -1)
            up_row = up_row.reshape(n_tensor, n_dp, -1).transpose(1, 0, 2)
            packed.append(jnp.concatenate([rows, up_row], -1))
        ours = jnp.where(is_first, packed[0], packed[1])
        other = swap(jnp.where(is_first, packed[1], packed[0]))
        little = (ours + other).astype(jnp.bfloat16)
        return little

    grads, got, moved, settled = [None] * number, [None] * number, [None] * number, [None] * number
    made = [0, 1, 3, 4, 5, 6]
    grad = cotangent
    last_down = weights_of(number - 1)
    params[1]["down"] = last_down
    last_bias = params[1]["small"][0][7:8]
    for r in range(8):
        layer, stage = 1 - r // 4, r % 4
        one, total = params[layer], sums[layer]
        rows = one["small"][0]
        tied, slots = [], []
        for c in range(number):
            if r == made[c] + 1:
                got[c] = scatter_one(*grads[c][:2])
                slots.append((got, c, len(got[c])))
                tied += got[c]
            elif r == made[c] + 2:
                stay, come = scatter_two(*grads[c][2:], got[c])
                moved[c] = [*stay, *come]
                if r < 7:
                    slots.append((moved, c, len(moved[c])))
                    tied += moved[c]
            elif r == made[c] + 3:
                settled[c] = scatter_column(moved[c][:2], moved[c][2:])
                slots.append((settled, c, 0))
                tied.append(settled[c])
        new = None
        if stage == 0:
            low, total["out"], total["up_bias"], new = down_backward(
                grad, one["hidden"], one["slope"], one["down"]
            )
            carry = [low]
        elif stage == 1:
            part = contract_wide(low, one["up"])
            new = up_grad(one["n2"], low)
            carry = [part]
        elif stage == 2:
            done = attention_backward(
                grad, part, swap(part), one["mid"], rows, one["saved"], one["qkvo"]
            )
            dmid, dz, dq, dk, dv, part, total["mid"], total["q"], total["v"] = done
            if layer == 0:
                new = attention_grad(one["n1"], dz, dq, dk, dv, one["saved"][4])
            carry = [part]
        else:
            if layer == 1:
                new = attention_grad(one["n1"], dz, dq, dk, dv, one["saved"][4])
            grad, total["one"] = value_backward(dmid, part, swap(part), one["u"], rows, layer == 1)
            carry = [grad]
            if r == 7:
                one_scale = jnp.ones((), jnp.float32)
                no_bias = jnp.zeros((1, grad.shape[1]), jnp.float32)
                carry = [small_grads()]
                grad_blocks = shifts(image_rows(one_scale, [grad], no_bias))
        if new is not None:
            c = made.index(r)
            grads[c] = new
            fresh = [g for g in new if g is not None]
        else:
            fresh = []
        if r == 3:
            last_part = contract_wide(params[1]["hidden"], last_down)
            carry.append(last_part)
        elif r == 4:
            out_blocks = image_rows(
                live, [params[1]["mid"], last_part, swap(last_part)], last_bias
            )
        if 4 <= r < 4 + n_tensor - 1:
            out_blocks[r - 3] = shift(out_blocks[r - 3], r - 3)
            carry += out_blocks
        if r < 8:
            done = tie(carry + fresh + tied, [])
            if stage == 0:
                low = done[0]
            elif stage == 1:
                part = done[0]
            elif stage == 2:
                part = done[0]
            elif r < 7:
                grad = done[0]
            else:
                little = done[0]
            if r == 3:
                last_part = done[1]
            elif 4 <= r < 4 + n_tensor - 1:
                out_blocks = done[1 : 1 + n_tensor]
            done = done[len(carry) :]
            if fresh:
                grads[c] = fill(done[: len(fresh)])
                done = done[len(fresh) :]
            for store, at, count in slots:
                store[at] = done[:count] if count else done[0]
                done = done[max(count, 1) :]

    room = jnp.zeros((n_dp, n_tensor, extra * wide - small_size), little.dtype)
    little = jnp.concatenate([little, room], -1).reshape(n_dp, n_tensor, extra, wide)
    little = by_arrival(little.transpose(0, 2, 1, 3).reshape(n_dp, extra, -1), spot)
    if n_dp != 4:
        little = lax.psum_scatter(little, "dp", scatter_dimension=0, tiled=True)[0]
    else:
        little = add(little[:2], swap_x(little[2:])).astype(jnp.bfloat16)
        little = add(little[0], swap_y(little[1])).astype(jnp.bfloat16)

    last = number - 1
    settled[last - 1] = scatter_column(moved[last - 1][:2], moved[last - 1][2:])
    stay, come = scatter_two(*grads[last][2:], got[last])
    done = tie([*grad_blocks, *stay, *come], [])
    grad_blocks, done = done[:n_tensor], done[n_tensor:]
    grad_rows, out_rows = by_image(grad_blocks), by_image(out_blocks)
    stay, come = done[:2], done[2:]
    if come:
        stay = [add(s, c).astype(jnp.bfloat16) for s, c in zip(stay, come)]
    settled[last] = scatter_column([*stay, little], [])
    little = settled[last][depth:].reshape(-1).astype(jnp.float32)
    settled[last] = settled[last][:depth]
    grad_vectors = little[:n_vec].reshape(vectors.shape)
    grad_bias = little[n_vec:small_size].reshape(fc1_bias.shape)

    own = jnp.where(is_first, grad_rows, out_rows)
    other = swap(jnp.where(is_first, out_rows, grad_rows))
    ends = [jnp.where(is_first, own, other), jnp.where(is_first, other, own)]
    boundary_out = jnp.concatenate(ends, 1)[:, :tokens].astype(jnp.float32)[None]
    if late:
        part, cut = late // 2, depth // 2
        for k in range(number):
            rows = settled[k]
            parts = [rows[:half_rows], rows[cut : cut + half_rows]]
            parts += [rows[half_rows:cut], rows[cut + half_rows :]]
            settled[k] = jnp.concatenate(parts, 0)
    lows, highs = [], []
    for kind in range(3):
        first, second = settled[last - kind], settled[last - kind - 3]
        kept = jnp.where(is_first, first, second)
        received = swap(jnp.where(is_first, second, first))
        lows.append(jnp.where(is_first, kept, received).astype(jnp.float32))
        highs.append(jnp.where(is_first, received, kept).astype(jnp.float32))
    low, high = [part[0].reshape(depth, 4, -1) for part in (lows, highs)]
    grad_qkv = jnp.concatenate([low[:, :3], high[:, :3]], 2)[None]
    grad_proj = jnp.concatenate([low[:, 3].T, high[:, 3].T], 0)[None]
    grad_up = jnp.concatenate([lows[1], highs[1]], 1)[None]
    grad_down = jnp.concatenate([lows[2].T, highs[2].T], 0)[None]
    return (boundary_out, grad_qkv, grad_proj, grad_up, grad_down, grad_vectors, grad_bias)


def solution(mesh):
    in_specs = (
        P("section", "dp", None, "tensor"),
        P("dp", None),
        P("section", "dp", None, "tensor"),
        P("section", "tensor", "dp"),
        P("section", "dp", "tensor"),
        P("section", "tensor", "dp"),
        P("section", None, "tensor", "dp"),
        P("section", "tensor", "dp"),
    )
    out_specs = (
        P("section", "dp", None, "tensor"),
        P("section", "dp", None, "tensor"),
        P("section", "tensor", "dp"),
        P("section", "dp", "tensor"),
        P("section", "tensor", "dp"),
        P("section", None, "tensor", "dp"),
        P("section", "tensor", "dp"),
    )
    return jax.shard_map(body, mesh=mesh, in_specs=in_specs, out_specs=out_specs, check_vma=False)
```

```python
import jax
import jax.numpy as jnp
from jax import lax
from jax.experimental import pallas as pl
from jax.experimental.pallas import tpu as pltpu
from jax.sharding import PartitionSpec as P

HD = 64
EPS = 1e-06


def swap(value):
    return lax.ppermute(value, "section", [(0, 1), (1, 0)])


def pair_sum(partial):
    low = partial.astype(jnp.bfloat16)
    return low.astype(jnp.float32) + swap(low).astype(jnp.float32)


def swap_x(value):
    n = lax.axis_size("dp")
    return lax.ppermute(value, "dp", [(i, i ^ 1) for i in range(n)])


def swap_y(value):
    n = lax.axis_size("dp")
    return lax.ppermute(value, "dp", [(i, i ^ 2) for i in range(n)])


def tie(values, others):
    count = len(values)

    def kernel(*refs):
        pass

    anywhere = pl.BlockSpec(memory_space=pl.ANY)
    done = pl.pallas_call(
        kernel,
        out_shape=[jax.ShapeDtypeStruct(v.shape, v.dtype) for v in values],
        in_specs=[anywhere] * (count + len(others)),
        out_specs=[anywhere] * count,
        input_output_aliases={i: i for i in range(count)},
    )(*values, *others)
    return list(done)


def gather_column(shard):
    return lax.all_gather(shard, "tensor", axis=1, tiled=True)


def exchange_one(first, second):
    if lax.axis_size("dp") != 4:
        return [lax.all_gather(v, "dp", axis=0, tiled=True) for v in (first, second)]
    return [swap_y(first), swap_x(second)]


def exchange_two(first, second, near_first, near_second):
    if lax.axis_size("dp") != 4:
        return []
    return [swap_x(first), swap_x(near_first), swap_y(second), swap_y(near_second)]


def arrived(first, second, near, far):
    if lax.axis_size("dp") != 4:
        return ([near[0]], [near[1]])
    return ([first, near[0], far[0], far[1]], [second, near[1], far[2], far[3]])


def row_cuts(depth):
    half = depth // 2
    if lax.axis_size("dp") != 4:
        return [(0, half), (half, depth), None, None]
    part = half // 2
    return [(part, half), (half + part, depth), (0, part), (half, half + part)]


def add(left, right):
    return left.astype(jnp.float32) + right.astype(jnp.float32)


def scatter_one(send_first, send_second):
    if lax.axis_size("dp") != 4:
        return [
            lax.psum_scatter(v, "dp", scatter_dimension=0, tiled=True)
            for v in (send_first, send_second)
        ]
    return [swap_x(send_first), swap_y(send_second)]


def scatter_two(keep_first, keep_second, got):
    if lax.axis_size("dp") != 4:
        return (got, [])
    stay, send = [], []
    for keep, new in zip((keep_first, keep_second), got):
        half = keep.shape[0] // 2
        send.append(add(keep[half:], new[half:]).astype(jnp.bfloat16))
        stay.append(add(keep[:half], new[:half]).astype(jnp.bfloat16))
    return (stay, [swap_y(send[0]), swap_x(send[1])])


def scatter_column(stay, come):
    if come:
        stay = [add(s, c).astype(jnp.bfloat16) for s, c in zip(stay, come)]
    return lax.psum_scatter(
        jnp.concatenate(stay, 0), "tensor", scatter_dimension=1, tiled=True
    )


def flip_axis(value, axis, bit):
    return jnp.where(bit == 1, jnp.flip(value, axis), value)


def relative(value, spot):
    n_dp = lax.axis_size("dp")
    lead = value.shape[:-1]
    k = len(lead)
    if n_dp != 4:
        cut = value.reshape(lead + (n_dp, 2, -1))
        return jnp.swapaxes(cut, k, k + 1).reshape(value.shape)
    cut = value.reshape(lead + (2, 2, 2, -1))
    cut = flip_axis(flip_axis(cut, k, spot // 2), k + 1, spot % 2)
    first = jnp.swapaxes(cut[..., 0, :], k, k + 1)
    second = cut[..., 1, :]
    return jnp.concatenate([first.reshape(lead + (-1,)), second.reshape(lead + (-1,))], -1)


def absolute(value, spot):
    n_dp = lax.axis_size("dp")
    lead = value.shape[:-1]
    k = len(lead)
    if n_dp != 4:
        cut = value.reshape(lead + (2, n_dp, -1))
        return jnp.swapaxes(cut, k, k + 1).reshape(value.shape)
    cut = value.reshape(lead + (2, 2, 2, -1))
    first = jnp.swapaxes(cut[..., 0, :, :, :], k, k + 1)
    second = cut[..., 1, :, :, :]
    cut = jnp.stack([first, second], k + 2)
    cut = flip_axis(flip_axis(cut, k, spot // 2), k + 1, spot % 2)
    return cut.reshape(value.shape)


def by_chip(blocks, spot):
    n_dp = lax.axis_size("dp")
    if n_dp != 4:
        return blocks
    cut = blocks.reshape((2, 2) + blocks.shape[1:])
    cut = jnp.swapaxes(cut, 0, 1)
    cut = flip_axis(flip_axis(cut, 0, spot // 2), 1, spot % 2)
    return cut.reshape(blocks.shape)


def by_arrival(blocks, spot):
    n_dp = lax.axis_size("dp")
    if n_dp != 4:
        return blocks
    cut = blocks.reshape((2, 2) + blocks.shape[1:])
    cut = flip_axis(flip_axis(cut, 0, spot // 2), 1, spot % 2)
    return jnp.swapaxes(cut, 0, 1).reshape(blocks.shape)


VMEM_BYTES = 50 * 2**20
BF = jnp.bfloat16
F32 = jnp.float32


def shape(dims, kind=jnp.bfloat16):
    return jax.ShapeDtypeStruct(dims, kind)


def run(kernel, outs, ins):
    block = pl.BlockSpec(memory_space=pltpu.VMEM)
    done = pl.pallas_call(
        kernel,
        out_shape=list(outs),
        in_specs=[block] * len(ins),
        out_specs=[block] * len(outs),
        cost_estimate=pl.CostEstimate(flops=1, bytes_accessed=1, transcendentals=0),
        compiler_params=pltpu.CompilerParams(vmem_limit_bytes=VMEM_BYTES),
    )(*ins)
    return list(done)


def nn(left, right):
    return lax.dot_general(left, right, (((1,), (0,)), ((), ())), preferred_element_type=F32)


def nt(left, right):
    return lax.dot_general(left, right, (((1,), (1,)), ((), ())), preferred_element_type=F32)


def tn(left, right):
    return lax.dot_general(left, right, (((0,), (0,)), ((), ())), preferred_element_type=F32)


def stack_rows(pieces, counts, cols):
    return jnp.concatenate([p[:n, cols] for p, n in zip(pieces, counts)], 0)


def center_scale(value):
    center = jnp.mean(value, -1, keepdims=True)
    spread = jnp.mean(value * value, -1, keepdims=True) - center * center
    factor = lax.rsqrt(spread + EPS)
    return ((value - center) * factor, factor)


def norm_backward(grad_normed, centred, factor, gain):
    scaled = grad_normed * gain
    return factor * (
        scaled
        - jnp.mean(scaled, -1, keepdims=True)
        - centred * jnp.mean(scaled * centred, -1, keepdims=True)
    )


def column_sum(value):
    return jnp.sum(value, 0, keepdims=True)


def attention_forward(tokens, terms, bias_row, low, weights, rows, q_bias, v_bias):
    pieces, counts = weights
    size, depth = terms[0].shape
    wide = pieces[0].shape[1]
    groups = wide // 512
    half = groups * 128
    n_terms, n_pieces = len(terms), len(pieces)

    def kernel(*refs):
        term_refs, refs = refs[:n_terms], refs[n_terms:]
        bias_ref, rows_ref, qb_ref, vb_ref = refs[:4]
        piece_refs, refs = refs[4 : 4 + n_pieces], refs[4 + n_pieces :]
        u_ref, n_ref, q_ref, k_ref, v_ref, p_ref, o_ref, part_ref = refs
        value = term_refs[0][...].astype(F32)
        for ref in term_refs[1:]:
            value = value + ref[...].astype(F32)
        if n_terms > 1:
            value = value + bias_ref[...]
        if low:
            value = value.astype(BF).astype(F32)
        u_ref[...] = value
        centred, factor = center_scale(value)
        n_ref[...] = (centred * rows_ref[0:1] + rows_ref[1:2]).astype(BF)
        lane = lax.broadcasted_iota(jnp.int32, (size, 128), 1)
        key_lane = lax.broadcasted_iota(jnp.int32, (size, size), 1)
        normed = n_ref[...]
        for g in range(groups):
            at = slice(g * 128, (g + 1) * 128)
            matrix = stack_rows(piece_refs, counts, slice(g * 512, g * 512 + 384))
            projected = nn(normed, matrix)
            q = (projected[:, :128] + qb_ref[:, at]).astype(BF)
            k = projected[:, 128:256].astype(BF)
            v = (projected[:, 256:384] + vb_ref[:, at]).astype(BF)
            q_ref[:, at] = q
            k_ref[:, at] = k
            v_ref[:, at] = v
            mixed = None
            for h in range(2):
                mine = (lane // HD) == h
                scores = nt(jnp.where(mine, q, jnp.zeros_like(q)), k) * HD ** (-0.5)
                scores = jnp.where(key_lane < tokens, scores, -1e30)
                highest = jnp.max(scores, -1, keepdims=True)
                exponent = jnp.exp(scores - highest)
                inverse = 1.0 / jnp.sum(exponent, -1, keepdims=True)
                soft = (exponent * inverse).astype(BF)
                p_ref[2 * g + h] = soft
                out = nn(soft, v)
                mixed = out if h == 0 else jnp.where(mine, out, mixed)
            o_ref[:, at] = mixed.astype(BF)
        matrix = jnp.concatenate(
            [stack_rows(piece_refs, counts, slice(g * 512 + 384, g * 512 + 512)) for g in range(groups)], 1
        )
        part_ref[...] = nt(o_ref[...], matrix).astype(BF)

    outs = [shape((size, depth), F32), shape((size, depth))] + [shape((size, half))] * 3
    outs += [shape((2 * groups, size, size)), shape((size, half)), shape((size, depth))]
    return run(kernel, outs, [*terms, bias_row, rows, q_bias, v_bias, *pieces])


def up_forward(terms, weights, rows, up_bias):
    pieces, counts = weights
    size, depth = terms[0].shape
    wide = pieces[0].shape[1]

    def kernel(*refs):
        u_ref, own_ref, far_ref, rows_ref, bias_ref = refs[:5]
        piece_refs = refs[5 : 5 + len(pieces)]
        mid_ref, n_ref, slope_ref, hidden_ref = refs[5 + len(pieces) :]
        value = u_ref[...] + own_ref[...].astype(F32) + far_ref[...].astype(F32) + rows_ref[4:5]
        mid_ref[...] = value
        centred, factor = center_scale(value)
        n_ref[...] = (centred * rows_ref[5:6] + rows_ref[6:7]).astype(BF)
        step = 512
        for at in range(0, wide, step):
            cols = slice(at, at + step)
            before = nn(n_ref[...], stack_rows(piece_refs, counts, cols)) + bias_ref[:, cols]
            cdf = 0.5 * (1.0 + lax.erf(before * 0.7071067811865476))
            density = jnp.exp(-0.5 * before * before) * 0.3989422804014327
            hidden_ref[:, cols] = (before * cdf).astype(BF)
            slope_ref[:, cols] = (cdf + before * density).astype(BF)

    outs = [shape((size, depth), F32), shape((size, depth)), shape((size, wide)), shape((size, wide))]
    return run(kernel, outs, [*terms, rows, up_bias, *pieces])


def contract_wide(left, weights):
    pieces, counts = weights
    size, wide = left.shape
    depth = sum(counts)

    def kernel(*refs):
        left_ref, piece_refs, out_ref = refs[0], refs[1:-1], refs[-1]
        matrix = stack_rows(piece_refs, counts, slice(0, wide))
        out_ref[...] = nt(left_ref[...], matrix).astype(BF)

    return run(kernel, [shape((size, depth))], [left, *pieces])[0]


def weight_outs(depth, wide):
    cuts = [c for c in row_cuts(depth) if c is not None]
    return cuts, [shape((c[1] - c[0], wide)) for c in cuts]


def fill(grads):
    return (list(grads) + [None, None])[:4]


def down_backward(grad_out, hidden, slope, weights):
    pieces, counts = weights
    size, depth = grad_out.shape
    wide = hidden.shape[1]
    cuts, grad_outs = weight_outs(depth, wide)

    def kernel(*refs):
        g_ref, hidden_ref, slope_ref = refs[:3]
        piece_refs, refs = refs[3 : 3 + len(pieces)], refs[3 + len(pieces) :]
        low_ref, sum_ref, bias_ref = refs[:3]
        sum_ref[...] = column_sum(g_ref[...])
        branch = g_ref[...].astype(BF)
        for cut, ref in zip(cuts, refs[3:]):
            ref[...] = tn(branch[:, cut[0] : cut[1]], hidden_ref[...]).astype(BF)
        step = 512
        for at in range(0, wide, step):
            cols = slice(at, at + step)
            back = nn(branch, stack_rows(piece_refs, counts, cols)) * slope_ref[:, cols].astype(F32)
            bias_ref[:, cols] = column_sum(back)
            low_ref[:, cols] = back.astype(BF)

    outs = [shape((size, wide)), shape((1, depth), F32), shape((1, wide), F32)] + grad_outs
    done = run(kernel, outs, [grad_out, hidden, slope, *pieces])
    return done[0], done[1], done[2], fill(done[3:])


def up_grad(normed, low):
    size, depth = normed.shape
    wide = low.shape[1]
    cuts, outs = weight_outs(depth, wide)

    def kernel(n_ref, low_ref, *refs):
        for cut, ref in zip(cuts, refs):
            ref[...] = tn(n_ref[:, cut[0] : cut[1]], low_ref[...]).astype(BF)

    return fill(run(kernel, outs, [normed, low]))


def attention_backward(grad_out, own, far, middle, rows, saved, weights):
    pieces, counts = weights
    size, depth = grad_out.shape
    wide = pieces[0].shape[1]
    groups = wide // 512
    half = groups * 128
    scale = HD ** (-0.5)

    def kernel(*refs):
        g_ref, own_ref, far_ref, mid_ref, rows_ref, q_ref, k_ref, v_ref, p_ref, o_ref = refs[:10]
        piece_refs, refs = refs[10 : 10 + len(pieces)], refs[10 + len(pieces) :]
        dmid_ref, dz_ref, dq_ref, dk_ref, dv_ref, part_ref, sum_ref, qs_ref, vs_ref = refs
        grad_normed = own_ref[...].astype(F32) + far_ref[...].astype(F32)
        centred, factor = center_scale(mid_ref[...])
        sum_ref[1:2] = column_sum(grad_normed * centred)
        sum_ref[2:3] = column_sum(grad_normed)
        dmid = g_ref[...] + norm_backward(grad_normed, centred, factor, rows_ref[5:6])
        dmid_ref[...] = dmid
        sum_ref[0:1] = column_sum(dmid)
        dz_ref[...] = dmid.astype(BF)
        lane = lax.broadcasted_iota(jnp.int32, (size, 128), 1)
        for g in range(groups):
            at = slice(g * 128, (g + 1) * 128)
            matrix = stack_rows(piece_refs, counts, slice(g * 512 + 384, g * 512 + 512))
            grad_mixed = nn(dz_ref[...], matrix).astype(BF)
            q, k, v = q_ref[:, at], k_ref[:, at], v_ref[:, at]
            inner = grad_mixed.astype(F32) * o_ref[:, at].astype(F32)
            dq, dk, dv = None, None, None
            for h in range(2):
                mine = (lane // HD) == h
                soft = p_ref[2 * g + h]
                none = jnp.zeros_like(q)
                do = jnp.where(mine, grad_mixed, none)
                total = jnp.sum(jnp.where(mine, inner, 0.0), -1, keepdims=True)
                grad_soft = nt(do, v)
                grad_scores = (soft.astype(F32) * (grad_soft - total)).astype(BF)
                new_q = nn(grad_scores, k)
                new_k = tn(jnp.where(mine, q, none), grad_scores)
                new_v = tn(do, soft)
                dq = new_q if h == 0 else jnp.where(mine, new_q, dq)
                dk = new_k if h == 0 else dk + new_k
                dv = new_v if h == 0 else dv + new_v
            dq, dk, dv = dq * scale, dk.T * scale, dv.T
            qs_ref[:, at] = column_sum(dq)
            vs_ref[:, at] = column_sum(dv)
            dq_ref[:, at] = dq.astype(BF)
            dk_ref[:, at] = dk.astype(BF)
            dv_ref[:, at] = dv.astype(BF)
        total = None
        for g in range(groups):
            at = slice(g * 128, (g + 1) * 128)
            left = jnp.concatenate([dq_ref[:, at], dk_ref[:, at], dv_ref[:, at]], 1)
            new = nt(left, stack_rows(piece_refs, counts, slice(g * 512, g * 512 + 384)))
            total = new if g == 0 else total + new
        part_ref[...] = total.astype(BF)

    outs = [shape((size, depth), F32), shape((size, depth))] + [shape((size, half))] * 3
    outs += [shape((size, depth)), shape((3, depth), F32)] + [shape((1, half), F32)] * 2
    return run(kernel, outs, [grad_out, own, far, middle, rows, *saved, *pieces])


def attention_grad(normed, dz, dq, dk, dv, mixed):
    size, depth = normed.shape
    groups = dq.shape[1] // 128
    cuts, outs = weight_outs(depth, groups * 512)

    def kernel(n_ref, dz_ref, dq_ref, dk_ref, dv_ref, o_ref, *refs):
        for cut, ref in zip(cuts, refs):
            rows = slice(cut[0], cut[1])
            for g in range(groups):
                at = slice(g * 128, (g + 1) * 128)
                right = jnp.concatenate([dq_ref[:, at], dk_ref[:, at], dv_ref[:, at]], 1)
                ref[:, g * 512 : g * 512 + 384] = tn(n_ref[:, rows], right).astype(BF)
                ref[:, g * 512 + 384 : g * 512 + 512] = tn(dz_ref[:, rows], o_ref[:, at]).astype(BF)

    return fill(run(kernel, outs, [normed, dz, dq, dk, dv, mixed]))


def value_backward(dmid, own, far, value, rows, low):
    size, depth = dmid.shape

    def kernel(dmid_ref, own_ref, far_ref, u_ref, rows_ref, out_ref, sum_ref):
        grad_normed = own_ref[...].astype(F32) + far_ref[...].astype(F32)
        centred, factor = center_scale(u_ref[...])
        sum_ref[0:1] = column_sum(grad_normed * centred)
        sum_ref[1:2] = column_sum(grad_normed)
        out = dmid_ref[...] + norm_backward(grad_normed, centred, factor, rows_ref[0:1])
        if low:
            out = out.astype(BF).astype(F32)
        out_ref[...] = out

    outs = [shape((size, depth), F32), shape((2, depth), F32)]
    return run(kernel, outs, [dmid, own, far, value, rows])


def block_lanes(spot, chunk):
    ry, rx = chunk // 2 ^ spot // 2, chunk % 2 ^ spot % 2
    return [(rx * 2 + ry) * 128, 512 + (ry * 2 + rx) * 128]


def place_in(lanes, blocks):
    size, width = blocks[0].shape
    half = width // 2

    def kernel(lanes_ref, *refs):
        out_ref = refs[-1]
        for d, ref in enumerate(refs[:-1]):
            for h in range(2):
                at = pl.multiple_of(lanes_ref[2 * d + h], 128)
                out_ref[:, pl.ds(at, half)] = ref[:, h * half : (h + 1) * half]

    block = pl.BlockSpec(memory_space=pltpu.VMEM)
    return pl.pallas_call(
        kernel,
        out_shape=shape((size, width * len(blocks))),
        in_specs=[pl.BlockSpec(memory_space=pltpu.SMEM)] + [block] * len(blocks),
        out_specs=block,
        compiler_params=pltpu.CompilerParams(vmem_limit_bytes=VMEM_BYTES),
    )(lanes, *blocks)


def place_out(numbers, scale, terms, bias_row, count):
    size, depth = terms[0].shape
    width = depth // count
    half = width // 2

    def kernel(numbers_ref, scale_ref, *refs):
        term_refs, bias_ref, out_ref = refs[: len(terms)], refs[-2], refs[-1]
        start = pl.multiple_of(numbers_ref[2 * count], 8)
        rows = pl.ds(start, size // 2)
        for d in range(count):
            for h in range(2):
                lanes = pl.ds(pl.multiple_of(numbers_ref[2 * d + h], 128), half)
                value = term_refs[0][rows, lanes]
                for ref in term_refs[1:]:
                    value = value + ref[rows, lanes]
                value = (value + bias_ref[:, lanes]) * scale_ref[0]
                out_ref[d, :, h * half : (h + 1) * half] = value.astype(BF)

    block = pl.BlockSpec(memory_space=pltpu.VMEM)
    scalar = pl.BlockSpec(memory_space=pltpu.SMEM)
    return pl.pallas_call(
        kernel,
        out_shape=shape((count, size // 2, width)),
        in_specs=[scalar, scalar] + [block] * (len(terms) + 1),
        out_specs=block,
        compiler_params=pltpu.CompilerParams(vmem_limit_bytes=VMEM_BYTES),
    )(numbers, scale, *terms, bias_row)


def shift(block, d):
    n = lax.axis_size("tensor")
    return lax.ppermute(block, "tensor", [(i, (i + d) % n) for i in range(n)])


def shifts(blocks):
    return [blocks[0]] + [shift(block, d) for d, block in enumerate(blocks) if d > 0]


def half_cols(core, whole, n_tensor):
    cut = whole.reshape(whole.shape[:-1] + (n_tensor, 2, -1))
    cut = jnp.where(core == 0, cut[..., 0, :], cut[..., 1, :])
    return cut.reshape(whole.shape[:-1] + (-1,))


def spread_cols(core, half, n_tensor):
    cut = half.reshape(half.shape[:-1] + (n_tensor, 1, -1))
    none = jnp.zeros_like(cut)
    both = jnp.concatenate(
        [jnp.where(core == 0, cut, none), jnp.where(core == 0, none, cut)], -2
    )
    return both.reshape(half.shape[:-1] + (-1,))


def body(boundary_in, counts, qkv_weight, proj_weight, fc1_weight, fc2_weight, vectors, fc1_bias):
    core = lax.axis_index("section")
    is_first = core == 0
    place = lax.axis_index("tensor")
    spot = lax.axis_index("dp")
    n_dp, n_tensor = lax.axis_size("dp"), lax.axis_size("tensor")
    slots_per_batch = boundary_in.shape[1] // counts.shape[1]
    live = (place % slots_per_batch < counts[0, place // slots_per_batch]).astype(jnp.float32)
    depth = qkv_weight.shape[1]
    mid = depth // 2
    n_vec = vectors.size

    small_size = n_vec + fc1_bias.size
    packs = []
    for part in range(2):
        cuts = [
            jnp.split(qkv_weight[0], 2, 2)[part].reshape(depth, -1),
            jnp.split(proj_weight[0], 2, 0)[part].T,
            jnp.split(fc1_weight[0], 2, 1)[part],
            jnp.split(fc2_weight[0], 2, 0)[part].T,
        ]
        packs.append(jnp.concatenate(cuts, 1))
    wide = packs[0].shape[1] // 3
    extra = 16
    small = jnp.concatenate([vectors.reshape(-1), fc1_bias.reshape(-1)])
    small = jnp.pad(small, (0, extra * wide - small_size)).reshape(extra, wide)
    small = jnp.pad(small, ((0, 0), (0, 2 * wide)))
    kept = jnp.concatenate([jnp.where(is_first, packs[0], packs[1]), small], 0)
    received = swap(
        jnp.concatenate([jnp.where(is_first, packs[1], packs[0]), small], 0)
    )
    shards = (jnp.where(is_first, kept, received), jnp.where(is_first, received, kept))
    columns = []
    for layer in range(2):
        for number in range(3):
            cols = shards[layer][:, number * wide : (number + 1) * wide]
            if layer == 0 and number == 0:
                room = extra // 2
                both = [shard[depth : depth + room, :wide] for shard in shards]
                cols = jnp.concatenate([cols[:depth], *both], 0)
            else:
                cols = cols[:depth]
            columns.append(cols)

    tokens = boundary_in.shape[2]
    pad = -tokens % 16
    reach = (tokens + pad) // 2
    ends_in = jnp.pad(boundary_in[0].astype(jnp.bfloat16), ((0, 0), (0, pad), (0, 0)))
    ends_low, ends_high = ends_in[:, :reach], ends_in[:, reach:]
    ends_got = swap(jnp.where(is_first, ends_high, ends_low))
    half_in = jnp.where(is_first, ends_low, ends_got)
    half_cot = jnp.where(is_first, ends_got, ends_high)

    below = [(place - d) % n_tensor for d in range(n_tensor)]
    above = [(place + d) % n_tensor for d in range(n_tensor)]

    def to_send(half):
        return [lax.dynamic_index_in_dim(half, j, 0, False) for j in above]

    def image_half(blocks):
        if n_dp == 4:
            lanes = [lane for t in below for lane in block_lanes(spot, t)]
            return place_in(jnp.stack(lanes).astype(jnp.int32), blocks)
        blocks = jnp.stack(blocks)
        blocks = [lax.dynamic_index_in_dim(blocks, (place - i) % n_tensor, 0, False) for i in range(n_tensor)]
        return relative(jnp.concatenate(blocks, 1), spot)

    def whole_image(half):
        other = swap(half)
        both = [jnp.where(is_first, half, other), jnp.where(is_first, other, half)]
        return jnp.concatenate(both, 0)

    def image_rows(scale, terms, bias_row):
        if n_dp == 4:
            numbers = [lane for t in above for lane in block_lanes(spot, t)]
            numbers.append(jnp.where(is_first, 0, reach))
            numbers = jnp.stack(numbers).astype(jnp.int32)
            blocks = place_out(numbers, scale.reshape(1), terms, bias_row, n_tensor)
            return [blocks[d] for d in range(n_tensor)]
        image = absolute((sum(terms[1:], terms[0]) + bias_row) * scale, spot).astype(jnp.bfloat16)
        half = jnp.where(is_first, image[:reach], image[reach:])
        half = half.reshape(reach, n_tensor, -1).transpose(1, 0, 2)
        return to_send(half)

    def by_image(blocks):
        blocks = jnp.stack(blocks)
        blocks = [lax.dynamic_index_in_dim(blocks, (place - i) % n_tensor, 0, False) for i in range(n_tensor)]
        return jnp.stack(blocks)

    def small_of(extras):
        if n_dp != 4:
            extras = lax.all_gather(extras, "dp", axis=0, tiled=True)
        else:
            over = lax.ppermute(extras, "dp", [(i, i ^ 3) for i in range(n_dp)])
            extras = jnp.concatenate([extras, swap_y(extras), swap_x(extras), over], 0)
        both = by_chip(extras.reshape(n_dp, extra, -1), spot).astype(jnp.float32)
        both = both.reshape(n_dp, 2, extra // 2, n_tensor, wide).transpose(1, 0, 3, 2, 4)
        both = both.reshape(2, n_dp, n_tensor, -1)
        rows = both[..., :n_vec].reshape(2, n_dp, n_tensor, 8, -1)
        rows = relative(rows.transpose(0, 3, 2, 1, 4).reshape(2, 8, -1), spot)
        bias = both[..., n_vec:small_size].transpose(0, 2, 1, 3).reshape(2, -1)
        plain = both[..., :n_vec].reshape(2, n_dp, n_tensor, 8, -1)[..., 2:4, :]
        plain = plain.transpose(0, 3, 2, 1, 4).reshape(2, 2, -1)
        parts = [half_cols(core, plain[:, 0], n_tensor), half_cols(core, plain[:, 1], n_tensor)]
        parts.append(half_cols(core, bias, n_tensor))
        return [(rows[i], parts[0][i : i + 1], parts[1][i : i + 1], parts[2][i : i + 1]) for i in range(2)]

    number = len(columns)
    halves, near, far = [None] * number, [None] * number, [None] * number
    params = [dict(), dict()]
    blocks_in, blocks_cot = to_send(half_in), to_send(half_cot)
    pair, state = None, None

    def weights_of(k):
        first, second = arrived(*halves[k], near[k], far[k])
        return (first + second, [p.shape[0] for p in first + second])

    for r in range(number + 1):
        tied = []
        if r < number:
            tied.append(gather_column(columns[r]))
        if 0 <= r - 1 < number:
            near[r - 1] = exchange_one(*halves[r - 1])
        if r == 1:
            smalls = small_of(extra_rows)
            blocks_in = shifts(blocks_in)
        if 2 <= r <= 1 + n_tensor - 1:
            blocks_cot[r - 1] = shift(blocks_cot[r - 1], r - 1)
        if r == number - 1:
            cot_half = image_half(blocks_cot)
        if r == number:
            cotangent = whole_image(cot_half).astype(jnp.float32) * live
        ready = []
        k = r - 2
        if k >= 0:
            layer, kind = k // 3, k % 3
            one = params[layer]
            weights = weights_of(k)
            rows, q_bias, v_bias, up_bias = one["small"]
            if pair is not None:
                pair = [pair[0], swap(pair[0])]
            if kind == 0:
                one["qkvo"] = weights
                if layer == 0:
                    terms = [whole_image(image_half(blocks_in)).astype(jnp.float32)]
                else:
                    terms = [state, *pair]
                bias_row = params[0]["small"][0][7:8]
                done = attention_forward(
                    tokens, terms, bias_row, layer == 1, weights, rows, q_bias, v_bias
                )
                one["u"], one["n1"], one["saved"], part = done[0], done[1], done[2:7], done[7]
                pair, ready = [part], [part]
            elif kind == 1:
                one["up"] = weights
                one["mid"], one["n2"], one["slope"], one["hidden"] = up_forward(
                    [one["u"], *pair], weights, rows, up_bias
                )
                pair, ready = None, [one["hidden"]]
            else:
                one["down"] = weights
                state = one["mid"]
                part = contract_wide(one["hidden"], weights)
                pair, ready = [part], [part]
        if r <= number:
            count = len(ready)
            extras = list(ready)
            if 0 <= r - 1 < number:
                if ready:
                    done = tie(near[r - 1] + extras, [])
                    near[r - 1], extras = done[: len(near[r - 1])], done[len(near[r - 1]) :]
                far[r - 1] = exchange_two(*halves[r - 1], *near[r - 1])
                tied += near[r - 1] + far[r - 1]
            if r <= 1:
                extras += blocks_in
            if r == 1:
                extras += [v for layer in range(2) for v in smalls[layer]]
            if 1 <= r <= number - 2:
                extras += blocks_cot
            elif r == number - 1:
                extras.append(cot_half)
            elif r == number:
                extras.append(cotangent)
            if r + 1 < number:
                extras.append(columns[r + 1])
            done = tie(tied + extras, [])
            if r + 1 < number:
                columns[r + 1] = done.pop()
            if 1 <= r <= number - 2:
                done, blocks_cot = done[:-n_tensor], done[-n_tensor:]
            elif r == number - 1:
                cot_half = done.pop()
            elif r == number:
                cotangent = done.pop()
            if r == 1:
                done, smalls = done[:-8], done[-8:]
                params[0]["small"], params[1]["small"] = smalls[:4], smalls[4:]
            if r <= 1:
                done, blocks_in = done[:-n_tensor], done[-n_tensor:]
            if count and kind == 1:
                one["hidden"] = done[-1]
            elif count:
                pair = [done[-1]]
            at = 0
            if r < number:
                halves[r] = (done[0][:mid], done[0][mid:depth])
                if r == 0:
                    extra_rows = done[0][depth:]
                at = 1
            if 0 <= r - 1 < number:
                near[r - 1] = done[at : at + 2]
                far[r - 1] = done[at + 2 : at + 2 + len(far[r - 1])]

    sums = [dict(), dict()]

    def small_grads():
        packed = []
        for layer in range(2):
            total = sums[layer]
            full = jnp.concatenate([total["one"], total["mid"], total["out"]], 0)
            full = absolute(jnp.where(core == layer, full, 0.0), spot)
            q_row = spread_cols(core, total["q"][0], n_tensor)
            v_row = spread_cols(core, total["v"][0], n_tensor)
            up_row = spread_cols(core, total["up_bias"][0], n_tensor)
            rows = jnp.concatenate([full[:2], q_row[None], v_row[None], full[2:]], 0)
            rows = rows.reshape(8, n_tensor, n_dp, -1).transpose(2, 1, 0, 3).reshape(n_dp, n_tensor, -1)
            up_row = up_row.reshape(n_tensor, n_dp, -1).transpose(1, 0, 2)
            packed.append(jnp.concatenate([rows, up_row], -1))
        ours = jnp.where(is_first, packed[0], packed[1])
        other = swap(jnp.where(is_first, packed[1], packed[0]))
        little = (ours + other).astype(jnp.bfloat16)
        return little

    grads, got, moved, settled = [None] * number, [None] * number, [None] * number, [None] * number
    grad = cotangent
    last_down = weights_of(number - 1)
    params[1]["down"] = last_down
    last_bias = params[1]["small"][0][7:8]
    rounds = [[(1, 0)], [(1, 1)], [(1, 2)], [(1, 3), (0, 0)], [(0, 1)], [(0, 2)], [(0, 3)]]
    first_at = [1, 2, 3, 4, 5, 6]
    late = [2, 5]
    for r, stages in enumerate(rounds):
        tied, slots = [], []

        def await_all(store, at, arrays):
            slots.append((store, at, len(arrays)))
            tied.extend(arrays)

        for c in range(number):
            if r == first_at[c] and c not in late:
                got[c] = scatter_one(*grads[c][:2])
                await_all(got, c, got[c])
            elif r == first_at[c] + 1:
                stay, come = scatter_two(*grads[c][2:], got[c])
                moved[c] = [*stay, *come]
                if r < len(rounds) - 1:
                    await_all(moved, c, moved[c])
            elif r == first_at[c] + 2:
                settled[c] = [scatter_column(moved[c][:2], moved[c][2:])]
                await_all(settled, c, settled[c])
        for layer, stage in stages:
            one, total = params[layer], sums[layer]
            rows = one["small"][0]
            if stage == 0:
                low, total["out"], total["up_bias"], new = down_backward(
                    grad, one["hidden"], one["slope"], one["down"]
                )
                grads[3 * (1 - layer)] = new
                keep = [low]
            elif stage == 1:
                part = contract_wide(low, one["up"])
                grads[3 * (1 - layer) + 1] = up_grad(one["n2"], low)
                keep = [part]
            elif stage == 2:
                done = attention_backward(
                    grad, part, swap(part), one["mid"], rows, one["saved"], one["qkvo"]
                )
                dmid, dz, dq, dk, dv, part, total["mid"], total["q"], total["v"] = done
                keep = [part, dz]
            else:
                c = 3 * (1 - layer) + 2
                grads[c] = attention_grad(one["n1"], dz, dq, dk, dv, one["saved"][4])
                got[c] = scatter_one(*grads[c][:2])
                await_all(got, c, got[c])
                grad, total["one"] = value_backward(
                    dmid, part, swap(part), one["u"], rows, layer == 1
                )
                keep = []
        if r == 4:
            last_part = contract_wide(params[1]["hidden"], last_down)
            keep.append(last_part)
        elif r == 3:
            keep.append(params[1]["hidden"])
        elif r == 5:
            out_blocks = shifts(
                image_rows(live, [params[1]["mid"], last_part, swap(last_part)], last_bias)
            )
            keep += out_blocks
        elif r == 6:
            one_scale = jnp.ones((), jnp.float32)
            no_bias = jnp.zeros((1, grad.shape[1]), jnp.float32)
            little = small_grads()
            keep.append(little)
            grad_blocks = shifts(image_rows(one_scale, [grad], no_bias))
        waiting = []
        for c in range(number):
            if grads[c] is None or r > first_at[c]:
                continue
            fresh = [g for g in grads[c] if g is not None]
            if r == first_at[c]:
                if c not in late:
                    continue
                fresh = [g for g in grads[c][2:] if g is not None]
            waiting.append((c, len(fresh)))
            keep += fresh
        done = tie(keep + tied, [])
        if r == 0:
            low, done = done[0], done[1:]
        elif r == 3:
            low, params[1]["hidden"], done = done[0], done[1], done[2:]
        elif r == 1:
            part, done = done[0], done[1:]
        elif r == 2 or r == 5:
            part, dz, done = done[0], done[1], done[2:]
        elif r == 4:
            part, last_part, done = done[0], done[1], done[2:]
        if r == 5:
            out_blocks, done = done[:n_tensor], done[n_tensor:]
        elif r == 6:
            little, done = done[0], done[1:]
        for c, count in waiting:
            if r == first_at[c]:
                grads[c][2 : 2 + count] = done[:count]
            else:
                grads[c] = fill(done[:count])
            done = done[count:]
        for store, at, count in slots:
            store[at] = done[:count]
            done = done[count:]

    room = jnp.zeros((n_dp, n_tensor, extra * wide - small_size), little.dtype)
    little = jnp.concatenate([little, room], -1).reshape(n_dp, n_tensor, extra, wide)
    little = by_arrival(little.transpose(0, 2, 1, 3).reshape(n_dp, extra, -1), spot)
    if n_dp != 4:
        little = lax.psum_scatter(little, "dp", scatter_dimension=0, tiled=True)[0]
    else:
        little = add(little[:2], swap_x(little[2:])).astype(jnp.bfloat16)
        little = add(little[0], swap_y(little[1])).astype(jnp.bfloat16)

    last = number - 1
    settled = [value[0] if value else None for value in settled]
    settled[last - 1] = scatter_column(moved[last - 1][:2], moved[last - 1][2:])
    stay, come = scatter_two(*grads[last][2:], got[last])
    done = tie([*grad_blocks, *stay, *come], [])
    grad_blocks, done = done[:n_tensor], done[n_tensor:]
    grad_rows, out_rows = by_image(grad_blocks), by_image(out_blocks)
    stay, come = done[:2], done[2:]
    if come:
        stay = [add(s, c).astype(jnp.bfloat16) for s, c in zip(stay, come)]
    settled[last] = scatter_column([*stay, little], [])
    little = settled[last][depth:].reshape(-1).astype(jnp.float32)
    settled[last] = settled[last][:depth]
    grad_vectors = little[:n_vec].reshape(vectors.shape)
    grad_bias = little[n_vec:small_size].reshape(fc1_bias.shape)

    own = jnp.where(is_first, grad_rows, out_rows)
    other = swap(jnp.where(is_first, out_rows, grad_rows))
    ends = [jnp.where(is_first, own, other), jnp.where(is_first, other, own)]
    boundary_out = jnp.concatenate(ends, 1)[:, :tokens].astype(jnp.float32)[None]
    lows, highs = [], []
    for kind in range(3):
        first, second = settled[last - kind], settled[last - kind - 3]
        kept = jnp.where(is_first, first, second)
        received = swap(jnp.where(is_first, second, first))
        lows.append(jnp.where(is_first, kept, received).astype(jnp.float32))
        highs.append(jnp.where(is_first, received, kept).astype(jnp.float32))
    low, high = [part[0].reshape(depth, 4, -1) for part in (lows, highs)]
    grad_qkv = jnp.concatenate([low[:, :3], high[:, :3]], 2)[None]
    grad_proj = jnp.concatenate([low[:, 3].T, high[:, 3].T], 0)[None]
    grad_up = jnp.concatenate([lows[1], highs[1]], 1)[None]
    grad_down = jnp.concatenate([lows[2].T, highs[2].T], 0)[None]
    return (boundary_out, grad_qkv, grad_proj, grad_up, grad_down, grad_vectors, grad_bias)


def solution(mesh):
    in_specs = (
        P("section", "dp", None, "tensor"),
        P("dp", None),
        P("section", "dp", None, "tensor"),
        P("section", "tensor", "dp"),
        P("section", "dp", "tensor"),
        P("section", "tensor", "dp"),
        P("section", None, "tensor", "dp"),
        P("section", "tensor", "dp"),
    )
    out_specs = (
        P("section", "dp", None, "tensor"),
        P("section", "dp", None, "tensor"),
        P("section", "tensor", "dp"),
        P("section", "dp", "tensor"),
        P("section", "tensor", "dp"),
        P("section", None, "tensor", "dp"),
        P("section", "tensor", "dp"),
    )
    return jax.shard_map(body, mesh=mesh, in_specs=in_specs, out_specs=out_specs, check_vma=False)
```

```python
import jax
import jax.numpy as jnp
from jax import lax
from jax.experimental import pallas as pl
from jax.experimental.pallas import tpu as pltpu
from jax.sharding import PartitionSpec as P

HD = 64
EPS = 1e-06


def swap(value):
    return lax.ppermute(value, "section", [(0, 1), (1, 0)])


def pair_sum(partial):
    low = partial.astype(jnp.bfloat16)
    return low.astype(jnp.float32) + swap(low).astype(jnp.float32)


def swap_x(value):
    n = lax.axis_size("dp")
    return lax.ppermute(value, "dp", [(i, i ^ 1) for i in range(n)])


def swap_y(value):
    n = lax.axis_size("dp")
    return lax.ppermute(value, "dp", [(i, i ^ 2) for i in range(n)])


def tie(values, others):
    count = len(values)

    def kernel(*refs):
        pass

    anywhere = pl.BlockSpec(memory_space=pl.ANY)
    done = pl.pallas_call(
        kernel,
        out_shape=[jax.ShapeDtypeStruct(v.shape, v.dtype) for v in values],
        in_specs=[anywhere] * (count + len(others)),
        out_specs=[anywhere] * count,
        input_output_aliases={i: i for i in range(count)},
    )(*values, *others)
    return list(done)


def gather_column(shard):
    return lax.all_gather(shard, "tensor", axis=1, tiled=True)


def exchange_one(first, second):
    if lax.axis_size("dp") != 4:
        return [lax.all_gather(v, "dp", axis=0, tiled=True) for v in (first, second)]
    return [swap_y(first), swap_x(second)]


def exchange_two(first, second, near_first, near_second):
    if lax.axis_size("dp") != 4:
        return []
    return [swap_x(first), swap_x(near_first), swap_y(second), swap_y(near_second)]


def arrived(first, second, near, far):
    if lax.axis_size("dp") != 4:
        return ([near[0]], [near[1]])
    return ([first, near[0], far[0], far[1]], [second, near[1], far[2], far[3]])


def row_cuts(depth):
    half = depth // 2
    if lax.axis_size("dp") != 4:
        return [(0, half), (half, depth), None, None]
    part = half // 2
    return [(part, half), (half + part, depth), (0, part), (half, half + part)]


def add(left, right):
    return left.astype(jnp.float32) + right.astype(jnp.float32)


def scatter_one(send_first, send_second):
    if lax.axis_size("dp") != 4:
        return [
            lax.psum_scatter(v, "dp", scatter_dimension=0, tiled=True)
            for v in (send_first, send_second)
        ]
    return [swap_x(send_first), swap_y(send_second)]


def scatter_two(keep_first, keep_second, got):
    if lax.axis_size("dp") != 4:
        return (got, [])
    stay, send = [], []
    for keep, new in zip((keep_first, keep_second), got):
        half = keep.shape[0] // 2
        send.append(add(keep[half:], new[half:]).astype(jnp.bfloat16))
        stay.append(add(keep[:half], new[:half]).astype(jnp.bfloat16))
    return (stay, [swap_y(send[0]), swap_x(send[1])])


def scatter_column(stay, come):
    if come:
        stay = [add(s, c).astype(jnp.bfloat16) for s, c in zip(stay, come)]
    return lax.psum_scatter(
        jnp.concatenate(stay, 0), "tensor", scatter_dimension=1, tiled=True
    )


def flip_axis(value, axis, bit):
    return jnp.where(bit == 1, jnp.flip(value, axis), value)


def relative(value, spot):
    n_dp = lax.axis_size("dp")
    lead = value.shape[:-1]
    k = len(lead)
    if n_dp != 4:
        cut = value.reshape(lead + (n_dp, 2, -1))
        return jnp.swapaxes(cut, k, k + 1).reshape(value.shape)
    cut = value.reshape(lead + (2, 2, 2, -1))
    cut = flip_axis(flip_axis(cut, k, spot // 2), k + 1, spot % 2)
    first = jnp.swapaxes(cut[..., 0, :], k, k + 1)
    second = cut[..., 1, :]
    return jnp.concatenate([first.reshape(lead + (-1,)), second.reshape(lead + (-1,))], -1)


def absolute(value, spot):
    n_dp = lax.axis_size("dp")
    lead = value.shape[:-1]
    k = len(lead)
    if n_dp != 4:
        cut = value.reshape(lead + (2, n_dp, -1))
        return jnp.swapaxes(cut, k, k + 1).reshape(value.shape)
    cut = value.reshape(lead + (2, 2, 2, -1))
    first = jnp.swapaxes(cut[..., 0, :, :, :], k, k + 1)
    second = cut[..., 1, :, :, :]
    cut = jnp.stack([first, second], k + 2)
    cut = flip_axis(flip_axis(cut, k, spot // 2), k + 1, spot % 2)
    return cut.reshape(value.shape)


def by_chip(blocks, spot):
    n_dp = lax.axis_size("dp")
    if n_dp != 4:
        return blocks
    cut = blocks.reshape((2, 2) + blocks.shape[1:])
    cut = jnp.swapaxes(cut, 0, 1)
    cut = flip_axis(flip_axis(cut, 0, spot // 2), 1, spot % 2)
    return cut.reshape(blocks.shape)


def by_arrival(blocks, spot):
    n_dp = lax.axis_size("dp")
    if n_dp != 4:
        return blocks
    cut = blocks.reshape((2, 2) + blocks.shape[1:])
    cut = flip_axis(flip_axis(cut, 0, spot // 2), 1, spot % 2)
    return jnp.swapaxes(cut, 0, 1).reshape(blocks.shape)


VMEM_BYTES = 50 * 2**20
BF = jnp.bfloat16
F32 = jnp.float32


def shape(dims, kind=jnp.bfloat16):
    return jax.ShapeDtypeStruct(dims, kind)


def run(kernel, outs, ins):
    block = pl.BlockSpec(memory_space=pltpu.VMEM)
    done = pl.pallas_call(
        kernel,
        out_shape=list(outs),
        in_specs=[block] * len(ins),
        out_specs=[block] * len(outs),
        cost_estimate=pl.CostEstimate(flops=1, bytes_accessed=1, transcendentals=0),
        compiler_params=pltpu.CompilerParams(vmem_limit_bytes=VMEM_BYTES),
    )(*ins)
    return list(done)


def nn(left, right):
    return lax.dot_general(left, right, (((1,), (0,)), ((), ())), preferred_element_type=F32)


def nt(left, right):
    return lax.dot_general(left, right, (((1,), (1,)), ((), ())), preferred_element_type=F32)


def tn(left, right):
    return lax.dot_general(left, right, (((0,), (0,)), ((), ())), preferred_element_type=F32)


def stack_rows(pieces, counts, cols):
    return jnp.concatenate([p[:n, cols] for p, n in zip(pieces, counts)], 0)


def center_scale(value):
    center = jnp.mean(value, -1, keepdims=True)
    spread = jnp.mean(value * value, -1, keepdims=True) - center * center
    factor = lax.rsqrt(spread + EPS)
    return ((value - center) * factor, factor)


def norm_backward(grad_normed, centred, factor, gain):
    scaled = grad_normed * gain
    return factor * (
        scaled
        - jnp.mean(scaled, -1, keepdims=True)
        - centred * jnp.mean(scaled * centred, -1, keepdims=True)
    )


def column_sum(value):
    return jnp.sum(value, 0, keepdims=True)


def attention_forward(tokens, terms, bias_row, low, weights, rows, q_bias, v_bias):
    pieces, counts = weights
    size, depth = terms[0].shape
    wide = pieces[0].shape[1]
    groups = wide // 512
    half = groups * 128
    n_terms, n_pieces = len(terms), len(pieces)

    def kernel(*refs):
        term_refs, refs = refs[:n_terms], refs[n_terms:]
        bias_ref, rows_ref, qb_ref, vb_ref = refs[:4]
        piece_refs, refs = refs[4 : 4 + n_pieces], refs[4 + n_pieces :]
        u_ref, n_ref, q_ref, k_ref, v_ref, p_ref, o_ref, part_ref = refs
        value = term_refs[0][...].astype(F32)
        for ref in term_refs[1:]:
            value = value + ref[...].astype(F32)
        if n_terms > 1:
            value = value + bias_ref[...]
        if low:
            value = value.astype(BF).astype(F32)
        u_ref[...] = value
        centred, factor = center_scale(value)
        n_ref[...] = (centred * rows_ref[0:1] + rows_ref[1:2]).astype(BF)
        lane = lax.broadcasted_iota(jnp.int32, (size, 128), 1)
        key_lane = lax.broadcasted_iota(jnp.int32, (size, size), 1)
        normed = n_ref[...]
        for g in range(groups):
            at = slice(g * 128, (g + 1) * 128)
            matrix = stack_rows(piece_refs, counts, slice(g * 512, g * 512 + 384))
            projected = nn(normed, matrix)
            q = (projected[:, :128] + qb_ref[:, at]).astype(BF)
            k = projected[:, 128:256].astype(BF)
            v = (projected[:, 256:384] + vb_ref[:, at]).astype(BF)
            q_ref[:, at] = q
            k_ref[:, at] = k
            v_ref[:, at] = v
            mixed = None
            for h in range(2):
                mine = (lane // HD) == h
                scores = nt(jnp.where(mine, q, jnp.zeros_like(q)), k) * HD ** (-0.5)
                scores = jnp.where(key_lane < tokens, scores, -1e30)
                highest = jnp.max(scores, -1, keepdims=True)
                exponent = jnp.exp(scores - highest)
                inverse = 1.0 / jnp.sum(exponent, -1, keepdims=True)
                soft = (exponent * inverse).astype(BF)
                p_ref[2 * g + h] = soft
                out = nn(soft, v)
                mixed = out if h == 0 else jnp.where(mine, out, mixed)
            o_ref[:, at] = mixed.astype(BF)
        matrix = jnp.concatenate(
            [stack_rows(piece_refs, counts, slice(g * 512 + 384, g * 512 + 512)) for g in range(groups)], 1
        )
        part_ref[...] = nt(o_ref[...], matrix).astype(BF)

    outs = [shape((size, depth), F32), shape((size, depth))] + [shape((size, half))] * 3
    outs += [shape((2 * groups, size, size)), shape((size, half)), shape((size, depth))]
    return run(kernel, outs, [*terms, bias_row, rows, q_bias, v_bias, *pieces])


def up_forward(terms, weights, rows, up_bias):
    pieces, counts = weights
    size, depth = terms[0].shape
    wide = pieces[0].shape[1]

    def kernel(*refs):
        u_ref, own_ref, far_ref, rows_ref, bias_ref = refs[:5]
        piece_refs = refs[5 : 5 + len(pieces)]
        mid_ref, n_ref, slope_ref, hidden_ref = refs[5 + len(pieces) :]
        value = u_ref[...] + own_ref[...].astype(F32) + far_ref[...].astype(F32) + rows_ref[4:5]
        mid_ref[...] = value
        centred, factor = center_scale(value)
        n_ref[...] = (centred * rows_ref[5:6] + rows_ref[6:7]).astype(BF)
        step = 512
        for at in range(0, wide, step):
            cols = slice(at, at + step)
            before = nn(n_ref[...], stack_rows(piece_refs, counts, cols)) + bias_ref[:, cols]
            cdf = 0.5 * (1.0 + lax.erf(before * 0.7071067811865476))
            density = jnp.exp(-0.5 * before * before) * 0.3989422804014327
            hidden_ref[:, cols] = (before * cdf).astype(BF)
            slope_ref[:, cols] = (cdf + before * density).astype(BF)

    outs = [shape((size, depth), F32), shape((size, depth)), shape((size, wide)), shape((size, wide))]
    return run(kernel, outs, [*terms, rows, up_bias, *pieces])


def contract_wide(left, weights):
    pieces, counts = weights
    size, wide = left.shape
    depth = sum(counts)

    def kernel(*refs):
        left_ref, piece_refs, out_ref = refs[0], refs[1:-1], refs[-1]
        matrix = stack_rows(piece_refs, counts, slice(0, wide))
        out_ref[...] = nt(left_ref[...], matrix).astype(BF)

    return run(kernel, [shape((size, depth))], [left, *pieces])[0]


def weight_outs(depth, wide):
    cuts = [c for c in row_cuts(depth) if c is not None]
    return cuts, [shape((c[1] - c[0], wide)) for c in cuts]


def fill(grads):
    return (list(grads) + [None, None])[:4]


def down_grad(grad_out, hidden):
    size, depth = grad_out.shape
    cuts, outs = weight_outs(depth, hidden.shape[1])

    def kernel(g_ref, hidden_ref, sum_ref, *refs):
        sum_ref[...] = column_sum(g_ref[...])
        branch = g_ref[...].astype(BF)
        for cut, ref in zip(cuts, refs):
            ref[...] = tn(branch[:, cut[0] : cut[1]], hidden_ref[...]).astype(BF)

    done = run(kernel, [shape((1, depth), F32)] + outs, [grad_out, hidden])
    return done[0], fill(done[1:])


def down_backward(grad_out, slope, weights):
    pieces, counts = weights
    size, depth = grad_out.shape
    wide = slope.shape[1]

    def kernel(*refs):
        g_ref, slope_ref, piece_refs = refs[0], refs[1], refs[2:-2]
        low_ref, bias_ref = refs[-2:]
        branch = g_ref[...].astype(BF)
        step = 512
        for at in range(0, wide, step):
            cols = slice(at, at + step)
            back = nn(branch, stack_rows(piece_refs, counts, cols)) * slope_ref[:, cols].astype(F32)
            bias_ref[:, cols] = column_sum(back)
            low_ref[:, cols] = back.astype(BF)

    outs = [shape((size, wide)), shape((1, wide), F32)]
    return run(kernel, outs, [grad_out, slope, *pieces])


def up_grad(normed, low):
    size, depth = normed.shape
    wide = low.shape[1]
    cuts, outs = weight_outs(depth, wide)

    def kernel(n_ref, low_ref, *refs):
        for cut, ref in zip(cuts, refs):
            ref[...] = tn(n_ref[:, cut[0] : cut[1]], low_ref[...]).astype(BF)

    return fill(run(kernel, outs, [normed, low]))


def attention_backward(grad_out, own, far, middle, rows, saved, weights):
    pieces, counts = weights
    size, depth = grad_out.shape
    wide = pieces[0].shape[1]
    groups = wide // 512
    half = groups * 128
    scale = HD ** (-0.5)

    def kernel(*refs):
        g_ref, own_ref, far_ref, mid_ref, rows_ref, q_ref, k_ref, v_ref, p_ref, o_ref = refs[:10]
        piece_refs, refs = refs[10 : 10 + len(pieces)], refs[10 + len(pieces) :]
        dmid_ref, dz_ref, dq_ref, dk_ref, dv_ref, part_ref, sum_ref, qs_ref, vs_ref = refs
        grad_normed = own_ref[...].astype(F32) + far_ref[...].astype(F32)
        centred, factor = center_scale(mid_ref[...])
        sum_ref[1:2] = column_sum(grad_normed * centred)
        sum_ref[2:3] = column_sum(grad_normed)
        dmid = g_ref[...] + norm_backward(grad_normed, centred, factor, rows_ref[5:6])
        dmid_ref[...] = dmid
        sum_ref[0:1] = column_sum(dmid)
        dz_ref[...] = dmid.astype(BF)
        lane = lax.broadcasted_iota(jnp.int32, (size, 128), 1)
        for g in range(groups):
            at = slice(g * 128, (g + 1) * 128)
            matrix = stack_rows(piece_refs, counts, slice(g * 512 + 384, g * 512 + 512))
            grad_mixed = nn(dz_ref[...], matrix).astype(BF)
            q, k, v = q_ref[:, at], k_ref[:, at], v_ref[:, at]
            inner = grad_mixed.astype(F32) * o_ref[:, at].astype(F32)
            dq, dk, dv = None, None, None
            for h in range(2):
                mine = (lane // HD) == h
                soft = p_ref[2 * g + h]
                none = jnp.zeros_like(q)
                do = jnp.where(mine, grad_mixed, none)
                total = jnp.sum(jnp.where(mine, inner, 0.0), -1, keepdims=True)
                grad_soft = nt(do, v)
                grad_scores = (soft.astype(F32) * (grad_soft - total)).astype(BF)
                new_q = nn(grad_scores, k)
                new_k = tn(jnp.where(mine, q, none), grad_scores)
                new_v = tn(do, soft)
                dq = new_q if h == 0 else jnp.where(mine, new_q, dq)
                dk = new_k if h == 0 else dk + new_k
                dv = new_v if h == 0 else dv + new_v
            dq, dk, dv = dq * scale, dk.T * scale, dv.T
            qs_ref[:, at] = column_sum(dq)
            vs_ref[:, at] = column_sum(dv)
            dq_ref[:, at] = dq.astype(BF)
            dk_ref[:, at] = dk.astype(BF)
            dv_ref[:, at] = dv.astype(BF)
        total = None
        for g in range(groups):
            at = slice(g * 128, (g + 1) * 128)
            left = jnp.concatenate([dq_ref[:, at], dk_ref[:, at], dv_ref[:, at]], 1)
            new = nt(left, stack_rows(piece_refs, counts, slice(g * 512, g * 512 + 384)))
            total = new if g == 0 else total + new
        part_ref[...] = total.astype(BF)

    outs = [shape((size, depth), F32), shape((size, depth))] + [shape((size, half))] * 3
    outs += [shape((size, depth)), shape((3, depth), F32)] + [shape((1, half), F32)] * 2
    return run(kernel, outs, [grad_out, own, far, middle, rows, *saved, *pieces])


def attention_grad(normed, dz, dq, dk, dv, mixed):
    size, depth = normed.shape
    groups = dq.shape[1] // 128
    cuts, outs = weight_outs(depth, groups * 512)

    def kernel(n_ref, dz_ref, dq_ref, dk_ref, dv_ref, o_ref, *refs):
        for cut, ref in zip(cuts, refs):
            rows = slice(cut[0], cut[1])
            for g in range(groups):
                at = slice(g * 128, (g + 1) * 128)
                right = jnp.concatenate([dq_ref[:, at], dk_ref[:, at], dv_ref[:, at]], 1)
                ref[:, g * 512 : g * 512 + 384] = tn(n_ref[:, rows], right).astype(BF)
                ref[:, g * 512 + 384 : g * 512 + 512] = tn(dz_ref[:, rows], o_ref[:, at]).astype(BF)

    return fill(run(kernel, outs, [normed, dz, dq, dk, dv, mixed]))


def value_backward(dmid, own, far, value, rows, low):
    size, depth = dmid.shape

    def kernel(dmid_ref, own_ref, far_ref, u_ref, rows_ref, out_ref, sum_ref):
        grad_normed = own_ref[...].astype(F32) + far_ref[...].astype(F32)
        centred, factor = center_scale(u_ref[...])
        sum_ref[0:1] = column_sum(grad_normed * centred)
        sum_ref[1:2] = column_sum(grad_normed)
        out = dmid_ref[...] + norm_backward(grad_normed, centred, factor, rows_ref[0:1])
        if low:
            out = out.astype(BF).astype(F32)
        out_ref[...] = out

    outs = [shape((size, depth), F32), shape((2, depth), F32)]
    return run(kernel, outs, [dmid, own, far, value, rows])


def block_lanes(spot, chunk):
    ry, rx = chunk // 2 ^ spot // 2, chunk % 2 ^ spot % 2
    return [(rx * 2 + ry) * 128, 512 + (ry * 2 + rx) * 128]


def place_in(lanes, blocks):
    size, width = blocks[0].shape
    half = width // 2

    def kernel(lanes_ref, *refs):
        out_ref = refs[-1]
        for d, ref in enumerate(refs[:-1]):
            for h in range(2):
                at = pl.multiple_of(lanes_ref[2 * d + h], 128)
                out_ref[:, pl.ds(at, half)] = ref[:, h * half : (h + 1) * half]

    block = pl.BlockSpec(memory_space=pltpu.VMEM)
    return pl.pallas_call(
        kernel,
        out_shape=shape((size, width * len(blocks))),
        in_specs=[pl.BlockSpec(memory_space=pltpu.SMEM)] + [block] * len(blocks),
        out_specs=block,
        compiler_params=pltpu.CompilerParams(vmem_limit_bytes=VMEM_BYTES),
    )(lanes, *blocks)


def place_out(numbers, scale, terms, bias_row, count):
    size, depth = terms[0].shape
    width = depth // count
    half = width // 2

    def kernel(numbers_ref, scale_ref, *refs):
        term_refs, bias_ref, out_ref = refs[: len(terms)], refs[-2], refs[-1]
        start = pl.multiple_of(numbers_ref[2 * count], 8)
        rows = pl.ds(start, size // 2)
        for d in range(count):
            for h in range(2):
                lanes = pl.ds(pl.multiple_of(numbers_ref[2 * d + h], 128), half)
                value = term_refs[0][rows, lanes]
                for ref in term_refs[1:]:
                    value = value + ref[rows, lanes]
                value = (value + bias_ref[:, lanes]) * scale_ref[0]
                out_ref[d, :, h * half : (h + 1) * half] = value.astype(BF)

    block = pl.BlockSpec(memory_space=pltpu.VMEM)
    scalar = pl.BlockSpec(memory_space=pltpu.SMEM)
    return pl.pallas_call(
        kernel,
        out_shape=shape((count, size // 2, width)),
        in_specs=[scalar, scalar] + [block] * (len(terms) + 1),
        out_specs=block,
        compiler_params=pltpu.CompilerParams(vmem_limit_bytes=VMEM_BYTES),
    )(numbers, scale, *terms, bias_row)


def shift(block, d):
    n = lax.axis_size("tensor")
    return lax.ppermute(block, "tensor", [(i, (i + d) % n) for i in range(n)])


def shifts(blocks):
    return [blocks[0]] + [shift(block, d) for d, block in enumerate(blocks) if d > 0]


def half_cols(core, whole, n_tensor):
    cut = whole.reshape(whole.shape[:-1] + (n_tensor, 2, -1))
    cut = jnp.where(core == 0, cut[..., 0, :], cut[..., 1, :])
    return cut.reshape(whole.shape[:-1] + (-1,))


def spread_cols(core, half, n_tensor):
    cut = half.reshape(half.shape[:-1] + (n_tensor, 1, -1))
    none = jnp.zeros_like(cut)
    both = jnp.concatenate(
        [jnp.where(core == 0, cut, none), jnp.where(core == 0, none, cut)], -2
    )
    return both.reshape(half.shape[:-1] + (-1,))


def body(boundary_in, counts, qkv_weight, proj_weight, fc1_weight, fc2_weight, vectors, fc1_bias):
    core = lax.axis_index("section")
    is_first = core == 0
    place = lax.axis_index("tensor")
    spot = lax.axis_index("dp")
    n_dp, n_tensor = lax.axis_size("dp"), lax.axis_size("tensor")
    slots_per_batch = boundary_in.shape[1] // counts.shape[1]
    live = (place % slots_per_batch < counts[0, place // slots_per_batch]).astype(jnp.float32)
    depth = qkv_weight.shape[1]
    mid = depth // 2
    n_vec = vectors.size

    small_size = n_vec + fc1_bias.size
    packs = []
    for part in range(2):
        cuts = [
            jnp.split(qkv_weight[0], 2, 2)[part].reshape(depth, -1),
            jnp.split(proj_weight[0], 2, 0)[part].T,
            jnp.split(fc1_weight[0], 2, 1)[part],
            jnp.split(fc2_weight[0], 2, 0)[part].T,
        ]
        packs.append(jnp.concatenate(cuts, 1))
    wide = packs[0].shape[1] // 3
    extra = 16
    small = jnp.concatenate([vectors.reshape(-1), fc1_bias.reshape(-1)])
    small = jnp.pad(small, (0, extra * wide - small_size)).reshape(extra, wide)
    small = jnp.pad(small, ((0, 0), (0, 2 * wide)))
    kept = jnp.concatenate([jnp.where(is_first, packs[0], packs[1]), small], 0)
    received = swap(
        jnp.concatenate([jnp.where(is_first, packs[1], packs[0]), small], 0)
    )
    shards = (jnp.where(is_first, kept, received), jnp.where(is_first, received, kept))
    columns = []
    for layer in range(2):
        for number in range(3):
            cols = shards[layer][:, number * wide : (number + 1) * wide]
            if layer == 0 and number == 0:
                room = extra // 2
                both = [shard[depth : depth + room, :wide] for shard in shards]
                cols = jnp.concatenate([cols[:depth], *both], 0)
            else:
                cols = cols[:depth]
            columns.append(cols)

    tokens = boundary_in.shape[2]
    pad = -tokens % 16
    reach = (tokens + pad) // 2
    ends_in = jnp.pad(boundary_in[0].astype(jnp.bfloat16), ((0, 0), (0, pad), (0, 0)))
    ends_low, ends_high = ends_in[:, :reach], ends_in[:, reach:]
    ends_got = swap(jnp.where(is_first, ends_high, ends_low))
    half_in = jnp.where(is_first, ends_low, ends_got)
    half_cot = jnp.where(is_first, ends_got, ends_high)

    below = [(place - d) % n_tensor for d in range(n_tensor)]
    above = [(place + d) % n_tensor for d in range(n_tensor)]

    def to_send(half):
        return [lax.dynamic_index_in_dim(half, j, 0, False) for j in above]

    def image_half(blocks):
        if n_dp == 4:
            lanes = [lane for t in below for lane in block_lanes(spot, t)]
            return place_in(jnp.stack(lanes).astype(jnp.int32), blocks)
        blocks = jnp.stack(blocks)
        blocks = [lax.dynamic_index_in_dim(blocks, (place - i) % n_tensor, 0, False) for i in range(n_tensor)]
        return relative(jnp.concatenate(blocks, 1), spot)

    def whole_image(half):
        other = swap(half)
        both = [jnp.where(is_first, half, other), jnp.where(is_first, other, half)]
        return jnp.concatenate(both, 0)

    def image_rows(scale, terms, bias_row):
        if n_dp == 4:
            numbers = [lane for t in above for lane in block_lanes(spot, t)]
            numbers.append(jnp.where(is_first, 0, reach))
            numbers = jnp.stack(numbers).astype(jnp.int32)
            blocks = place_out(numbers, scale.reshape(1), terms, bias_row, n_tensor)
            return [blocks[d] for d in range(n_tensor)]
        image = absolute((sum(terms[1:], terms[0]) + bias_row) * scale, spot).astype(jnp.bfloat16)
        half = jnp.where(is_first, image[:reach], image[reach:])
        half = half.reshape(reach, n_tensor, -1).transpose(1, 0, 2)
        return to_send(half)

    def by_image(blocks):
        blocks = jnp.stack(blocks)
        blocks = [lax.dynamic_index_in_dim(blocks, (place - i) % n_tensor, 0, False) for i in range(n_tensor)]
        return jnp.stack(blocks)

    def small_of(extras):
        if n_dp != 4:
            extras = lax.all_gather(extras, "dp", axis=0, tiled=True)
        else:
            over = lax.ppermute(extras, "dp", [(i, i ^ 3) for i in range(n_dp)])
            extras = jnp.concatenate([extras, swap_y(extras), swap_x(extras), over], 0)
        both = by_chip(extras.reshape(n_dp, extra, -1), spot).astype(jnp.float32)
        both = both.reshape(n_dp, 2, extra // 2, n_tensor, wide).transpose(1, 0, 3, 2, 4)
        both = both.reshape(2, n_dp, n_tensor, -1)
        rows = both[..., :n_vec].reshape(2, n_dp, n_tensor, 8, -1)
        rows = relative(rows.transpose(0, 3, 2, 1, 4).reshape(2, 8, -1), spot)
        bias = both[..., n_vec:small_size].transpose(0, 2, 1, 3).reshape(2, -1)
        plain = both[..., :n_vec].reshape(2, n_dp, n_tensor, 8, -1)[..., 2:4, :]
        plain = plain.transpose(0, 3, 2, 1, 4).reshape(2, 2, -1)
        parts = [half_cols(core, plain[:, 0], n_tensor), half_cols(core, plain[:, 1], n_tensor)]
        parts.append(half_cols(core, bias, n_tensor))
        return [(rows[i], parts[0][i : i + 1], parts[1][i : i + 1], parts[2][i : i + 1]) for i in range(2)]

    number = len(columns)
    halves, near, far = [None] * number, [None] * number, [None] * number
    params = [dict(), dict()]
    blocks_in, blocks_cot = to_send(half_in), to_send(half_cot)
    pair, state = None, None

    def weights_of(k):
        first, second = arrived(*halves[k], near[k], far[k])
        return (first + second, [p.shape[0] for p in first + second])

    for r in range(number + 1):
        tied = []
        if r < number:
            tied.append(gather_column(columns[r]))
        if 0 <= r - 1 < number:
            near[r - 1] = exchange_one(*halves[r - 1])
        if r == 1:
            smalls = small_of(extra_rows)
            blocks_in = shifts(blocks_in)
        if 2 <= r <= 1 + n_tensor - 1:
            blocks_cot[r - 1] = shift(blocks_cot[r - 1], r - 1)
        if r == number - 1:
            cot_half = image_half(blocks_cot)
        if r == number:
            cotangent = whole_image(cot_half).astype(jnp.float32) * live
        ready = []
        k = r - 2
        if k >= 0:
            layer, kind = k // 3, k % 3
            one = params[layer]
            weights = weights_of(k)
            rows, q_bias, v_bias, up_bias = one["small"]
            if pair is not None:
                pair = [pair[0], swap(pair[0])]
            if kind == 0:
                one["qkvo"] = weights
                if layer == 0:
                    terms = [whole_image(image_half(blocks_in)).astype(jnp.float32)]
                else:
                    terms = [state, *pair]
                bias_row = params[0]["small"][0][7:8]
                done = attention_forward(
                    tokens, terms, bias_row, layer == 1, weights, rows, q_bias, v_bias
                )
                one["u"], one["n1"], one["saved"], part = done[0], done[1], done[2:7], done[7]
                pair, ready = [part], [part]
            elif kind == 1:
                one["up"] = weights
                one["mid"], one["n2"], one["slope"], one["hidden"] = up_forward(
                    [one["u"], *pair], weights, rows, up_bias
                )
                pair, ready = None, [one["hidden"]]
            else:
                one["down"] = weights
                state = one["mid"]
                part = contract_wide(one["hidden"], weights)
                pair, ready = [part], [part]
        if r <= number:
            count = len(ready)
            extras = list(ready)
            if 0 <= r - 1 < number:
                if ready:
                    done = tie(near[r - 1] + extras, [])
                    near[r - 1], extras = done[: len(near[r - 1])], done[len(near[r - 1]) :]
                far[r - 1] = exchange_two(*halves[r - 1], *near[r - 1])
                tied += near[r - 1] + far[r - 1]
            if r == number:
                last_sum, first_grads = down_grad(cotangent, extras[0])
                first_grads = [g for g in first_grads if g is not None]
                extras += first_grads
            if r <= 1:
                extras += blocks_in
            if r == 1:
                extras += [v for layer in range(2) for v in smalls[layer]]
            if 1 <= r <= number - 2:
                extras += blocks_cot
            elif r == number - 1:
                extras.append(cot_half)
            elif r == number:
                extras.append(cotangent)
            if r + 1 < number:
                extras.append(columns[r + 1])
            done = tie(tied + extras, [])
            if r + 1 < number:
                columns[r + 1] = done.pop()
            if 1 <= r <= number - 2:
                done, blocks_cot = done[:-n_tensor], done[-n_tensor:]
            elif r == number - 1:
                cot_half = done.pop()
            elif r == number:
                cotangent = done.pop()
                done, first_grads = done[: -len(first_grads)], done[-len(first_grads) :]
            if r == 1:
                done, smalls = done[:-8], done[-8:]
                params[0]["small"], params[1]["small"] = smalls[:4], smalls[4:]
            if r <= 1:
                done, blocks_in = done[:-n_tensor], done[-n_tensor:]
            if count and kind == 1:
                one["hidden"] = done[-1]
            elif count:
                pair = [done[-1]]
            at = 0
            if r < number:
                halves[r] = (done[0][:mid], done[0][mid:depth])
                if r == 0:
                    extra_rows = done[0][depth:]
                at = 1
            if 0 <= r - 1 < number:
                near[r - 1] = done[at : at + 2]
                far[r - 1] = done[at + 2 : at + 2 + len(far[r - 1])]

    sums = [dict(), dict()]

    def small_grads():
        packed = []
        for layer in range(2):
            total = sums[layer]
            full = jnp.concatenate([total["one"], total["mid"], total["out"]], 0)
            full = absolute(jnp.where(core == layer, full, 0.0), spot)
            q_row = spread_cols(core, total["q"][0], n_tensor)
            v_row = spread_cols(core, total["v"][0], n_tensor)
            up_row = spread_cols(core, total["up_bias"][0], n_tensor)
            rows = jnp.concatenate([full[:2], q_row[None], v_row[None], full[2:]], 0)
            rows = rows.reshape(8, n_tensor, n_dp, -1).transpose(2, 1, 0, 3).reshape(n_dp, n_tensor, -1)
            up_row = up_row.reshape(n_tensor, n_dp, -1).transpose(1, 0, 2)
            packed.append(jnp.concatenate([rows, up_row], -1))
        ours = jnp.where(is_first, packed[0], packed[1])
        other = swap(jnp.where(is_first, packed[1], packed[0]))
        little = (ours + other).astype(jnp.bfloat16)
        return little

    grads, got, moved, settled = [None] * number, [None] * number, [None] * number, [None] * number
    made = [0, 1, 3, 4, 5, 6]
    grad = cotangent
    last_down = weights_of(number - 1)
    params[1]["down"] = last_down
    last_bias = params[1]["small"][0][7:8]
    grads[0] = fill(first_grads)
    sums[1]["out"] = last_sum
    for r in range(1, 8):
        layer, stage = 1 - r // 4, r % 4
        one, total = params[layer], sums[layer]
        rows = one["small"][0]
        tied, slots = [], []
        for c in range(number):
            if r == made[c] + 1:
                got[c] = scatter_one(*grads[c][:2])
                slots.append((got, c, len(got[c])))
                tied += got[c]
            elif r == made[c] + 2:
                stay, come = scatter_two(*grads[c][2:], got[c])
                moved[c] = [*stay, *come]
                if r < 7:
                    slots.append((moved, c, len(moved[c])))
                    tied += moved[c]
            elif r == made[c] + 3:
                settled[c] = scatter_column(moved[c][:2], moved[c][2:])
                slots.append((settled, c, 0))
                tied.append(settled[c])
        new = None
        if stage == 0:
            total["out"], new = down_grad(grad, one["hidden"])
        if stage == 0 or r == 1:
            low, total["up_bias"] = down_backward(grad, one["slope"], one["down"])
            carry = [low]
        if stage == 1:
            part = contract_wide(low, one["up"])
            new = up_grad(one["n2"], low)
            carry = [part]
        if stage == 2:
            done = attention_backward(
                grad, part, swap(part), one["mid"], rows, one["saved"], one["qkvo"]
            )
            dmid, dz, dq, dk, dv, part, total["mid"], total["q"], total["v"] = done
            if layer == 0:
                new = attention_grad(one["n1"], dz, dq, dk, dv, one["saved"][4])
            carry = [part]
        if stage == 3:
            if layer == 1:
                new = attention_grad(one["n1"], dz, dq, dk, dv, one["saved"][4])
            grad, total["one"] = value_backward(dmid, part, swap(part), one["u"], rows, layer == 1)
            carry = [grad]
            if r == 7:
                one_scale = jnp.ones((), jnp.float32)
                no_bias = jnp.zeros((1, grad.shape[1]), jnp.float32)
                carry = [small_grads()]
                grad_blocks = shifts(image_rows(one_scale, [grad], no_bias))
        if new is not None:
            c = made.index(r)
            grads[c] = new
            fresh = [g for g in new if g is not None]
        else:
            fresh = []
        if r == 3:
            last_part = contract_wide(params[1]["hidden"], last_down)
            carry.append(last_part)
        elif r == 4:
            out_blocks = image_rows(
                live, [params[1]["mid"], last_part, swap(last_part)], last_bias
            )
        if 4 <= r < 4 + n_tensor - 1:
            out_blocks[r - 3] = shift(out_blocks[r - 3], r - 3)
            carry += out_blocks
        if r < 8:
            done = tie(carry + fresh + tied, [])
            if stage == 0:
                low = done[0]
            elif stage == 1:
                part = done[0]
            elif stage == 2:
                part = done[0]
            elif r < 7:
                grad = done[0]
            else:
                little = done[0]
            if r == 3:
                last_part = done[1]
            elif 4 <= r < 4 + n_tensor - 1:
                out_blocks = done[1 : 1 + n_tensor]
            done = done[len(carry) :]
            if fresh:
                grads[c] = fill(done[: len(fresh)])
                done = done[len(fresh) :]
            for store, at, count in slots:
                store[at] = done[:count] if count else done[0]
                done = done[max(count, 1) :]

    room = jnp.zeros((n_dp, n_tensor, extra * wide - small_size), little.dtype)
    little = jnp.concatenate([little, room], -1).reshape(n_dp, n_tensor, extra, wide)
    little = by_arrival(little.transpose(0, 2, 1, 3).reshape(n_dp, extra, -1), spot)
    if n_dp != 4:
        little = lax.psum_scatter(little, "dp", scatter_dimension=0, tiled=True)[0]
    else:
        over = lax.ppermute(little[3], "dp", [(i, i ^ 3) for i in range(n_dp)])
        little = add(little[0], swap_y(little[1])) + add(swap_x(little[2]), over)
        little = little.astype(jnp.bfloat16)

    last = number - 1
    settled[last - 1] = scatter_column(moved[last - 1][:2], moved[last - 1][2:])
    stay, come = scatter_two(*grads[last][2:], got[last])
    done = tie([*grad_blocks, *stay, *come], [])
    grad_blocks, done = done[:n_tensor], done[n_tensor:]
    grad_rows, out_rows = by_image(grad_blocks), by_image(out_blocks)
    stay, come = done[:2], done[2:]
    if come:
        stay = [add(s, c).astype(jnp.bfloat16) for s, c in zip(stay, come)]
    settled[last] = scatter_column([*stay, little], [])
    little = settled[last][depth:].reshape(-1).astype(jnp.float32)
    settled[last] = settled[last][:depth]
    grad_vectors = little[:n_vec].reshape(vectors.shape)
    grad_bias = little[n_vec:small_size].reshape(fc1_bias.shape)

    own = jnp.where(is_first, grad_rows, out_rows)
    other = swap(jnp.where(is_first, out_rows, grad_rows))
    ends = [jnp.where(is_first, own, other), jnp.where(is_first, other, own)]
    boundary_out = jnp.concatenate(ends, 1)[:, :tokens].astype(jnp.float32)[None]
    lows, highs = [], []
    for kind in range(3):
        first, second = settled[last - kind], settled[last - kind - 3]
        kept = jnp.where(is_first, first, second)
        received = swap(jnp.where(is_first, second, first))
        lows.append(jnp.where(is_first, kept, received).astype(jnp.float32))
        highs.append(jnp.where(is_first, received, kept).astype(jnp.float32))
    low, high = [part[0].reshape(depth, 4, -1) for part in (lows, highs)]
    grad_qkv = jnp.concatenate([low[:, :3], high[:, :3]], 2)[None]
    grad_proj = jnp.concatenate([low[:, 3].T, high[:, 3].T], 0)[None]
    grad_up = jnp.concatenate([lows[1], highs[1]], 1)[None]
    grad_down = jnp.concatenate([lows[2].T, highs[2].T], 0)[None]
    return (boundary_out, grad_qkv, grad_proj, grad_up, grad_down, grad_vectors, grad_bias)


def solution(mesh):
    in_specs = (
        P("section", "dp", None, "tensor"),
        P("dp", None),
        P("section", "dp", None, "tensor"),
        P("section", "tensor", "dp"),
        P("section", "dp", "tensor"),
        P("section", "tensor", "dp"),
        P("section", None, "tensor", "dp"),
        P("section", "tensor", "dp"),
    )
    out_specs = (
        P("section", "dp", None, "tensor"),
        P("section", "dp", None, "tensor"),
        P("section", "tensor", "dp"),
        P("section", "dp", "tensor"),
        P("section", "tensor", "dp"),
        P("section", None, "tensor", "dp"),
        P("section", "tensor", "dp"),
    )
    return jax.shard_map(body, mesh=mesh, in_specs=in_specs, out_specs=out_specs, check_vma=False)
```

```python
import jax
import jax.numpy as jnp
from jax import lax
from jax.experimental import pallas as pl
from jax.experimental.pallas import tpu as pltpu
from jax.sharding import PartitionSpec as P

HD = 64
EPS = 1e-06


def swap(value):
    return lax.ppermute(value, "section", [(0, 1), (1, 0)])


def pair_sum(partial):
    low = partial.astype(jnp.bfloat16)
    return low.astype(jnp.float32) + swap(low).astype(jnp.float32)


def swap_x(value):
    n = lax.axis_size("dp")
    return lax.ppermute(value, "dp", [(i, i ^ 1) for i in range(n)])


def swap_y(value):
    n = lax.axis_size("dp")
    return lax.ppermute(value, "dp", [(i, i ^ 2) for i in range(n)])


def tie(values, others):
    count = len(values)

    def kernel(*refs):
        pass

    anywhere = pl.BlockSpec(memory_space=pl.ANY)
    done = pl.pallas_call(
        kernel,
        out_shape=[jax.ShapeDtypeStruct(v.shape, v.dtype) for v in values],
        in_specs=[anywhere] * (count + len(others)),
        out_specs=[anywhere] * count,
        input_output_aliases={i: i for i in range(count)},
    )(*values, *others)
    return list(done)


def gather_column(shard):
    return lax.all_gather(shard, "tensor", axis=1, tiled=True)


def exchange_one(first, second):
    if lax.axis_size("dp") != 4:
        return [lax.all_gather(v, "dp", axis=0, tiled=True) for v in (first, second)]
    return [swap_y(first), swap_x(second)]


def exchange_two(first, second, near_first, near_second):
    if lax.axis_size("dp") != 4:
        return []
    return [swap_x(first), swap_x(near_first), swap_y(second), swap_y(near_second)]


def arrived(first, second, near, far):
    if lax.axis_size("dp") != 4:
        return ([near[0]], [near[1]])
    return ([first, near[0], far[0], far[1]], [second, near[1], far[2], far[3]])


def row_cuts(depth):
    half = depth // 2
    if lax.axis_size("dp") != 4:
        return [(0, half), (half, depth), None, None]
    part = half // 2
    return [(part, half), (half + part, depth), (0, part), (half, half + part)]


def add(left, right):
    return left.astype(jnp.float32) + right.astype(jnp.float32)


def scatter_one(send_first, send_second):
    if lax.axis_size("dp") != 4:
        return [
            lax.psum_scatter(v, "dp", scatter_dimension=0, tiled=True)
            for v in (send_first, send_second)
        ]
    return [swap_x(send_first), swap_y(send_second)]


def scatter_two(keep_first, keep_second, got):
    if lax.axis_size("dp") != 4:
        return (got, [])
    stay, send = [], []
    for keep, new in zip((keep_first, keep_second), got):
        half = keep.shape[0] // 2
        send.append(add(keep[half:], new[half:]).astype(jnp.bfloat16))
        stay.append(add(keep[:half], new[:half]).astype(jnp.bfloat16))
    return (stay, [swap_y(send[0]), swap_x(send[1])])


def scatter_column(stay, come):
    if come:
        stay = [add(s, c).astype(jnp.bfloat16) for s, c in zip(stay, come)]
    return lax.psum_scatter(
        jnp.concatenate(stay, 0), "tensor", scatter_dimension=1, tiled=True
    )


def flip_axis(value, axis, bit):
    return jnp.where(bit == 1, jnp.flip(value, axis), value)


def relative(value, spot):
    n_dp = lax.axis_size("dp")
    lead = value.shape[:-1]
    k = len(lead)
    if n_dp != 4:
        cut = value.reshape(lead + (n_dp, 2, -1))
        return jnp.swapaxes(cut, k, k + 1).reshape(value.shape)
    cut = value.reshape(lead + (2, 2, 2, -1))
    cut = flip_axis(flip_axis(cut, k, spot // 2), k + 1, spot % 2)
    first = jnp.swapaxes(cut[..., 0, :], k, k + 1)
    second = cut[..., 1, :]
    return jnp.concatenate([first.reshape(lead + (-1,)), second.reshape(lead + (-1,))], -1)


def absolute(value, spot):
    n_dp = lax.axis_size("dp")
    lead = value.shape[:-1]
    k = len(lead)
    if n_dp != 4:
        cut = value.reshape(lead + (2, n_dp, -1))
        return jnp.swapaxes(cut, k, k + 1).reshape(value.shape)
    cut = value.reshape(lead + (2, 2, 2, -1))
    first = jnp.swapaxes(cut[..., 0, :, :, :], k, k + 1)
    second = cut[..., 1, :, :, :]
    cut = jnp.stack([first, second], k + 2)
    cut = flip_axis(flip_axis(cut, k, spot // 2), k + 1, spot % 2)
    return cut.reshape(value.shape)


def by_chip(blocks, spot):
    n_dp = lax.axis_size("dp")
    if n_dp != 4:
        return blocks
    cut = blocks.reshape((2, 2) + blocks.shape[1:])
    cut = jnp.swapaxes(cut, 0, 1)
    cut = flip_axis(flip_axis(cut, 0, spot // 2), 1, spot % 2)
    return cut.reshape(blocks.shape)


def by_arrival(blocks, spot):
    n_dp = lax.axis_size("dp")
    if n_dp != 4:
        return blocks
    cut = blocks.reshape((2, 2) + blocks.shape[1:])
    cut = flip_axis(flip_axis(cut, 0, spot // 2), 1, spot % 2)
    return jnp.swapaxes(cut, 0, 1).reshape(blocks.shape)


VMEM_BYTES = 50 * 2**20
BF = jnp.bfloat16
F32 = jnp.float32


def shape(dims, kind=jnp.bfloat16):
    return jax.ShapeDtypeStruct(dims, kind)


def run(kernel, outs, ins):
    block = pl.BlockSpec(memory_space=pltpu.VMEM)
    done = pl.pallas_call(
        kernel,
        out_shape=list(outs),
        in_specs=[block] * len(ins),
        out_specs=[block] * len(outs),
        cost_estimate=pl.CostEstimate(flops=1, bytes_accessed=1, transcendentals=0),
        compiler_params=pltpu.CompilerParams(vmem_limit_bytes=VMEM_BYTES),
    )(*ins)
    return list(done)


def nn(left, right):
    return lax.dot_general(left, right, (((1,), (0,)), ((), ())), preferred_element_type=F32)


def nt(left, right):
    return lax.dot_general(left, right, (((1,), (1,)), ((), ())), preferred_element_type=F32)


def tn(left, right):
    return lax.dot_general(left, right, (((0,), (0,)), ((), ())), preferred_element_type=F32)


def stack_rows(pieces, counts, cols):
    return jnp.concatenate([p[:n, cols] for p, n in zip(pieces, counts)], 0)


def center_scale(value):
    center = jnp.mean(value, -1, keepdims=True)
    spread = jnp.mean(value * value, -1, keepdims=True) - center * center
    factor = lax.rsqrt(spread + EPS)
    return ((value - center) * factor, factor)


def norm_backward(grad_normed, centred, factor, gain):
    scaled = grad_normed * gain
    return factor * (
        scaled
        - jnp.mean(scaled, -1, keepdims=True)
        - centred * jnp.mean(scaled * centred, -1, keepdims=True)
    )


def column_sum(value):
    return jnp.sum(value, 0, keepdims=True)


def attention_forward(tokens, terms, bias_row, low, weights, rows, q_bias, v_bias):
    pieces, counts = weights
    size, depth = terms[0].shape
    wide = pieces[0].shape[1]
    groups = wide // 512
    half = groups * 128
    n_terms, n_pieces = len(terms), len(pieces)

    def kernel(*refs):
        term_refs, refs = refs[:n_terms], refs[n_terms:]
        bias_ref, rows_ref, qb_ref, vb_ref = refs[:4]
        piece_refs, refs = refs[4 : 4 + n_pieces], refs[4 + n_pieces :]
        u_ref, n_ref, q_ref, k_ref, v_ref, p_ref, o_ref, part_ref = refs
        value = term_refs[0][...].astype(F32)
        for ref in term_refs[1:]:
            value = value + ref[...].astype(F32)
        if n_terms > 1:
            value = value + bias_ref[...]
        if low:
            value = value.astype(BF).astype(F32)
        u_ref[...] = value
        centred, factor = center_scale(value)
        n_ref[...] = (centred * rows_ref[0:1] + rows_ref[1:2]).astype(BF)
        lane = lax.broadcasted_iota(jnp.int32, (size, 128), 1)
        key_lane = lax.broadcasted_iota(jnp.int32, (size, size), 1)
        normed = n_ref[...]
        for g in range(groups):
            at = slice(g * 128, (g + 1) * 128)
            matrix = stack_rows(piece_refs, counts, slice(g * 512, g * 512 + 384))
            projected = nn(normed, matrix)
            q = (projected[:, :128] + qb_ref[:, at]).astype(BF)
            k = projected[:, 128:256].astype(BF)
            v = (projected[:, 256:384] + vb_ref[:, at]).astype(BF)
            q_ref[:, at] = q
            k_ref[:, at] = k
            v_ref[:, at] = v
            mixed = None
            for h in range(2):
                mine = (lane // HD) == h
                scores = nt(jnp.where(mine, q, jnp.zeros_like(q)), k) * HD ** (-0.5)
                scores = jnp.where(key_lane < tokens, scores, -1e30)
                highest = jnp.max(scores, -1, keepdims=True)
                exponent = jnp.exp(scores - highest)
                inverse = 1.0 / jnp.sum(exponent, -1, keepdims=True)
                soft = (exponent * inverse).astype(BF)
                p_ref[2 * g + h] = soft
                out = nn(soft, v)
                mixed = out if h == 0 else jnp.where(mine, out, mixed)
            o_ref[:, at] = mixed.astype(BF)
        matrix = jnp.concatenate(
            [stack_rows(piece_refs, counts, slice(g * 512 + 384, g * 512 + 512)) for g in range(groups)], 1
        )
        part_ref[...] = nt(o_ref[...], matrix).astype(BF)

    outs = [shape((size, depth), F32), shape((size, depth))] + [shape((size, half))] * 3
    outs += [shape((2 * groups, size, size)), shape((size, half)), shape((size, depth))]
    return run(kernel, outs, [*terms, bias_row, rows, q_bias, v_bias, *pieces])


def up_forward(terms, weights, rows, up_bias):
    pieces, counts = weights
    size, depth = terms[0].shape
    wide = pieces[0].shape[1]

    def kernel(*refs):
        u_ref, own_ref, far_ref, rows_ref, bias_ref = refs[:5]
        piece_refs = refs[5 : 5 + len(pieces)]
        mid_ref, n_ref, slope_ref, hidden_ref = refs[5 + len(pieces) :]
        value = u_ref[...] + own_ref[...].astype(F32) + far_ref[...].astype(F32) + rows_ref[4:5]
        mid_ref[...] = value
        centred, factor = center_scale(value)
        n_ref[...] = (centred * rows_ref[5:6] + rows_ref[6:7]).astype(BF)
        step = 512
        for at in range(0, wide, step):
            cols = slice(at, at + step)
            before = nn(n_ref[...], stack_rows(piece_refs, counts, cols)) + bias_ref[:, cols]
            cdf = 0.5 * (1.0 + lax.erf(before * 0.7071067811865476))
            density = jnp.exp(-0.5 * before * before) * 0.3989422804014327
            hidden_ref[:, cols] = (before * cdf).astype(BF)
            slope_ref[:, cols] = (cdf + before * density).astype(BF)

    outs = [shape((size, depth), F32), shape((size, depth)), shape((size, wide)), shape((size, wide))]
    return run(kernel, outs, [*terms, rows, up_bias, *pieces])


def contract_wide(left, weights):
    pieces, counts = weights
    size, wide = left.shape
    depth = sum(counts)

    def kernel(*refs):
        left_ref, piece_refs, out_ref = refs[0], refs[1:-1], refs[-1]
        matrix = stack_rows(piece_refs, counts, slice(0, wide))
        out_ref[...] = nt(left_ref[...], matrix).astype(BF)

    return run(kernel, [shape((size, depth))], [left, *pieces])[0]


def weight_outs(depth, wide):
    cuts = [c for c in row_cuts(depth) if c is not None]
    return cuts, [shape((c[1] - c[0], wide)) for c in cuts]


def fill(grads):
    return (list(grads) + [None, None])[:4]


def down_grad(grad_out, hidden):
    size, depth = grad_out.shape
    cuts, outs = weight_outs(depth, hidden.shape[1])

    def kernel(g_ref, hidden_ref, sum_ref, *refs):
        sum_ref[...] = column_sum(g_ref[...])
        branch = g_ref[...].astype(BF)
        for cut, ref in zip(cuts, refs):
            ref[...] = tn(branch[:, cut[0] : cut[1]], hidden_ref[...]).astype(BF)

    done = run(kernel, [shape((1, depth), F32)] + outs, [grad_out, hidden])
    return done[0], fill(done[1:])


def down_backward(grad_out, slope, weights):
    pieces, counts = weights
    size, depth = grad_out.shape
    wide = slope.shape[1]

    def kernel(*refs):
        g_ref, slope_ref, piece_refs = refs[0], refs[1], refs[2:-2]
        low_ref, bias_ref = refs[-2:]
        branch = g_ref[...].astype(BF)
        step = 512
        for at in range(0, wide, step):
            cols = slice(at, at + step)
            back = nn(branch, stack_rows(piece_refs, counts, cols)) * slope_ref[:, cols].astype(F32)
            bias_ref[:, cols] = column_sum(back)
            low_ref[:, cols] = back.astype(BF)

    outs = [shape((size, wide)), shape((1, wide), F32)]
    return run(kernel, outs, [grad_out, slope, *pieces])


def up_grad(normed, low):
    size, depth = normed.shape
    wide = low.shape[1]
    cuts, outs = weight_outs(depth, wide)

    def kernel(n_ref, low_ref, *refs):
        for cut, ref in zip(cuts, refs):
            ref[...] = tn(n_ref[:, cut[0] : cut[1]], low_ref[...]).astype(BF)

    return fill(run(kernel, outs, [normed, low]))


def attention_backward(grad_out, own, far, middle, rows, saved, weights):
    pieces, counts = weights
    size, depth = grad_out.shape
    wide = pieces[0].shape[1]
    groups = wide // 512
    half = groups * 128
    scale = HD ** (-0.5)

    def kernel(*refs):
        g_ref, own_ref, far_ref, mid_ref, rows_ref, q_ref, k_ref, v_ref, p_ref, o_ref = refs[:10]
        piece_refs, refs = refs[10 : 10 + len(pieces)], refs[10 + len(pieces) :]
        dmid_ref, dz_ref, dq_ref, dk_ref, dv_ref, part_ref, sum_ref, qs_ref, vs_ref = refs
        grad_normed = own_ref[...].astype(F32) + far_ref[...].astype(F32)
        centred, factor = center_scale(mid_ref[...])
        sum_ref[1:2] = column_sum(grad_normed * centred)
        sum_ref[2:3] = column_sum(grad_normed)
        dmid = g_ref[...] + norm_backward(grad_normed, centred, factor, rows_ref[5:6])
        dmid_ref[...] = dmid
        sum_ref[0:1] = column_sum(dmid)
        dz_ref[...] = dmid.astype(BF)
        lane = lax.broadcasted_iota(jnp.int32, (size, 128), 1)
        for g in range(groups):
            at = slice(g * 128, (g + 1) * 128)
            matrix = stack_rows(piece_refs, counts, slice(g * 512 + 384, g * 512 + 512))
            grad_mixed = nn(dz_ref[...], matrix).astype(BF)
            q, k, v = q_ref[:, at], k_ref[:, at], v_ref[:, at]
            inner = grad_mixed.astype(F32) * o_ref[:, at].astype(F32)
            dq, dk, dv = None, None, None
            for h in range(2):
                mine = (lane // HD) == h
                soft = p_ref[2 * g + h]
                none = jnp.zeros_like(q)
                do = jnp.where(mine, grad_mixed, none)
                total = jnp.sum(jnp.where(mine, inner, 0.0), -1, keepdims=True)
                grad_soft = nt(do, v)
                grad_scores = (soft.astype(F32) * (grad_soft - total)).astype(BF)
                new_q = nn(grad_scores, k)
                new_k = tn(jnp.where(mine, q, none), grad_scores)
                new_v = tn(do, soft)
                dq = new_q if h == 0 else jnp.where(mine, new_q, dq)
                dk = new_k if h == 0 else dk + new_k
                dv = new_v if h == 0 else dv + new_v
            dq, dk, dv = dq * scale, dk.T * scale, dv.T
            qs_ref[:, at] = column_sum(dq)
            vs_ref[:, at] = column_sum(dv)
            dq_ref[:, at] = dq.astype(BF)
            dk_ref[:, at] = dk.astype(BF)
            dv_ref[:, at] = dv.astype(BF)
        total = None
        for g in range(groups):
            at = slice(g * 128, (g + 1) * 128)
            left = jnp.concatenate([dq_ref[:, at], dk_ref[:, at], dv_ref[:, at]], 1)
            new = nt(left, stack_rows(piece_refs, counts, slice(g * 512, g * 512 + 384)))
            total = new if g == 0 else total + new
        part_ref[...] = total.astype(BF)

    outs = [shape((size, depth), F32), shape((size, depth))] + [shape((size, half))] * 3
    outs += [shape((size, depth)), shape((3, depth), F32)] + [shape((1, half), F32)] * 2
    return run(kernel, outs, [grad_out, own, far, middle, rows, *saved, *pieces])


def attention_grad(normed, dz, dq, dk, dv, mixed):
    size, depth = normed.shape
    groups = dq.shape[1] // 128
    cuts, outs = weight_outs(depth, groups * 512)

    def kernel(n_ref, dz_ref, dq_ref, dk_ref, dv_ref, o_ref, *refs):
        for cut, ref in zip(cuts, refs):
            rows = slice(cut[0], cut[1])
            for g in range(groups):
                at = slice(g * 128, (g + 1) * 128)
                right = jnp.concatenate([dq_ref[:, at], dk_ref[:, at], dv_ref[:, at]], 1)
                ref[:, g * 512 : g * 512 + 384] = tn(n_ref[:, rows], right).astype(BF)
                ref[:, g * 512 + 384 : g * 512 + 512] = tn(dz_ref[:, rows], o_ref[:, at]).astype(BF)

    return fill(run(kernel, outs, [normed, dz, dq, dk, dv, mixed]))


def value_backward(dmid, own, far, value, rows, low):
    size, depth = dmid.shape

    def kernel(dmid_ref, own_ref, far_ref, u_ref, rows_ref, out_ref, sum_ref):
        grad_normed = own_ref[...].astype(F32) + far_ref[...].astype(F32)
        centred, factor = center_scale(u_ref[...])
        sum_ref[0:1] = column_sum(grad_normed * centred)
        sum_ref[1:2] = column_sum(grad_normed)
        out = dmid_ref[...] + norm_backward(grad_normed, centred, factor, rows_ref[0:1])
        if low:
            out = out.astype(BF).astype(F32)
        out_ref[...] = out

    outs = [shape((size, depth), F32), shape((2, depth), F32)]
    return run(kernel, outs, [dmid, own, far, value, rows])


def block_lanes(spot, chunk):
    ry, rx = chunk // 2 ^ spot // 2, chunk % 2 ^ spot % 2
    return [(rx * 2 + ry) * 128, 512 + (ry * 2 + rx) * 128]


def place_in(lanes, blocks):
    size, width = blocks[0].shape
    half = width // 2

    def kernel(lanes_ref, *refs):
        out_ref = refs[-1]
        for d, ref in enumerate(refs[:-1]):
            for h in range(2):
                at = pl.multiple_of(lanes_ref[2 * d + h], 128)
                out_ref[:, pl.ds(at, half)] = ref[:, h * half : (h + 1) * half]

    block = pl.BlockSpec(memory_space=pltpu.VMEM)
    return pl.pallas_call(
        kernel,
        out_shape=shape((size, width * len(blocks))),
        in_specs=[pl.BlockSpec(memory_space=pltpu.SMEM)] + [block] * len(blocks),
        out_specs=block,
        compiler_params=pltpu.CompilerParams(vmem_limit_bytes=VMEM_BYTES),
    )(lanes, *blocks)


def place_out(numbers, scale, terms, bias_row, count):
    size, depth = terms[0].shape
    width = depth // count
    half = width // 2

    def kernel(numbers_ref, scale_ref, *refs):
        term_refs, bias_ref, out_ref = refs[: len(terms)], refs[-2], refs[-1]
        start = pl.multiple_of(numbers_ref[2 * count], 8)
        rows = pl.ds(start, size // 2)
        for d in range(count):
            for h in range(2):
                lanes = pl.ds(pl.multiple_of(numbers_ref[2 * d + h], 128), half)
                value = term_refs[0][rows, lanes]
                for ref in term_refs[1:]:
                    value = value + ref[rows, lanes]
                value = (value + bias_ref[:, lanes]) * scale_ref[0]
                out_ref[d, :, h * half : (h + 1) * half] = value.astype(BF)

    block = pl.BlockSpec(memory_space=pltpu.VMEM)
    scalar = pl.BlockSpec(memory_space=pltpu.SMEM)
    return pl.pallas_call(
        kernel,
        out_shape=shape((count, size // 2, width)),
        in_specs=[scalar, scalar] + [block] * (len(terms) + 1),
        out_specs=block,
        compiler_params=pltpu.CompilerParams(vmem_limit_bytes=VMEM_BYTES),
    )(numbers, scale, *terms, bias_row)


def shift(block, d):
    n = lax.axis_size("tensor")
    return lax.ppermute(block, "tensor", [(i, (i + d) % n) for i in range(n)])


def shifts(blocks):
    return [blocks[0]] + [shift(block, d) for d, block in enumerate(blocks) if d > 0]


def half_cols(core, whole, n_tensor):
    cut = whole.reshape(whole.shape[:-1] + (n_tensor, 2, -1))
    cut = jnp.where(core == 0, cut[..., 0, :], cut[..., 1, :])
    return cut.reshape(whole.shape[:-1] + (-1,))


def spread_cols(core, half, n_tensor):
    cut = half.reshape(half.shape[:-1] + (n_tensor, 1, -1))
    none = jnp.zeros_like(cut)
    both = jnp.concatenate(
        [jnp.where(core == 0, cut, none), jnp.where(core == 0, none, cut)], -2
    )
    return both.reshape(half.shape[:-1] + (-1,))


def body(boundary_in, counts, qkv_weight, proj_weight, fc1_weight, fc2_weight, vectors, fc1_bias):
    core = lax.axis_index("section")
    is_first = core == 0
    place = lax.axis_index("tensor")
    spot = lax.axis_index("dp")
    n_dp, n_tensor = lax.axis_size("dp"), lax.axis_size("tensor")
    slots_per_batch = boundary_in.shape[1] // counts.shape[1]
    live = (place % slots_per_batch < counts[0, place // slots_per_batch]).astype(jnp.float32)
    depth = qkv_weight.shape[1]
    mid = depth // 2
    n_vec = vectors.size

    small_size = n_vec + fc1_bias.size
    packs = []
    for part in range(2):
        cuts = [
            jnp.split(qkv_weight[0], 2, 2)[part].reshape(depth, -1),
            jnp.split(proj_weight[0], 2, 0)[part].T,
            jnp.split(fc1_weight[0], 2, 1)[part],
            jnp.split(fc2_weight[0], 2, 0)[part].T,
        ]
        packs.append(jnp.concatenate(cuts, 1))
    wide = packs[0].shape[1] // 3
    extra = 16
    small = jnp.concatenate([vectors.reshape(-1), fc1_bias.reshape(-1)])
    small = jnp.pad(small, (0, extra * wide - small_size)).reshape(extra, wide)
    small = jnp.pad(small, ((0, 0), (0, 2 * wide)))
    kept = jnp.concatenate([jnp.where(is_first, packs[0], packs[1]), small], 0)
    received = swap(
        jnp.concatenate([jnp.where(is_first, packs[1], packs[0]), small], 0)
    )
    shards = (jnp.where(is_first, kept, received), jnp.where(is_first, received, kept))
    columns = []
    for layer in range(2):
        for number in range(3):
            cols = shards[layer][:, number * wide : (number + 1) * wide]
            if layer == 0 and number == 0:
                room = extra // 2
                both = [shard[depth : depth + room, :wide] for shard in shards]
                cols = jnp.concatenate([cols[:depth], *both], 0)
            else:
                cols = cols[:depth]
            columns.append(cols)

    tokens = boundary_in.shape[2]
    pad = -tokens % 16
    reach = (tokens + pad) // 2
    ends_in = jnp.pad(boundary_in[0].astype(jnp.bfloat16), ((0, 0), (0, pad), (0, 0)))
    ends_low, ends_high = ends_in[:, :reach], ends_in[:, reach:]
    ends_got = swap(jnp.where(is_first, ends_high, ends_low))
    half_in = jnp.where(is_first, ends_low, ends_got)
    half_cot = jnp.where(is_first, ends_got, ends_high)

    below = [(place - d) % n_tensor for d in range(n_tensor)]
    above = [(place + d) % n_tensor for d in range(n_tensor)]

    def to_send(half):
        return [lax.dynamic_index_in_dim(half, j, 0, False) for j in above]

    def image_half(blocks):
        if n_dp == 4:
            lanes = [lane for t in below for lane in block_lanes(spot, t)]
            return place_in(jnp.stack(lanes).astype(jnp.int32), blocks)
        blocks = jnp.stack(blocks)
        blocks = [lax.dynamic_index_in_dim(blocks, (place - i) % n_tensor, 0, False) for i in range(n_tensor)]
        return relative(jnp.concatenate(blocks, 1), spot)

    def whole_image(half):
        other = swap(half)
        both = [jnp.where(is_first, half, other), jnp.where(is_first, other, half)]
        return jnp.concatenate(both, 0)

    def image_rows(scale, terms, bias_row):
        if n_dp == 4:
            numbers = [lane for t in above for lane in block_lanes(spot, t)]
            numbers.append(jnp.where(is_first, 0, reach))
            numbers = jnp.stack(numbers).astype(jnp.int32)
            blocks = place_out(numbers, scale.reshape(1), terms, bias_row, n_tensor)
            return [blocks[d] for d in range(n_tensor)]
        image = absolute((sum(terms[1:], terms[0]) + bias_row) * scale, spot).astype(jnp.bfloat16)
        half = jnp.where(is_first, image[:reach], image[reach:])
        half = half.reshape(reach, n_tensor, -1).transpose(1, 0, 2)
        return to_send(half)

    def by_image(blocks):
        blocks = jnp.stack(blocks)
        blocks = [lax.dynamic_index_in_dim(blocks, (place - i) % n_tensor, 0, False) for i in range(n_tensor)]
        return jnp.stack(blocks)

    def small_of(extras):
        if n_dp != 4:
            extras = lax.all_gather(extras, "dp", axis=0, tiled=True)
        else:
            over = lax.ppermute(extras, "dp", [(i, i ^ 3) for i in range(n_dp)])
            extras = jnp.concatenate([extras, swap_y(extras), swap_x(extras), over], 0)
        both = by_chip(extras.reshape(n_dp, extra, -1), spot).astype(jnp.float32)
        both = both.reshape(n_dp, 2, extra // 2, n_tensor, wide).transpose(1, 0, 3, 2, 4)
        both = both.reshape(2, n_dp, n_tensor, -1)
        rows = both[..., :n_vec].reshape(2, n_dp, n_tensor, 8, -1)
        rows = relative(rows.transpose(0, 3, 2, 1, 4).reshape(2, 8, -1), spot)
        bias = both[..., n_vec:small_size].transpose(0, 2, 1, 3).reshape(2, -1)
        plain = both[..., :n_vec].reshape(2, n_dp, n_tensor, 8, -1)[..., 2:4, :]
        plain = plain.transpose(0, 3, 2, 1, 4).reshape(2, 2, -1)
        parts = [half_cols(core, plain[:, 0], n_tensor), half_cols(core, plain[:, 1], n_tensor)]
        parts.append(half_cols(core, bias, n_tensor))
        return [(rows[i], parts[0][i : i + 1], parts[1][i : i + 1], parts[2][i : i + 1]) for i in range(2)]

    number = len(columns)
    halves, near, far = [None] * number, [None] * number, [None] * number
    params = [dict(), dict()]
    blocks_in, blocks_cot = to_send(half_in), to_send(half_cot)
    pair, state = None, None

    def weights_of(k):
        first, second = arrived(*halves[k], near[k], far[k])
        return (first + second, [p.shape[0] for p in first + second])

    for r in range(number + 1):
        tied = []
        if r < number:
            tied.append(gather_column(columns[r]))
        if 0 <= r - 1 < number:
            near[r - 1] = exchange_one(*halves[r - 1])
        if r == 1:
            smalls = small_of(extra_rows)
            blocks_in = shifts(blocks_in)
        if 2 <= r <= 1 + n_tensor - 1:
            blocks_cot[r - 1] = shift(blocks_cot[r - 1], r - 1)
        if r == number - 1:
            cot_half = image_half(blocks_cot)
        if r == number:
            cotangent = whole_image(cot_half).astype(jnp.float32) * live
        ready = []
        k = r - 2
        if k >= 0:
            layer, kind = k // 3, k % 3
            one = params[layer]
            weights = weights_of(k)
            rows, q_bias, v_bias, up_bias = one["small"]
            if pair is not None:
                pair = [pair[0], swap(pair[0])]
            if kind == 0:
                one["qkvo"] = weights
                if layer == 0:
                    terms = [whole_image(image_half(blocks_in)).astype(jnp.float32)]
                else:
                    terms = [state, *pair]
                bias_row = params[0]["small"][0][7:8]
                done = attention_forward(
                    tokens, terms, bias_row, layer == 1, weights, rows, q_bias, v_bias
                )
                one["u"], one["n1"], one["saved"], part = done[0], done[1], done[2:7], done[7]
                pair, ready = [part], [part]
            elif kind == 1:
                one["up"] = weights
                one["mid"], one["n2"], one["slope"], one["hidden"] = up_forward(
                    [one["u"], *pair], weights, rows, up_bias
                )
                pair, ready = None, [one["hidden"]]
            else:
                one["down"] = weights
                state = one["mid"]
                part = contract_wide(one["hidden"], weights)
                pair, ready = [part], [part]
        if r <= number:
            count = len(ready)
            extras = list(ready)
            if 0 <= r - 1 < number:
                if ready:
                    done = tie(near[r - 1] + extras, [])
                    near[r - 1], extras = done[: len(near[r - 1])], done[len(near[r - 1]) :]
                far[r - 1] = exchange_two(*halves[r - 1], *near[r - 1])
                tied += near[r - 1] + far[r - 1]
            if r == number:
                last_sum, first_grads = down_grad(cotangent, extras[0])
                first_grads = [g for g in first_grads if g is not None]
                extras += first_grads
            if r <= 1:
                extras += blocks_in
            if r == 1:
                extras += [v for layer in range(2) for v in smalls[layer]]
            if 1 <= r <= number - 2:
                extras += blocks_cot
            elif r == number - 1:
                extras.append(cot_half)
            elif r == number:
                extras.append(cotangent)
            if r + 1 < number:
                extras.append(columns[r + 1])
            done = tie(tied + extras, [])
            if r + 1 < number:
                columns[r + 1] = done.pop()
            if 1 <= r <= number - 2:
                done, blocks_cot = done[:-n_tensor], done[-n_tensor:]
            elif r == number - 1:
                cot_half = done.pop()
            elif r == number:
                cotangent = done.pop()
                done, first_grads = done[: -len(first_grads)], done[-len(first_grads) :]
            if r == 1:
                done, smalls = done[:-8], done[-8:]
                params[0]["small"], params[1]["small"] = smalls[:4], smalls[4:]
            if r <= 1:
                done, blocks_in = done[:-n_tensor], done[-n_tensor:]
            if count and kind == 1:
                one["hidden"] = done[-1]
            elif count:
                pair = [done[-1]]
            at = 0
            if r < number:
                halves[r] = (done[0][:mid], done[0][mid:depth])
                if r == 0:
                    extra_rows = done[0][depth:]
                at = 1
            if 0 <= r - 1 < number:
                near[r - 1] = done[at : at + 2]
                far[r - 1] = done[at + 2 : at + 2 + len(far[r - 1])]

    sums = [dict(), dict()]

    def small_grads():
        packed = []
        for layer in range(2):
            total = sums[layer]
            full = jnp.concatenate([total["one"], total["mid"], total["out"]], 0)
            full = absolute(jnp.where(core == layer, full, 0.0), spot)
            q_row = spread_cols(core, total["q"][0], n_tensor)
            v_row = spread_cols(core, total["v"][0], n_tensor)
            up_row = spread_cols(core, total["up_bias"][0], n_tensor)
            rows = jnp.concatenate([full[:2], q_row[None], v_row[None], full[2:]], 0)
            rows = rows.reshape(8, n_tensor, n_dp, -1).transpose(2, 1, 0, 3).reshape(n_dp, n_tensor, -1)
            up_row = up_row.reshape(n_tensor, n_dp, -1).transpose(1, 0, 2)
            packed.append(jnp.concatenate([rows, up_row], -1))
        ours = jnp.where(is_first, packed[0], packed[1])
        other = swap(jnp.where(is_first, packed[1], packed[0]))
        little = (ours + other).astype(jnp.bfloat16)
        return little

    grads, got, moved, settled = [None] * number, [None] * number, [None] * number, [None] * number
    made = [0, 1, 3, 4, 5, 6]
    grad = cotangent
    last_down = weights_of(number - 1)
    params[1]["down"] = last_down
    last_bias = params[1]["small"][0][7:8]
    grads[0] = fill(first_grads)
    sums[1]["out"] = last_sum
    for r in range(1, 8):
        layer, stage = 1 - r // 4, r % 4
        one, total = params[layer], sums[layer]
        rows = one["small"][0]
        tied, slots = [], []
        for c in range(number):
            if r == made[c] + 1:
                got[c] = scatter_one(*grads[c][:2])
                slots.append((got, c, len(got[c])))
                tied += got[c]
            elif r == made[c] + 2:
                stay, come = scatter_two(*grads[c][2:], got[c])
                moved[c] = [*stay, *come]
                slots.append((moved, c, len(moved[c])))
                tied += moved[c]
            elif r == made[c] + 3:
                settled[c] = scatter_column(moved[c][:2], moved[c][2:])
                slots.append((settled, c, 0))
                tied.append(settled[c])
        new = None
        if stage == 0:
            total["out"], new = down_grad(grad, one["hidden"])
        if stage == 0 or r == 1:
            low, total["up_bias"] = down_backward(grad, one["slope"], one["down"])
            carry = [low]
        if stage == 1:
            part = contract_wide(low, one["up"])
            new = up_grad(one["n2"], low)
            carry = [part]
        if stage == 2:
            done = attention_backward(
                grad, part, swap(part), one["mid"], rows, one["saved"], one["qkvo"]
            )
            dmid, dz, dq, dk, dv, part, total["mid"], total["q"], total["v"] = done
            if layer == 0:
                new = attention_grad(one["n1"], dz, dq, dk, dv, one["saved"][4])
            carry = [part]
        if stage == 3:
            if layer == 1:
                new = attention_grad(one["n1"], dz, dq, dk, dv, one["saved"][4])
            grad, total["one"] = value_backward(dmid, part, swap(part), one["u"], rows, layer == 1)
            carry = [grad]
            if r == 7:
                one_scale = jnp.ones((), jnp.float32)
                no_bias = jnp.zeros((1, grad.shape[1]), jnp.float32)
                carry = [small_grads(), *shifts(image_rows(one_scale, [grad], no_bias))]
        if new is not None:
            c = made.index(r)
            grads[c] = new
            fresh = [g for g in new if g is not None]
        else:
            fresh = []
        if r == 3:
            last_part = contract_wide(params[1]["hidden"], last_down)
            carry.append(last_part)
        elif r == 4:
            out_blocks = image_rows(
                live, [params[1]["mid"], last_part, swap(last_part)], last_bias
            )
        if 4 <= r < 4 + n_tensor - 1:
            out_blocks[r - 3] = shift(out_blocks[r - 3], r - 3)
            carry += out_blocks
        if r < 8:
            done = tie(carry + fresh + tied, [])
            if stage == 0:
                low = done[0]
            elif stage == 1:
                part = done[0]
            elif stage == 2:
                part = done[0]
            elif r < 7:
                grad = done[0]
            else:
                little, grad_blocks = done[0], done[1 : 1 + n_tensor]
            if r == 3:
                last_part = done[1]
            elif 4 <= r < 4 + n_tensor - 1:
                out_blocks = done[1 : 1 + n_tensor]
            done = done[len(carry) :]
            if fresh:
                grads[c] = fill(done[: len(fresh)])
                done = done[len(fresh) :]
            for store, at, count in slots:
                store[at] = done[:count] if count else done[0]
                done = done[max(count, 1) :]

    room = jnp.zeros((n_dp, n_tensor, extra * wide - small_size), little.dtype)
    little = jnp.concatenate([little, room], -1).reshape(n_dp, n_tensor, extra, wide)
    little = by_arrival(little.transpose(0, 2, 1, 3).reshape(n_dp, extra, -1), spot)
    if n_dp != 4:
        little = lax.psum_scatter(little, "dp", scatter_dimension=0, tiled=True)[0]
    else:
        over = lax.ppermute(little[3], "dp", [(i, i ^ 3) for i in range(n_dp)])
        little = add(little[0], swap_y(little[1])) + add(swap_x(little[2]), over)
        little = little.astype(jnp.bfloat16)

    last = number - 1
    settled[last - 1] = scatter_column(moved[last - 1][:2], moved[last - 1][2:])
    stay, come = scatter_two(*grads[last][2:], got[last])
    grad_rows, out_rows = by_image(grad_blocks), by_image(out_blocks)
    if come:
        stay = [add(s, c).astype(jnp.bfloat16) for s, c in zip(stay, come)]
    settled[last] = scatter_column([*stay, little], [])
    little = settled[last][depth:].reshape(-1).astype(jnp.float32)
    settled[last] = settled[last][:depth]
    grad_vectors = little[:n_vec].reshape(vectors.shape)
    grad_bias = little[n_vec:small_size].reshape(fc1_bias.shape)

    own = jnp.where(is_first, grad_rows, out_rows)
    other = swap(jnp.where(is_first, out_rows, grad_rows))
    ends = [jnp.where(is_first, own, other), jnp.where(is_first, other, own)]
    boundary_out = jnp.concatenate(ends, 1)[:, :tokens].astype(jnp.float32)[None]
    lows, highs = [], []
    for kind in range(3):
        first, second = settled[last - kind], settled[last - kind - 3]
        kept = jnp.where(is_first, first, second)
        received = swap(jnp.where(is_first, second, first))
        lows.append(jnp.where(is_first, kept, received).astype(jnp.float32))
        highs.append(jnp.where(is_first, received, kept).astype(jnp.float32))
    low, high = [part[0].reshape(depth, 4, -1) for part in (lows, highs)]
    grad_qkv = jnp.concatenate([low[:, :3], high[:, :3]], 2)[None]
    grad_proj = jnp.concatenate([low[:, 3].T, high[:, 3].T], 0)[None]
    grad_up = jnp.concatenate([lows[1], highs[1]], 1)[None]
    grad_down = jnp.concatenate([lows[2].T, highs[2].T], 0)[None]
    return (boundary_out, grad_qkv, grad_proj, grad_up, grad_down, grad_vectors, grad_bias)


def solution(mesh):
    in_specs = (
        P("section", "dp", None, "tensor"),
        P("dp", None),
        P("section", "dp", None, "tensor"),
        P("section", "tensor", "dp"),
        P("section", "dp", "tensor"),
        P("section", "tensor", "dp"),
        P("section", None, "tensor", "dp"),
        P("section", "tensor", "dp"),
    )
    out_specs = (
        P("section", "dp", None, "tensor"),
        P("section", "dp", None, "tensor"),
        P("section", "tensor", "dp"),
        P("section", "dp", "tensor"),
        P("section", "tensor", "dp"),
        P("section", None, "tensor", "dp"),
        P("section", "tensor", "dp"),
    )
    return jax.shard_map(body, mesh=mesh, in_specs=in_specs, out_specs=out_specs, check_vma=False)
```

```python
import jax
import jax.numpy as jnp
from jax import lax
from jax.experimental import pallas as pl
from jax.experimental.pallas import tpu as pltpu
from jax.sharding import PartitionSpec as P

HD = 64
EPS = 1e-06


def swap(value):
    return lax.ppermute(value, "section", [(0, 1), (1, 0)])


def pair_sum(partial):
    low = partial.astype(jnp.bfloat16)
    return low.astype(jnp.float32) + swap(low).astype(jnp.float32)


def swap_x(value):
    n = lax.axis_size("dp")
    return lax.ppermute(value, "dp", [(i, i ^ 1) for i in range(n)])


def swap_y(value):
    n = lax.axis_size("dp")
    return lax.ppermute(value, "dp", [(i, i ^ 2) for i in range(n)])


def tie(values, others):
    count = len(values)

    def kernel(*refs):
        pass

    anywhere = pl.BlockSpec(memory_space=pl.ANY)
    done = pl.pallas_call(
        kernel,
        out_shape=[jax.ShapeDtypeStruct(v.shape, v.dtype) for v in values],
        in_specs=[anywhere] * (count + len(others)),
        out_specs=[anywhere] * count,
        input_output_aliases={i: i for i in range(count)},
    )(*values, *others)
    return list(done)


def gather_column(shard):
    return lax.all_gather(shard, "tensor", axis=1, tiled=True)


def exchange_one(first, second):
    if lax.axis_size("dp") != 4:
        return [lax.all_gather(v, "dp", axis=0, tiled=True) for v in (first, second)]
    return [swap_y(first), swap_x(second)]


def exchange_two(first, second, near_first, near_second):
    if lax.axis_size("dp") != 4:
        return []
    return [swap_x(first), swap_x(near_first), swap_y(second), swap_y(near_second)]


def arrived(first, second, near, far):
    if lax.axis_size("dp") != 4:
        return ([near[0]], [near[1]])
    return ([first, near[0], far[0], far[1]], [second, near[1], far[2], far[3]])


def row_cuts(depth):
    half = depth // 2
    if lax.axis_size("dp") != 4:
        return [(0, half), (half, depth), None, None]
    part = half // 2
    return [(part, half), (half + part, depth), (0, part), (half, half + part)]


def add(left, right):
    return left.astype(jnp.float32) + right.astype(jnp.float32)


def scatter_one(send_first, send_second):
    if lax.axis_size("dp") != 4:
        return [
            lax.psum_scatter(v, "dp", scatter_dimension=0, tiled=True)
            for v in (send_first, send_second)
        ]
    return [swap_x(send_first), swap_y(send_second)]


def scatter_two(keep_first, keep_second, got):
    if lax.axis_size("dp") != 4:
        return (got, [])
    stay, send = [], []
    for keep, new in zip((keep_first, keep_second), got):
        half = keep.shape[0] // 2
        send.append(add(keep[half:], new[half:]).astype(jnp.bfloat16))
        stay.append(add(keep[:half], new[:half]).astype(jnp.bfloat16))
    return (stay, [swap_y(send[0]), swap_x(send[1])])


def scatter_column(stay, come):
    if come:
        stay = [add(s, c).astype(jnp.bfloat16) for s, c in zip(stay, come)]
    return lax.psum_scatter(
        jnp.concatenate(stay, 0), "tensor", scatter_dimension=1, tiled=True
    )


def flip_axis(value, axis, bit):
    return jnp.where(bit == 1, jnp.flip(value, axis), value)


def relative(value, spot):
    n_dp = lax.axis_size("dp")
    lead = value.shape[:-1]
    k = len(lead)
    if n_dp != 4:
        cut = value.reshape(lead + (n_dp, 2, -1))
        return jnp.swapaxes(cut, k, k + 1).reshape(value.shape)
    cut = value.reshape(lead + (2, 2, 2, -1))
    cut = flip_axis(flip_axis(cut, k, spot // 2), k + 1, spot % 2)
    first = jnp.swapaxes(cut[..., 0, :], k, k + 1)
    second = cut[..., 1, :]
    return jnp.concatenate([first.reshape(lead + (-1,)), second.reshape(lead + (-1,))], -1)


def absolute(value, spot):
    n_dp = lax.axis_size("dp")
    lead = value.shape[:-1]
    k = len(lead)
    if n_dp != 4:
        cut = value.reshape(lead + (2, n_dp, -1))
        return jnp.swapaxes(cut, k, k + 1).reshape(value.shape)
    cut = value.reshape(lead + (2, 2, 2, -1))
    first = jnp.swapaxes(cut[..., 0, :, :, :], k, k + 1)
    second = cut[..., 1, :, :, :]
    cut = jnp.stack([first, second], k + 2)
    cut = flip_axis(flip_axis(cut, k, spot // 2), k + 1, spot % 2)
    return cut.reshape(value.shape)


def by_chip(blocks, spot):
    n_dp = lax.axis_size("dp")
    if n_dp != 4:
        return blocks
    cut = blocks.reshape((2, 2) + blocks.shape[1:])
    cut = jnp.swapaxes(cut, 0, 1)
    cut = flip_axis(flip_axis(cut, 0, spot // 2), 1, spot % 2)
    return cut.reshape(blocks.shape)


def by_arrival(blocks, spot):
    n_dp = lax.axis_size("dp")
    if n_dp != 4:
        return blocks
    cut = blocks.reshape((2, 2) + blocks.shape[1:])
    cut = flip_axis(flip_axis(cut, 0, spot // 2), 1, spot % 2)
    return jnp.swapaxes(cut, 0, 1).reshape(blocks.shape)


VMEM_BYTES = 50 * 2**20
BF = jnp.bfloat16
F32 = jnp.float32


def shape(dims, kind=jnp.bfloat16):
    return jax.ShapeDtypeStruct(dims, kind)


def run(kernel, outs, ins):
    block = pl.BlockSpec(memory_space=pltpu.VMEM)
    done = pl.pallas_call(
        kernel,
        out_shape=list(outs),
        in_specs=[block] * len(ins),
        out_specs=[block] * len(outs),
        cost_estimate=pl.CostEstimate(flops=1, bytes_accessed=1, transcendentals=0),
        compiler_params=pltpu.CompilerParams(vmem_limit_bytes=VMEM_BYTES),
    )(*ins)
    return list(done)


def nn(left, right):
    return lax.dot_general(left, right, (((1,), (0,)), ((), ())), preferred_element_type=F32)


def nt(left, right):
    return lax.dot_general(left, right, (((1,), (1,)), ((), ())), preferred_element_type=F32)


def tn(left, right):
    return lax.dot_general(left, right, (((0,), (0,)), ((), ())), preferred_element_type=F32)


def stack_rows(pieces, counts, cols):
    return jnp.concatenate([p[:n, cols] for p, n in zip(pieces, counts)], 0)


def center_scale(value):
    center = jnp.mean(value, -1, keepdims=True)
    spread = jnp.mean(value * value, -1, keepdims=True) - center * center
    factor = lax.rsqrt(spread + EPS)
    return ((value - center) * factor, factor)


def norm_backward(grad_normed, centred, factor, gain):
    scaled = grad_normed * gain
    return factor * (
        scaled
        - jnp.mean(scaled, -1, keepdims=True)
        - centred * jnp.mean(scaled * centred, -1, keepdims=True)
    )


def column_sum(value):
    return jnp.sum(value, 0, keepdims=True)


def attention_forward(tokens, terms, bias_row, low, weights, rows, q_bias, v_bias):
    pieces, counts = weights
    size, depth = terms[0].shape
    wide = pieces[0].shape[1]
    groups = wide // 512
    half = groups * 128
    n_terms, n_pieces = len(terms), len(pieces)

    def kernel(*refs):
        term_refs, refs = refs[:n_terms], refs[n_terms:]
        bias_ref, rows_ref, qb_ref, vb_ref = refs[:4]
        piece_refs, refs = refs[4 : 4 + n_pieces], refs[4 + n_pieces :]
        u_ref, n_ref, q_ref, k_ref, v_ref, p_ref, o_ref, part_ref = refs
        value = term_refs[0][...].astype(F32)
        for ref in term_refs[1:]:
            value = value + ref[...].astype(F32)
        if n_terms > 1:
            value = value + bias_ref[...]
        if low:
            value = value.astype(BF).astype(F32)
        u_ref[...] = value
        centred, factor = center_scale(value)
        n_ref[...] = (centred * rows_ref[0:1] + rows_ref[1:2]).astype(BF)
        lane = lax.broadcasted_iota(jnp.int32, (size, 128), 1)
        key_lane = lax.broadcasted_iota(jnp.int32, (size, size), 1)
        normed = n_ref[...]
        for g in range(groups):
            at = slice(g * 128, (g + 1) * 128)
            matrix = stack_rows(piece_refs, counts, slice(g * 512, g * 512 + 384))
            projected = nn(normed, matrix)
            q = (projected[:, :128] + qb_ref[:, at]).astype(BF)
            k = projected[:, 128:256].astype(BF)
            v = (projected[:, 256:384] + vb_ref[:, at]).astype(BF)
            q_ref[:, at] = q
            k_ref[:, at] = k
            v_ref[:, at] = v
            mixed = None
            for h in range(2):
                mine = (lane // HD) == h
                scores = nt(jnp.where(mine, q, jnp.zeros_like(q)), k) * HD ** (-0.5)
                scores = jnp.where(key_lane < tokens, scores, -1e30)
                highest = jnp.max(scores, -1, keepdims=True)
                exponent = jnp.exp(scores - highest)
                inverse = 1.0 / jnp.sum(exponent, -1, keepdims=True)
                soft = (exponent * inverse).astype(BF)
                p_ref[2 * g + h] = soft
                out = nn(soft, v)
                mixed = out if h == 0 else jnp.where(mine, out, mixed)
            o_ref[:, at] = mixed.astype(BF)
        matrix = jnp.concatenate(
            [stack_rows(piece_refs, counts, slice(g * 512 + 384, g * 512 + 512)) for g in range(groups)], 1
        )
        part_ref[...] = nt(o_ref[...], matrix).astype(BF)

    outs = [shape((size, depth), F32), shape((size, depth))] + [shape((size, half))] * 3
    outs += [shape((2 * groups, size, size)), shape((size, half)), shape((size, depth))]
    return run(kernel, outs, [*terms, bias_row, rows, q_bias, v_bias, *pieces])


def up_forward(terms, weights, rows, up_bias):
    pieces, counts = weights
    size, depth = terms[0].shape
    wide = pieces[0].shape[1]

    def kernel(*refs):
        u_ref, own_ref, far_ref, rows_ref, bias_ref = refs[:5]
        piece_refs = refs[5 : 5 + len(pieces)]
        mid_ref, n_ref, slope_ref, hidden_ref = refs[5 + len(pieces) :]
        value = u_ref[...] + own_ref[...].astype(F32) + far_ref[...].astype(F32) + rows_ref[4:5]
        mid_ref[...] = value
        centred, factor = center_scale(value)
        n_ref[...] = (centred * rows_ref[5:6] + rows_ref[6:7]).astype(BF)
        step = 512
        for at in range(0, wide, step):
            cols = slice(at, at + step)
            before = nn(n_ref[...], stack_rows(piece_refs, counts, cols)) + bias_ref[:, cols]
            cdf = 0.5 * (1.0 + lax.erf(before * 0.7071067811865476))
            density = jnp.exp(-0.5 * before * before) * 0.3989422804014327
            hidden_ref[:, cols] = (before * cdf).astype(BF)
            slope_ref[:, cols] = (cdf + before * density).astype(BF)

    outs = [shape((size, depth), F32), shape((size, depth)), shape((size, wide)), shape((size, wide))]
    return run(kernel, outs, [*terms, rows, up_bias, *pieces])


def contract_wide(left, weights):
    pieces, counts = weights
    size, wide = left.shape
    depth = sum(counts)

    def kernel(*refs):
        left_ref, piece_refs, out_ref = refs[0], refs[1:-1], refs[-1]
        matrix = stack_rows(piece_refs, counts, slice(0, wide))
        out_ref[...] = nt(left_ref[...], matrix).astype(BF)

    return run(kernel, [shape((size, depth))], [left, *pieces])[0]


def weight_outs(depth, wide):
    cuts = [c for c in row_cuts(depth) if c is not None]
    return cuts, [shape((c[1] - c[0], wide)) for c in cuts]


def fill(grads):
    return (list(grads) + [None, None])[:4]


def down_grad(grad_out, hidden):
    size, depth = grad_out.shape
    cuts, outs = weight_outs(depth, hidden.shape[1])

    def kernel(g_ref, hidden_ref, sum_ref, *refs):
        sum_ref[...] = column_sum(g_ref[...])
        branch = g_ref[...].astype(BF)
        for cut, ref in zip(cuts, refs):
            ref[...] = tn(branch[:, cut[0] : cut[1]], hidden_ref[...]).astype(BF)

    done = run(kernel, [shape((1, depth), F32)] + outs, [grad_out, hidden])
    return done[0], fill(done[1:])


def down_backward(grad_out, slope, weights):
    pieces, counts = weights
    size, depth = grad_out.shape
    wide = slope.shape[1]

    def kernel(*refs):
        g_ref, slope_ref, piece_refs = refs[0], refs[1], refs[2:-2]
        low_ref, bias_ref = refs[-2:]
        branch = g_ref[...].astype(BF)
        step = 512
        for at in range(0, wide, step):
            cols = slice(at, at + step)
            back = nn(branch, stack_rows(piece_refs, counts, cols)) * slope_ref[:, cols].astype(F32)
            bias_ref[:, cols] = column_sum(back)
            low_ref[:, cols] = back.astype(BF)

    outs = [shape((size, wide)), shape((1, wide), F32)]
    return run(kernel, outs, [grad_out, slope, *pieces])


def up_grad(normed, low):
    size, depth = normed.shape
    wide = low.shape[1]
    cuts, outs = weight_outs(depth, wide)

    def kernel(n_ref, low_ref, *refs):
        for cut, ref in zip(cuts, refs):
            ref[...] = tn(n_ref[:, cut[0] : cut[1]], low_ref[...]).astype(BF)

    return fill(run(kernel, outs, [normed, low]))


def attention_backward(grad_out, own, far, middle, rows, saved, weights):
    pieces, counts = weights
    size, depth = grad_out.shape
    wide = pieces[0].shape[1]
    groups = wide // 512
    half = groups * 128
    scale = HD ** (-0.5)

    def kernel(*refs):
        g_ref, own_ref, far_ref, mid_ref, rows_ref, q_ref, k_ref, v_ref, p_ref, o_ref = refs[:10]
        piece_refs, refs = refs[10 : 10 + len(pieces)], refs[10 + len(pieces) :]
        dmid_ref, dz_ref, dq_ref, dk_ref, dv_ref, part_ref, sum_ref, qs_ref, vs_ref = refs
        grad_normed = own_ref[...].astype(F32) + far_ref[...].astype(F32)
        centred, factor = center_scale(mid_ref[...])
        sum_ref[1:2] = column_sum(grad_normed * centred)
        sum_ref[2:3] = column_sum(grad_normed)
        dmid = g_ref[...] + norm_backward(grad_normed, centred, factor, rows_ref[5:6])
        dmid_ref[...] = dmid
        sum_ref[0:1] = column_sum(dmid)
        dz_ref[...] = dmid.astype(BF)
        lane = lax.broadcasted_iota(jnp.int32, (size, 128), 1)
        for g in range(groups):
            at = slice(g * 128, (g + 1) * 128)
            matrix = stack_rows(piece_refs, counts, slice(g * 512 + 384, g * 512 + 512))
            grad_mixed = nn(dz_ref[...], matrix).astype(BF)
            q, k, v = q_ref[:, at], k_ref[:, at], v_ref[:, at]
            inner = grad_mixed.astype(F32) * o_ref[:, at].astype(F32)
            dq, dk, dv = None, None, None
            for h in range(2):
                mine = (lane // HD) == h
                soft = p_ref[2 * g + h]
                none = jnp.zeros_like(q)
                do = jnp.where(mine, grad_mixed, none)
                total = jnp.sum(jnp.where(mine, inner, 0.0), -1, keepdims=True)
                grad_soft = nt(do, v)
                grad_scores = (soft.astype(F32) * (grad_soft - total)).astype(BF)
                new_q = nn(grad_scores, k)
                new_k = tn(jnp.where(mine, q, none), grad_scores)
                new_v = tn(do, soft)
                dq = new_q if h == 0 else jnp.where(mine, new_q, dq)
                dk = new_k if h == 0 else dk + new_k
                dv = new_v if h == 0 else dv + new_v
            dq, dk, dv = dq * scale, dk.T * scale, dv.T
            qs_ref[:, at] = column_sum(dq)
            vs_ref[:, at] = column_sum(dv)
            dq_ref[:, at] = dq.astype(BF)
            dk_ref[:, at] = dk.astype(BF)
            dv_ref[:, at] = dv.astype(BF)
        total = None
        for g in range(groups):
            at = slice(g * 128, (g + 1) * 128)
            left = jnp.concatenate([dq_ref[:, at], dk_ref[:, at], dv_ref[:, at]], 1)
            new = nt(left, stack_rows(piece_refs, counts, slice(g * 512, g * 512 + 384)))
            total = new if g == 0 else total + new
        part_ref[...] = total.astype(BF)

    outs = [shape((size, depth), F32), shape((size, depth))] + [shape((size, half))] * 3
    outs += [shape((size, depth)), shape((3, depth), F32)] + [shape((1, half), F32)] * 2
    return run(kernel, outs, [grad_out, own, far, middle, rows, *saved, *pieces])


def attention_grad(normed, dz, dq, dk, dv, mixed):
    size, depth = normed.shape
    groups = dq.shape[1] // 128
    cuts, outs = weight_outs(depth, groups * 512)

    def kernel(n_ref, dz_ref, dq_ref, dk_ref, dv_ref, o_ref, *refs):
        for cut, ref in zip(cuts, refs):
            rows = slice(cut[0], cut[1])
            for g in range(groups):
                at = slice(g * 128, (g + 1) * 128)
                right = jnp.concatenate([dq_ref[:, at], dk_ref[:, at], dv_ref[:, at]], 1)
                ref[:, g * 512 : g * 512 + 384] = tn(n_ref[:, rows], right).astype(BF)
                ref[:, g * 512 + 384 : g * 512 + 512] = tn(dz_ref[:, rows], o_ref[:, at]).astype(BF)

    return fill(run(kernel, outs, [normed, dz, dq, dk, dv, mixed]))


def value_backward(dmid, own, far, value, rows, low):
    size, depth = dmid.shape

    def kernel(dmid_ref, own_ref, far_ref, u_ref, rows_ref, out_ref, sum_ref):
        grad_normed = own_ref[...].astype(F32) + far_ref[...].astype(F32)
        centred, factor = center_scale(u_ref[...])
        sum_ref[0:1] = column_sum(grad_normed * centred)
        sum_ref[1:2] = column_sum(grad_normed)
        out = dmid_ref[...] + norm_backward(grad_normed, centred, factor, rows_ref[0:1])
        if low:
            out = out.astype(BF).astype(F32)
        out_ref[...] = out

    outs = [shape((size, depth), F32), shape((2, depth), F32)]
    return run(kernel, outs, [dmid, own, far, value, rows])


def block_lanes(spot, chunk):
    ry, rx = chunk // 2 ^ spot // 2, chunk % 2 ^ spot % 2
    return [(rx * 2 + ry) * 128, 512 + (ry * 2 + rx) * 128]


def place_in(lanes, blocks):
    size, width = blocks[0].shape
    half = width // 2

    def kernel(lanes_ref, *refs):
        out_ref = refs[-1]
        for d, ref in enumerate(refs[:-1]):
            for h in range(2):
                at = pl.multiple_of(lanes_ref[2 * d + h], 128)
                out_ref[:, pl.ds(at, half)] = ref[:, h * half : (h + 1) * half]

    block = pl.BlockSpec(memory_space=pltpu.VMEM)
    return pl.pallas_call(
        kernel,
        out_shape=shape((size, width * len(blocks))),
        in_specs=[pl.BlockSpec(memory_space=pltpu.SMEM)] + [block] * len(blocks),
        out_specs=block,
        compiler_params=pltpu.CompilerParams(vmem_limit_bytes=VMEM_BYTES),
    )(lanes, *blocks)


def place_out(numbers, scale, terms, bias_row, count):
    size, depth = terms[0].shape
    width = depth // count
    half = width // 2

    def kernel(numbers_ref, scale_ref, *refs):
        term_refs, bias_ref, out_ref = refs[: len(terms)], refs[-2], refs[-1]
        start = pl.multiple_of(numbers_ref[2 * count], 8)
        rows = pl.ds(start, size // 2)
        for d in range(count):
            for h in range(2):
                lanes = pl.ds(pl.multiple_of(numbers_ref[2 * d + h], 128), half)
                value = term_refs[0][rows, lanes]
                for ref in term_refs[1:]:
                    value = value + ref[rows, lanes]
                value = (value + bias_ref[:, lanes]) * scale_ref[0]
                out_ref[d, :, h * half : (h + 1) * half] = value.astype(BF)

    block = pl.BlockSpec(memory_space=pltpu.VMEM)
    scalar = pl.BlockSpec(memory_space=pltpu.SMEM)
    return pl.pallas_call(
        kernel,
        out_shape=shape((count, size // 2, width)),
        in_specs=[scalar, scalar] + [block] * (len(terms) + 1),
        out_specs=block,
        compiler_params=pltpu.CompilerParams(vmem_limit_bytes=VMEM_BYTES),
    )(numbers, scale, *terms, bias_row)


def shift(block, d):
    n = lax.axis_size("tensor")
    return lax.ppermute(block, "tensor", [(i, (i + d) % n) for i in range(n)])


def shifts(blocks):
    return [blocks[0]] + [shift(block, d) for d, block in enumerate(blocks) if d > 0]


def half_cols(core, whole, n_tensor):
    cut = whole.reshape(whole.shape[:-1] + (n_tensor, 2, -1))
    cut = jnp.where(core == 0, cut[..., 0, :], cut[..., 1, :])
    return cut.reshape(whole.shape[:-1] + (-1,))


def spread_cols(core, half, n_tensor):
    cut = half.reshape(half.shape[:-1] + (n_tensor, 1, -1))
    none = jnp.zeros_like(cut)
    both = jnp.concatenate(
        [jnp.where(core == 0, cut, none), jnp.where(core == 0, none, cut)], -2
    )
    return both.reshape(half.shape[:-1] + (-1,))


def body(boundary_in, counts, qkv_weight, proj_weight, fc1_weight, fc2_weight, vectors, fc1_bias):
    core = lax.axis_index("section")
    is_first = core == 0
    place = lax.axis_index("tensor")
    spot = lax.axis_index("dp")
    n_dp, n_tensor = lax.axis_size("dp"), lax.axis_size("tensor")
    slots_per_batch = boundary_in.shape[1] // counts.shape[1]
    live = (place % slots_per_batch < counts[0, place // slots_per_batch]).astype(jnp.float32)
    depth = qkv_weight.shape[1]
    mid = depth // 2
    n_vec = vectors.size

    small_size = n_vec + fc1_bias.size
    packs = []
    for part in range(2):
        cuts = [
            jnp.split(qkv_weight[0], 2, 2)[part].reshape(depth, -1),
            jnp.split(proj_weight[0], 2, 0)[part].T,
            jnp.split(fc1_weight[0], 2, 1)[part],
            jnp.split(fc2_weight[0], 2, 0)[part].T,
        ]
        packs.append(jnp.concatenate(cuts, 1))
    wide = packs[0].shape[1] // 3
    extra = 16
    small = jnp.concatenate([vectors.reshape(-1), fc1_bias.reshape(-1)])
    small = jnp.pad(small, (0, extra * wide - small_size)).reshape(extra, wide)
    small = jnp.pad(small, ((0, 0), (0, 2 * wide)))
    kept = jnp.concatenate([jnp.where(is_first, packs[0], packs[1]), small], 0)
    received = swap(
        jnp.concatenate([jnp.where(is_first, packs[1], packs[0]), small], 0)
    )
    shards = (jnp.where(is_first, kept, received), jnp.where(is_first, received, kept))
    columns = []
    for layer in range(2):
        for number in range(3):
            cols = shards[layer][:, number * wide : (number + 1) * wide]
            if layer == 0 and number == 0:
                room = extra // 2
                both = [shard[depth : depth + room, :wide] for shard in shards]
                cols = jnp.concatenate([cols[:depth], *both], 0)
            else:
                cols = cols[:depth]
            columns.append(cols)

    tokens = boundary_in.shape[2]
    pad = -tokens % 16
    reach = (tokens + pad) // 2
    ends_in = jnp.pad(boundary_in[0].astype(jnp.bfloat16), ((0, 0), (0, pad), (0, 0)))
    ends_low, ends_high = ends_in[:, :reach], ends_in[:, reach:]
    ends_got = swap(jnp.where(is_first, ends_high, ends_low))
    half_in = jnp.where(is_first, ends_low, ends_got)
    half_cot = jnp.where(is_first, ends_got, ends_high)

    below = [(place - d) % n_tensor for d in range(n_tensor)]
    above = [(place + d) % n_tensor for d in range(n_tensor)]

    def to_send(half):
        return [lax.dynamic_index_in_dim(half, j, 0, False) for j in above]

    def image_half(blocks):
        if n_dp == 4:
            lanes = [lane for t in below for lane in block_lanes(spot, t)]
            return place_in(jnp.stack(lanes).astype(jnp.int32), blocks)
        blocks = jnp.stack(blocks)
        blocks = [lax.dynamic_index_in_dim(blocks, (place - i) % n_tensor, 0, False) for i in range(n_tensor)]
        return relative(jnp.concatenate(blocks, 1), spot)

    def whole_image(half):
        other = swap(half)
        both = [jnp.where(is_first, half, other), jnp.where(is_first, other, half)]
        return jnp.concatenate(both, 0)

    def image_rows(scale, terms, bias_row):
        if n_dp == 4:
            numbers = [lane for t in above for lane in block_lanes(spot, t)]
            numbers.append(jnp.where(is_first, 0, reach))
            numbers = jnp.stack(numbers).astype(jnp.int32)
            blocks = place_out(numbers, scale.reshape(1), terms, bias_row, n_tensor)
            return [blocks[d] for d in range(n_tensor)]
        image = absolute((sum(terms[1:], terms[0]) + bias_row) * scale, spot).astype(jnp.bfloat16)
        half = jnp.where(is_first, image[:reach], image[reach:])
        half = half.reshape(reach, n_tensor, -1).transpose(1, 0, 2)
        return to_send(half)

    def by_image(blocks):
        blocks = jnp.stack(blocks)
        blocks = [lax.dynamic_index_in_dim(blocks, (place - i) % n_tensor, 0, False) for i in range(n_tensor)]
        return jnp.stack(blocks)

    def small_of(extras):
        if n_dp != 4:
            extras = lax.all_gather(extras, "dp", axis=0, tiled=True)
        else:
            over = lax.ppermute(extras, "dp", [(i, i ^ 3) for i in range(n_dp)])
            extras = jnp.concatenate([extras, swap_y(extras), swap_x(extras), over], 0)
        both = by_chip(extras.reshape(n_dp, extra, -1), spot).astype(jnp.float32)
        both = both.reshape(n_dp, 2, extra // 2, n_tensor, wide).transpose(1, 0, 3, 2, 4)
        both = both.reshape(2, n_dp, n_tensor, -1)
        rows = both[..., :n_vec].reshape(2, n_dp, n_tensor, 8, -1)
        rows = relative(rows.transpose(0, 3, 2, 1, 4).reshape(2, 8, -1), spot)
        bias = both[..., n_vec:small_size].transpose(0, 2, 1, 3).reshape(2, -1)
        plain = both[..., :n_vec].reshape(2, n_dp, n_tensor, 8, -1)[..., 2:4, :]
        plain = plain.transpose(0, 3, 2, 1, 4).reshape(2, 2, -1)
        parts = [half_cols(core, plain[:, 0], n_tensor), half_cols(core, plain[:, 1], n_tensor)]
        parts.append(half_cols(core, bias, n_tensor))
        return [(rows[i], parts[0][i : i + 1], parts[1][i : i + 1], parts[2][i : i + 1]) for i in range(2)]

    number = len(columns)
    halves, near, far = [None] * number, [None] * number, [None] * number
    params = [dict(), dict()]
    blocks_in, blocks_cot = to_send(half_in), to_send(half_cot)
    pair, state = None, None

    def weights_of(k):
        first, second = arrived(*halves[k], near[k], far[k])
        return (first + second, [p.shape[0] for p in first + second])

    for r in range(number + 1):
        tied = []
        if r < number:
            tied.append(gather_column(columns[r]))
        if 0 <= r - 1 < number:
            near[r - 1] = exchange_one(*halves[r - 1])
        if r == 1:
            smalls = small_of(extra_rows)
            blocks_in = shifts(blocks_in)
        if 2 <= r <= 1 + n_tensor - 1:
            blocks_cot[r - 1] = shift(blocks_cot[r - 1], r - 1)
        if r == number - 1:
            cot_half = image_half(blocks_cot)
        if r == number:
            cotangent = whole_image(cot_half).astype(jnp.float32) * live
        ready = []
        k = r - 2
        if k >= 0:
            layer, kind = k // 3, k % 3
            one = params[layer]
            weights = weights_of(k)
            rows, q_bias, v_bias, up_bias = one["small"]
            if pair is not None:
                pair = [pair[0], swap(pair[0])]
            if kind == 0:
                one["qkvo"] = weights
                if layer == 0:
                    terms = [whole_image(image_half(blocks_in)).astype(jnp.float32)]
                else:
                    terms = [state, *pair]
                bias_row = params[0]["small"][0][7:8]
                done = attention_forward(
                    tokens, terms, bias_row, layer == 1, weights, rows, q_bias, v_bias
                )
                one["u"], one["n1"], one["saved"], part = done[0], done[1], done[2:7], done[7]
                pair, ready = [part], [part]
            elif kind == 1:
                one["up"] = weights
                one["mid"], one["n2"], one["slope"], one["hidden"] = up_forward(
                    [one["u"], *pair], weights, rows, up_bias
                )
                pair, ready = None, [one["hidden"]]
            else:
                one["down"] = weights
                state = one["mid"]
                part = contract_wide(one["hidden"], weights)
                pair, ready = [part], [part]
        if r <= number:
            count = len(ready)
            extras = list(ready)
            if 0 <= r - 1 < number:
                if ready:
                    done = tie(near[r - 1] + extras, [])
                    near[r - 1], extras = done[: len(near[r - 1])], done[len(near[r - 1]) :]
                far[r - 1] = exchange_two(*halves[r - 1], *near[r - 1])
                tied += near[r - 1] + far[r - 1]
            if r == number:
                last_sum, first_grads = down_grad(cotangent, extras[0])
                first_grads = [g for g in first_grads if g is not None]
                extras += first_grads
            if r <= 1:
                extras += blocks_in
            if r == 1:
                extras += [v for layer in range(2) for v in smalls[layer]]
            if 1 <= r <= number - 2:
                extras += blocks_cot
            elif r == number - 1:
                extras.append(cot_half)
            elif r == number:
                extras.append(cotangent)
            if r + 1 < number:
                extras.append(columns[r + 1])
            done = tie(tied + extras, [])
            if r + 1 < number:
                columns[r + 1] = done.pop()
            if 1 <= r <= number - 2:
                done, blocks_cot = done[:-n_tensor], done[-n_tensor:]
            elif r == number - 1:
                cot_half = done.pop()
            elif r == number:
                cotangent = done.pop()
                done, first_grads = done[: -len(first_grads)], done[-len(first_grads) :]
            if r == 1:
                done, smalls = done[:-8], done[-8:]
                params[0]["small"], params[1]["small"] = smalls[:4], smalls[4:]
            if r <= 1:
                done, blocks_in = done[:-n_tensor], done[-n_tensor:]
            if count and kind == 1:
                one["hidden"] = done[-1]
            elif count:
                pair = [done[-1]]
            at = 0
            if r < number:
                halves[r] = (done[0][:mid], done[0][mid:depth])
                if r == 0:
                    extra_rows = done[0][depth:]
                at = 1
            if 0 <= r - 1 < number:
                near[r - 1] = done[at : at + 2]
                far[r - 1] = done[at + 2 : at + 2 + len(far[r - 1])]

    sums = [dict(), dict()]

    def small_grads():
        packed = []
        for layer in range(2):
            total = sums[layer]
            full = jnp.concatenate([total["one"], total["mid"], total["out"]], 0)
            full = absolute(jnp.where(core == layer, full, 0.0), spot)
            q_row = spread_cols(core, total["q"][0], n_tensor)
            v_row = spread_cols(core, total["v"][0], n_tensor)
            up_row = spread_cols(core, total["up_bias"][0], n_tensor)
            rows = jnp.concatenate([full[:2], q_row[None], v_row[None], full[2:]], 0)
            rows = rows.reshape(8, n_tensor, n_dp, -1).transpose(2, 1, 0, 3).reshape(n_dp, n_tensor, -1)
            up_row = up_row.reshape(n_tensor, n_dp, -1).transpose(1, 0, 2)
            packed.append(jnp.concatenate([rows, up_row], -1))
        ours = jnp.where(is_first, packed[0], packed[1])
        other = swap(jnp.where(is_first, packed[1], packed[0]))
        little = (ours + other).astype(jnp.bfloat16)
        return little

    grads, got, moved, settled = [None] * number, [None] * number, [None] * number, [None] * number
    made = [0, 1, 3, 4, 5, 6]
    column_at = [4, 5, 6, 7]
    grad = cotangent
    last_down = weights_of(number - 1)
    params[1]["down"] = last_down
    last_bias = params[1]["small"][0][7:8]
    grads[0] = fill(first_grads)
    sums[1]["out"] = last_sum
    for r in range(1, 8):
        layer, stage = 1 - r // 4, r % 4
        one, total = params[layer], sums[layer]
        rows = one["small"][0]
        tied, slots = [], []
        for c in range(number):
            if r == made[c] + 1:
                got[c] = scatter_one(*grads[c][:2])
                slots.append((got, c, len(got[c])))
                tied += got[c]
            elif r == made[c] + 2:
                stay, come = scatter_two(*grads[c][2:], got[c])
                moved[c] = [*stay, *come]
                if r < 7:
                    slots.append((moved, c, len(moved[c])))
                    tied += moved[c]
            elif c < len(column_at) and r == column_at[c]:
                settled[c] = scatter_column(moved[c][:2], moved[c][2:])
                slots.append((settled, c, 0))
                tied.append(settled[c])
        new = None
        if stage == 0:
            total["out"], new = down_grad(grad, one["hidden"])
        if stage == 0 or r == 1:
            low, total["up_bias"] = down_backward(grad, one["slope"], one["down"])
            carry = [low]
        if stage == 1:
            part = contract_wide(low, one["up"])
            new = up_grad(one["n2"], low)
            carry = [part]
        if stage == 2:
            done = attention_backward(
                grad, part, swap(part), one["mid"], rows, one["saved"], one["qkvo"]
            )
            dmid, dz, dq, dk, dv, part, total["mid"], total["q"], total["v"] = done
            if layer == 0:
                new = attention_grad(one["n1"], dz, dq, dk, dv, one["saved"][4])
            carry = [part]
        if stage == 3:
            if layer == 1:
                new = attention_grad(one["n1"], dz, dq, dk, dv, one["saved"][4])
            grad, total["one"] = value_backward(dmid, part, swap(part), one["u"], rows, layer == 1)
            carry = [grad]
            if r == 7:
                done = tie([grad, *moved[4]], [])
                grad, moved[4] = done[0], done[1:]
                settled[4] = scatter_column(moved[4][:2], moved[4][2:])
                one_scale = jnp.ones((), jnp.float32)
                no_bias = jnp.zeros((1, grad.shape[1]), jnp.float32)
                carry = [small_grads(), *shifts(image_rows(one_scale, [grad], no_bias))]
        if new is not None:
            c = made.index(r)
            grads[c] = new
            fresh = [g for g in new if g is not None]
        else:
            fresh = []
        if r == 3:
            last_part = contract_wide(params[1]["hidden"], last_down)
            carry.append(last_part)
        elif r == 4:
            out_blocks = image_rows(
                live, [params[1]["mid"], last_part, swap(last_part)], last_bias
            )
        if 4 <= r < 4 + n_tensor - 1:
            out_blocks[r - 3] = shift(out_blocks[r - 3], r - 3)
            carry += out_blocks
        if r < 8:
            done = tie(carry + fresh + tied, [])
            if stage == 0:
                low = done[0]
            elif stage == 1:
                part = done[0]
            elif stage == 2:
                part = done[0]
            elif r < 7:
                grad = done[0]
            else:
                little, grad_blocks = done[0], done[1 : 1 + n_tensor]
            if r == 3:
                last_part = done[1]
            elif 4 <= r < 4 + n_tensor - 1:
                out_blocks = done[1 : 1 + n_tensor]
            done = done[len(carry) :]
            if fresh:
                grads[c] = fill(done[: len(fresh)])
                done = done[len(fresh) :]
            for store, at, count in slots:
                store[at] = done[:count] if count else done[0]
                done = done[max(count, 1) :]

    room = jnp.zeros((n_dp, n_tensor, extra * wide - small_size), little.dtype)
    little = jnp.concatenate([little, room], -1).reshape(n_dp, n_tensor, extra, wide)
    little = by_arrival(little.transpose(0, 2, 1, 3).reshape(n_dp, extra, -1), spot)
    if n_dp != 4:
        little = lax.psum_scatter(little, "dp", scatter_dimension=0, tiled=True)[0]
    else:
        over = lax.ppermute(little[3], "dp", [(i, i ^ 3) for i in range(n_dp)])
        little = add(little[0], swap_y(little[1])) + add(swap_x(little[2]), over)
        little = little.astype(jnp.bfloat16)

    last = number - 1
    stay, come = scatter_two(*grads[last][2:], got[last])
    grad_rows, out_rows = by_image(grad_blocks), by_image(out_blocks)
    if come:
        stay = [add(s, c).astype(jnp.bfloat16) for s, c in zip(stay, come)]
    settled[last] = scatter_column([*stay, little], [])
    little = settled[last][depth:].reshape(-1).astype(jnp.float32)
    settled[last] = settled[last][:depth]
    grad_vectors = little[:n_vec].reshape(vectors.shape)
    grad_bias = little[n_vec:small_size].reshape(fc1_bias.shape)

    own = jnp.where(is_first, grad_rows, out_rows)
    other = swap(jnp.where(is_first, out_rows, grad_rows))
    ends = [jnp.where(is_first, own, other), jnp.where(is_first, other, own)]
    boundary_out = jnp.concatenate(ends, 1)[:, :tokens].astype(jnp.float32)[None]
    lows, highs = [], []
    for kind in range(3):
        first, second = settled[last - kind], settled[last - kind - 3]
        kept = jnp.where(is_first, first, second)
        received = swap(jnp.where(is_first, second, first))
        lows.append(jnp.where(is_first, kept, received).astype(jnp.float32))
        highs.append(jnp.where(is_first, received, kept).astype(jnp.float32))
    low, high = [part[0].reshape(depth, 4, -1) for part in (lows, highs)]
    grad_qkv = jnp.concatenate([low[:, :3], high[:, :3]], 2)[None]
    grad_proj = jnp.concatenate([low[:, 3].T, high[:, 3].T], 0)[None]
    grad_up = jnp.concatenate([lows[1], highs[1]], 1)[None]
    grad_down = jnp.concatenate([lows[2].T, highs[2].T], 0)[None]
    return (boundary_out, grad_qkv, grad_proj, grad_up, grad_down, grad_vectors, grad_bias)


def solution(mesh):
    in_specs = (
        P("section", "dp", None, "tensor"),
        P("dp", None),
        P("section", "dp", None, "tensor"),
        P("section", "tensor", "dp"),
        P("section", "dp", "tensor"),
        P("section", "tensor", "dp"),
        P("section", None, "tensor", "dp"),
        P("section", "tensor", "dp"),
    )
    out_specs = (
        P("section", "dp", None, "tensor"),
        P("section", "dp", None, "tensor"),
        P("section", "tensor", "dp"),
        P("section", "dp", "tensor"),
        P("section", "tensor", "dp"),
        P("section", None, "tensor", "dp"),
        P("section", "tensor", "dp"),
    )
    return jax.shard_map(body, mesh=mesh, in_specs=in_specs, out_specs=out_specs, check_vma=False)
```

```python
import jax
import jax.numpy as jnp
from jax import lax
from jax.experimental import pallas as pl
from jax.experimental.pallas import tpu as pltpu
from jax.sharding import PartitionSpec as P

HD = 64
EPS = 1e-06


def swap(value):
    return lax.ppermute(value, "section", [(0, 1), (1, 0)])


def pair_sum(partial):
    low = partial.astype(jnp.bfloat16)
    return low.astype(jnp.float32) + swap(low).astype(jnp.float32)


def swap_x(value):
    n = lax.axis_size("dp")
    return lax.ppermute(value, "dp", [(i, i ^ 1) for i in range(n)])


def swap_y(value):
    n = lax.axis_size("dp")
    return lax.ppermute(value, "dp", [(i, i ^ 2) for i in range(n)])


def tie(values, others):
    count = len(values)

    def kernel(*refs):
        pass

    anywhere = pl.BlockSpec(memory_space=pl.ANY)
    done = pl.pallas_call(
        kernel,
        out_shape=[jax.ShapeDtypeStruct(v.shape, v.dtype) for v in values],
        in_specs=[anywhere] * (count + len(others)),
        out_specs=[anywhere] * count,
        input_output_aliases={i: i for i in range(count)},
    )(*values, *others)
    return list(done)


def gather_column(shard):
    return lax.all_gather(shard, "tensor", axis=1, tiled=True)


def exchange_one(first, second):
    if lax.axis_size("dp") != 4:
        return [lax.all_gather(v, "dp", axis=0, tiled=True) for v in (first, second)]
    return [swap_y(first), swap_x(second)]


def exchange_two(first, second, near_first, near_second):
    if lax.axis_size("dp") != 4:
        return []
    return [swap_x(first), swap_x(near_first), swap_y(second), swap_y(near_second)]


def arrived(first, second, near, far):
    if lax.axis_size("dp") != 4:
        return ([near[0]], [near[1]])
    return ([first, near[0], far[0], far[1]], [second, near[1], far[2], far[3]])


def row_cuts(depth):
    half = depth // 2
    if lax.axis_size("dp") != 4:
        return [(0, half), (half, depth), None, None]
    part = half // 2
    return [(part, half), (half + part, depth), (0, part), (half, half + part)]


def add(left, right):
    return left.astype(jnp.float32) + right.astype(jnp.float32)


def scatter_one(send_first, send_second):
    if lax.axis_size("dp") != 4:
        return [
            lax.psum_scatter(v, "dp", scatter_dimension=0, tiled=True)
            for v in (send_first, send_second)
        ]
    return [swap_x(send_first), swap_y(send_second)]


def scatter_two(keep_first, keep_second, got):
    if lax.axis_size("dp") != 4:
        return (got, [])
    stay, send = [], []
    for keep, new in zip((keep_first, keep_second), got):
        half = keep.shape[0] // 2
        send.append(add(keep[half:], new[half:]).astype(jnp.bfloat16))
        stay.append(add(keep[:half], new[:half]).astype(jnp.bfloat16))
    return (stay, [swap_y(send[0]), swap_x(send[1])])


def scatter_column(stay, come):
    if come:
        stay = [add(s, c).astype(jnp.bfloat16) for s, c in zip(stay, come)]
    return lax.psum_scatter(
        jnp.concatenate(stay, 0), "tensor", scatter_dimension=1, tiled=True
    )


def flip_axis(value, axis, bit):
    return jnp.where(bit == 1, jnp.flip(value, axis), value)


def relative(value, spot):
    n_dp = lax.axis_size("dp")
    lead = value.shape[:-1]
    k = len(lead)
    if n_dp != 4:
        cut = value.reshape(lead + (n_dp, 2, -1))
        return jnp.swapaxes(cut, k, k + 1).reshape(value.shape)
    cut = value.reshape(lead + (2, 2, 2, -1))
    cut = flip_axis(flip_axis(cut, k, spot // 2), k + 1, spot % 2)
    first = jnp.swapaxes(cut[..., 0, :], k, k + 1)
    second = cut[..., 1, :]
    return jnp.concatenate([first.reshape(lead + (-1,)), second.reshape(lead + (-1,))], -1)


def absolute(value, spot):
    n_dp = lax.axis_size("dp")
    lead = value.shape[:-1]
    k = len(lead)
    if n_dp != 4:
        cut = value.reshape(lead + (2, n_dp, -1))
        return jnp.swapaxes(cut, k, k + 1).reshape(value.shape)
    cut = value.reshape(lead + (2, 2, 2, -1))
    first = jnp.swapaxes(cut[..., 0, :, :, :], k, k + 1)
    second = cut[..., 1, :, :, :]
    cut = jnp.stack([first, second], k + 2)
    cut = flip_axis(flip_axis(cut, k, spot // 2), k + 1, spot % 2)
    return cut.reshape(value.shape)


def by_chip(blocks, spot):
    n_dp = lax.axis_size("dp")
    if n_dp != 4:
        return blocks
    cut = blocks.reshape((2, 2) + blocks.shape[1:])
    cut = jnp.swapaxes(cut, 0, 1)
    cut = flip_axis(flip_axis(cut, 0, spot // 2), 1, spot % 2)
    return cut.reshape(blocks.shape)


def by_arrival(blocks, spot):
    n_dp = lax.axis_size("dp")
    if n_dp != 4:
        return blocks
    cut = blocks.reshape((2, 2) + blocks.shape[1:])
    cut = flip_axis(flip_axis(cut, 0, spot // 2), 1, spot % 2)
    return jnp.swapaxes(cut, 0, 1).reshape(blocks.shape)


VMEM_BYTES = 50 * 2**20
BF = jnp.bfloat16
F32 = jnp.float32


def shape(dims, kind=jnp.bfloat16):
    return jax.ShapeDtypeStruct(dims, kind)


def run(kernel, outs, ins):
    block = pl.BlockSpec(memory_space=pltpu.VMEM)
    done = pl.pallas_call(
        kernel,
        out_shape=list(outs),
        in_specs=[block] * len(ins),
        out_specs=[block] * len(outs),
        cost_estimate=pl.CostEstimate(flops=1, bytes_accessed=1, transcendentals=0),
        compiler_params=pltpu.CompilerParams(vmem_limit_bytes=VMEM_BYTES),
    )(*ins)
    return list(done)


def nn(left, right):
    return lax.dot_general(left, right, (((1,), (0,)), ((), ())), preferred_element_type=F32)


def nt(left, right):
    return lax.dot_general(left, right, (((1,), (1,)), ((), ())), preferred_element_type=F32)


def tn(left, right):
    return lax.dot_general(left, right, (((0,), (0,)), ((), ())), preferred_element_type=F32)


def stack_rows(pieces, counts, cols):
    return jnp.concatenate([p[:n, cols] for p, n in zip(pieces, counts)], 0)


def center_scale(value):
    center = jnp.mean(value, -1, keepdims=True)
    spread = jnp.mean(value * value, -1, keepdims=True) - center * center
    factor = lax.rsqrt(spread + EPS)
    return ((value - center) * factor, factor)


def norm_backward(grad_normed, centred, factor, gain):
    scaled = grad_normed * gain
    return factor * (
        scaled
        - jnp.mean(scaled, -1, keepdims=True)
        - centred * jnp.mean(scaled * centred, -1, keepdims=True)
    )


def column_sum(value):
    return jnp.sum(value, 0, keepdims=True)


def attention_forward(tokens, terms, bias_row, low, weights, rows, q_bias, v_bias):
    pieces, counts = weights
    size, depth = terms[0].shape
    wide = pieces[0].shape[1]
    groups = wide // 512
    half = groups * 128
    n_terms, n_pieces = len(terms), len(pieces)

    def kernel(*refs):
        term_refs, refs = refs[:n_terms], refs[n_terms:]
        bias_ref, rows_ref, qb_ref, vb_ref = refs[:4]
        piece_refs, refs = refs[4 : 4 + n_pieces], refs[4 + n_pieces :]
        u_ref, n_ref, q_ref, k_ref, v_ref, p_ref, o_ref, part_ref = refs
        value = term_refs[0][...].astype(F32)
        for ref in term_refs[1:]:
            value = value + ref[...].astype(F32)
        if n_terms > 1:
            value = value + bias_ref[...]
        if low:
            value = value.astype(BF).astype(F32)
        u_ref[...] = value
        centred, factor = center_scale(value)
        n_ref[...] = (centred * rows_ref[0:1] + rows_ref[1:2]).astype(BF)
        lane = lax.broadcasted_iota(jnp.int32, (size, 128), 1)
        key_lane = lax.broadcasted_iota(jnp.int32, (size, size), 1)
        normed = n_ref[...]
        for g in range(groups):
            at = slice(g * 128, (g + 1) * 128)
            matrix = stack_rows(piece_refs, counts, slice(g * 512, g * 512 + 384))
            projected = nn(normed, matrix)
            q = (projected[:, :128] + qb_ref[:, at]).astype(BF)
            k = projected[:, 128:256].astype(BF)
            v = (projected[:, 256:384] + vb_ref[:, at]).astype(BF)
            q_ref[:, at] = q
            k_ref[:, at] = k
            v_ref[:, at] = v
            mixed = None
            for h in range(2):
                mine = (lane // HD) == h
                scores = nt(jnp.where(mine, q, jnp.zeros_like(q)), k) * HD ** (-0.5)
                scores = jnp.where(key_lane < tokens, scores, -1e30)
                highest = jnp.max(scores, -1, keepdims=True)
                exponent = jnp.exp(scores - highest)
                inverse = 1.0 / jnp.sum(exponent, -1, keepdims=True)
                soft = (exponent * inverse).astype(BF)
                p_ref[2 * g + h] = soft
                out = nn(soft, v)
                mixed = out if h == 0 else jnp.where(mine, out, mixed)
            o_ref[:, at] = mixed.astype(BF)
        matrix = jnp.concatenate(
            [stack_rows(piece_refs, counts, slice(g * 512 + 384, g * 512 + 512)) for g in range(groups)], 1
        )
        part_ref[...] = nt(o_ref[...], matrix).astype(BF)

    outs = [shape((size, depth), F32), shape((size, depth))] + [shape((size, half))] * 3
    outs += [shape((2 * groups, size, size)), shape((size, half)), shape((size, depth))]
    return run(kernel, outs, [*terms, bias_row, rows, q_bias, v_bias, *pieces])


def up_forward(terms, weights, rows, up_bias):
    pieces, counts = weights
    size, depth = terms[0].shape
    wide = pieces[0].shape[1]

    def kernel(*refs):
        u_ref, own_ref, far_ref, rows_ref, bias_ref = refs[:5]
        piece_refs = refs[5 : 5 + len(pieces)]
        mid_ref, n_ref, slope_ref, hidden_ref = refs[5 + len(pieces) :]
        value = u_ref[...] + own_ref[...].astype(F32) + far_ref[...].astype(F32) + rows_ref[4:5]
        mid_ref[...] = value
        centred, factor = center_scale(value)
        n_ref[...] = (centred * rows_ref[5:6] + rows_ref[6:7]).astype(BF)
        step = 512
        for at in range(0, wide, step):
            cols = slice(at, at + step)
            before = nn(n_ref[...], stack_rows(piece_refs, counts, cols)) + bias_ref[:, cols]
            cdf = 0.5 * (1.0 + lax.erf(before * 0.7071067811865476))
            density = jnp.exp(-0.5 * before * before) * 0.3989422804014327
            hidden_ref[:, cols] = (before * cdf).astype(BF)
            slope_ref[:, cols] = (cdf + before * density).astype(BF)

    outs = [shape((size, depth), F32), shape((size, depth)), shape((size, wide)), shape((size, wide))]
    return run(kernel, outs, [*terms, rows, up_bias, *pieces])


def contract_wide(left, weights):
    pieces, counts = weights
    size, wide = left.shape
    depth = sum(counts)

    def kernel(*refs):
        left_ref, piece_refs, out_ref = refs[0], refs[1:-1], refs[-1]
        matrix = stack_rows(piece_refs, counts, slice(0, wide))
        out_ref[...] = nt(left_ref[...], matrix).astype(BF)

    return run(kernel, [shape((size, depth))], [left, *pieces])[0]


def weight_outs(depth, wide):
    cuts = [c for c in row_cuts(depth) if c is not None]
    return cuts, [shape((c[1] - c[0], wide)) for c in cuts]


def fill(grads):
    return (list(grads) + [None, None])[:4]


def down_grad(grad_out, hidden):
    size, depth = grad_out.shape
    cuts, outs = weight_outs(depth, hidden.shape[1])

    def kernel(g_ref, hidden_ref, sum_ref, *refs):
        sum_ref[...] = column_sum(g_ref[...])
        branch = g_ref[...].astype(BF)
        for cut, ref in zip(cuts, refs):
            ref[...] = tn(branch[:, cut[0] : cut[1]], hidden_ref[...]).astype(BF)

    done = run(kernel, [shape((1, depth), F32)] + outs, [grad_out, hidden])
    return done[0], fill(done[1:])


def down_backward(grad_out, slope, weights):
    pieces, counts = weights
    size, depth = grad_out.shape
    wide = slope.shape[1]

    def kernel(*refs):
        g_ref, slope_ref, piece_refs = refs[0], refs[1], refs[2:-2]
        low_ref, bias_ref = refs[-2:]
        branch = g_ref[...].astype(BF)
        step = 512
        for at in range(0, wide, step):
            cols = slice(at, at + step)
            back = nn(branch, stack_rows(piece_refs, counts, cols)) * slope_ref[:, cols].astype(F32)
            bias_ref[:, cols] = column_sum(back)
            low_ref[:, cols] = back.astype(BF)

    outs = [shape((size, wide)), shape((1, wide), F32)]
    return run(kernel, outs, [grad_out, slope, *pieces])


def up_grad(normed, low):
    size, depth = normed.shape
    wide = low.shape[1]
    cuts, outs = weight_outs(depth, wide)

    def kernel(n_ref, low_ref, *refs):
        for cut, ref in zip(cuts, refs):
            ref[...] = tn(n_ref[:, cut[0] : cut[1]], low_ref[...]).astype(BF)

    return fill(run(kernel, outs, [normed, low]))


def attention_backward(grad_out, own, far, middle, rows, saved, weights):
    pieces, counts = weights
    size, depth = grad_out.shape
    wide = pieces[0].shape[1]
    groups = wide // 512
    half = groups * 128
    scale = HD ** (-0.5)

    def kernel(*refs):
        g_ref, own_ref, far_ref, mid_ref, rows_ref, q_ref, k_ref, v_ref, p_ref, o_ref = refs[:10]
        piece_refs, refs = refs[10 : 10 + len(pieces)], refs[10 + len(pieces) :]
        dmid_ref, dz_ref, dq_ref, dk_ref, dv_ref, part_ref, sum_ref, qs_ref, vs_ref = refs
        grad_normed = own_ref[...].astype(F32) + far_ref[...].astype(F32)
        centred, factor = center_scale(mid_ref[...])
        sum_ref[1:2] = column_sum(grad_normed * centred)
        sum_ref[2:3] = column_sum(grad_normed)
        dmid = g_ref[...] + norm_backward(grad_normed, centred, factor, rows_ref[5:6])
        dmid_ref[...] = dmid
        sum_ref[0:1] = column_sum(dmid)
        dz_ref[...] = dmid.astype(BF)
        lane = lax.broadcasted_iota(jnp.int32, (size, 128), 1)
        for g in range(groups):
            at = slice(g * 128, (g + 1) * 128)
            matrix = stack_rows(piece_refs, counts, slice(g * 512 + 384, g * 512 + 512))
            grad_mixed = nn(dz_ref[...], matrix).astype(BF)
            q, k, v = q_ref[:, at], k_ref[:, at], v_ref[:, at]
            inner = grad_mixed.astype(F32) * o_ref[:, at].astype(F32)
            dq, dk, dv = None, None, None
            for h in range(2):
                mine = (lane // HD) == h
                soft = p_ref[2 * g + h]
                none = jnp.zeros_like(q)
                do = jnp.where(mine, grad_mixed, none)
                total = jnp.sum(jnp.where(mine, inner, 0.0), -1, keepdims=True)
                grad_soft = nt(do, v)
                grad_scores = (soft.astype(F32) * (grad_soft - total)).astype(BF)
                new_q = nn(grad_scores, k)
                new_k = tn(jnp.where(mine, q, none), grad_scores)
                new_v = tn(do, soft)
                dq = new_q if h == 0 else jnp.where(mine, new_q, dq)
                dk = new_k if h == 0 else dk + new_k
                dv = new_v if h == 0 else dv + new_v
            dq, dk, dv = dq * scale, dk.T * scale, dv.T
            qs_ref[:, at] = column_sum(dq)
            vs_ref[:, at] = column_sum(dv)
            dq_ref[:, at] = dq.astype(BF)
            dk_ref[:, at] = dk.astype(BF)
            dv_ref[:, at] = dv.astype(BF)
        total = None
        for g in range(groups):
            at = slice(g * 128, (g + 1) * 128)
            left = jnp.concatenate([dq_ref[:, at], dk_ref[:, at], dv_ref[:, at]], 1)
            new = nt(left, stack_rows(piece_refs, counts, slice(g * 512, g * 512 + 384)))
            total = new if g == 0 else total + new
        part_ref[...] = total.astype(BF)

    outs = [shape((size, depth), F32), shape((size, depth))] + [shape((size, half))] * 3
    outs += [shape((size, depth)), shape((3, depth), F32)] + [shape((1, half), F32)] * 2
    return run(kernel, outs, [grad_out, own, far, middle, rows, *saved, *pieces])


def attention_grad(normed, dz, dq, dk, dv, mixed):
    size, depth = normed.shape
    groups = dq.shape[1] // 128
    cuts, outs = weight_outs(depth, groups * 512)

    def kernel(n_ref, dz_ref, dq_ref, dk_ref, dv_ref, o_ref, *refs):
        for cut, ref in zip(cuts, refs):
            rows = slice(cut[0], cut[1])
            for g in range(groups):
                at = slice(g * 128, (g + 1) * 128)
                right = jnp.concatenate([dq_ref[:, at], dk_ref[:, at], dv_ref[:, at]], 1)
                ref[:, g * 512 : g * 512 + 384] = tn(n_ref[:, rows], right).astype(BF)
                ref[:, g * 512 + 384 : g * 512 + 512] = tn(dz_ref[:, rows], o_ref[:, at]).astype(BF)

    return fill(run(kernel, outs, [normed, dz, dq, dk, dv, mixed]))


def value_backward(dmid, own, far, value, rows, low):
    size, depth = dmid.shape

    def kernel(dmid_ref, own_ref, far_ref, u_ref, rows_ref, out_ref, sum_ref):
        grad_normed = own_ref[...].astype(F32) + far_ref[...].astype(F32)
        centred, factor = center_scale(u_ref[...])
        sum_ref[0:1] = column_sum(grad_normed * centred)
        sum_ref[1:2] = column_sum(grad_normed)
        out = dmid_ref[...] + norm_backward(grad_normed, centred, factor, rows_ref[0:1])
        if low:
            out = out.astype(BF).astype(F32)
        out_ref[...] = out

    outs = [shape((size, depth), F32), shape((2, depth), F32)]
    return run(kernel, outs, [dmid, own, far, value, rows])


def block_lanes(spot, chunk):
    ry, rx = chunk // 2 ^ spot // 2, chunk % 2 ^ spot % 2
    return [(rx * 2 + ry) * 128, 512 + (ry * 2 + rx) * 128]


def place_in(lanes, blocks):
    size, width = blocks[0].shape
    half = width // 2

    def kernel(lanes_ref, *refs):
        out_ref = refs[-1]
        for d, ref in enumerate(refs[:-1]):
            for h in range(2):
                at = pl.multiple_of(lanes_ref[2 * d + h], 128)
                out_ref[:, pl.ds(at, half)] = ref[:, h * half : (h + 1) * half]

    block = pl.BlockSpec(memory_space=pltpu.VMEM)
    return pl.pallas_call(
        kernel,
        out_shape=shape((size, width * len(blocks))),
        in_specs=[pl.BlockSpec(memory_space=pltpu.SMEM)] + [block] * len(blocks),
        out_specs=block,
        compiler_params=pltpu.CompilerParams(vmem_limit_bytes=VMEM_BYTES),
    )(lanes, *blocks)


def place_out(numbers, scale, terms, bias_row, count):
    size, depth = terms[0].shape
    width = depth // count
    half = width // 2

    def kernel(numbers_ref, scale_ref, *refs):
        term_refs, bias_ref, out_ref = refs[: len(terms)], refs[-2], refs[-1]
        start = pl.multiple_of(numbers_ref[2 * count], 8)
        rows = pl.ds(start, size // 2)
        for d in range(count):
            for h in range(2):
                lanes = pl.ds(pl.multiple_of(numbers_ref[2 * d + h], 128), half)
                value = term_refs[0][rows, lanes]
                for ref in term_refs[1:]:
                    value = value + ref[rows, lanes]
                value = (value + bias_ref[:, lanes]) * scale_ref[0]
                out_ref[d, :, h * half : (h + 1) * half] = value.astype(BF)

    block = pl.BlockSpec(memory_space=pltpu.VMEM)
    scalar = pl.BlockSpec(memory_space=pltpu.SMEM)
    return pl.pallas_call(
        kernel,
        out_shape=shape((count, size // 2, width)),
        in_specs=[scalar, scalar] + [block] * (len(terms) + 1),
        out_specs=block,
        compiler_params=pltpu.CompilerParams(vmem_limit_bytes=VMEM_BYTES),
    )(numbers, scale, *terms, bias_row)


def shift(block, d):
    n = lax.axis_size("tensor")
    return lax.ppermute(block, "tensor", [(i, (i + d) % n) for i in range(n)])


def shifts(blocks):
    return [blocks[0]] + [shift(block, d) for d, block in enumerate(blocks) if d > 0]


def half_cols(core, whole, n_tensor):
    cut = whole.reshape(whole.shape[:-1] + (n_tensor, 2, -1))
    cut = jnp.where(core == 0, cut[..., 0, :], cut[..., 1, :])
    return cut.reshape(whole.shape[:-1] + (-1,))


def spread_cols(core, half, n_tensor):
    cut = half.reshape(half.shape[:-1] + (n_tensor, 1, -1))
    none = jnp.zeros_like(cut)
    both = jnp.concatenate(
        [jnp.where(core == 0, cut, none), jnp.where(core == 0, none, cut)], -2
    )
    return both.reshape(half.shape[:-1] + (-1,))


def body(boundary_in, counts, qkv_weight, proj_weight, fc1_weight, fc2_weight, vectors, fc1_bias):
    core = lax.axis_index("section")
    is_first = core == 0
    place = lax.axis_index("tensor")
    spot = lax.axis_index("dp")
    n_dp, n_tensor = lax.axis_size("dp"), lax.axis_size("tensor")
    slots_per_batch = boundary_in.shape[1] // counts.shape[1]
    live = (place % slots_per_batch < counts[0, place // slots_per_batch]).astype(jnp.float32)
    depth = qkv_weight.shape[1]
    mid = depth // 2
    n_vec = vectors.size

    small_size = n_vec + fc1_bias.size
    packs = []
    for part in range(2):
        cuts = [
            jnp.split(qkv_weight[0], 2, 2)[part].reshape(depth, -1),
            jnp.split(proj_weight[0], 2, 0)[part].T,
            jnp.split(fc1_weight[0], 2, 1)[part],
            jnp.split(fc2_weight[0], 2, 0)[part].T,
        ]
        packs.append(jnp.concatenate(cuts, 1))
    wide = packs[0].shape[1] // 3
    extra = 16
    small = jnp.concatenate([vectors.reshape(-1), fc1_bias.reshape(-1)])
    small = jnp.pad(small, (0, extra * wide - small_size)).reshape(extra, wide)
    small = jnp.pad(small, ((0, 0), (0, 2 * wide)))
    kept = jnp.concatenate([jnp.where(is_first, packs[0], packs[1]), small], 0)
    received = swap(
        jnp.concatenate([jnp.where(is_first, packs[1], packs[0]), small], 0)
    )
    shards = (jnp.where(is_first, kept, received), jnp.where(is_first, received, kept))
    columns = []
    for layer in range(2):
        for number in range(3):
            cols = shards[layer][:, number * wide : (number + 1) * wide]
            if layer == 0 and number == 0:
                room = extra // 2
                both = [shard[depth : depth + room, :wide] for shard in shards]
                cols = jnp.concatenate([cols[:depth], *both], 0)
            else:
                cols = cols[:depth]
            columns.append(cols)

    tokens = boundary_in.shape[2]
    pad = -tokens % 16
    reach = (tokens + pad) // 2
    ends_in = jnp.pad(boundary_in[0].astype(jnp.bfloat16), ((0, 0), (0, pad), (0, 0)))
    ends_low, ends_high = ends_in[:, :reach], ends_in[:, reach:]
    ends_got = swap(jnp.where(is_first, ends_high, ends_low))
    half_in = jnp.where(is_first, ends_low, ends_got)
    half_cot = jnp.where(is_first, ends_got, ends_high)

    below = [(place - d) % n_tensor for d in range(n_tensor)]
    above = [(place + d) % n_tensor for d in range(n_tensor)]

    def to_send(half):
        return [lax.dynamic_index_in_dim(half, j, 0, False) for j in above]

    def image_half(blocks):
        if n_dp == 4:
            lanes = [lane for t in below for lane in block_lanes(spot, t)]
            return place_in(jnp.stack(lanes).astype(jnp.int32), blocks)
        blocks = jnp.stack(blocks)
        blocks = [lax.dynamic_index_in_dim(blocks, (place - i) % n_tensor, 0, False) for i in range(n_tensor)]
        return relative(jnp.concatenate(blocks, 1), spot)

    def whole_image(half):
        other = swap(half)
        both = [jnp.where(is_first, half, other), jnp.where(is_first, other, half)]
        return jnp.concatenate(both, 0)

    def image_rows(scale, terms, bias_row):
        if n_dp == 4:
            numbers = [lane for t in above for lane in block_lanes(spot, t)]
            numbers.append(jnp.where(is_first, 0, reach))
            numbers = jnp.stack(numbers).astype(jnp.int32)
            blocks = place_out(numbers, scale.reshape(1), terms, bias_row, n_tensor)
            return [blocks[d] for d in range(n_tensor)]
        image = absolute((sum(terms[1:], terms[0]) + bias_row) * scale, spot).astype(jnp.bfloat16)
        half = jnp.where(is_first, image[:reach], image[reach:])
        half = half.reshape(reach, n_tensor, -1).transpose(1, 0, 2)
        return to_send(half)

    def by_image(blocks):
        blocks = jnp.stack(blocks)
        blocks = [lax.dynamic_index_in_dim(blocks, (place - i) % n_tensor, 0, False) for i in range(n_tensor)]
        return jnp.stack(blocks)

    def small_of(extras):
        if n_dp != 4:
            extras = lax.all_gather(extras, "dp", axis=0, tiled=True)
        else:
            over = lax.ppermute(extras, "dp", [(i, i ^ 3) for i in range(n_dp)])
            extras = jnp.concatenate([extras, swap_y(extras), swap_x(extras), over], 0)
        both = by_chip(extras.reshape(n_dp, extra, -1), spot).astype(jnp.float32)
        both = both.reshape(n_dp, 2, extra // 2, n_tensor, wide).transpose(1, 0, 3, 2, 4)
        both = both.reshape(2, n_dp, n_tensor, -1)
        rows = both[..., :n_vec].reshape(2, n_dp, n_tensor, 8, -1)
        rows = relative(rows.transpose(0, 3, 2, 1, 4).reshape(2, 8, -1), spot)
        bias = both[..., n_vec:small_size].transpose(0, 2, 1, 3).reshape(2, -1)
        plain = both[..., :n_vec].reshape(2, n_dp, n_tensor, 8, -1)[..., 2:4, :]
        plain = plain.transpose(0, 3, 2, 1, 4).reshape(2, 2, -1)
        parts = [half_cols(core, plain[:, 0], n_tensor), half_cols(core, plain[:, 1], n_tensor)]
        parts.append(half_cols(core, bias, n_tensor))
        return [(rows[i], parts[0][i : i + 1], parts[1][i : i + 1], parts[2][i : i + 1]) for i in range(2)]

    number = len(columns)
    halves, near, far = [None] * number, [None] * number, [None] * number
    params = [dict(), dict()]
    blocks_in, blocks_cot = to_send(half_in), to_send(half_cot)
    pair, state = None, None

    def weights_of(k):
        first, second = arrived(*halves[k], near[k], far[k])
        return (first + second, [p.shape[0] for p in first + second])

    for r in range(number + 1):
        tied = []
        if r < number:
            tied.append(gather_column(columns[r]))
        if 0 <= r - 1 < number:
            near[r - 1] = exchange_one(*halves[r - 1])
        if r == 1:
            smalls = small_of(extra_rows)
            blocks_in = shifts(blocks_in)
        if 2 <= r <= 1 + n_tensor - 1:
            blocks_cot[r - 1] = shift(blocks_cot[r - 1], r - 1)
        if r == number - 1:
            cot_half = image_half(blocks_cot)
        if r == number:
            cotangent = whole_image(cot_half).astype(jnp.float32) * live
        ready = []
        k = r - 2
        if k >= 0:
            layer, kind = k // 3, k % 3
            one = params[layer]
            weights = weights_of(k)
            rows, q_bias, v_bias, up_bias = one["small"]
            if pair is not None:
                pair = [pair[0], swap(pair[0])]
            if kind == 0:
                one["qkvo"] = weights
                if layer == 0:
                    terms = [whole_image(image_half(blocks_in)).astype(jnp.float32)]
                else:
                    terms = [state, *pair]
                bias_row = params[0]["small"][0][7:8]
                done = attention_forward(
                    tokens, terms, bias_row, layer == 1, weights, rows, q_bias, v_bias
                )
                one["u"], one["n1"], one["saved"], part = done[0], done[1], done[2:7], done[7]
                pair, ready = [part], [part]
            elif kind == 1:
                one["up"] = weights
                one["mid"], one["n2"], one["slope"], one["hidden"] = up_forward(
                    [one["u"], *pair], weights, rows, up_bias
                )
                pair, ready = None, [one["hidden"]]
            else:
                one["down"] = weights
                state = one["mid"]
                part = contract_wide(one["hidden"], weights)
                pair, ready = [part], [part]
        if r <= number:
            count = len(ready)
            extras = list(ready)
            if 0 <= r - 1 < number:
                if ready:
                    done = tie(near[r - 1] + extras, [])
                    near[r - 1], extras = done[: len(near[r - 1])], done[len(near[r - 1]) :]
                far[r - 1] = exchange_two(*halves[r - 1], *near[r - 1])
                tied += near[r - 1] + far[r - 1]
            if r == number:
                last_sum, first_grads = down_grad(cotangent, extras[0])
                first_grads = [g for g in first_grads if g is not None]
                extras += first_grads
            if r <= 1:
                extras += blocks_in
            if r == 1:
                extras += [v for layer in range(2) for v in smalls[layer]]
            if 1 <= r <= number - 2:
                extras += blocks_cot
            elif r == number - 1:
                extras.append(cot_half)
            elif r == number:
                extras.append(cotangent)
            if r + 1 < number:
                extras.append(columns[r + 1])
            done = tie(tied + extras, [])
            if r + 1 < number:
                columns[r + 1] = done.pop()
            if 1 <= r <= number - 2:
                done, blocks_cot = done[:-n_tensor], done[-n_tensor:]
            elif r == number - 1:
                cot_half = done.pop()
            elif r == number:
                cotangent = done.pop()
                done, first_grads = done[: -len(first_grads)], done[-len(first_grads) :]
            if r == 1:
                done, smalls = done[:-8], done[-8:]
                params[0]["small"], params[1]["small"] = smalls[:4], smalls[4:]
            if r <= 1:
                done, blocks_in = done[:-n_tensor], done[-n_tensor:]
            if count and kind == 1:
                one["hidden"] = done[-1]
            elif count:
                pair = [done[-1]]
            at = 0
            if r < number:
                halves[r] = (done[0][:mid], done[0][mid:depth])
                if r == 0:
                    extra_rows = done[0][depth:]
                at = 1
            if 0 <= r - 1 < number:
                near[r - 1] = done[at : at + 2]
                far[r - 1] = done[at + 2 : at + 2 + len(far[r - 1])]

    sums = [dict(), dict()]

    def small_grads():
        packed = []
        for layer in range(2):
            total = sums[layer]
            full = jnp.concatenate([total["one"], total["mid"], total["out"]], 0)
            full = absolute(jnp.where(core == layer, full, 0.0), spot)
            q_row = spread_cols(core, total["q"][0], n_tensor)
            v_row = spread_cols(core, total["v"][0], n_tensor)
            up_row = spread_cols(core, total["up_bias"][0], n_tensor)
            rows = jnp.concatenate([full[:2], q_row[None], v_row[None], full[2:]], 0)
            rows = rows.reshape(8, n_tensor, n_dp, -1).transpose(2, 1, 0, 3).reshape(n_dp, n_tensor, -1)
            up_row = up_row.reshape(n_tensor, n_dp, -1).transpose(1, 0, 2)
            packed.append(jnp.concatenate([rows, up_row], -1))
        ours = jnp.where(is_first, packed[0], packed[1])
        other = swap(jnp.where(is_first, packed[1], packed[0]))
        little = (ours + other).astype(jnp.bfloat16)
        return little

    grads, got, moved, settled = [None] * number, [None] * number, [None] * number, [None] * number
    made = [0, 1, 3, 4, 5, 6]
    column_at = [4, 5, 6, 7]
    grad = cotangent
    last_down = weights_of(number - 1)
    params[1]["down"] = last_down
    last_bias = params[1]["small"][0][7:8]
    grads[0] = fill(first_grads)
    sums[1]["out"] = last_sum
    for r in range(1, 8):
        layer, stage = 1 - r // 4, r % 4
        one, total = params[layer], sums[layer]
        rows = one["small"][0]
        tied, slots = [], []
        for c in range(number):
            if r == made[c] + 1:
                got[c] = scatter_one(*grads[c][:2])
                slots.append((got, c, len(got[c])))
                tied += got[c]
            elif r == made[c] + 2:
                stay, come = scatter_two(*grads[c][2:], got[c])
                moved[c] = [*stay, *come]
                if r < 7:
                    slots.append((moved, c, len(moved[c])))
                    tied += moved[c]
            elif c < len(column_at) and r == column_at[c]:
                settled[c] = scatter_column(moved[c][:2], moved[c][2:])
                slots.append((settled, c, 0))
                tied.append(settled[c])
        new = None
        if stage == 0:
            total["out"], new = down_grad(grad, one["hidden"])
        if stage == 0 or r == 1:
            low, total["up_bias"] = down_backward(grad, one["slope"], one["down"])
            carry = [low]
        if stage == 1:
            part = contract_wide(low, one["up"])
            new = up_grad(one["n2"], low)
            carry = [part]
        if stage == 2:
            done = attention_backward(
                grad, part, swap(part), one["mid"], rows, one["saved"], one["qkvo"]
            )
            dmid, dz, dq, dk, dv, part, total["mid"], total["q"], total["v"] = done
            if layer == 0:
                new = attention_grad(one["n1"], dz, dq, dk, dv, one["saved"][4])
            carry = [part]
        if stage == 3:
            if layer == 1:
                new = attention_grad(one["n1"], dz, dq, dk, dv, one["saved"][4])
            grad, total["one"] = value_backward(dmid, part, swap(part), one["u"], rows, layer == 1)
            carry = [grad]
            if r == 7:
                done = tie([grad, *moved[4]], [])
                grad, moved[4] = done[0], done[1:]
                settled[4] = scatter_column(moved[4][:2], moved[4][2:])
                one_scale = jnp.ones((), jnp.float32)
                no_bias = jnp.zeros((1, grad.shape[1]), jnp.float32)
                carry = [small_grads(), *shifts(image_rows(one_scale, [grad], no_bias))]
        if new is not None:
            c = made.index(r)
            grads[c] = new
            fresh = [g for g in new if g is not None]
        else:
            fresh = []
        if r == 3:
            last_part = contract_wide(params[1]["hidden"], last_down)
            carry.append(last_part)
        elif r == 4:
            out_blocks = image_rows(
                live, [params[1]["mid"], last_part, swap(last_part)], last_bias
            )
        if 4 <= r < 7:
            for d in ((), (1,), range(2, n_tensor))[r - 4]:
                out_blocks[d] = shift(out_blocks[d], d)
            carry += out_blocks
        if r < 8:
            done = tie(carry + fresh + tied, [])
            if stage == 0:
                low = done[0]
            elif stage == 1:
                part = done[0]
            elif stage == 2:
                part = done[0]
            elif r < 7:
                grad = done[0]
            else:
                little, grad_blocks = done[0], done[1 : 1 + n_tensor]
            if r == 3:
                last_part = done[1]
            elif 4 <= r < 7:
                out_blocks = done[1 : 1 + n_tensor]
            done = done[len(carry) :]
            if fresh:
                grads[c] = fill(done[: len(fresh)])
                done = done[len(fresh) :]
            for store, at, count in slots:
                store[at] = done[:count] if count else done[0]
                done = done[max(count, 1) :]

    room = jnp.zeros((n_dp, n_tensor, extra * wide - small_size), little.dtype)
    little = jnp.concatenate([little, room], -1).reshape(n_dp, n_tensor, extra, wide)
    little = by_arrival(little.transpose(0, 2, 1, 3).reshape(n_dp, extra, -1), spot)
    if n_dp != 4:
        little = lax.psum_scatter(little, "dp", scatter_dimension=0, tiled=True)[0]
    else:
        over = lax.ppermute(little[3], "dp", [(i, i ^ 3) for i in range(n_dp)])
        little = add(little[0], swap_y(little[1])) + add(swap_x(little[2]), over)
        little = little.astype(jnp.bfloat16)

    last = number - 1
    stay, come = scatter_two(*grads[last][2:], got[last])
    grad_rows, out_rows = by_image(grad_blocks), by_image(out_blocks)
    if come:
        stay = [add(s, c).astype(jnp.bfloat16) for s, c in zip(stay, come)]
    settled[last] = scatter_column([*stay, little], [])
    little = settled[last][depth:].reshape(-1).astype(jnp.float32)
    settled[last] = settled[last][:depth]
    grad_vectors = little[:n_vec].reshape(vectors.shape)
    grad_bias = little[n_vec:small_size].reshape(fc1_bias.shape)

    own = jnp.where(is_first, grad_rows, out_rows)
    other = swap(jnp.where(is_first, out_rows, grad_rows))
    ends = [jnp.where(is_first, own, other), jnp.where(is_first, other, own)]
    boundary_out = jnp.concatenate(ends, 1)[:, :tokens].astype(jnp.float32)[None]
    lows, highs = [], []
    for kind in range(3):
        first, second = settled[last - kind], settled[last - kind - 3]
        kept = jnp.where(is_first, first, second)
        received = swap(jnp.where(is_first, second, first))
        lows.append(jnp.where(is_first, kept, received).astype(jnp.float32))
        highs.append(jnp.where(is_first, received, kept).astype(jnp.float32))
    low, high = [part[0].reshape(depth, 4, -1) for part in (lows, highs)]
    grad_qkv = jnp.concatenate([low[:, :3], high[:, :3]], 2)[None]
    grad_proj = jnp.concatenate([low[:, 3].T, high[:, 3].T], 0)[None]
    grad_up = jnp.concatenate([lows[1], highs[1]], 1)[None]
    grad_down = jnp.concatenate([lows[2].T, highs[2].T], 0)[None]
    return (boundary_out, grad_qkv, grad_proj, grad_up, grad_down, grad_vectors, grad_bias)


def solution(mesh):
    in_specs = (
        P("section", "dp", None, "tensor"),
        P("dp", None),
        P("section", "dp", None, "tensor"),
        P("section", "tensor", "dp"),
        P("section", "dp", "tensor"),
        P("section", "tensor", "dp"),
        P("section", None, "tensor", "dp"),
        P("section", "tensor", "dp"),
    )
    out_specs = (
        P("section", "dp", None, "tensor"),
        P("section", "dp", None, "tensor"),
        P("section", "tensor", "dp"),
        P("section", "dp", "tensor"),
        P("section", "tensor", "dp"),
        P("section", None, "tensor", "dp"),
        P("section", "tensor", "dp"),
    )
    return jax.shard_map(body, mesh=mesh, in_specs=in_specs, out_specs=out_specs, check_vma=False)
```
